32 devices in a mesh: dp: 8 (over z, x), cls: 4 (over y, core).
Axes of the slice: x: 2, y: 2, z: 4, core: 2. Of those that a mesh axis runs over, the one named last changes fastest.
Arguments:
- particles: bfloat16 [64, 2, 288, 128], P('dp'), may hold values from -20 to 20
- references: bfloat16 [288, 2, 200, 128], P('dp', None, 'cls'), may hold values from -9 to 9
- ctf_table: float32 [16, 128], replicated, may hold values from -0.1 to 0.1
- rot_offset: int32 [200], P('cls'), may hold values from 0 to 7
- prior_shift: int32 [64, 2], P('dp'), may hold values from -8 to 8
- defocus_group: int32 [64], P('dp'), may hold values from 0 to 15
Outputs:
- log_evidence: float32 [64], P('dp')
- class_posterior: float32 [64, 200], P('dp', 'cls')
- class_sums: float32 [288, 2, 200, 128], P('dp', None, 'cls')
The draws below stay inside these ranges and needn't reach their ends.
All inputs are finite; a program needn't handle non-finite values.
Results may differ from the reference program's by a relative error of at most 0.0056.
Values may be sent and summed in bfloat16 or wider, within the bound.
No kernel may reach another device: no remote copies, remote signals or barrier semaphores. Data moves between devices by JAX's collectives and lax.ppermute only.
A program may use at most 384 MiB of HBM per device.

```python
import math
import jax
import jax.numpy as jnp
from jax import lax

CYCLES = 128
ROTS = 36
ANG_STEP = 8
ANGLES = 288
SHIFT_SIDE = 5
CLASSES = 200
GROUPS = 16
PARTICLES = 64


def shared_integers(key):
    offsets = jax.random.randint(jax.random.fold_in(key, 11), (PARTICLES, 2), -8, 9).astype(jnp.int32)
    offsets = offsets.at[0, 0].set(8).at[0, 1].set(-8)
    groups = jax.random.randint(jax.random.fold_in(key, 12), (PARTICLES,), 0, GROUPS).astype(jnp.int32)
    particle_index = jnp.arange(PARTICLES, dtype=jnp.int32)
    groups = jnp.where(particle_index % 8 == 5, GROUPS - 1, groups).astype(jnp.int32)
    groups = groups.at[0].set(GROUPS - 1).at[1].set(0)
    rotation = jax.random.randint(jax.random.fold_in(key, 13), (CLASSES,), 0, ANG_STEP).astype(jnp.int32)
    rotation = rotation.at[0].set(ANG_STEP - 1).at[1].set(0)
    return (offsets, groups, rotation)


def shared_floats(key):
    spectra_all = jnp.clip(jax.random.normal(jax.random.fold_in(key, 21), (ANGLES, 2, CLASSES, CYCLES), jnp.float32), -6.0, 6.0) * 1.5
    amplitude = jnp.exp(jax.random.uniform(jax.random.fold_in(key, 23), (GROUPS, 1), jnp.float32, math.log(0.01), math.log(0.1)))
    amplitude = amplitude.at[GROUPS - 1, 0].set(0.1)
    ctf_rows = amplitude * jax.random.uniform(jax.random.fold_in(key, 22), (GROUPS, CYCLES), jnp.float32, -1.0, 1.0)
    return (spectra_all, ctf_rows)


def draw_references(key, part):
    return shared_floats(key)[0].astype(jnp.bfloat16)


def draw_ctf_table(key, part):
    return shared_floats(key)[1].astype(jnp.float32)


def draw_rot_offset(key, part):
    return shared_integers(key)[2]


def draw_prior_shift(key, part):
    return shared_integers(key)[0]


def draw_defocus_group(key, part):
    return shared_integers(key)[1]


def draw_particles(key, part):
    noise_field = jnp.clip(jax.random.normal(jax.random.fold_in(key, 31), (PARTICLES, 2, ANGLES, CYCLES), jnp.float32), -6.0, 6.0)
    return noise_field.astype(jnp.bfloat16)


def setup_inputs(seed: int = 0) -> dict:
    streams_of = jax.random.split(jax.random.key(seed), 7)
    return {
        "particles": draw_particles(jax.random.fold_in(streams_of[6], 71), 0),
        "references": draw_references(jax.random.fold_in(streams_of[6], 71), 0),
        "ctf_table": draw_ctf_table(jax.random.fold_in(streams_of[6], 71), 0),
        "rot_offset": draw_rot_offset(jax.random.fold_in(streams_of[6], 71), 0),
        "prior_shift": draw_prior_shift(jax.random.fold_in(streams_of[6], 71), 0),
        "defocus_group": draw_defocus_group(jax.random.fold_in(streams_of[6], 71), 0),
    }


two_pi = 2.0 * math.pi


def fourier_rows(angles):
    index_grid = jnp.arange(angles, dtype=jnp.int32)
    phase_index = (index_grid[:, None] * index_grid[None, :]) % angles
    radians = phase_index.astype(jnp.float32) * (two_pi / angles)
    cosine = jnp.cos(radians)
    sine_part = jnp.sin(radians)
    table_full = jnp.stack([jnp.stack([cosine, sine_part], 1), jnp.stack([-sine_part, cosine], 1)], 1)
    return table_full.reshape(2 * angles, 2 * angles).astype(jnp.bfloat16)


def rotation_tables(freq_rows, offsets, angles):
    rotation_steps = jnp.arange(ROTS, dtype=jnp.int32) * ANG_STEP
    angle_grid = rotation_steps[None, :] + offsets[:, None]
    phase_index = (freq_rows[:, None, None] * angle_grid[None, :, :]) % angles
    radians = phase_index.astype(jnp.float32) * (two_pi / angles)
    return jnp.cos(radians), jnp.sin(radians)


def reference(particles, references, ctf_table, rot_offset, prior_shift, defocus_group):
    angles = ANGLES
    cycles = CYCLES
    shifts = SHIFT_SIDE * SHIFT_SIDE
    top_score_value = lax.Precision.HIGHEST
    table_wide = fourier_rows(angles).astype(jnp.float32)
    spectra_all = references.astype(jnp.float32)
    power_sums = jnp.einsum('mxcr,gr->cg', spectra_all * spectra_all, ctf_table * ctf_table, precision=top_score_value)
    cos_all, sin_all = rotation_tables(jnp.arange(angles, dtype=jnp.int32), rot_offset, angles)
    theta_grid = jnp.arange(angles, dtype=jnp.int32).astype(jnp.float32) * (two_pi / angles)
    radius = (jnp.arange(cycles, dtype=jnp.int32) + 1).astype(jnp.float32) / (2.0 * cycles)
    shift_index = jnp.arange(shifts, dtype=jnp.int32)
    along_x = shift_index // SHIFT_SIDE - SHIFT_SIDE // 2
    along_y = shift_index % SHIFT_SIDE - SHIFT_SIDE // 2

    def one_particle(summed, inputs):
        image, offset, group = inputs
        shift_x = (offset[0] + along_x).astype(jnp.float32)
        shift_y = (offset[1] + along_y).astype(jnp.float32)
        argument = two_pi * radius[None, None, :] * (shift_x[None, :, None] * jnp.cos(theta_grid)[:, None, None]
                                                      + shift_y[None, :, None] * jnp.sin(theta_grid)[:, None, None])
        cosine = jnp.cos(argument)
        sine_part = jnp.sin(argument)
        real_part = image[0].astype(jnp.float32)[:, None, :]
        imag_part = image[1].astype(jnp.float32)[:, None, :]
        shifted = jnp.stack([real_part * cosine + imag_part * sine_part,
                             imag_part * cosine - real_part * sine_part]).astype(jnp.bfloat16)
        shifted = lax.optimization_barrier(shifted).astype(jnp.float32)
        spectrum = jnp.dot(table_wide, shifted.reshape(2 * angles, shifts * cycles), precision=top_score_value)
        spectrum = spectrum.reshape(angles, 2, shifts, cycles)
        ctf_row = ctf_table[group]
        weighted = (spectrum * ctf_row[None, None, None, :]).astype(jnp.bfloat16)
        weighted = lax.optimization_barrier(weighted).astype(jnp.float32)
        product = jnp.einsum('mxsr,mycr->mxsyc', weighted, spectra_all, precision=top_score_value)
        real_correlation = product[:, 0, :, 0] + product[:, 1, :, 1]
        imag_correlation = product[:, 1, :, 0] - product[:, 0, :, 1]
        cross_sums = (jnp.einsum('msc,mck->sck', real_correlation, cos_all, precision=top_score_value)
                      - jnp.einsum('msc,mck->sck', imag_correlation, sin_all, precision=top_score_value))
        class_power = power_sums[:, group]
        scores = cross_sums / angles - 0.5 * class_power[None, :, None] / angles
        peak_score = jnp.max(scores)
        log_total = peak_score + jnp.log(jnp.sum(jnp.exp(scores - peak_score)))
        weights = jnp.exp(scores - log_total)
        posterior = jnp.sum(weights, axis=(0, 2))
        real_returned = jnp.einsum('sck,mck->msc', weights, cos_all, precision=top_score_value).astype(jnp.bfloat16)
        imag_returned = jnp.einsum('sck,mck->msc', weights, sin_all, precision=top_score_value).astype(jnp.bfloat16)
        real_returned = lax.optimization_barrier(real_returned).astype(jnp.float32)
        imag_returned = lax.optimization_barrier(imag_returned).astype(jnp.float32)
        weighted_real = weighted[:, 0]
        weighted_imaginary = weighted[:, 1]
        real_accumulated = (jnp.einsum('jlh,jlv->jhv', real_returned, weighted_real, precision=top_score_value)
                    - jnp.einsum('jlh,jlv->jhv', imag_returned, weighted_imaginary, precision=top_score_value))
        imag_accumulated = (jnp.einsum('jlh,jlv->jhv', real_returned, weighted_imaginary, precision=top_score_value)
                    + jnp.einsum('jlh,jlv->jhv', imag_returned, weighted_real, precision=top_score_value))
        summed = summed + jnp.stack([real_accumulated, imag_accumulated], 1)
        return summed, (log_total, posterior)

    start_sums = jnp.zeros((angles, 2, CLASSES, cycles), jnp.float32)
    summed, outputs = lax.scan(one_particle, start_sums, (particles, prior_shift, defocus_group))
    log_evidence, class_posterior = outputs
    return log_evidence, class_posterior, summed
```

```python
import functools
import math

import jax
import jax.numpy as jnp
import ml_dtypes
import numpy as np
from jax import lax
from jax.experimental import pallas as pl
from jax.experimental.pallas import tpu as pltpu
from jax.sharding import PartitionSpec as P

ROTS = 36
ANG_STEP = 8
SHIFT_SIDE = 5
SHIFTS = SHIFT_SIDE * SHIFT_SIDE
LANES = 128
HALF = 64
GROUP = 4
ROWS = 16
FOLD = ROTS // 2 + 1

two_pi = 2.0 * math.pi
f32 = jnp.float32
bf16 = jnp.bfloat16
VMEM_LIMIT = 56 * 1024 * 1024


def fourier_rows(angles):
    index_grid = np.arange(angles)
    radians = (index_grid[:, None] * index_grid[None, :] % angles) * (two_pi / angles)
    cosine, sine_part = np.cos(radians), np.sin(radians)
    table_full = np.concatenate(
        [np.concatenate([cosine, sine_part], 1), np.concatenate([-sine_part, cosine], 1)], 0
    )
    return table_full.astype(np.float32).astype(ml_dtypes.bfloat16)


def shift_tables(angles, cycles):
    theta = np.arange(angles) * (two_pi / angles)
    radius = (np.arange(cycles) + 1) / (2.0 * cycles)
    turns = np.stack([np.cos(theta), np.sin(theta)])[:, :, None] * radius
    steps = np.arange(SHIFT_SIDE) - SHIFT_SIDE // 2
    phase = two_pi * turns[:, None] * steps[None, :, None, None]
    factors = np.stack([np.cos(phase), -np.sin(phase)], 2)
    return turns.astype(np.float32), factors.astype(np.float32)


def fold_tables():
    k = np.arange(FOLD // 2 + 1)[:, None]
    m = np.arange(FOLD)[None, :]
    radians = (k * m % ROTS) * (two_pi / ROTS)
    cosine = np.repeat(np.cos(radians)[:, :, None], HALF, 2)
    sine_part = np.repeat(np.sin(radians)[:, :, None], HALF, 2)
    to_score = np.concatenate([cosine, -sine_part], 2).astype(np.float32)
    to_back = np.concatenate([cosine, sine_part], 2).astype(np.float32)
    return to_score.reshape(-1, LANES), to_back.reshape(-1, LANES)


def cos_sin_of_turns(turns):
    frac = turns - jnp.floor(turns + 0.5)
    w = frac * two_pi
    w2 = w * w
    cosine = jnp.full_like(w, 1.0 / math.factorial(16))
    for n in range(14, -1, -2):
        cosine = cosine * w2 + (-1.0) ** (n // 2) / math.factorial(n)
    sine_part = jnp.full_like(w, 1.0 / math.factorial(17))
    for n in range(15, 0, -2):
        sine_part = sine_part * w2 + (-1.0) ** (n // 2) / math.factorial(n)
    return cosine, sine_part * w


def spectra_kernel(
    shift_ref, part_ref, ctf_ref, table_ref, turns_ref, factor_ref, out_ref, base_ref, data_ref, re_ref, im_ref
):
    step = pl.program_id(0)
    count, _, angles, cycles = part_ref.shape
    chunk = 32
    per_step = ROWS // count if count < ROWS else 1

    @pl.when(step == 0)
    def _():
        for p in range(count):
            sx = shift_ref[p, 0].astype(f32)
            sy = shift_ref[p, 1].astype(f32)

            def turn(n, carry):
                rows = pl.ds(pl.multiple_of(n * chunk, chunk), chunk)
                cosine, sine_part = cos_sin_of_turns(sx * turns_ref[0, rows, :] + sy * turns_ref[1, rows, :])
                re = part_ref[p, 0, rows, :].astype(f32)
                im = part_ref[p, 1, rows, :].astype(f32)
                base_ref[p, 0, rows, :] = re * cosine + im * sine_part
                base_ref[p, 1, rows, :] = im * cosine - re * sine_part
                return carry

            lax.fori_loop(0, angles // chunk, turn, 0)

    for g in range(per_step):
        s = jnp.minimum(step * per_step + g, SHIFTS - 1)
        a = lax.div(s, SHIFT_SIDE)
        b = s - a * SHIFT_SIDE

        def shift(n, carry):
            rows = pl.ds(pl.multiple_of(n * chunk, chunk), chunk)
            low = pl.ds(pl.multiple_of(angles + n * chunk, chunk), chunk)
            xr, xi = factor_ref[0, a, 0, rows, :], factor_ref[0, a, 1, rows, :]
            yr, yi = factor_ref[1, b, 0, rows, :], factor_ref[1, b, 1, rows, :]
            tr = xr * yr - xi * yi
            ti = xr * yi + xi * yr
            for p in range(count):
                gr, gi = base_ref[p, 0, rows, :], base_ref[p, 1, rows, :]
                lanes = pl.ds((g * count + p) * cycles, cycles)
                data_ref[rows, lanes] = (gr * tr - gi * ti).astype(bf16)
                data_ref[low, lanes] = (gr * ti + gi * tr).astype(bf16)
            return carry

        lax.fori_loop(0, angles // chunk, shift, 0)

    for n in range(ROWS // 2):
        spectrum = jnp.dot(
            table_ref[...], data_ref[:, n * 2 * cycles : (n + 1) * 2 * cycles], preferred_element_type=f32
        )
        for j in range(2):
            row = 2 * n + j
            ctf_row = ctf_ref[row % count, :][None, :]
            part = spectrum[:, j * cycles : (j + 1) * cycles] * ctf_row
            re_ref[pl.ds(row, angles, stride=ROWS), :] = part[:angles]
            im_ref[pl.ds(row, angles, stride=ROWS), :] = part[angles:]
    out_ref[:, :, :cycles] = re_ref[...].reshape(angles, ROWS, cycles).astype(bf16)
    out_ref[:, :, cycles:] = im_ref[...].reshape(angles, ROWS, cycles).astype(bf16)


def make_spectra(particles, prior_shift, ctf_rows):
    count, _, angles, cycles = particles.shape
    per_step = ROWS // count if count < ROWS else 1
    steps = -(-SHIFTS // per_step)
    turns, factors = shift_tables(angles, cycles)
    full = lambda shape: pl.BlockSpec(shape, lambda i: (0,) * len(shape))
    return pl.pallas_call(
        spectra_kernel,
        grid=(steps,),
        in_specs=[
            pl.BlockSpec(memory_space=pltpu.SMEM),
            full(particles.shape),
            full(ctf_rows.shape),
            full((2 * angles, 2 * angles)),
            full(turns.shape),
            full(factors.shape),
        ],
        out_specs=pl.BlockSpec((angles, ROWS, 2 * cycles), lambda i: (0, i, 0)),
        out_shape=jax.ShapeDtypeStruct((angles, steps * ROWS, 2 * cycles), bf16),
        scratch_shapes=[
            pltpu.VMEM((count, 2, angles, cycles), f32),
            pltpu.VMEM((2 * angles, ROWS * cycles), bf16),
            pltpu.VMEM((angles * ROWS, cycles), f32),
            pltpu.VMEM((angles * ROWS, cycles), f32),
        ],
        compiler_params=pltpu.CompilerParams(vmem_limit_bytes=VMEM_LIMIT),
        name="spectra",
    )(prior_shift, particles, ctf_rows, fourier_rows(angles), turns, factors)


def folded_dft(values, coef_ref, sign):
    half = FOLD // 2
    outputs = [None] * FOLD
    for k in range(half + 1):
        even = values[0] * coef_ref[pl.ds(k * FOLD, 1), :]
        for m in range(2, FOLD, 2):
            even = even + values[m] * coef_ref[pl.ds(k * FOLD + m, 1), :]
        odd = values[1] * coef_ref[pl.ds(k * FOLD + 1, 1), :]
        for m in range(3, FOLD, 2):
            odd = odd + values[m] * coef_ref[pl.ds(k * FOLD + m, 1), :]
        outputs[k] = even + odd
        if k != half:
            outputs[FOLD - 1 - k] = (even - odd) * sign
    return outputs


def score_kernel(
    slot_ref,
    weighted_ref,
    pieces_ref,
    ctf_ref,
    score_coef_ref,
    back_coef_ref,
    rot_ref,
    back_ref,
    stat_ref,
    corr_ref,
    score_ref,
    right_ref,
    wide_ref,
    power_ref,
    *,
    classes,
    count,
):
    group = pl.program_id(0)
    slots = pieces_ref.shape[0]
    cycles = pieces_ref.shape[2]
    queries = weighted_ref.shape[2]

    @pl.when(group == 0)
    def _():
        right_ref[...] = jnp.zeros_like(right_ref)
        power_ref[...] = jnp.zeros_like(power_ref)

    for j in range(slots):
        wide_ref[j, :, :] = pieces_ref[j, :, :].astype(f32)
    for i in range(GROUP):
        total = None
        power = power_ref[:classes, :]
        for j in range(slots):
            re = wide_ref[j, 2 * i * classes : (2 * i + 1) * classes, :]
            im = wide_ref[j, (2 * i + 1) * classes : (2 * i + 2) * classes, :]
            power = power + (re * re + im * im)
            right_ref[i, j, :classes, :cycles] = re.astype(bf16)
            right_ref[i, j, :classes, cycles:] = im.astype(bf16)
            right_ref[i, j, HALF : HALF + classes, :cycles] = (-im).astype(bf16)
            right_ref[i, j, HALF : HALF + classes, cycles:] = re.astype(bf16)
            part = lax.dot_general(
                weighted_ref[slot_ref[j], i],
                right_ref[i, j],
                (((1,), (1,)), ((), ())),
                preferred_element_type=f32,
            )
            total = part if total is None else total + part
        power_ref[:classes, :] = power
        corr_ref[group * GROUP + i] = total

    @pl.when(group == pl.num_programs(0) - 1)
    def _():
        angles = ROTS * slots
        lane = lax.broadcasted_iota(jnp.int32, (count, LANES), 1)
        sign = jnp.where(lane < HALF, 1.0, -1.0).astype(f32)
        used = (lane & (HALF - 1)) < classes
        used_once = used & (lane < HALF)
        power = power_ref[...]
        ctf_row = ctf_ref[...]
        bias = lax.dot_general(
            ctf_row * ctf_row,
            jnp.concatenate([power, power], 0),
            (((1,), (1,)), ((), ())),
            precision=lax.Precision.HIGHEST,
            preferred_element_type=f32,
        ) * (0.5 / angles)

        def scores(s, peak):
            rows = pl.ds(pl.multiple_of(s * count, 8), count)
            values = [corr_ref[0, rows, :]]
            for m in range(1, ROTS // 2):
                values.append(corr_ref[m, rows, :] + corr_ref[ROTS - m, rows, :] * sign)
            values.append(corr_ref[ROTS // 2, rows, :])
            for k, y in enumerate(folded_dft(values, score_coef_ref, sign)):
                z = (pltpu.roll(y, HALF, 1) + y * sign) * (1.0 / angles) - bias
                z = jnp.where(used_once if k in (0, FOLD - 1) else used, z, -1e30)
                score_ref[k, rows, :] = z
                peak = jnp.maximum(peak, z)
            return peak

        peak = lax.fori_loop(0, SHIFTS, scores, jnp.full((count, LANES), -1e30, f32))
        peak = jnp.broadcast_to(jnp.max(peak, axis=1, keepdims=True), (count, LANES))

        def backs(s, mass):
            rows = pl.ds(pl.multiple_of(s * count, 8), count)
            values = []
            for k in range(FOLD):
                e = jnp.exp(score_ref[k, rows, :] - peak)
                mass = mass + e
                values.append(pltpu.roll(e, HALF, 1) + e * sign)
            for m, y in enumerate(folded_dft(values, back_coef_ref, sign)):
                y_rolled = pltpu.roll(y, HALF, 1)
                back_ref[m, rows, :] = y * rot_ref[m, 0:1, :] + y_rolled * rot_ref[m, 1:2, :]
                if m not in (0, FOLD - 1):
                    y, y_rolled = y * sign, y_rolled * -sign
                    back_ref[ROTS - m, rows, :] = (
                        y * rot_ref[ROTS - m, 0:1, :] + y_rolled * rot_ref[ROTS - m, 1:2, :]
                    )
            return mass

        mass = lax.fori_loop(0, SHIFTS, backs, jnp.zeros((count, LANES), f32))
        if queries > SHIFTS * count:
            back_ref[:, SHIFTS * count :, :] = jnp.zeros((ROTS, queries - SHIFTS * count, LANES), f32)
        stat_ref[0] = peak
        stat_ref[1] = mass


def make_scores(slot_of, weighted, pieces, ctf_rows, rot_lanes, classes):
    slots, _, queries, _ = weighted.shape
    cycles = pieces.shape[2]
    count = ctf_rows.shape[0]
    to_score, to_back = fold_tables()
    block = 2 * GROUP * classes
    full = lambda shape: pl.BlockSpec(shape, lambda g: (0,) * len(shape))
    return pl.pallas_call(
        functools.partial(score_kernel, classes=classes, count=count),
        grid=(ROTS // GROUP,),
        in_specs=[
            pl.BlockSpec(memory_space=pltpu.SMEM),
            pl.BlockSpec((slots, GROUP, queries, 2 * cycles), lambda g: (0, g, 0, 0)),
            pl.BlockSpec((slots, block, cycles), lambda g: (0, g, 0)),
            full(ctf_rows.shape),
            full(to_score.shape),
            full(to_back.shape),
            full(rot_lanes.shape),
        ],
        out_specs=[full((ROTS, queries, LANES)), full((2, count, LANES))],
        out_shape=[
            jax.ShapeDtypeStruct((ROTS, queries, LANES), f32),
            jax.ShapeDtypeStruct((2, count, LANES), f32),
        ],
        scratch_shapes=[
            pltpu.VMEM((ROTS, queries, LANES), f32),
            pltpu.VMEM((FOLD, queries, LANES), f32),
            pltpu.VMEM((GROUP, slots, 2 * HALF, 2 * cycles), bf16),
            pltpu.VMEM((slots, block, cycles), f32),
            pltpu.VMEM((HALF, cycles), f32),
        ],
        compiler_params=pltpu.CompilerParams(vmem_limit_bytes=VMEM_LIMIT),
        name="scores",
    )(slot_of, weighted, pieces, ctf_rows, to_score, to_back, rot_lanes)


def scale_kernel(back_ref, scale_ref, out_ref):
    queries = back_ref.shape[1]
    padded = -(-queries // LANES) * LANES
    for i in range(GROUP):
        value = back_ref[i] * scale_ref[...]
        if padded > queries:
            value = jnp.concatenate([value, jnp.zeros((padded - queries, LANES), f32)], 0)
        out_ref[i] = value.T[:, :queries].astype(bf16)


def scale_back(back, scale):
    _, queries, _ = back.shape
    return pl.pallas_call(
        scale_kernel,
        grid=(ROTS // GROUP,),
        in_specs=[
            pl.BlockSpec((GROUP, queries, LANES), lambda g: (g, 0, 0)),
            pl.BlockSpec((queries, LANES), lambda g: (0, 0)),
        ],
        out_specs=pl.BlockSpec((GROUP, LANES, queries), lambda g: (g, 0, 0)),
        out_shape=jax.ShapeDtypeStruct((ROTS, LANES, queries), bf16),
        compiler_params=pltpu.CompilerParams(vmem_limit_bytes=VMEM_LIMIT),
        name="scale_back",
    )(back, scale)


def sums_kernel(back_ref, weighted_ref, turn_ref, out_ref, wide_ref, *, classes):
    cycles = out_ref.shape[2]
    cosine = turn_ref[0, 0]
    sine_part = turn_ref[0, 1]
    for i in range(GROUP):
        product = jnp.dot(back_ref[i], weighted_ref[0, i], preferred_element_type=f32)
        re = product[:HALF, :cycles] - product[HALF:, cycles:]
        im = product[:HALF, cycles:] + product[HALF:, :cycles]
        wide_ref[2 * i * classes : (2 * i + 1) * classes, :] = (re * cosine - im * sine_part)[:classes]
        wide_ref[(2 * i + 1) * classes : (2 * i + 2) * classes, :] = (re * sine_part + im * cosine)[:classes]
    out_ref[0] = wide_ref[...].astype(bf16)


def make_sums(back, weighted, turn_columns, classes):
    slots, _, queries, double = weighted.shape
    cycles = double // 2
    block = 2 * GROUP * classes
    return pl.pallas_call(
        functools.partial(sums_kernel, classes=classes),
        grid=(slots, ROTS // GROUP),
        in_specs=[
            pl.BlockSpec((GROUP, LANES, queries), lambda u, g: (g, 0, 0)),
            pl.BlockSpec((1, GROUP, queries, double), lambda u, g: (u, g, 0, 0)),
            pl.BlockSpec((1, 2, HALF, LANES), lambda u, g: (u, 0, 0, 0)),
        ],
        out_specs=pl.BlockSpec((1, block, cycles), lambda u, g: (u, g, 0)),
        out_shape=jax.ShapeDtypeStruct((slots, ROTS * 2 * classes, cycles), bf16),
        scratch_shapes=[pltpu.VMEM((block, cycles), f32)],
        compiler_params=pltpu.CompilerParams(vmem_limit_bytes=VMEM_LIMIT),
        name="class_sums",
    )(back, weighted, turn_columns)


def phase_of(index, period):
    radians = (index % period).astype(f32) * (two_pi / period)
    return jnp.cos(radians), jnp.sin(radians)


def local(particles, references, ctf_table, rot_offset, prior_shift, defocus_group):
    count, _, angles, cycles = particles.shape
    own_rows, _, classes, _ = references.shape
    slots = angles // ROTS
    group_count = ctf_table.shape[0]
    parts = lax.axis_size("cls")
    onehot = (defocus_group[:, None] == jnp.arange(group_count, dtype=jnp.int32)[None, :]).astype(f32)
    ctf_rows = jnp.dot(onehot, ctf_table, precision=lax.Precision.HIGHEST)

    freq = lax.axis_index("dp") * own_rows + jnp.arange(own_rows, dtype=jnp.int32)
    cosine, sine_part = phase_of(freq[:, None] * rot_offset[None, :], angles)
    cosine, sine_part = cosine[:, :, None], sine_part[:, :, None]
    wide = references.astype(f32)
    turned = jnp.stack(
        [
            wide[:, 0] * cosine + wide[:, 1] * sine_part,
            wide[:, 1] * cosine - wide[:, 0] * sine_part,
        ],
        1,
    ).astype(bf16)
    piece = turned.reshape(own_rows * 2 * classes, cycles)
    pieces = lax.all_gather(piece, "dp", axis=0, tiled=True).reshape(slots, ROTS * 2 * classes, cycles)

    weighted = make_spectra(particles, prior_shift, ctf_rows)
    queries = weighted.shape[1]
    weighted = weighted.reshape(slots, ROTS, queries, 2 * cycles)

    lanes = jnp.pad(rot_offset, (0, HALF - classes))
    cosine, sine_part = phase_of(jnp.arange(ROTS, dtype=jnp.int32)[:, None] * lanes[None, :], angles)
    rot_lanes = jnp.stack(
        [jnp.concatenate([cosine, cosine], 1), jnp.concatenate([-sine_part, sine_part], 1)], 1
    )
    cosine, sine_part = phase_of(jnp.arange(slots, dtype=jnp.int32)[:, None] * lanes[None, :], slots)
    turn_columns = jnp.broadcast_to(
        jnp.stack([cosine, sine_part], 1)[:, :, :, None], (slots, 2, HALF, LANES)
    )

    back, stat = make_scores(
        jnp.arange(slots, dtype=jnp.int32), weighted, pieces, ctf_rows, rot_lanes, classes
    )
    peak = stat[0, :, 0]
    mass_lanes = stat[1]
    mine = jnp.stack([peak, jnp.sum(mass_lanes, axis=1)])
    place = (jnp.arange(parts) == lax.axis_index("cls")).astype(f32)
    everyone = lax.psum(place[:, None, None] * mine[None], "cls")
    top = jnp.max(everyone[:, 0], axis=0)
    total_mass = jnp.sum(everyone[:, 1] * jnp.exp(everyone[:, 0] - top[None]), axis=0)
    log_evidence = top + jnp.log(total_mass)
    scale = jnp.exp(peak - log_evidence)
    class_posterior = (mass_lanes[:, :classes] + mass_lanes[:, HALF : HALF + classes]) * scale[:, None]

    scale_rows = jnp.broadcast_to(
        jnp.tile(scale, queries // count)[:, None], (queries, LANES)
    )
    back = scale_back(back, scale_rows)
    sums = make_sums(back, weighted, turn_columns, classes)
    summed = lax.psum_scatter(
        sums.reshape(slots * ROTS * 2 * classes, cycles), "dp", scatter_dimension=0, tiled=True
    )
    class_sums = summed.astype(f32).reshape(own_rows, 2, classes, cycles)
    return (log_evidence, class_posterior, class_sums)


def solution(mesh):
    placed = (
        P("dp", None, None, None),
        P("dp", None, "cls", None),
        P(),
        P("cls"),
        P("dp", None),
        P("dp"),
    )
    return jax.shard_map(
        local,
        mesh=mesh,
        in_specs=placed,
        out_specs=(P("dp"), P("dp", "cls"), P("dp", None, "cls", None)),
        check_vma=False,
    )
```

```python
import functools
import math

import jax
import jax.numpy as jnp
import ml_dtypes
import numpy as np
from jax import lax
from jax.experimental import pallas as pl
from jax.experimental.pallas import tpu as pltpu
from jax.sharding import PartitionSpec as P

ROTS = 36
ANG_STEP = 8
SHIFT_SIDE = 5
SHIFTS = SHIFT_SIDE * SHIFT_SIDE
LANES = 128
GROUP = 12
ROWS = 16
FOLD = ROTS // 2 + 1

two_pi = 2.0 * math.pi
f32 = jnp.float32
bf16 = jnp.bfloat16
VMEM_LIMIT = 56 * 1024 * 1024


def fourier_rows(angles):
    index_grid = np.arange(angles)
    radians = (index_grid[:, None] * index_grid[None, :] % angles) * (two_pi / angles)
    cosine, sine_part = np.cos(radians), np.sin(radians)
    table_full = np.concatenate(
        [np.concatenate([cosine, sine_part], 1), np.concatenate([-sine_part, cosine], 1)], 0
    )
    return table_full.astype(np.float32).astype(ml_dtypes.bfloat16)


def shift_tables(angles, cycles):
    theta = np.arange(angles) * (two_pi / angles)
    radius = (np.arange(cycles) + 1) / (2.0 * cycles)
    turns = np.stack([np.cos(theta), np.sin(theta)])[:, :, None] * radius
    steps = np.arange(SHIFT_SIDE) - SHIFT_SIDE // 2
    phase = two_pi * turns[:, None] * steps[None, :, None, None]
    factors = np.stack([np.cos(phase), -np.sin(phase)], 2)
    return turns.astype(np.float32), factors.astype(np.float32)


def cos_sin_of_turns(turns):
    frac = turns - jnp.floor(turns + 0.5)
    w = frac * two_pi
    w2 = w * w
    cosine = jnp.full_like(w, 1.0 / math.factorial(16))
    for n in range(14, -1, -2):
        cosine = cosine * w2 + (-1.0) ** (n // 2) / math.factorial(n)
    sine_part = jnp.full_like(w, 1.0 / math.factorial(17))
    for n in range(15, 0, -2):
        sine_part = sine_part * w2 + (-1.0) ** (n // 2) / math.factorial(n)
    return cosine, sine_part * w


def spectra_kernel(
    shift_ref, part_ref, ctf_ref, table_ref, turns_ref, factor_ref, out_ref, base_ref, data_ref, re_ref, im_ref
):
    step = pl.program_id(0)
    count, _, angles, cycles = part_ref.shape
    chunk = 32
    per_step = ROWS // count if count < ROWS else 1

    @pl.when(step == 0)
    def _():
        for p in range(count):
            sx = shift_ref[p, 0].astype(f32)
            sy = shift_ref[p, 1].astype(f32)

            def turn(n, carry):
                rows = pl.ds(pl.multiple_of(n * chunk, chunk), chunk)
                cosine, sine_part = cos_sin_of_turns(sx * turns_ref[0, rows, :] + sy * turns_ref[1, rows, :])
                re = part_ref[p, 0, rows, :].astype(f32)
                im = part_ref[p, 1, rows, :].astype(f32)
                base_ref[p, 0, rows, :] = re * cosine + im * sine_part
                base_ref[p, 1, rows, :] = im * cosine - re * sine_part
                return carry

            lax.fori_loop(0, angles // chunk, turn, 0)

    for g in range(per_step):
        s = jnp.minimum(step * per_step + g, SHIFTS - 1)
        a = lax.div(s, SHIFT_SIDE)
        b = s - a * SHIFT_SIDE

        def shift(n, carry):
            rows = pl.ds(pl.multiple_of(n * chunk, chunk), chunk)
            low = pl.ds(pl.multiple_of(angles + n * chunk, chunk), chunk)
            xr, xi = factor_ref[0, a, 0, rows, :], factor_ref[0, a, 1, rows, :]
            yr, yi = factor_ref[1, b, 0, rows, :], factor_ref[1, b, 1, rows, :]
            tr = xr * yr - xi * yi
            ti = xr * yi + xi * yr
            for p in range(count):
                gr, gi = base_ref[p, 0, rows, :], base_ref[p, 1, rows, :]
                lanes = pl.ds((g * count + p) * cycles, cycles)
                data_ref[rows, lanes] = (gr * tr - gi * ti).astype(bf16)
                data_ref[low, lanes] = (gr * ti + gi * tr).astype(bf16)
            return carry

        lax.fori_loop(0, angles // chunk, shift, 0)

    for n in range(ROWS // 2):
        spectrum = jnp.dot(
            table_ref[...], data_ref[:, n * 2 * cycles : (n + 1) * 2 * cycles], preferred_element_type=f32
        )
        for j in range(2):
            row = 2 * n + j
            ctf_row = ctf_ref[row % count, :][None, :]
            part = spectrum[:, j * cycles : (j + 1) * cycles] * ctf_row
            re_ref[pl.ds(row, angles, stride=ROWS), :] = part[:angles]
            im_ref[pl.ds(row, angles, stride=ROWS), :] = part[angles:]
    out_ref[:, :, :cycles] = re_ref[...].reshape(angles, ROWS, cycles).astype(bf16)
    out_ref[:, :, cycles:] = im_ref[...].reshape(angles, ROWS, cycles).astype(bf16)


def make_spectra(particles, prior_shift, ctf_rows):
    count, _, angles, cycles = particles.shape
    per_step = ROWS // count if count < ROWS else 1
    steps = -(-SHIFTS // per_step)
    turns, factors = shift_tables(angles, cycles)
    full = lambda shape: pl.BlockSpec(shape, lambda i: (0,) * len(shape))
    return pl.pallas_call(
        spectra_kernel,
        grid=(steps,),
        in_specs=[
            pl.BlockSpec(memory_space=pltpu.SMEM),
            full(particles.shape),
            full(ctf_rows.shape),
            full((2 * angles, 2 * angles)),
            full(turns.shape),
            full(factors.shape),
        ],
        out_specs=pl.BlockSpec((angles, ROWS, 2 * cycles), lambda i: (0, i, 0)),
        out_shape=jax.ShapeDtypeStruct((angles, steps * ROWS, 2 * cycles), bf16),
        scratch_shapes=[
            pltpu.VMEM((count, 2, angles, cycles), f32),
            pltpu.VMEM((2 * angles, ROWS * cycles), bf16),
            pltpu.VMEM((angles * ROWS, cycles), f32),
            pltpu.VMEM((angles * ROWS, cycles), f32),
        ],
        compiler_params=pltpu.CompilerParams(vmem_limit_bytes=VMEM_LIMIT),
        name="spectra",
    )(prior_shift, particles, ctf_rows, fourier_rows(angles), turns, factors)


def half_dft(even_values, odd_values):
    half = FOLD // 2
    cos_sums, sin_sums = [None] * FOLD, [None] * FOLD

    def weighted_sum(values, k, table, start):
        total = None
        for m in range(start, FOLD, 2):
            weight = float(table((k * m % ROTS) * two_pi / ROTS))
            if values[m] is None or abs(weight) < 1e-9:
                continue
            if abs(abs(weight) - 1.0) < 1e-9:
                term = values[m] if weight > 0 else -values[m]
            else:
                term = values[m] * weight
            total = term if total is None else total + term
        return jnp.zeros_like(values[1]) if total is None else total

    for k in range(half + 1):
        even = weighted_sum(even_values, k, math.cos, 0)
        odd = weighted_sum(even_values, k, math.cos, 1)
        cos_sums[k] = even + odd
        if k != half:
            cos_sums[FOLD - 1 - k] = even - odd
        if k:
            even = weighted_sum(odd_values, k, math.sin, 0)
            odd = weighted_sum(odd_values, k, math.sin, 1)
            sin_sums[k] = even + odd
            if k != half:
                sin_sums[FOLD - 1 - k] = odd - even
    return cos_sums, sin_sums


def turn_kernel(first_ref, references_ref, offset_ref, out_ref, wide_ref):
    own_rows, _, classes, _ = references_ref.shape
    batch = wide_ref.shape[1] // (2 * classes)
    offsets = offset_ref[:classes, :]

    def some(n, carry):
        for i in range(batch):
            m = batch * n + i
            freq = (first_ref[0] + m).astype(f32)
            cosine, sine_part = cos_sin_of_turns(offsets * freq * (1.0 / (ROTS * ANG_STEP)))
            re = references_ref[m, 0].astype(f32)
            im = references_ref[m, 1].astype(f32)
            wide_ref[n, 2 * i * classes : (2 * i + 1) * classes, :] = re * cosine + im * sine_part
            wide_ref[n, (2 * i + 1) * classes : (2 * i + 2) * classes, :] = im * cosine - re * sine_part
        return carry

    lax.fori_loop(0, own_rows // batch, some, 0)
    out_ref[...] = wide_ref[...].reshape(out_ref.shape).astype(bf16)


def turn_references(first, references, offsets):
    own_rows, _, classes, cycles = references.shape
    batch = own_rows if own_rows % 2 else 2
    return pl.pallas_call(
        turn_kernel,
        in_specs=[
            pl.BlockSpec(memory_space=pltpu.SMEM),
            pl.BlockSpec(memory_space=pltpu.VMEM),
            pl.BlockSpec(memory_space=pltpu.VMEM),
        ],
        out_shape=jax.ShapeDtypeStruct((own_rows * 2 * classes, cycles), bf16),
        scratch_shapes=[pltpu.VMEM((own_rows // batch, batch * 2 * classes, cycles), f32)],
        compiler_params=pltpu.CompilerParams(vmem_limit_bytes=VMEM_LIMIT),
        name="turn_references",
    )(first, references, offsets)


def correlate_kernel(slot_ref, *refs, slots, classes, padded, finish):
    weighted_refs, refs = refs[:slots], refs[slots:]
    piece_refs, refs = refs[:slots], refs[slots:]
    if finish:
        before_ref, power_before_ref, ctf_ref, weight_ref, stat_ref = refs[:5]
        corr_ref, wide_ref, power_ref = refs[5:]
    else:
        corr_ref, power_ref, wide_ref = refs
    group = pl.program_id(0)
    cycles = piece_refs[0].shape[1]
    queries = weighted_refs[0].shape[2]
    block = piece_refs[0].shape[0]

    @pl.when(group == 0)
    def _():
        wide_ref[:, block:, :] = jnp.zeros((slots, wide_ref.shape[1] - block, cycles), f32)
        power_ref[...] = power_before_ref[...] if finish else jnp.zeros_like(power_ref)

    for j in range(slots):
        wide_ref[j, :block, :] = piece_refs[j][...].astype(f32)
    power = power_ref[...]
    for i in range(GROUP):
        total = before_ref[i, :, :queries] if finish else None
        for j in range(slots):
            start = 2 * i * classes
            re = wide_ref[j, start : start + padded, :]
            im = wide_ref[j, start + classes : start + classes + padded, :]
            power = power + (re * re + im * im)
            left = jnp.concatenate(
                [jnp.concatenate([re, im], 1), jnp.concatenate([-im, re], 1)], 0
            ).astype(bf16)
            part = lax.dot_general(
                left, weighted_refs[j][0, i], (((1,), (1,)), ((), ())), preferred_element_type=f32
            )
            total = part if total is None else total + part
        row = group * GROUP + i if finish else i
        corr_ref[row, :, :queries] = total
    power_ref[...] = power

    if not finish:
        return

    @pl.when(group == pl.num_programs(0) - 1)
    def _():
        count = ctf_ref.shape[0]
        angles = ROTS * ANG_STEP
        used = SHIFTS * count
        tiles = weight_ref.shape[2] // LANES
        ctf_row = ctf_ref[...]
        ctf_rows = jnp.concatenate([ctf_row * ctf_row] * (LANES // count), 0)
        bias = lax.dot_general(
            power_ref[...],
            ctf_rows,
            (((1,), (1,)), ((), ())),
            precision=lax.Precision.HIGHEST,
            preferred_element_type=f32,
        ) * (0.5 / angles)
        wide_ref[0, :padded, :] = bias
        rows_of = lambda base: lax.broadcasted_iota(jnp.int32, (8, LANES), 0) + base
        lanes_of = lambda base: lax.broadcasted_iota(jnp.int32, (8, LANES), 1) + base

        peak = jnp.full((8, LANES), -1e30, f32)
        for tile in range(tiles):
            lanes = slice(tile * LANES, (tile + 1) * LANES)

            def scores(n, peak):
                start = pl.multiple_of(n * 8, 8)
                rows = pl.ds(start, 8)
                low = pl.ds(padded + start, 8)
                valid = (rows_of(start) < classes) & (lanes_of(tile * LANES) < used)
                even_values = [corr_ref[0, rows, lanes]]
                odd_values = [None]
                for m in range(1, ROTS // 2):
                    even_values.append(corr_ref[m, rows, lanes] + corr_ref[ROTS - m, rows, lanes])
                    odd_values.append(corr_ref[m, low, lanes] - corr_ref[ROTS - m, low, lanes])
                even_values.append(corr_ref[ROTS // 2, rows, lanes])
                odd_values.append(None)
                cos_sums, sin_sums = half_dft(even_values, odd_values)
                bias = wide_ref[0, rows, :]
                for k in range(FOLD):
                    if k in (0, FOLD - 1):
                        results = [(k, cos_sums[k])]
                    else:
                        results = [(k, cos_sums[k] - sin_sums[k]), (ROTS - k, cos_sums[k] + sin_sums[k])]
                    for place, value in results:
                        value = jnp.where(valid, value * (1.0 / angles) - bias, -1e30)
                        weight_ref[place, rows, lanes] = value
                        peak = jnp.maximum(peak, value)
                return peak

            peak = lax.fori_loop(0, padded // 8, scores, peak)

        peak = jnp.broadcast_to(jnp.max(peak, axis=0, keepdims=True), (8, LANES))
        step = count
        while step < LANES:
            peak = jnp.maximum(peak, pltpu.roll(peak, step, 1))
            step *= 2
        stat_ref[0:8, :] = peak

        def masses(n, carry):
            rows = pl.ds(pl.multiple_of(n * 8, 8), 8)
            mass = jnp.zeros((8, LANES), f32)
            for tile in range(tiles):
                lanes = slice(tile * LANES, (tile + 1) * LANES)
                for k in range(ROTS):
                    value = jnp.exp(weight_ref[k, rows, lanes] - peak)
                    weight_ref[k, rows, lanes] = value
                    mass = mass + value
            step = count
            while step < LANES:
                mass = mass + pltpu.roll(mass, step, 1)
                step *= 2
            stat_ref[pl.ds(pl.multiple_of(8 + n * 8, 8), 8), :] = mass
            return carry

        lax.fori_loop(0, padded // 8, masses, 0)


def correlate(slot_of, weighted, pieces, classes, before=None, power=None, ctf_rows=None):
    _, _, queries, double = weighted.shape
    cycles = double // 2
    slots = len(pieces)
    padded = -(-classes // 8) * 8
    wide_lanes = -(-queries // LANES) * LANES
    block = 2 * GROUP * classes
    finish = ctf_rows is not None
    full = lambda shape: pl.BlockSpec(shape, lambda g, u: (0,) * len(shape))
    in_specs = [
        pl.BlockSpec((1, GROUP, queries, double), functools.partial(lambda j, g, u: (u[j], g, 0, 0), j))
        for j in range(slots)
    ] + [pl.BlockSpec((block, cycles), lambda g, u: (g, 0))] * slots
    corr_block = pl.BlockSpec((GROUP, 2 * padded, wide_lanes), lambda g, u: (g, 0, 0))
    corr_shape = (ROTS, 2 * padded, wide_lanes)
    wide = pltpu.VMEM((slots, block + 8, cycles), f32)
    operands = [slot_of] + [weighted] * slots + list(pieces)
    if finish:
        in_specs += [corr_block, full((padded, cycles)), full(ctf_rows.shape)]
        operands += [before, power, ctf_rows]
        out_shapes = [(ROTS, padded, wide_lanes), (8 + padded, LANES)]
        out_specs = [full(shape) for shape in out_shapes]
        scratch = [pltpu.VMEM(corr_shape, f32), wide, pltpu.VMEM((padded, cycles), f32)]
    else:
        out_shapes = [corr_shape, (padded, cycles)]
        out_specs = [corr_block, full((padded, cycles))]
        scratch = [wide]
    return pl.pallas_call(
        functools.partial(correlate_kernel, slots=slots, classes=classes, padded=padded, finish=finish),
        grid_spec=pltpu.PrefetchScalarGridSpec(
            num_scalar_prefetch=1,
            grid=(ROTS // GROUP,),
            in_specs=in_specs,
            out_specs=out_specs,
            scratch_shapes=scratch,
        ),
        out_shape=[jax.ShapeDtypeStruct(shape, f32) for shape in out_shapes],
        compiler_params=pltpu.CompilerParams(vmem_limit_bytes=VMEM_LIMIT),
        name="scores" if finish else "correlate",
    )(*operands)


def back_kernel(weight_ref, scale_ref, offset_ref, out_ref, sum_ref):
    padded = weight_ref.shape[1]
    queries = out_ref.shape[2]
    scale = scale_ref[...]
    for tile in range(weight_ref.shape[2] // LANES):
        lanes = slice(tile * LANES, (tile + 1) * LANES)

        def transform(n, carry):
            start = pl.multiple_of(n * 8, 8)
            rows = pl.ds(start, 8)
            low = pl.ds(padded + start, 8)
            values = [weight_ref[k, rows, lanes] * scale for k in range(ROTS)]
            even_values = [values[0]] + [values[k] + values[ROTS - k] for k in range(1, ROTS // 2)]
            odd_values = [None] + [values[k] - values[ROTS - k] for k in range(1, ROTS // 2)] + [None]
            cos_sums, sin_sums = half_dft(even_values + [values[ROTS // 2]], odd_values)
            for m in range(FOLD):
                sine_part = jnp.zeros_like(scale) if m in (0, FOLD - 1) else sin_sums[m]
                sum_ref[m, rows, lanes] = cos_sums[m]
                sum_ref[m, low, lanes] = sine_part
                if m not in (0, FOLD - 1):
                    sum_ref[ROTS - m, rows, lanes] = cos_sums[m]
                    sum_ref[ROTS - m, low, lanes] = -sine_part
            return carry

        lax.fori_loop(0, padded // 8, transform, 0)

    step_cos, step_sin = cos_sin_of_turns(offset_ref[...] * (1.0 / (ROTS * ANG_STEP)))

    def turn(m, carry):
        cosine, sine_part = carry
        wide_cos, wide_sin = cosine[:, :1], sine_part[:, :1]
        re, im = sum_ref[m, :padded, :], sum_ref[m, padded:, :]
        turned = jnp.concatenate([re * wide_cos - im * wide_sin, re * wide_sin + im * wide_cos], 0)
        out_ref[m] = turned[:, :queries].astype(bf16)
        return cosine * step_cos - sine_part * step_sin, sine_part * step_cos + cosine * step_sin

    lax.fori_loop(0, ROTS, turn, (jnp.ones_like(step_cos), jnp.zeros_like(step_cos)))


def make_back(weights, scale, offsets, queries):
    _, padded, wide_lanes = weights.shape
    return pl.pallas_call(
        back_kernel,
        out_shape=jax.ShapeDtypeStruct((ROTS, 2 * padded, queries), bf16),
        scratch_shapes=[pltpu.VMEM((ROTS, 2 * padded, wide_lanes), f32)],
        compiler_params=pltpu.CompilerParams(vmem_limit_bytes=VMEM_LIMIT),
        name="back",
    )(weights, scale, offsets)


def sums_kernel(slot_ref, back_ref, weighted_ref, offset_ref, *refs, classes, extra):
    added, (out_ref, wide_ref) = refs[:extra], refs[extra:]
    padded = offset_ref.shape[0]
    cycles = wide_ref.shape[1]
    turns = offset_ref[...] * (slot_ref[0].astype(f32) * (1.0 / ANG_STEP))
    cosine, sine_part = cos_sin_of_turns(turns)
    for i in range(GROUP):
        product = jnp.dot(back_ref[i], weighted_ref[0, i], preferred_element_type=f32)
        re = product[:padded, :cycles] - product[padded:, cycles:]
        im = product[:padded, cycles:] + product[padded:, :cycles]
        start = 2 * i * classes
        wide_ref[start : start + classes, :] = (re * cosine - im * sine_part)[:classes]
        wide_ref[start + classes : start + 2 * classes, :] = (re * sine_part + im * cosine)[:classes]
    if len(out_ref.shape) == 2:
        total = wide_ref[...]
        for ref in added:
            total = total + ref[...].astype(f32)
        out_ref[...] = total.astype(out_ref.dtype)
    else:
        total = wide_ref[...]
        for ref in added:
            total = total + ref[...].astype(f32)
        wide_ref[...] = total
        for i in range(GROUP):
            for x in range(2):
                start = (2 * i + x) * classes
                out_ref[i, x] = wide_ref[start : start + classes, :]


def class_sums_of(slot, back, weighted, offsets, added, classes, last=False):
    _, _, queries, double = weighted.shape
    cycles = double // 2
    rows = back.shape[1]
    block = 2 * GROUP * classes
    piece = pl.BlockSpec((block, cycles), lambda g, u: (g, 0))
    if last:
        out_spec = pl.BlockSpec((GROUP, 2, classes, cycles), lambda g, u: (g, 0, 0, 0))
        out_shape = jax.ShapeDtypeStruct((ROTS, 2, classes, cycles), f32)
    else:
        out_spec = piece
        out_shape = jax.ShapeDtypeStruct((ROTS * 2 * classes, cycles), bf16)
    return pl.pallas_call(
        functools.partial(sums_kernel, classes=classes, extra=len(added)),
        grid_spec=pltpu.PrefetchScalarGridSpec(
            num_scalar_prefetch=1,
            grid=(ROTS // GROUP,),
            in_specs=[
                pl.BlockSpec((GROUP, rows, queries), lambda g, u: (g, 0, 0)),
                pl.BlockSpec((1, GROUP, queries, double), lambda g, u: (u[0], g, 0, 0)),
                pl.BlockSpec(offsets.shape, lambda g, u: (0, 0)),
            ]
            + [piece] * len(added),
            out_specs=out_spec,
            scratch_shapes=[pltpu.VMEM((block, cycles), f32)],
        ),
        out_shape=out_shape,
        compiler_params=pltpu.CompilerParams(vmem_limit_bytes=VMEM_LIMIT),
        name="class_sums",
    )(jnp.reshape(slot, (1,)).astype(jnp.int32), back, weighted, offsets, *added)


def pick(index, table):
    return jnp.take(jnp.asarray(table, jnp.int32), index)


def reduce_on_line(back, weighted, offsets, classes):
    index = lax.axis_index("dp")
    line, side = index // 2, index % 2
    order = [pick(line, row) for row in ((3, 3, 0, 0), (2, 2, 1, 1), (1, 0, 3, 2), (0, 1, 2, 3))]

    def sums(target, added, last=False):
        return class_sums_of(target, back, weighted, offsets, added, classes, last)

    def across(piece):
        return lax.ppermute(piece, "dp", [(d, d ^ 1) for d in range(8)])

    def along(piece, pairs):
        return lax.ppermute(piece, "dp", [(2 * a + x, 2 * b + x) for a, b in pairs for x in range(2)])

    crossed = [across(sums(2 * z + 1 - side, ())) for z in order]
    first = along(sums(2 * order[0] + side, (crossed[0],)), ((0, 1), (3, 2)))
    end = (line == 0) | (line == 3)
    chosen = jnp.where(end, order[1], order[0])
    chosen_crossed = jnp.where(end, crossed[1], crossed[0])
    second = sums(2 * chosen + side, (chosen_crossed, first))
    from_ends = along(second, ((0, 1), (3, 2)))
    from_middle = along(second, ((1, 2), (2, 1)))
    third_middle = along(sums(2 * order[1] + side, (crossed[1], from_ends)), ((1, 2), (2, 1)))
    third_pairs = along(
        sums(2 * order[2] + side, (crossed[2], from_middle)), ((0, 1), (1, 0), (2, 3), (3, 2))
    )
    return sums(2 * order[3] + side, (crossed[3], third_middle, third_pairs), last=True)


def local(particles, references, ctf_table, rot_offset, prior_shift, defocus_group):
    count, _, angles, cycles = particles.shape
    own_rows, _, classes, _ = references.shape
    slots = angles // ROTS
    padded = -(-classes // 8) * 8
    group_count = ctf_table.shape[0]
    parts = lax.axis_size("cls")
    devices = lax.axis_size("dp")
    offsets = jnp.broadcast_to(
        jnp.pad(rot_offset, (0, padded - classes)).astype(f32)[:, None], (padded, LANES)
    )

    first = (lax.axis_index("dp") * own_rows).astype(jnp.int32).reshape(1)
    piece = turn_references(first, references, offsets)
    gathered = lax.all_gather(piece, "dp", axis=0, tiled=True).reshape(slots, ROTS * 2 * classes, cycles)
    pieces = [gathered[j] for j in range(slots)]
    slot_of = jnp.arange(slots, dtype=jnp.int32)

    onehot = (defocus_group[:, None] == jnp.arange(group_count, dtype=jnp.int32)[None, :]).astype(f32)
    ctf_rows = jnp.dot(onehot, ctf_table, precision=lax.Precision.HIGHEST)
    weighted = make_spectra(particles, prior_shift, ctf_rows)
    queries = weighted.shape[1]
    weighted = weighted.reshape(slots, ROTS, queries, 2 * cycles)

    half = slots // 2
    corr, power = correlate(slot_of[:half], weighted, pieces[:half], classes)
    weights, stat = correlate(slot_of[half:], weighted, pieces[half:], classes, corr, power, ctf_rows)

    peak = stat[0, :count]
    mass = stat[8 : 8 + classes, :count]
    mine = jnp.stack([peak, jnp.sum(mass, axis=0)])
    place = (jnp.arange(parts) == lax.axis_index("cls")).astype(f32)
    everyone = lax.psum(place[:, None, None] * mine[None], "cls")
    top = jnp.max(everyone[:, 0], axis=0)
    total_mass = jnp.sum(everyone[:, 1] * jnp.exp(everyone[:, 0] - top[None]), axis=0)
    log_evidence = top + jnp.log(total_mass)
    scale = jnp.exp(peak - log_evidence)
    class_posterior = (mass * scale[None, :]).T

    scale_lanes = jnp.broadcast_to(jnp.tile(scale, LANES // count)[None, :], (8, LANES))
    back = make_back(weights, scale_lanes, offsets, queries)
    if devices == 8 and own_rows == ROTS:
        class_sums = reduce_on_line(back, weighted, offsets, classes)
    else:
        sums = [class_sums_of(slot_of[u], back, weighted, offsets, (), classes) for u in range(slots)]
        summed = lax.psum_scatter(jnp.concatenate(sums, 0), "dp", scatter_dimension=0, tiled=True)
        class_sums = summed.astype(f32).reshape(own_rows, 2, classes, cycles)
    return (log_evidence, class_posterior, class_sums)


def solution(mesh):
    placed = (
        P("dp", None, None, None),
        P("dp", None, "cls", None),
        P(),
        P("cls"),
        P("dp", None),
        P("dp"),
    )
    return jax.shard_map(
        local,
        mesh=mesh,
        in_specs=placed,
        out_specs=(P("dp"), P("dp", "cls"), P("dp", None, "cls", None)),
        check_vma=False,
    )
```

```python
import functools
import math

import jax
import jax.numpy as jnp
import ml_dtypes
import numpy as np
from jax import lax
from jax.experimental import pallas as pl
from jax.experimental.pallas import tpu as pltpu
from jax.sharding import PartitionSpec as P

ROTS = 36
ANG_STEP = 8
SHIFT_SIDE = 5
SHIFTS = SHIFT_SIDE * SHIFT_SIDE
LANES = 128
GROUP = 12
ROWS = 16
FOLD = ROTS // 2 + 1

two_pi = 2.0 * math.pi
f32 = jnp.float32
bf16 = jnp.bfloat16
VMEM_LIMIT = 56 * 1024 * 1024


def fourier_rows(angles):
    index_grid = np.arange(angles)
    radians = (index_grid[:, None] * index_grid[None, :] % angles) * (two_pi / angles)
    cosine, sine_part = np.cos(radians), np.sin(radians)
    table_full = np.concatenate(
        [np.concatenate([cosine, sine_part], 1), np.concatenate([-sine_part, cosine], 1)], 0
    )
    return table_full.astype(np.float32).astype(ml_dtypes.bfloat16)


def shift_tables(angles, cycles):
    theta = np.arange(angles) * (two_pi / angles)
    radius = (np.arange(cycles) + 1) / (2.0 * cycles)
    turns = np.stack([np.cos(theta), np.sin(theta)])[:, :, None] * radius
    steps = np.arange(SHIFT_SIDE) - SHIFT_SIDE // 2
    phase = two_pi * turns[:, None] * steps[None, :, None, None]
    factors = np.stack([np.cos(phase), -np.sin(phase)], 2)
    return turns.astype(np.float32), factors.astype(np.float32)


def cos_sin_of_turns(turns):
    frac = turns - jnp.floor(turns + 0.5)
    w = frac * two_pi
    w2 = w * w
    cosine = jnp.full_like(w, 1.0 / math.factorial(16))
    for n in range(14, -1, -2):
        cosine = cosine * w2 + (-1.0) ** (n // 2) / math.factorial(n)
    sine_part = jnp.full_like(w, 1.0 / math.factorial(17))
    for n in range(15, 0, -2):
        sine_part = sine_part * w2 + (-1.0) ** (n // 2) / math.factorial(n)
    return cosine, sine_part * w


def base_kernel(shift_ref, part_ref, turns_ref, base_ref):
    p = pl.program_id(0)
    sx = shift_ref[0, p].astype(f32)
    sy = shift_ref[1, p].astype(f32)
    chunk = 32

    def turn(n, carry):
        rows = pl.ds(pl.multiple_of(n * chunk, chunk), chunk)
        cosine, sine_part = cos_sin_of_turns(sx * turns_ref[0, rows, :] + sy * turns_ref[1, rows, :])
        re = part_ref[0, 0, rows, :].astype(f32)
        im = part_ref[0, 1, rows, :].astype(f32)
        base_ref[0, 0, rows, :] = re * cosine + im * sine_part
        base_ref[0, 1, rows, :] = im * cosine - re * sine_part
        return carry

    lax.fori_loop(0, part_ref.shape[2] // chunk, turn, 0)


def make_base(particles, prior_shift):
    count, _, angles, cycles = particles.shape
    turns, _ = shift_tables(angles, cycles)
    image = pl.BlockSpec((1, 2, angles, cycles), lambda p: (p, 0, 0, 0))
    return pl.pallas_call(
        base_kernel,
        grid=(count,),
        in_specs=[
            pl.BlockSpec(memory_space=pltpu.SMEM),
            image,
            pl.BlockSpec(turns.shape, lambda p: (0, 0, 0)),
        ],
        out_specs=image,
        out_shape=jax.ShapeDtypeStruct(particles.shape, f32),
        compiler_params=pltpu.CompilerParams(vmem_limit_bytes=VMEM_LIMIT),
        name="centre",
    )(prior_shift.T, particles, turns)


def spectra_kernel(base_ref, ctf_ref, table_ref, *refs, per_step):
    factor_refs, refs = refs[: 2 * per_step], refs[2 * per_step :]
    out_ref, data_ref, re_ref, im_ref = refs[-4:]
    count, _, angles, cycles = base_ref.shape
    chunk = 32

    for g in range(per_step):
        x_ref, y_ref = factor_refs[2 * g], factor_refs[2 * g + 1]

        def shift(n, carry):
            rows = pl.ds(pl.multiple_of(n * chunk, chunk), chunk)
            low = pl.ds(pl.multiple_of(angles + n * chunk, chunk), chunk)
            xr, xi = x_ref[0, 0, 0, rows, :], x_ref[0, 0, 1, rows, :]
            yr, yi = y_ref[0, 0, 0, rows, :], y_ref[0, 0, 1, rows, :]
            tr = xr * yr - xi * yi
            ti = xr * yi + xi * yr
            for p in range(count):
                gr, gi = base_ref[p, 0, rows, :], base_ref[p, 1, rows, :]
                lanes = pl.ds((g * count + p) * cycles, cycles)
                data_ref[rows, lanes] = (gr * tr - gi * ti).astype(bf16)
                data_ref[low, lanes] = (gr * ti + gi * tr).astype(bf16)
            return carry

        lax.fori_loop(0, angles // chunk, shift, 0)

    for n in range(ROWS // 2):
        spectrum = jnp.dot(
            table_ref[...], data_ref[:, n * 2 * cycles : (n + 1) * 2 * cycles], preferred_element_type=f32
        )
        for j in range(2):
            row = 2 * n + j
            ctf_row = ctf_ref[row % count, :][None, :]
            part = spectrum[:, j * cycles : (j + 1) * cycles] * ctf_row
            re_ref[pl.ds(row, angles, stride=ROWS), :] = part[:angles]
            im_ref[pl.ds(row, angles, stride=ROWS), :] = part[angles:]
    out_ref[:, :, :cycles] = re_ref[...].reshape(angles, ROWS, cycles).astype(bf16)
    out_ref[:, :, cycles:] = im_ref[...].reshape(angles, ROWS, cycles).astype(bf16)


def spectra_steps(count):
    per_step = ROWS // count if count < ROWS else 1
    return per_step, -(-SHIFTS // per_step)


def make_spectra(base, ctf_rows, first, last, before=None, after=()):
    count, _, angles, cycles = base.shape
    per_step, steps = spectra_steps(count)
    _, factors = shift_tables(angles, cycles)
    full = lambda shape: pl.BlockSpec(shape, lambda i: (0,) * len(shape))

    def factor_spec(g, axis):
        def place(i):
            s = jnp.minimum((i + first) * per_step + g, SHIFTS - 1)
            a = lax.div(s, jnp.int32(SHIFT_SIDE))
            return (axis, s - a * SHIFT_SIDE if axis else a, 0, 0, 0)

        return pl.BlockSpec((1, 1, 2, angles, cycles), place)

    untouched = ([] if before is None else [before]) + list(after)
    in_specs = (
        [full(base.shape), full(ctf_rows.shape), full((2 * angles, 2 * angles))]
        + [factor_spec(g, axis) for g in range(per_step) for axis in range(2)]
        + [pl.BlockSpec(memory_space=pl.ANY)] * len(untouched)
    )
    return pl.pallas_call(
        functools.partial(spectra_kernel, per_step=per_step),
        grid=(last - first,),
        in_specs=in_specs,
        out_specs=pl.BlockSpec((angles, ROWS, 2 * cycles), lambda i: (0, i + first, 0)),
        out_shape=jax.ShapeDtypeStruct((angles, steps * ROWS, 2 * cycles), bf16),
        scratch_shapes=[
            pltpu.VMEM((2 * angles, ROWS * cycles), bf16),
            pltpu.VMEM((angles * ROWS, cycles), f32),
            pltpu.VMEM((angles * ROWS, cycles), f32),
        ],
        input_output_aliases={} if before is None else {3 + 2 * per_step: 0},
        compiler_params=pltpu.CompilerParams(vmem_limit_bytes=VMEM_LIMIT),
        name="spectra",
    )(base, ctf_rows, fourier_rows(angles), *[factors] * (2 * per_step), *untouched)


def half_dft(even_values, odd_values):
    half = FOLD // 2
    cos_sums, sin_sums = [None] * FOLD, [None] * FOLD

    def weighted_sum(values, k, table, start):
        total = None
        for m in range(start, FOLD, 2):
            weight = float(table((k * m % ROTS) * two_pi / ROTS))
            if values[m] is None or abs(weight) < 1e-9:
                continue
            if abs(abs(weight) - 1.0) < 1e-9:
                term = values[m] if weight > 0 else -values[m]
            else:
                term = values[m] * weight
            total = term if total is None else total + term
        return jnp.zeros_like(values[1]) if total is None else total

    for k in range(half + 1):
        even = weighted_sum(even_values, k, math.cos, 0)
        odd = weighted_sum(even_values, k, math.cos, 1)
        cos_sums[k] = even + odd
        if k != half:
            cos_sums[FOLD - 1 - k] = even - odd
        if k:
            even = weighted_sum(odd_values, k, math.sin, 0)
            odd = weighted_sum(odd_values, k, math.sin, 1)
            sin_sums[k] = even + odd
            if k != half:
                sin_sums[FOLD - 1 - k] = odd - even
    return cos_sums, sin_sums


def turn_kernel(first_ref, offset_ref, references_ref, out_ref, column_ref, in_ref, wide_ref):
    rows, cycles = references_ref.shape
    classes = offset_ref.shape[0]
    own_rows = rows // (2 * classes)
    in_ref[...] = references_ref[...].astype(f32)
    row = lax.broadcasted_iota(jnp.int32, (8, LANES), 0)
    lane = lax.broadcasted_iota(jnp.int32, (8, LANES), 1)
    freq = (lane + first_ref[0]).astype(f32) * (1.0 / (ROTS * ANG_STEP))
    tables = []
    for start in range(0, classes, 8):
        column = jnp.zeros((8, LANES), jnp.int32)
        for c in range(start, min(start + 8, classes)):
            column = jnp.where(row == c - start, offset_ref[c], column)
        column = column.astype(f32)
        column_ref[start : start + 8, :] = column
        tables.append(cos_sin_of_turns(column * freq))
    cosine = jnp.concatenate([c for c, _ in tables], 0)
    sine_part = jnp.concatenate([s for _, s in tables], 0)
    for m in range(own_rows):
        re_rows = pl.ds(2 * m * classes, classes, stride=2)
        im_rows = pl.ds(2 * m * classes + 1, classes, stride=2)
        c, s = cosine[:classes, m : m + 1], sine_part[:classes, m : m + 1]
        re, im = in_ref[re_rows, :], in_ref[im_rows, :]
        wide_ref[re_rows, :] = re * c + im * s
        wide_ref[im_rows, :] = im * c - re * s
    out_ref[...] = wide_ref[...].astype(bf16)


def turn_references(first, offsets, references):
    padded = -(-offsets.shape[0] // 8) * 8
    return pl.pallas_call(
        turn_kernel,
        in_specs=[
            pl.BlockSpec(memory_space=pltpu.SMEM),
            pl.BlockSpec(memory_space=pltpu.SMEM),
            pl.BlockSpec(memory_space=pltpu.VMEM),
        ],
        out_shape=[
            jax.ShapeDtypeStruct(references.shape, bf16),
            jax.ShapeDtypeStruct((padded, LANES), f32),
        ],
        scratch_shapes=[pltpu.VMEM(references.shape, f32)] * 2,
        compiler_params=pltpu.CompilerParams(vmem_limit_bytes=VMEM_LIMIT),
        name="turn_references",
    )(first, offsets, references)


def correlate_kernel(*refs, slots, classes, padded, finish):
    part_ref, refs = refs[slots], refs[slots + 1 :]
    weighted_refs, refs = refs[:slots], refs[slots:]
    piece_refs, refs = refs[:slots], refs[slots:]
    if finish:
        before_ref, power_before_ref, ctf_ref, weight_ref, stat_ref, share_ref = refs[:6]
        corr_ref, wide_ref, power_ref = refs[6:]
    else:
        corr_ref, power_ref, wide_ref = refs
    group = pl.program_id(0)
    cycles = piece_refs[0].shape[1]
    queries = weighted_refs[0].shape[2]
    block = piece_refs[0].shape[0]

    @pl.when(group == 0)
    def _():
        wide_ref[:, block:, :] = jnp.zeros((slots, wide_ref.shape[1] - block, cycles), f32)
        power_ref[...] = power_before_ref[...] if finish else jnp.zeros_like(power_ref)

    for j in range(slots):
        wide_ref[j, :block, :] = piece_refs[j][...].astype(f32)
    power = power_ref[...]
    for i in range(GROUP):
        total = before_ref[i, :, :queries] if finish else None
        for j in range(slots):
            re = wide_ref[j, pl.ds(2 * i * classes, padded, stride=2), :]
            im = wide_ref[j, pl.ds(2 * i * classes + 1, padded, stride=2), :]
            power = power + (re * re + im * im)
            left = jnp.concatenate(
                [jnp.concatenate([re, im], 1), jnp.concatenate([-im, re], 1)], 0
            ).astype(bf16)
            part = lax.dot_general(
                left, weighted_refs[j][0, i], (((1,), (1,)), ((), ())), preferred_element_type=f32
            )
            total = part if total is None else total + part
        row = group * GROUP + i if finish else i
        corr_ref[row, :, :queries] = total
    power_ref[...] = power

    if not finish:
        return

    @pl.when(group == pl.num_programs(0) - 1)
    def _():
        count = ctf_ref.shape[0]
        angles = ROTS * ANG_STEP
        used = SHIFTS * count
        tiles = weight_ref.shape[2] // LANES
        ctf_row = ctf_ref[...]
        ctf_rows = jnp.concatenate([ctf_row * ctf_row] * (LANES // count), 0)
        bias = lax.dot_general(
            power_ref[...],
            ctf_rows,
            (((1,), (1,)), ((), ())),
            precision=lax.Precision.HIGHEST,
            preferred_element_type=f32,
        ) * (0.5 / angles)
        wide_ref[0, :padded, :] = bias
        rows_of = lambda base: lax.broadcasted_iota(jnp.int32, (8, LANES), 0) + base
        lanes_of = lambda base: lax.broadcasted_iota(jnp.int32, (8, LANES), 1) + base

        peak = jnp.full((8, LANES), -1e30, f32)
        for tile in range(tiles):
            lanes = slice(tile * LANES, (tile + 1) * LANES)

            def scores(n, peak):
                start = pl.multiple_of(n * 8, 8)
                rows = pl.ds(start, 8)
                low = pl.ds(padded + start, 8)
                valid = (rows_of(start) < classes) & (lanes_of(tile * LANES) < used)
                even_values = [corr_ref[0, rows, lanes]]
                odd_values = [None]
                for m in range(1, ROTS // 2):
                    even_values.append(corr_ref[m, rows, lanes] + corr_ref[ROTS - m, rows, lanes])
                    odd_values.append(corr_ref[m, low, lanes] - corr_ref[ROTS - m, low, lanes])
                even_values.append(corr_ref[ROTS // 2, rows, lanes])
                odd_values.append(None)
                cos_sums, sin_sums = half_dft(even_values, odd_values)
                bias = wide_ref[0, rows, :]
                for k in range(FOLD):
                    if k in (0, FOLD - 1):
                        results = [(k, cos_sums[k])]
                    else:
                        results = [(k, cos_sums[k] - sin_sums[k]), (ROTS - k, cos_sums[k] + sin_sums[k])]
                    for place, value in results:
                        value = jnp.where(valid, value * (1.0 / angles) - bias, -1e30)
                        weight_ref[place, rows, lanes] = value
                        peak = jnp.maximum(peak, value)
                return peak

            peak = lax.fori_loop(0, padded // 8, scores, peak)

        peak = jnp.broadcast_to(jnp.max(peak, axis=0, keepdims=True), (8, LANES))
        step = count
        while step < LANES:
            peak = jnp.maximum(peak, pltpu.roll(peak, step, 1))
            step *= 2
        stat_ref[0:8, :] = peak

        def masses(n, whole):
            rows = pl.ds(pl.multiple_of(n * 8, 8), 8)
            mass = jnp.zeros((8, LANES), f32)
            for tile in range(tiles):
                lanes = slice(tile * LANES, (tile + 1) * LANES)
                for k in range(ROTS):
                    value = jnp.exp(weight_ref[k, rows, lanes] - peak)
                    weight_ref[k, rows, lanes] = value
                    mass = mass + value
            step = count
            while step < LANES:
                mass = mass + pltpu.roll(mass, step, 1)
                step *= 2
            stat_ref[pl.ds(pl.multiple_of(8 + n * 8, 8), 8), :] = mass
            return whole + mass

        whole = lax.fori_loop(0, padded // 8, masses, jnp.zeros((8, LANES), f32))
        share = jnp.concatenate([peak[:1], jnp.sum(whole, axis=0, keepdims=True)], 0)
        for j in range(share_ref.shape[0]):
            share_ref[j] = jnp.where(part_ref[0] == j, share, 0.0)


def correlate(slot_of, weighted, pieces, classes, part, before=None, power=None, ctf_rows=None, parts=1):
    _, _, queries, double = weighted.shape
    cycles = double // 2
    slots = len(pieces)
    padded = -(-classes // 8) * 8
    wide_lanes = -(-queries // LANES) * LANES
    block = 2 * GROUP * classes
    finish = ctf_rows is not None
    full = lambda shape: pl.BlockSpec(shape, lambda g, *u: (0,) * len(shape))
    in_specs = [
        pl.BlockSpec((1, GROUP, queries, double), functools.partial(lambda j, g, *u: (u[j][0], g, 0, 0), j))
        for j in range(slots)
    ] + [pl.BlockSpec((block, cycles), lambda g, *u: (g, 0))] * slots
    corr_block = pl.BlockSpec((GROUP, 2 * padded, wide_lanes), lambda g, *u: (g, 0, 0))
    corr_shape = (ROTS, 2 * padded, wide_lanes)
    wide = pltpu.VMEM((slots, block + ROWS, cycles), f32)
    scalars = [jnp.reshape(n, (1,)).astype(jnp.int32) for n in (*slot_of, part)]
    operands = scalars + [weighted] * slots + list(pieces)
    if finish:
        in_specs += [corr_block, full((padded, cycles)), full(ctf_rows.shape)]
        operands += [before, power, ctf_rows]
        out_shapes = [(ROTS, padded, wide_lanes), (8 + padded, LANES), (parts, 2, LANES)]
        out_specs = [full(shape) for shape in out_shapes]
        scratch = [pltpu.VMEM(corr_shape, f32), wide, pltpu.VMEM((padded, cycles), f32)]
    else:
        out_shapes = [corr_shape, (padded, cycles)]
        out_specs = [corr_block, full((padded, cycles))]
        scratch = [wide]
    return pl.pallas_call(
        functools.partial(correlate_kernel, slots=slots, classes=classes, padded=padded, finish=finish),
        grid_spec=pltpu.PrefetchScalarGridSpec(
            num_scalar_prefetch=len(scalars),
            grid=(ROTS // GROUP,),
            in_specs=in_specs,
            out_specs=out_specs,
            scratch_shapes=scratch,
        ),
        out_shape=[jax.ShapeDtypeStruct(shape, f32) for shape in out_shapes],
        compiler_params=pltpu.CompilerParams(vmem_limit_bytes=VMEM_LIMIT),
        name="scores" if finish else "correlate",
    )(*operands)


def back_kernel(weight_ref, stat_ref, share_ref, offset_ref, out_ref, evidence_ref, posterior_ref, sum_ref):
    padded = weight_ref.shape[1]
    queries = out_ref.shape[2]
    shares = [share_ref[j] for j in range(share_ref.shape[0])]
    top = shares[0][:1]
    for share in shares[1:]:
        top = jnp.maximum(top, share[:1])
    mass = sum(share[1:] * jnp.exp(share[:1] - top) for share in shares)
    evidence = jnp.broadcast_to(top + jnp.log(mass), (8, LANES))
    scale = jnp.exp(stat_ref[:8, :] - evidence)
    evidence_ref[...] = evidence
    posterior_ref[...] = stat_ref[8:, :] * scale[:1]
    for tile in range(weight_ref.shape[2] // LANES):
        lanes = slice(tile * LANES, (tile + 1) * LANES)

        def transform(n, carry):
            start = pl.multiple_of(n * 8, 8)
            rows = pl.ds(start, 8)
            low = pl.ds(padded + start, 8)
            values = [weight_ref[k, rows, lanes] * scale for k in range(ROTS)]
            even_values = [values[0]] + [values[k] + values[ROTS - k] for k in range(1, ROTS // 2)]
            odd_values = [None] + [values[k] - values[ROTS - k] for k in range(1, ROTS // 2)] + [None]
            cos_sums, sin_sums = half_dft(even_values + [values[ROTS // 2]], odd_values)
            for m in range(FOLD):
                sine_part = jnp.zeros_like(scale) if m in (0, FOLD - 1) else sin_sums[m]
                sum_ref[m, rows, lanes] = cos_sums[m]
                sum_ref[m, low, lanes] = sine_part
                if m not in (0, FOLD - 1):
                    sum_ref[ROTS - m, rows, lanes] = cos_sums[m]
                    sum_ref[ROTS - m, low, lanes] = -sine_part
            return carry

        lax.fori_loop(0, padded // 8, transform, 0)

    step_cos, step_sin = cos_sin_of_turns(offset_ref[...] * (1.0 / (ROTS * ANG_STEP)))

    def turn(m, carry):
        cosine, sine_part = carry
        for tile in range(weight_ref.shape[2] // LANES):
            lanes = slice(tile * LANES, (tile + 1) * LANES)
            kept = slice(tile * LANES, min((tile + 1) * LANES, queries))
            re, im = sum_ref[m, :padded, lanes], sum_ref[m, padded:, lanes]
            turned = jnp.concatenate([re * cosine - im * sine_part, re * sine_part + im * cosine], 0)
            out_ref[m, :, kept] = turned[:, : kept.stop - kept.start].astype(bf16)
        return cosine * step_cos - sine_part * step_sin, sine_part * step_cos + cosine * step_sin

    lax.fori_loop(0, ROTS, turn, (jnp.ones_like(step_cos), jnp.zeros_like(step_cos)))


def make_back(weights, stat, shares, offsets, queries):
    _, padded, wide_lanes = weights.shape
    return pl.pallas_call(
        back_kernel,
        out_shape=[
            jax.ShapeDtypeStruct((ROTS, 2 * padded, queries), bf16),
            jax.ShapeDtypeStruct((8, LANES), f32),
            jax.ShapeDtypeStruct((padded, LANES), f32),
        ],
        scratch_shapes=[pltpu.VMEM((ROTS, 2 * padded, wide_lanes), f32)],
        compiler_params=pltpu.CompilerParams(vmem_limit_bytes=VMEM_LIMIT),
        name="back",
    )(weights, stat, shares, offsets)


def sums_kernel(slot_ref, back_ref, weighted_ref, offset_ref, out_ref, wide_ref, *, classes):
    padded = offset_ref.shape[0]
    cycles = wide_ref.shape[1]
    turns = offset_ref[...] * (slot_ref[0].astype(f32) * (1.0 / ANG_STEP))
    cosine, sine_part = cos_sin_of_turns(turns)
    for i in range(GROUP):
        product = jnp.dot(back_ref[i], weighted_ref[0, i], preferred_element_type=f32)
        re = product[:padded, :cycles] - product[padded:, cycles:]
        im = product[:padded, cycles:] + product[padded:, :cycles]
        start = 2 * i * classes
        wide_ref[pl.ds(start, classes, stride=2), :] = (re * cosine - im * sine_part)[:classes]
        wide_ref[pl.ds(start + 1, classes, stride=2), :] = (re * sine_part + im * cosine)[:classes]
    out_ref[...] = wide_ref[...].astype(out_ref.dtype)


def class_sums_of(slot, back, weighted, offsets, classes, dtype):
    _, _, queries, double = weighted.shape
    cycles = double // 2
    rows = back.shape[1]
    block = 2 * GROUP * classes
    piece = pl.BlockSpec((block, cycles), lambda g, u: (g, 0))
    return pl.pallas_call(
        functools.partial(sums_kernel, classes=classes),
        grid_spec=pltpu.PrefetchScalarGridSpec(
            num_scalar_prefetch=1,
            grid=(ROTS // GROUP,),
            in_specs=[
                pl.BlockSpec((GROUP, rows, queries), lambda g, u: (g, 0, 0)),
                pl.BlockSpec((1, GROUP, queries, double), lambda g, u: (u[0], g, 0, 0)),
                pl.BlockSpec(offsets.shape, lambda g, u: (0, 0)),
            ],
            out_specs=piece,
            scratch_shapes=[pltpu.VMEM((block, cycles), f32)],
        ),
        out_shape=jax.ShapeDtypeStruct((ROTS * 2 * classes, cycles), dtype),
        compiler_params=pltpu.CompilerParams(vmem_limit_bytes=VMEM_LIMIT),
        name="class_sums",
    )(jnp.reshape(slot, (1,)).astype(jnp.int32), back, weighted, offsets)


def across(piece):
    return lax.ppermute(piece, "dp", [(d, d ^ 1) for d in range(8)])


def along(piece, pairs):
    return lax.ppermute(piece, "dp", [(2 * a + x, 2 * b + x) for a, b in pairs for x in range(2)])


def gather_on_line(piece, base, ctf_rows):
    index = lax.axis_index("dp")
    line, side = index // 2, index % 2
    _, steps = spectra_steps(base.shape[0])
    cuts = [0, 3 * steps // 13, 7 * steps // 13, 11 * steps // 13, steps]

    own_crossed = across(piece)
    near = along(piece, ((0, 1), (1, 0), (2, 3), (3, 2)))
    middle = along(piece, ((1, 2), (2, 1)))
    weighted = make_spectra(base, ctf_rows, cuts[0], cuts[1])
    weighted, near, middle, own_crossed = lax.optimization_barrier((weighted, near, middle, own_crossed))
    near_crossed = across(near)
    far_middle = along(near, ((1, 2), (2, 1)))
    end = along(middle, ((1, 0), (2, 3)))
    weighted = make_spectra(base, ctf_rows, cuts[1], cuts[2], weighted)
    weighted, far_middle, end, near_crossed = lax.optimization_barrier(
        (weighted, far_middle, end, near_crossed)
    )
    third = middle + end
    third_crossed = across(third)
    far_end = along(far_middle, ((1, 0), (2, 3)))
    weighted = make_spectra(base, ctf_rows, cuts[2], cuts[3], weighted)
    weighted, far_end, third_crossed = lax.optimization_barrier((weighted, far_end, third_crossed))
    fourth = far_middle + far_end
    fourth_crossed = across(fourth)
    weighted = make_spectra(base, ctf_rows, cuts[3], cuts[4], weighted)

    pieces = [piece, own_crossed, near, near_crossed, third, third_crossed, fourth, fourth_crossed]
    places = [line, line ^ 1, jnp.where(line < 2, 2, 1), jnp.where(line < 2, 3, 0)]
    slot_of = [2 * place + s for place in places for s in (side, 1 - side)]
    return weighted, pieces, slot_of


def reduce_on_line(back, weighted, offsets, classes):
    index = lax.axis_index("dp")
    line, side = index // 2, index % 2
    order = [jnp.where(line < 2, 3, 0), jnp.where(line < 2, 2, 1), line ^ 1, line]
    theirs = [class_sums_of(2 * z + 1 - side, back, weighted, offsets, classes, bf16) for z in order]
    ours = [class_sums_of(2 * z + side, back, weighted, offsets, classes, f32) for z in order]
    at_end = (line == 0) | (line == 3)

    crossed = [across(theirs[0])]
    crossed[0], theirs[1], theirs[2], ours[0] = lax.optimization_barrier(
        (crossed[0], theirs[1], theirs[2], ours[0])
    )
    crossed.append(across(theirs[1]))
    farthest = ours[0] + crossed[0].astype(f32)
    first = along(farthest.astype(bf16), ((0, 1), (3, 2)))
    crossed[1], theirs[2], theirs[3], ours[1], ours[2] = lax.optimization_barrier(
        (crossed[1], theirs[2], theirs[3], ours[1], ours[2])
    )
    crossed.append(across(theirs[2]))
    next_farthest = ours[1] + crossed[1].astype(f32)
    second = (jnp.where(at_end, next_farthest, farthest) + first.astype(f32)).astype(bf16)
    from_ends = along(second, ((0, 1), (3, 2)))
    from_middle = along(second, ((1, 2), (2, 1)))
    crossed[2], theirs[3], ours[3] = lax.optimization_barrier((crossed[2], theirs[3], ours[3]))
    crossed.append(across(theirs[3]))
    third = (next_farthest + from_ends.astype(f32)).astype(bf16)
    third = along(third, ((1, 2), (2, 1)))
    fourth = (ours[2] + crossed[2].astype(f32) + from_middle.astype(f32)).astype(bf16)
    fourth = along(fourth, ((0, 1), (1, 0), (2, 3), (3, 2)))
    return ours[3] + crossed[3].astype(f32) + third.astype(f32) + fourth.astype(f32)


def local(particles, references, ctf_table, rot_offset, prior_shift, defocus_group):
    count, _, angles, cycles = particles.shape
    own_rows, _, classes, _ = references.shape
    slots = angles // ROTS
    group_count = ctf_table.shape[0]
    devices = lax.axis_size("dp")

    first = (lax.axis_index("dp") * own_rows).astype(jnp.int32).reshape(1)
    rows = jnp.transpose(references, (0, 2, 1, 3)).reshape(own_rows * 2 * classes, cycles)
    piece, offsets = turn_references(first, rot_offset, rows)

    onehot = (defocus_group[:, None] == jnp.arange(group_count, dtype=jnp.int32)[None, :]).astype(f32)
    ctf_rows = jnp.dot(onehot, ctf_table, precision=lax.Precision.HIGHEST)
    base = make_base(particles, prior_shift)
    on_line = devices == 8 and own_rows == ROTS
    if on_line:
        weighted, pieces, slot_of = gather_on_line(piece, base, ctf_rows)
    else:
        gathered = lax.all_gather(piece, "dp", axis=0, tiled=True)
        gathered = gathered.reshape(slots, ROTS * 2 * classes, cycles)
        pieces = [gathered[j] for j in range(slots)]
        slot_of = list(range(slots))
        weighted = make_spectra(base, ctf_rows, 0, spectra_steps(count)[1])
    queries = weighted.shape[1]
    weighted = weighted.reshape(slots, ROTS, queries, 2 * cycles)

    half = slots // 2
    part = lax.axis_index("cls")
    corr, power = correlate(slot_of[:half], weighted, pieces[:half], classes, part)
    weights, stat, share = correlate(
        slot_of[half:], weighted, pieces[half:], classes, part, corr, power, ctf_rows, lax.axis_size("cls")
    )
    shares = lax.psum(share, "cls")
    back, evidence, posterior = make_back(weights, stat, shares, offsets, queries)
    log_evidence = evidence[0, :count]
    class_posterior = posterior[:classes, :count].T
    if on_line:
        class_rows = reduce_on_line(back, weighted, offsets, classes)
    else:
        sums = [class_sums_of(slot_of[u], back, weighted, offsets, classes, bf16) for u in range(slots)]
        summed = lax.psum_scatter(jnp.concatenate(sums, 0), "dp", scatter_dimension=0, tiled=True)
        class_rows = summed.astype(f32)
    class_sums = jnp.transpose(class_rows.reshape(own_rows, classes, 2, cycles), (0, 2, 1, 3))
    return (log_evidence, class_posterior, class_sums)


def solution(mesh):
    placed = (
        P("dp", None, None, None),
        P("dp", None, "cls", None),
        P(),
        P("cls"),
        P("dp", None),
        P("dp"),
    )
    return jax.shard_map(
        local,
        mesh=mesh,
        in_specs=placed,
        out_specs=(P("dp"), P("dp", "cls"), P("dp", None, "cls", None)),
        check_vma=False,
    )
```

```python
import functools
import math

import jax
import jax.numpy as jnp
import ml_dtypes
import numpy as np
from jax import lax
from jax.experimental import pallas as pl
from jax.experimental.pallas import tpu as pltpu
from jax.sharding import PartitionSpec as P

ROTS = 36
ANG_STEP = 8
SHIFT_SIDE = 5
SHIFTS = SHIFT_SIDE * SHIFT_SIDE
LANES = 128
GROUP = 12
ROWS = 16
APART = 17
FOLD = ROTS // 2 + 1

two_pi = 2.0 * math.pi
f32 = jnp.float32
bf16 = jnp.bfloat16
VMEM_LIMIT = 56 * 1024 * 1024


def fourier_rows(angles):
    index_grid = np.arange(angles)
    radians = (index_grid[:, None] * index_grid[None, :] % angles) * (two_pi / angles)
    cosine, sine_part = np.cos(radians), np.sin(radians)
    table_full = np.concatenate(
        [np.concatenate([cosine, sine_part], 1), np.concatenate([-sine_part, cosine], 1)], 0
    )
    return table_full.astype(np.float32).astype(ml_dtypes.bfloat16)


def shift_tables(angles, cycles):
    theta = np.arange(angles) * (two_pi / angles)
    radius = (np.arange(cycles) + 1) / (2.0 * cycles)
    turns = np.stack([np.cos(theta), np.sin(theta)])[:, :, None] * radius
    steps = np.arange(SHIFT_SIDE) - SHIFT_SIDE // 2
    phase = two_pi * turns[:, None] * steps[None, :, None, None]
    factors = np.stack([np.cos(phase), -np.sin(phase)], 2)
    return turns.astype(np.float32), factors.astype(np.float32)


def cos_sin_of_turns(turns):
    frac = turns - jnp.floor(turns + 0.5)
    w = frac * two_pi
    w2 = w * w
    cosine = jnp.full_like(w, 1.0 / math.factorial(16))
    for n in range(14, -1, -2):
        cosine = cosine * w2 + (-1.0) ** (n // 2) / math.factorial(n)
    sine_part = jnp.full_like(w, 1.0 / math.factorial(17))
    for n in range(15, 0, -2):
        sine_part = sine_part * w2 + (-1.0) ** (n // 2) / math.factorial(n)
    return cosine, sine_part * w


def base_kernel(shift_ref, part_ref, turns_ref, base_ref):
    p = pl.program_id(0)
    sx = shift_ref[0, p].astype(f32)
    sy = shift_ref[1, p].astype(f32)
    chunk = 32

    def turn(n, carry):
        rows = pl.ds(pl.multiple_of(n * chunk, chunk), chunk)
        cosine, sine_part = cos_sin_of_turns(sx * turns_ref[0, rows, :] + sy * turns_ref[1, rows, :])
        re = part_ref[0, 0, rows, :].astype(f32)
        im = part_ref[0, 1, rows, :].astype(f32)
        base_ref[0, 0, rows, :] = re * cosine + im * sine_part
        base_ref[0, 1, rows, :] = im * cosine - re * sine_part
        return carry

    lax.fori_loop(0, part_ref.shape[2] // chunk, turn, 0)


def make_base(particles, prior_shift):
    count, _, angles, cycles = particles.shape
    turns, _ = shift_tables(angles, cycles)
    image = pl.BlockSpec((1, 2, angles, cycles), lambda p: (p, 0, 0, 0))
    return pl.pallas_call(
        base_kernel,
        grid=(count,),
        in_specs=[
            pl.BlockSpec(memory_space=pltpu.SMEM),
            image,
            pl.BlockSpec(turns.shape, lambda p: (0, 0, 0)),
        ],
        out_specs=image,
        out_shape=jax.ShapeDtypeStruct(particles.shape, f32),
        compiler_params=pltpu.CompilerParams(vmem_limit_bytes=VMEM_LIMIT),
        name="centre",
    )(prior_shift.T, particles, turns)


def spectra_kernel(base_ref, ctf_ref, table_ref, *refs, per_step):
    factor_refs, refs = refs[: 2 * per_step], refs[2 * per_step :]
    out_ref, data_ref, re_ref, im_ref = refs[-4:]
    count, _, angles, cycles = base_ref.shape
    chunk = 32

    for g in range(per_step):
        x_ref, y_ref = factor_refs[2 * g], factor_refs[2 * g + 1]

        def shift(n, carry):
            rows = pl.ds(pl.multiple_of(n * chunk, chunk), chunk)
            low = pl.ds(pl.multiple_of(angles + n * chunk, chunk), chunk)
            xr, xi = x_ref[0, 0, 0, rows, :], x_ref[0, 0, 1, rows, :]
            yr, yi = y_ref[0, 0, 0, rows, :], y_ref[0, 0, 1, rows, :]
            tr = xr * yr - xi * yi
            ti = xr * yi + xi * yr
            for p in range(count):
                gr, gi = base_ref[p, 0, rows, :], base_ref[p, 1, rows, :]
                lanes = pl.ds((g * count + p) * cycles, cycles)
                data_ref[rows, lanes] = (gr * tr - gi * ti).astype(bf16)
                data_ref[low, lanes] = (gr * ti + gi * tr).astype(bf16)
            return carry

        lax.fori_loop(0, angles // chunk, shift, 0)

    for n in range(ROWS // 2):
        spectrum = jnp.dot(
            table_ref[...], data_ref[:, n * 2 * cycles : (n + 1) * 2 * cycles], preferred_element_type=f32
        )
        for j in range(2):
            row = 2 * n + j
            ctf_row = ctf_ref[row % count, :][None, :]
            part = spectrum[:, j * cycles : (j + 1) * cycles] * ctf_row
            re_ref[pl.ds(row, angles, stride=APART), :] = part[:angles]
            im_ref[pl.ds(row, angles, stride=APART), :] = part[angles:]
    for m in range(angles):
        out_ref[m, :, :cycles] = re_ref[m * APART : m * APART + ROWS, :].astype(bf16)
        out_ref[m, :, cycles:] = im_ref[m * APART : m * APART + ROWS, :].astype(bf16)


def spectra_steps(count):
    per_step = ROWS // count if count < ROWS else 1
    return per_step, -(-SHIFTS // per_step)


def make_spectra(base, ctf_rows, first, last, before=None, after=()):
    count, _, angles, cycles = base.shape
    per_step, steps = spectra_steps(count)
    _, factors = shift_tables(angles, cycles)
    full = lambda shape: pl.BlockSpec(shape, lambda i: (0,) * len(shape))

    def factor_spec(g, axis):
        def place(i):
            s = jnp.minimum((i + first) * per_step + g, SHIFTS - 1)
            a = lax.div(s, jnp.int32(SHIFT_SIDE))
            return (axis, s - a * SHIFT_SIDE if axis else a, 0, 0, 0)

        return pl.BlockSpec((1, 1, 2, angles, cycles), place)

    untouched = ([] if before is None else [before]) + list(after)
    in_specs = (
        [full(base.shape), full(ctf_rows.shape), full((2 * angles, 2 * angles))]
        + [factor_spec(g, axis) for g in range(per_step) for axis in range(2)]
        + [pl.BlockSpec(memory_space=pl.ANY)] * len(untouched)
    )
    return pl.pallas_call(
        functools.partial(spectra_kernel, per_step=per_step),
        grid=(last - first,),
        in_specs=in_specs,
        out_specs=pl.BlockSpec((angles, ROWS, 2 * cycles), lambda i: (0, i + first, 0)),
        out_shape=jax.ShapeDtypeStruct((angles, steps * ROWS, 2 * cycles), bf16),
        scratch_shapes=[
            pltpu.VMEM((2 * angles, ROWS * cycles), bf16),
            pltpu.VMEM((angles * APART, cycles), f32),
            pltpu.VMEM((angles * APART, cycles), f32),
        ],
        input_output_aliases={} if before is None else {3 + 2 * per_step: 0},
        compiler_params=pltpu.CompilerParams(vmem_limit_bytes=VMEM_LIMIT),
        name="spectra",
    )(base, ctf_rows, fourier_rows(angles), *[factors] * (2 * per_step), *untouched)


def half_dft(even_values, odd_values):
    half = FOLD // 2
    cos_sums, sin_sums = [None] * FOLD, [None] * FOLD

    def weighted_sum(values, k, table, start):
        total = None
        for m in range(start, FOLD, 2):
            weight = float(table((k * m % ROTS) * two_pi / ROTS))
            if values[m] is None or abs(weight) < 1e-9:
                continue
            if abs(abs(weight) - 1.0) < 1e-9:
                term = values[m] if weight > 0 else -values[m]
            else:
                term = values[m] * weight
            total = term if total is None else total + term
        return jnp.zeros_like(values[1]) if total is None else total

    for k in range(half + 1):
        even = weighted_sum(even_values, k, math.cos, 0)
        odd = weighted_sum(even_values, k, math.cos, 1)
        cos_sums[k] = even + odd
        if k != half:
            cos_sums[FOLD - 1 - k] = even - odd
        if k:
            even = weighted_sum(odd_values, k, math.sin, 0)
            odd = weighted_sum(odd_values, k, math.sin, 1)
            sin_sums[k] = even + odd
            if k != half:
                sin_sums[FOLD - 1 - k] = odd - even
    return cos_sums, sin_sums


def turn_kernel(first_ref, offset_ref, references_ref, out_ref, column_ref, in_ref, wide_ref):
    rows, cycles = references_ref.shape
    classes = offset_ref.shape[0]
    own_rows = rows // (2 * classes)
    in_ref[...] = references_ref[...].astype(f32)
    row = lax.broadcasted_iota(jnp.int32, (8, LANES), 0)
    lane = lax.broadcasted_iota(jnp.int32, (8, LANES), 1)
    freq = (lane + first_ref[0]).astype(f32) * (1.0 / (ROTS * ANG_STEP))
    tables = []
    for start in range(0, classes, 8):
        column = jnp.zeros((8, LANES), jnp.int32)
        for c in range(start, min(start + 8, classes)):
            column = jnp.where(row == c - start, offset_ref[c], column)
        column = column.astype(f32)
        column_ref[start : start + 8, :] = column
        tables.append(cos_sin_of_turns(column * freq))
    cosine = jnp.concatenate([c for c, _ in tables], 0)
    sine_part = jnp.concatenate([s for _, s in tables], 0)
    for m in range(own_rows):
        re_rows = pl.ds(2 * m * classes, classes, stride=2)
        im_rows = pl.ds(2 * m * classes + 1, classes, stride=2)
        c, s = cosine[:classes, m : m + 1], sine_part[:classes, m : m + 1]
        re, im = in_ref[re_rows, :], in_ref[im_rows, :]
        wide_ref[re_rows, :] = re * c + im * s
        wide_ref[im_rows, :] = im * c - re * s
    out_ref[...] = wide_ref[...].astype(bf16)


def turn_references(first, offsets, references):
    padded = -(-offsets.shape[0] // 8) * 8
    return pl.pallas_call(
        turn_kernel,
        in_specs=[
            pl.BlockSpec(memory_space=pltpu.SMEM),
            pl.BlockSpec(memory_space=pltpu.SMEM),
            pl.BlockSpec(memory_space=pltpu.VMEM),
        ],
        out_shape=[
            jax.ShapeDtypeStruct(references.shape, bf16),
            jax.ShapeDtypeStruct((padded, LANES), f32),
        ],
        scratch_shapes=[pltpu.VMEM(references.shape, f32)] * 2,
        compiler_params=pltpu.CompilerParams(vmem_limit_bytes=VMEM_LIMIT),
        name="turn_references",
    )(first, offsets, references)


def correlate_kernel(*refs, slots, classes, padded, finish):
    part_ref, refs = refs[slots], refs[slots + 1 :]
    weighted_refs, refs = refs[:slots], refs[slots:]
    piece_refs, refs = refs[:slots], refs[slots:]
    if finish:
        before_ref, power_before_ref, ctf_ref, weight_ref, stat_ref, share_ref = refs[:6]
        corr_ref, wide_ref, power_ref = refs[6:]
    else:
        corr_ref, power_ref, wide_ref = refs
    group = pl.program_id(0)
    cycles = piece_refs[0].shape[1]
    queries = weighted_refs[0].shape[2]
    block = piece_refs[0].shape[0]

    @pl.when(group == 0)
    def _():
        wide_ref[:, block:, :] = jnp.zeros((slots, wide_ref.shape[1] - block, cycles), f32)
        power_ref[...] = power_before_ref[...] if finish else jnp.zeros_like(power_ref)

    for j in range(slots):
        wide_ref[j, :block, :] = piece_refs[j][...].astype(f32)
    power = power_ref[...]
    for i in range(GROUP):
        total = before_ref[i, :, :queries] if finish else None
        for j in range(slots):
            re = wide_ref[j, pl.ds(2 * i * classes, padded, stride=2), :]
            im = wide_ref[j, pl.ds(2 * i * classes + 1, padded, stride=2), :]
            power = power + (re * re + im * im)
            left = jnp.concatenate(
                [jnp.concatenate([re, im], 1), jnp.concatenate([-im, re], 1)], 0
            ).astype(bf16)
            part = lax.dot_general(
                left, weighted_refs[j][0, i], (((1,), (1,)), ((), ())), preferred_element_type=f32
            )
            total = part if total is None else total + part
        row = group * GROUP + i if finish else i
        corr_ref[row, :, :queries] = total
    power_ref[...] = power

    if not finish:
        return

    @pl.when(group == pl.num_programs(0) - 1)
    def _():
        count = ctf_ref.shape[0]
        angles = ROTS * ANG_STEP
        used = SHIFTS * count
        tiles = weight_ref.shape[2] // LANES
        ctf_row = ctf_ref[...]
        ctf_rows = jnp.concatenate([ctf_row * ctf_row] * (LANES // count), 0)
        bias = lax.dot_general(
            power_ref[...],
            ctf_rows,
            (((1,), (1,)), ((), ())),
            precision=lax.Precision.HIGHEST,
            preferred_element_type=f32,
        ) * (0.5 / angles)
        wide_ref[0, :padded, :] = bias
        rows_of = lambda base: lax.broadcasted_iota(jnp.int32, (8, LANES), 0) + base
        lanes_of = lambda base: lax.broadcasted_iota(jnp.int32, (8, LANES), 1) + base

        peak = jnp.full((8, LANES), -1e30, f32)
        for tile in range(tiles):
            lanes = slice(tile * LANES, (tile + 1) * LANES)

            def scores(n, peak):
                start = pl.multiple_of(n * 8, 8)
                rows = pl.ds(start, 8)
                low = pl.ds(padded + start, 8)
                valid = (rows_of(start) < classes) & (lanes_of(tile * LANES) < used)
                even_values = [corr_ref[0, rows, lanes]]
                odd_values = [None]
                for m in range(1, ROTS // 2):
                    even_values.append(corr_ref[m, rows, lanes] + corr_ref[ROTS - m, rows, lanes])
                    odd_values.append(corr_ref[m, low, lanes] - corr_ref[ROTS - m, low, lanes])
                even_values.append(corr_ref[ROTS // 2, rows, lanes])
                odd_values.append(None)
                cos_sums, sin_sums = half_dft(even_values, odd_values)
                bias = wide_ref[0, rows, :]
                for k in range(FOLD):
                    if k in (0, FOLD - 1):
                        results = [(k, cos_sums[k])]
                    else:
                        results = [(k, cos_sums[k] - sin_sums[k]), (ROTS - k, cos_sums[k] + sin_sums[k])]
                    for place, value in results:
                        value = jnp.where(valid, value * (1.0 / angles) - bias, -1e30)
                        weight_ref[place, rows, lanes] = value
                        peak = jnp.maximum(peak, value)
                return peak

            peak = lax.fori_loop(0, padded // 8, scores, peak)

        peak = jnp.broadcast_to(jnp.max(peak, axis=0, keepdims=True), (8, LANES))
        step = count
        while step < LANES:
            peak = jnp.maximum(peak, pltpu.roll(peak, step, 1))
            step *= 2
        stat_ref[0:8, :] = peak

        def masses(n, whole):
            rows = pl.ds(pl.multiple_of(n * 8, 8), 8)
            mass = jnp.zeros((8, LANES), f32)
            for tile in range(tiles):
                lanes = slice(tile * LANES, (tile + 1) * LANES)
                for k in range(ROTS):
                    value = jnp.exp(weight_ref[k, rows, lanes] - peak)
                    weight_ref[k, rows, lanes] = value
                    mass = mass + value
            step = count
            while step < LANES:
                mass = mass + pltpu.roll(mass, step, 1)
                step *= 2
            stat_ref[pl.ds(pl.multiple_of(8 + n * 8, 8), 8), :] = mass
            return whole + mass

        whole = lax.fori_loop(0, padded // 8, masses, jnp.zeros((8, LANES), f32))
        share = jnp.concatenate([peak[:1], jnp.sum(whole, axis=0, keepdims=True)], 0)
        for j in range(share_ref.shape[0]):
            share_ref[j] = jnp.where(part_ref[0] == j, share, 0.0)


def correlate(slot_of, weighted, pieces, classes, part, before=None, power=None, ctf_rows=None, parts=1):
    _, _, queries, double = weighted.shape
    cycles = double // 2
    slots = len(pieces)
    padded = -(-classes // 8) * 8
    wide_lanes = -(-queries // LANES) * LANES
    block = 2 * GROUP * classes
    finish = ctf_rows is not None
    full = lambda shape: pl.BlockSpec(shape, lambda g, *u: (0,) * len(shape))
    in_specs = [
        pl.BlockSpec((1, GROUP, queries, double), functools.partial(lambda j, g, *u: (u[j][0], g, 0, 0), j))
        for j in range(slots)
    ] + [pl.BlockSpec((block, cycles), lambda g, *u: (g, 0))] * slots
    corr_block = pl.BlockSpec((GROUP, 2 * padded, wide_lanes), lambda g, *u: (g, 0, 0))
    corr_shape = (ROTS, 2 * padded, wide_lanes)
    wide = pltpu.VMEM((slots, block + ROWS, cycles), f32)
    scalars = [jnp.reshape(n, (1,)).astype(jnp.int32) for n in (*slot_of, part)]
    operands = scalars + [weighted] * slots + list(pieces)
    if finish:
        in_specs += [corr_block, full((padded, cycles)), full(ctf_rows.shape)]
        operands += [before, power, ctf_rows]
        out_shapes = [(ROTS, padded, wide_lanes), (8 + padded, LANES), (parts, 2, LANES)]
        out_specs = [full(shape) for shape in out_shapes]
        scratch = [pltpu.VMEM(corr_shape, f32), wide, pltpu.VMEM((padded, cycles), f32)]
    else:
        out_shapes = [corr_shape, (padded, cycles)]
        out_specs = [corr_block, full((padded, cycles))]
        scratch = [wide]
    return pl.pallas_call(
        functools.partial(correlate_kernel, slots=slots, classes=classes, padded=padded, finish=finish),
        grid_spec=pltpu.PrefetchScalarGridSpec(
            num_scalar_prefetch=len(scalars),
            grid=(ROTS // GROUP,),
            in_specs=in_specs,
            out_specs=out_specs,
            scratch_shapes=scratch,
        ),
        out_shape=[jax.ShapeDtypeStruct(shape, f32) for shape in out_shapes],
        compiler_params=pltpu.CompilerParams(vmem_limit_bytes=VMEM_LIMIT),
        name="scores" if finish else "correlate",
    )(*operands)


def back_kernel(weight_ref, stat_ref, share_ref, offset_ref, out_ref, evidence_ref, posterior_ref, sum_ref):
    padded = weight_ref.shape[1]
    queries = out_ref.shape[2]
    shares = [share_ref[j] for j in range(share_ref.shape[0])]
    top = shares[0][:1]
    for share in shares[1:]:
        top = jnp.maximum(top, share[:1])
    mass = sum(share[1:] * jnp.exp(share[:1] - top) for share in shares)
    evidence = jnp.broadcast_to(top + jnp.log(mass), (8, LANES))
    scale = jnp.exp(stat_ref[:8, :] - evidence)
    evidence_ref[...] = evidence
    posterior_ref[...] = stat_ref[8:, :] * scale[:1]
    for tile in range(weight_ref.shape[2] // LANES):
        lanes = slice(tile * LANES, (tile + 1) * LANES)

        def transform(n, carry):
            start = pl.multiple_of(n * 8, 8)
            rows = pl.ds(start, 8)
            low = pl.ds(padded + start, 8)
            values = [weight_ref[k, rows, lanes] * scale for k in range(ROTS)]
            even_values = [values[0]] + [values[k] + values[ROTS - k] for k in range(1, ROTS // 2)]
            odd_values = [None] + [values[k] - values[ROTS - k] for k in range(1, ROTS // 2)] + [None]
            cos_sums, sin_sums = half_dft(even_values + [values[ROTS // 2]], odd_values)
            for m in range(FOLD):
                sine_part = jnp.zeros_like(scale) if m in (0, FOLD - 1) else sin_sums[m]
                sum_ref[m, rows, lanes] = cos_sums[m]
                sum_ref[m, low, lanes] = sine_part
                if m not in (0, FOLD - 1):
                    sum_ref[ROTS - m, rows, lanes] = cos_sums[m]
                    sum_ref[ROTS - m, low, lanes] = -sine_part
            return carry

        lax.fori_loop(0, padded // 8, transform, 0)

    step_cos, step_sin = cos_sin_of_turns(offset_ref[...] * (1.0 / (ROTS * ANG_STEP)))

    def turn(m, carry):
        cosine, sine_part = carry
        for tile in range(weight_ref.shape[2] // LANES):
            lanes = slice(tile * LANES, (tile + 1) * LANES)
            kept = slice(tile * LANES, min((tile + 1) * LANES, queries))
            re, im = sum_ref[m, :padded, lanes], sum_ref[m, padded:, lanes]
            turned = jnp.concatenate([re * cosine - im * sine_part, re * sine_part + im * cosine], 0)
            out_ref[m, :, kept] = turned[:, : kept.stop - kept.start].astype(bf16)
        return cosine * step_cos - sine_part * step_sin, sine_part * step_cos + cosine * step_sin

    lax.fori_loop(0, ROTS, turn, (jnp.ones_like(step_cos), jnp.zeros_like(step_cos)))


def make_back(weights, stat, shares, offsets, queries):
    _, padded, wide_lanes = weights.shape
    return pl.pallas_call(
        back_kernel,
        out_shape=[
            jax.ShapeDtypeStruct((ROTS, 2 * padded, queries), bf16),
            jax.ShapeDtypeStruct((8, LANES), f32),
            jax.ShapeDtypeStruct((padded, LANES), f32),
        ],
        scratch_shapes=[pltpu.VMEM((ROTS, 2 * padded, wide_lanes), f32)],
        compiler_params=pltpu.CompilerParams(vmem_limit_bytes=VMEM_LIMIT),
        name="back",
    )(weights, stat, shares, offsets)


def sums_kernel(slot_ref, back_ref, weighted_ref, offset_ref, out_ref, wide_ref, *, classes):
    padded = offset_ref.shape[0]
    cycles = wide_ref.shape[1]
    turns = offset_ref[...] * (slot_ref[0].astype(f32) * (1.0 / ANG_STEP))
    cosine, sine_part = cos_sin_of_turns(turns)
    for i in range(GROUP):
        product = jnp.dot(back_ref[i], weighted_ref[0, i], preferred_element_type=f32)
        re = product[:padded, :cycles] - product[padded:, cycles:]
        im = product[:padded, cycles:] + product[padded:, :cycles]
        start = 2 * i * classes
        wide_ref[pl.ds(start, classes, stride=2), :] = (re * cosine - im * sine_part)[:classes]
        wide_ref[pl.ds(start + 1, classes, stride=2), :] = (re * sine_part + im * cosine)[:classes]
    out_ref[...] = wide_ref[...].astype(out_ref.dtype)


def class_sums_of(slot, back, weighted, offsets, classes, dtype):
    _, _, queries, double = weighted.shape
    cycles = double // 2
    rows = back.shape[1]
    block = 2 * GROUP * classes
    piece = pl.BlockSpec((block, cycles), lambda g, u: (g, 0))
    return pl.pallas_call(
        functools.partial(sums_kernel, classes=classes),
        grid_spec=pltpu.PrefetchScalarGridSpec(
            num_scalar_prefetch=1,
            grid=(ROTS // GROUP,),
            in_specs=[
                pl.BlockSpec((GROUP, rows, queries), lambda g, u: (g, 0, 0)),
                pl.BlockSpec((1, GROUP, queries, double), lambda g, u: (u[0], g, 0, 0)),
                pl.BlockSpec(offsets.shape, lambda g, u: (0, 0)),
            ],
            out_specs=piece,
            scratch_shapes=[pltpu.VMEM((block, cycles), f32)],
        ),
        out_shape=jax.ShapeDtypeStruct((ROTS * 2 * classes, cycles), dtype),
        compiler_params=pltpu.CompilerParams(vmem_limit_bytes=VMEM_LIMIT),
        name="class_sums",
    )(jnp.reshape(slot, (1,)).astype(jnp.int32), back, weighted, offsets)


def across(piece):
    return lax.ppermute(piece, "dp", [(d, d ^ 1) for d in range(8)])


def along(piece, pairs):
    return lax.ppermute(piece, "dp", [(2 * a + x, 2 * b + x) for a, b in pairs for x in range(2)])


def gather_on_line(piece, base, ctf_rows):
    index = lax.axis_index("dp")
    line, side = index // 2, index % 2
    _, steps = spectra_steps(base.shape[0])
    cuts = [0, 3 * steps // 13, 7 * steps // 13, 11 * steps // 13, steps]

    own_crossed = across(piece)
    near = along(piece, ((0, 1), (1, 0), (2, 3), (3, 2)))
    middle = along(piece, ((1, 2), (2, 1)))
    weighted = make_spectra(base, ctf_rows, cuts[0], cuts[1])
    weighted, near, middle, own_crossed = lax.optimization_barrier((weighted, near, middle, own_crossed))
    near_crossed = across(near)
    far_middle = along(near, ((1, 2), (2, 1)))
    end = along(middle, ((1, 0), (2, 3)))
    weighted = make_spectra(base, ctf_rows, cuts[1], cuts[2], weighted)
    weighted, far_middle, end, near_crossed = lax.optimization_barrier(
        (weighted, far_middle, end, near_crossed)
    )
    third = middle + end
    third_crossed = across(third)
    far_end = along(far_middle, ((1, 0), (2, 3)))
    weighted = make_spectra(base, ctf_rows, cuts[2], cuts[3], weighted)
    weighted, far_end, third_crossed = lax.optimization_barrier((weighted, far_end, third_crossed))
    fourth = far_middle + far_end
    fourth_crossed = across(fourth)
    weighted = make_spectra(base, ctf_rows, cuts[3], cuts[4], weighted)

    pieces = [piece, own_crossed, near, near_crossed, third, third_crossed, fourth, fourth_crossed]
    places = [line, line ^ 1, jnp.where(line < 2, 2, 1), jnp.where(line < 2, 3, 0)]
    slot_of = [2 * place + s for place in places for s in (side, 1 - side)]
    return weighted, pieces, slot_of


def reduce_on_line(back, weighted, offsets, classes):
    index = lax.axis_index("dp")
    line, side = index // 2, index % 2
    order = [jnp.where(line < 2, 3, 0), jnp.where(line < 2, 2, 1), line ^ 1, line]
    theirs = [class_sums_of(2 * z + 1 - side, back, weighted, offsets, classes, bf16) for z in order]
    ours = [class_sums_of(2 * z + side, back, weighted, offsets, classes, f32) for z in order]
    at_end = (line == 0) | (line == 3)

    crossed = [across(theirs[0])]
    crossed[0], theirs[1], theirs[2], ours[0], ours[1] = lax.optimization_barrier(
        (crossed[0], theirs[1], theirs[2], ours[0], ours[1])
    )
    crossed.append(across(theirs[1]))
    farthest = ours[0] + crossed[0].astype(f32)
    first = along(farthest.astype(bf16), ((0, 1), (3, 2)))
    crossed[1], theirs[2], theirs[3], ours[2], ours[3] = lax.optimization_barrier(
        (crossed[1], theirs[2], theirs[3], ours[2], ours[3])
    )
    crossed.append(across(theirs[2]))
    next_farthest = ours[1] + crossed[1].astype(f32)
    second = (jnp.where(at_end, next_farthest, farthest) + first.astype(f32)).astype(bf16)
    from_ends = along(second, ((0, 1), (3, 2)))
    from_middle = along(second, ((1, 2), (2, 1)))
    crossed[2], theirs[3] = lax.optimization_barrier((crossed[2], theirs[3]))
    crossed.append(across(theirs[3]))
    third = (next_farthest + from_ends.astype(f32)).astype(bf16)
    third = along(third, ((1, 2), (2, 1)))
    fourth = (ours[2] + crossed[2].astype(f32) + from_middle.astype(f32)).astype(bf16)
    fourth = along(fourth, ((0, 1), (1, 0), (2, 3), (3, 2)))
    return ours[3] + crossed[3].astype(f32) + third.astype(f32) + fourth.astype(f32)


def local(particles, references, ctf_table, rot_offset, prior_shift, defocus_group):
    count, _, angles, cycles = particles.shape
    own_rows, _, classes, _ = references.shape
    slots = angles // ROTS
    group_count = ctf_table.shape[0]
    devices = lax.axis_size("dp")

    first = (lax.axis_index("dp") * own_rows).astype(jnp.int32).reshape(1)
    rows = jnp.transpose(references, (0, 2, 1, 3)).reshape(own_rows * 2 * classes, cycles)
    piece, offsets = turn_references(first, rot_offset, rows)

    onehot = (defocus_group[:, None] == jnp.arange(group_count, dtype=jnp.int32)[None, :]).astype(f32)
    ctf_rows = jnp.dot(onehot, ctf_table, precision=lax.Precision.HIGHEST)
    base = make_base(particles, prior_shift)
    on_line = devices == 8 and own_rows == ROTS
    if on_line:
        weighted, pieces, slot_of = gather_on_line(piece, base, ctf_rows)
    else:
        gathered = lax.all_gather(piece, "dp", axis=0, tiled=True)
        gathered = gathered.reshape(slots, ROTS * 2 * classes, cycles)
        pieces = [gathered[j] for j in range(slots)]
        slot_of = list(range(slots))
        weighted = make_spectra(base, ctf_rows, 0, spectra_steps(count)[1])
    queries = weighted.shape[1]
    weighted = weighted.reshape(slots, ROTS, queries, 2 * cycles)

    half = slots // 2
    part = lax.axis_index("cls")
    corr, power = correlate(slot_of[:half], weighted, pieces[:half], classes, part)
    weights, stat, share = correlate(
        slot_of[half:], weighted, pieces[half:], classes, part, corr, power, ctf_rows, lax.axis_size("cls")
    )
    shares = lax.psum(share, "cls")
    back, evidence, posterior = make_back(weights, stat, shares, offsets, queries)
    log_evidence = evidence[0, :count]
    class_posterior = posterior[:classes, :count].T
    if on_line:
        class_rows = reduce_on_line(back, weighted, offsets, classes)
    else:
        sums = [class_sums_of(slot_of[u], back, weighted, offsets, classes, bf16) for u in range(slots)]
        summed = lax.psum_scatter(jnp.concatenate(sums, 0), "dp", scatter_dimension=0, tiled=True)
        class_rows = summed.astype(f32)
    class_sums = jnp.transpose(class_rows.reshape(own_rows, classes, 2, cycles), (0, 2, 1, 3))
    return (log_evidence, class_posterior, class_sums)


def solution(mesh):
    placed = (
        P("dp", None, None, None),
        P("dp", None, "cls", None),
        P(),
        P("cls"),
        P("dp", None),
        P("dp"),
    )
    return jax.shard_map(
        local,
        mesh=mesh,
        in_specs=placed,
        out_specs=(P("dp"), P("dp", "cls"), P("dp", None, "cls", None)),
        check_vma=False,
    )
```

```python
import functools
import math

import jax
import jax.numpy as jnp
import ml_dtypes
import numpy as np
from jax import lax
from jax.experimental import pallas as pl
from jax.experimental.pallas import tpu as pltpu
from jax.sharding import PartitionSpec as P

ROTS = 36
ANG_STEP = 8
SHIFT_SIDE = 5
SHIFTS = SHIFT_SIDE * SHIFT_SIDE
LANES = 128
GROUP = 12
ROWS = 16
APART = 17
FOLD = ROTS // 2 + 1

two_pi = 2.0 * math.pi
f32 = jnp.float32
bf16 = jnp.bfloat16
VMEM_LIMIT = 56 * 1024 * 1024


def fourier_rows(angles):
    index_grid = np.arange(angles)
    radians = (index_grid[:, None] * index_grid[None, :] % angles) * (two_pi / angles)
    cosine, sine_part = np.cos(radians), np.sin(radians)
    table_full = np.concatenate(
        [np.concatenate([cosine, sine_part], 1), np.concatenate([-sine_part, cosine], 1)], 0
    )
    return table_full.astype(np.float32).astype(ml_dtypes.bfloat16)


def shift_tables(angles, cycles):
    theta = np.arange(angles) * (two_pi / angles)
    radius = (np.arange(cycles) + 1) / (2.0 * cycles)
    turns = np.stack([np.cos(theta), np.sin(theta)])[:, :, None] * radius
    steps = np.arange(SHIFT_SIDE) - SHIFT_SIDE // 2
    phase = two_pi * turns[:, None] * steps[None, :, None, None]
    factors = np.stack([np.cos(phase), -np.sin(phase)], 2)
    return turns.astype(np.float32), factors.astype(np.float32)


def cos_sin_of_turns(turns):
    frac = turns - jnp.floor(turns + 0.5)
    w = frac * two_pi
    w2 = w * w
    cosine = jnp.full_like(w, 1.0 / math.factorial(16))
    for n in range(14, -1, -2):
        cosine = cosine * w2 + (-1.0) ** (n // 2) / math.factorial(n)
    sine_part = jnp.full_like(w, 1.0 / math.factorial(17))
    for n in range(15, 0, -2):
        sine_part = sine_part * w2 + (-1.0) ** (n // 2) / math.factorial(n)
    return cosine, sine_part * w


def base_kernel(shift_ref, part_ref, turns_ref, base_ref):
    here, _, angles, _ = part_ref.shape
    chunk = 32
    for q in range(here):
        p = pl.program_id(0) * here + q
        sx = shift_ref[0, p].astype(f32)
        sy = shift_ref[1, p].astype(f32)

        def turn(n, carry):
            rows = pl.ds(pl.multiple_of(n * chunk, chunk), chunk)
            cosine, sine_part = cos_sin_of_turns(sx * turns_ref[0, rows, :] + sy * turns_ref[1, rows, :])
            re = part_ref[q, 0, rows, :].astype(f32)
            im = part_ref[q, 1, rows, :].astype(f32)
            base_ref[q, 0, rows, :] = re * cosine + im * sine_part
            base_ref[q, 1, rows, :] = im * cosine - re * sine_part
            return carry

        lax.fori_loop(0, angles // chunk, turn, 0)


def make_base(particles, prior_shift):
    count, _, angles, cycles = particles.shape
    turns, _ = shift_tables(angles, cycles)
    here = count // 2
    image = pl.BlockSpec((here, 2, angles, cycles), lambda p: (p, 0, 0, 0))
    return pl.pallas_call(
        base_kernel,
        grid=(2,),
        in_specs=[
            pl.BlockSpec(memory_space=pltpu.SMEM),
            image,
            pl.BlockSpec(turns.shape, lambda p: (0, 0, 0)),
        ],
        out_specs=image,
        out_shape=jax.ShapeDtypeStruct(particles.shape, f32),
        compiler_params=pltpu.CompilerParams(vmem_limit_bytes=VMEM_LIMIT),
        name="centre",
    )(prior_shift.T, particles, turns)


def spectra_kernel(base_ref, ctf_ref, table_ref, *refs, per_step):
    factor_refs, refs = refs[: 2 * per_step], refs[2 * per_step :]
    chunks = ROWS // 2
    out_ref, turn_ref, re_ref, im_ref = refs[-4 - chunks : -chunks]
    data_refs = refs[-chunks:]
    count, _, angles, cycles = base_ref.shape
    chunk = 32

    for g in range(per_step):
        x_ref, y_ref = factor_refs[2 * g], factor_refs[2 * g + 1]
        for start in range(0, angles, chunk):
            rows = slice(start, start + chunk)
            xr, xi = x_ref[0, 0, 0, rows, :], x_ref[0, 0, 1, rows, :]
            yr, yi = y_ref[0, 0, 0, rows, :], y_ref[0, 0, 1, rows, :]
            turn_ref[g, 0, rows, :] = xr * yr - xi * yi
            turn_ref[g, 1, rows, :] = xr * yi + xi * yr

    def shift(n):
        for j in range(2):
            g, p = (2 * n + j) // count, (2 * n + j) % count
            lanes = slice(j * cycles, (j + 1) * cycles)
            for start in range(0, angles, chunk):
                rows = slice(start, start + chunk)
                tr, ti = turn_ref[g, 0, rows, :], turn_ref[g, 1, rows, :]
                gr, gi = base_ref[p, 0, rows, :], base_ref[p, 1, rows, :]
                data_refs[n][rows, lanes] = (gr * tr - gi * ti).astype(bf16)
                data_refs[n][angles + start : angles + start + chunk, lanes] = (gr * ti + gi * tr).astype(bf16)

    shift(0)
    for n in range(chunks):
        if n + 1 < chunks:
            shift(n + 1)
        spectrum = jnp.dot(table_ref[...], data_refs[n][...], preferred_element_type=f32)
        for j in range(2):
            row = 2 * n + j
            ctf_row = ctf_ref[row % count, :][None, :]
            part = spectrum[:, j * cycles : (j + 1) * cycles] * ctf_row
            re_ref[pl.ds(row, angles, stride=APART), :] = part[:angles]
            im_ref[pl.ds(row, angles, stride=APART), :] = part[angles:]
    for m in range(angles):
        out_ref[m, :, :cycles] = re_ref[m * APART : m * APART + ROWS, :].astype(bf16)
        out_ref[m, :, cycles:] = im_ref[m * APART : m * APART + ROWS, :].astype(bf16)


def spectra_steps(count):
    per_step = ROWS // count if count < ROWS else 1
    return per_step, -(-SHIFTS // per_step)


def make_spectra(base, ctf_rows, first, last, before=None, after=()):
    count, _, angles, cycles = base.shape
    per_step, steps = spectra_steps(count)
    _, factors = shift_tables(angles, cycles)
    full = lambda shape: pl.BlockSpec(shape, lambda i: (0,) * len(shape))

    def factor_spec(g, axis):
        def place(i):
            s = jnp.minimum((i + first) * per_step + g, SHIFTS - 1)
            a = lax.div(s, jnp.int32(SHIFT_SIDE))
            return (axis, s - a * SHIFT_SIDE if axis else a, 0, 0, 0)

        return pl.BlockSpec((1, 1, 2, angles, cycles), place)

    untouched = ([] if before is None else [before]) + list(after)
    in_specs = (
        [full(base.shape), full(ctf_rows.shape), full((2 * angles, 2 * angles))]
        + [factor_spec(g, axis) for g in range(per_step) for axis in range(2)]
        + [pl.BlockSpec(memory_space=pl.ANY)] * len(untouched)
    )
    return pl.pallas_call(
        functools.partial(spectra_kernel, per_step=per_step),
        grid=(last - first,),
        in_specs=in_specs,
        out_specs=pl.BlockSpec((angles, ROWS, 2 * cycles), lambda i: (0, i + first, 0)),
        out_shape=jax.ShapeDtypeStruct((angles, steps * ROWS, 2 * cycles), bf16),
        scratch_shapes=[
            pltpu.VMEM((per_step, 2, angles, cycles), f32),
            pltpu.VMEM((angles * APART, cycles), f32),
            pltpu.VMEM((angles * APART, cycles), f32),
        ]
        + [pltpu.VMEM((2 * angles, 2 * cycles), bf16)] * (ROWS // 2),
        input_output_aliases={} if before is None else {3 + 2 * per_step: 0},
        compiler_params=pltpu.CompilerParams(vmem_limit_bytes=VMEM_LIMIT),
        name="spectra",
    )(base, ctf_rows, fourier_rows(angles), *[factors] * (2 * per_step), *untouched)


def half_dft(even_values, odd_values):
    half = FOLD // 2
    cos_sums, sin_sums = [None] * FOLD, [None] * FOLD

    def weighted_sum(values, k, table, start):
        total = None
        for m in range(start, FOLD, 2):
            weight = float(table((k * m % ROTS) * two_pi / ROTS))
            if values[m] is None or abs(weight) < 1e-9:
                continue
            if abs(abs(weight) - 1.0) < 1e-9:
                term = values[m] if weight > 0 else -values[m]
            else:
                term = values[m] * weight
            total = term if total is None else total + term
        return jnp.zeros_like(values[1]) if total is None else total

    for k in range(half + 1):
        even = weighted_sum(even_values, k, math.cos, 0)
        odd = weighted_sum(even_values, k, math.cos, 1)
        cos_sums[k] = even + odd
        if k != half:
            cos_sums[FOLD - 1 - k] = even - odd
        if k:
            even = weighted_sum(odd_values, k, math.sin, 0)
            odd = weighted_sum(odd_values, k, math.sin, 1)
            sin_sums[k] = even + odd
            if k != half:
                sin_sums[FOLD - 1 - k] = odd - even
    return cos_sums, sin_sums


def turn_kernel(first_ref, offset_ref, references_ref, out_ref, column_ref, in_ref, wide_ref):
    rows, cycles = references_ref.shape
    classes = offset_ref.shape[0]
    own_rows = rows // (2 * classes)
    in_ref[...] = references_ref[...].astype(f32)
    row = lax.broadcasted_iota(jnp.int32, (8, LANES), 0)
    lane = lax.broadcasted_iota(jnp.int32, (8, LANES), 1)
    freq = (lane + first_ref[0]).astype(f32) * (1.0 / (ROTS * ANG_STEP))
    tables = []
    for start in range(0, classes, 8):
        column = jnp.zeros((8, LANES), jnp.int32)
        for c in range(start, min(start + 8, classes)):
            column = jnp.where(row == c - start, offset_ref[c], column)
        column = column.astype(f32)
        column_ref[start : start + 8, :] = column
        tables.append(cos_sin_of_turns(column * freq))
    cosine = jnp.concatenate([c for c, _ in tables], 0)
    sine_part = jnp.concatenate([s for _, s in tables], 0)
    for m in range(own_rows):
        re_rows = pl.ds(2 * m * classes, classes, stride=2)
        im_rows = pl.ds(2 * m * classes + 1, classes, stride=2)
        c, s = cosine[:classes, m : m + 1], sine_part[:classes, m : m + 1]
        re, im = in_ref[re_rows, :], in_ref[im_rows, :]
        wide_ref[re_rows, :] = re * c + im * s
        wide_ref[im_rows, :] = im * c - re * s
    out_ref[...] = wide_ref[...].astype(bf16)


def turn_references(first, offsets, references):
    padded = -(-offsets.shape[0] // 8) * 8
    return pl.pallas_call(
        turn_kernel,
        in_specs=[
            pl.BlockSpec(memory_space=pltpu.SMEM),
            pl.BlockSpec(memory_space=pltpu.SMEM),
            pl.BlockSpec(memory_space=pltpu.VMEM),
        ],
        out_shape=[
            jax.ShapeDtypeStruct(references.shape, bf16),
            jax.ShapeDtypeStruct((padded, LANES), f32),
        ],
        scratch_shapes=[pltpu.VMEM(references.shape, f32)] * 2,
        compiler_params=pltpu.CompilerParams(vmem_limit_bytes=VMEM_LIMIT),
        name="turn_references",
    )(first, offsets, references)


def correlate_kernel(*refs, slots, classes, padded, finish):
    part_ref, refs = refs[slots], refs[slots + 1 :]
    weighted_refs, refs = refs[:slots], refs[slots:]
    piece_refs, refs = refs[:slots], refs[slots:]
    if finish:
        before_ref, power_before_ref, ctf_ref, weight_ref, stat_ref, share_ref = refs[:6]
        corr_ref, wide_ref, power_ref = refs[6:]
    else:
        corr_ref, power_ref, wide_ref = refs
    group = pl.program_id(0)
    cycles = piece_refs[0].shape[1]
    queries = weighted_refs[0].shape[2]
    block = piece_refs[0].shape[0]

    @pl.when(group == 0)
    def _():
        wide_ref[:, block:, :] = jnp.zeros((slots, wide_ref.shape[1] - block, cycles), f32)
        power_ref[...] = power_before_ref[...] if finish else jnp.zeros_like(power_ref)

    for j in range(slots):
        wide_ref[j, :block, :] = piece_refs[j][...].astype(f32)
    power = power_ref[...]
    for i in range(GROUP):
        total = before_ref[i, :, :queries] if finish else None
        for j in range(slots):
            re = wide_ref[j, pl.ds(2 * i * classes, padded, stride=2), :]
            im = wide_ref[j, pl.ds(2 * i * classes + 1, padded, stride=2), :]
            power = power + (re * re + im * im)
            left = jnp.concatenate(
                [jnp.concatenate([re, im], 1), jnp.concatenate([-im, re], 1)], 0
            ).astype(bf16)
            part = lax.dot_general(
                left, weighted_refs[j][0, i], (((1,), (1,)), ((), ())), preferred_element_type=f32
            )
            total = part if total is None else total + part
        row = group * GROUP + i if finish else i
        corr_ref[row, :, :queries] = total
    power_ref[...] = power

    if not finish:
        return

    @pl.when(group == pl.num_programs(0) - 1)
    def _():
        count = ctf_ref.shape[0]
        angles = ROTS * ANG_STEP
        used = SHIFTS * count
        tiles = weight_ref.shape[2] // LANES
        ctf_row = ctf_ref[...]
        ctf_rows = jnp.concatenate([ctf_row * ctf_row] * (LANES // count), 0)
        bias = lax.dot_general(
            power_ref[...],
            ctf_rows,
            (((1,), (1,)), ((), ())),
            precision=lax.Precision.HIGHEST,
            preferred_element_type=f32,
        ) * (0.5 / angles)
        wide_ref[0, :padded, :] = bias
        rows_of = lambda base: lax.broadcasted_iota(jnp.int32, (8, LANES), 0) + base
        lanes_of = lambda base: lax.broadcasted_iota(jnp.int32, (8, LANES), 1) + base

        peak = jnp.full((8, LANES), -1e30, f32)
        for tile in range(tiles):
            lanes = slice(tile * LANES, (tile + 1) * LANES)

            def scores(n, peak):
                start = pl.multiple_of(n * 8, 8)
                rows = pl.ds(start, 8)
                low = pl.ds(padded + start, 8)
                valid = (rows_of(start) < classes) & (lanes_of(tile * LANES) < used)
                even_values = [corr_ref[0, rows, lanes]]
                odd_values = [None]
                for m in range(1, ROTS // 2):
                    even_values.append(corr_ref[m, rows, lanes] + corr_ref[ROTS - m, rows, lanes])
                    odd_values.append(corr_ref[m, low, lanes] - corr_ref[ROTS - m, low, lanes])
                even_values.append(corr_ref[ROTS // 2, rows, lanes])
                odd_values.append(None)
                cos_sums, sin_sums = half_dft(even_values, odd_values)
                bias = wide_ref[0, rows, :]
                for k in range(FOLD):
                    if k in (0, FOLD - 1):
                        results = [(k, cos_sums[k])]
                    else:
                        results = [(k, cos_sums[k] - sin_sums[k]), (ROTS - k, cos_sums[k] + sin_sums[k])]
                    for place, value in results:
                        value = jnp.where(valid, value * (1.0 / angles) - bias, -1e30)
                        weight_ref[place, rows, lanes] = value
                        peak = jnp.maximum(peak, value)
                return peak

            peak = lax.fori_loop(0, padded // 8, scores, peak)

        peak = jnp.broadcast_to(jnp.max(peak, axis=0, keepdims=True), (8, LANES))
        step = count
        while step < LANES:
            peak = jnp.maximum(peak, pltpu.roll(peak, step, 1))
            step *= 2
        stat_ref[0:8, :] = peak

        def masses(n, whole):
            rows = pl.ds(pl.multiple_of(n * 8, 8), 8)
            mass = jnp.zeros((8, LANES), f32)
            for tile in range(tiles):
                lanes = slice(tile * LANES, (tile + 1) * LANES)
                for k in range(ROTS):
                    value = jnp.exp(weight_ref[k, rows, lanes] - peak)
                    weight_ref[k, rows, lanes] = value
                    mass = mass + value
            step = count
            while step < LANES:
                mass = mass + pltpu.roll(mass, step, 1)
                step *= 2
            stat_ref[pl.ds(pl.multiple_of(8 + n * 8, 8), 8), :] = mass
            return whole + mass

        whole = lax.fori_loop(0, padded // 8, masses, jnp.zeros((8, LANES), f32))
        share = jnp.concatenate([peak[:1], jnp.sum(whole, axis=0, keepdims=True)], 0)
        for j in range(share_ref.shape[0]):
            share_ref[j] = jnp.where(part_ref[0] == j, share, 0.0)


def correlate(slot_of, weighted, pieces, classes, part, before=None, power=None, ctf_rows=None, parts=1):
    _, _, queries, double = weighted.shape
    cycles = double // 2
    slots = len(pieces)
    padded = -(-classes // 8) * 8
    wide_lanes = -(-queries // LANES) * LANES
    block = 2 * GROUP * classes
    finish = ctf_rows is not None
    full = lambda shape: pl.BlockSpec(shape, lambda g, *u: (0,) * len(shape))
    in_specs = [
        pl.BlockSpec((1, GROUP, queries, double), functools.partial(lambda j, g, *u: (u[j][0], g, 0, 0), j))
        for j in range(slots)
    ] + [pl.BlockSpec((block, cycles), lambda g, *u: (g, 0))] * slots
    corr_block = pl.BlockSpec((GROUP, 2 * padded, wide_lanes), lambda g, *u: (g, 0, 0))
    corr_shape = (ROTS, 2 * padded, wide_lanes)
    wide = pltpu.VMEM((slots, block + ROWS, cycles), f32)
    scalars = [jnp.reshape(n, (1,)).astype(jnp.int32) for n in (*slot_of, part)]
    operands = scalars + [weighted] * slots + list(pieces)
    if finish:
        in_specs += [corr_block, full((padded, cycles)), full(ctf_rows.shape)]
        operands += [before, power, ctf_rows]
        out_shapes = [(ROTS, padded, wide_lanes), (8 + padded, LANES), (parts, 2, LANES)]
        out_specs = [full(shape) for shape in out_shapes]
        scratch = [pltpu.VMEM(corr_shape, f32), wide, pltpu.VMEM((padded, cycles), f32)]
    else:
        out_shapes = [corr_shape, (padded, cycles)]
        out_specs = [corr_block, full((padded, cycles))]
        scratch = [wide]
    return pl.pallas_call(
        functools.partial(correlate_kernel, slots=slots, classes=classes, padded=padded, finish=finish),
        grid_spec=pltpu.PrefetchScalarGridSpec(
            num_scalar_prefetch=len(scalars),
            grid=(ROTS // GROUP,),
            in_specs=in_specs,
            out_specs=out_specs,
            scratch_shapes=scratch,
        ),
        out_shape=[jax.ShapeDtypeStruct(shape, f32) for shape in out_shapes],
        compiler_params=pltpu.CompilerParams(vmem_limit_bytes=VMEM_LIMIT),
        name="scores" if finish else "correlate",
    )(*operands)


def back_kernel(weight_ref, stat_ref, share_ref, offset_ref, out_ref, evidence_ref, posterior_ref, sum_ref):
    padded = weight_ref.shape[1]
    queries = out_ref.shape[2]
    shares = [share_ref[j] for j in range(share_ref.shape[0])]
    top = shares[0][:1]
    for share in shares[1:]:
        top = jnp.maximum(top, share[:1])
    mass = sum(share[1:] * jnp.exp(share[:1] - top) for share in shares)
    evidence = jnp.broadcast_to(top + jnp.log(mass), (8, LANES))
    scale = jnp.exp(stat_ref[:8, :] - evidence)
    evidence_ref[...] = evidence
    posterior_ref[...] = stat_ref[8:, :] * scale[:1]
    for tile in range(weight_ref.shape[2] // LANES):
        lanes = slice(tile * LANES, (tile + 1) * LANES)

        def transform(n, carry):
            start = pl.multiple_of(n * 8, 8)
            rows = pl.ds(start, 8)
            low = pl.ds(padded + start, 8)
            values = [weight_ref[k, rows, lanes] * scale for k in range(ROTS)]
            even_values = [values[0]] + [values[k] + values[ROTS - k] for k in range(1, ROTS // 2)]
            odd_values = [None] + [values[k] - values[ROTS - k] for k in range(1, ROTS // 2)] + [None]
            cos_sums, sin_sums = half_dft(even_values + [values[ROTS // 2]], odd_values)
            for m in range(FOLD):
                sine_part = jnp.zeros_like(scale) if m in (0, FOLD - 1) else sin_sums[m]
                sum_ref[m, rows, lanes] = cos_sums[m]
                sum_ref[m, low, lanes] = sine_part
                if m not in (0, FOLD - 1):
                    sum_ref[ROTS - m, rows, lanes] = cos_sums[m]
                    sum_ref[ROTS - m, low, lanes] = -sine_part
            return carry

        lax.fori_loop(0, padded // 8, transform, 0)

    step_cos, step_sin = cos_sin_of_turns(offset_ref[...] * (1.0 / (ROTS * ANG_STEP)))

    def turn(m, carry):
        cosine, sine_part = carry
        for tile in range(weight_ref.shape[2] // LANES):
            lanes = slice(tile * LANES, (tile + 1) * LANES)
            kept = slice(tile * LANES, min((tile + 1) * LANES, queries))
            re, im = sum_ref[m, :padded, lanes], sum_ref[m, padded:, lanes]
            turned = jnp.concatenate([re * cosine - im * sine_part, re * sine_part + im * cosine], 0)
            out_ref[m, :, kept] = turned[:, : kept.stop - kept.start].astype(bf16)
        return cosine * step_cos - sine_part * step_sin, sine_part * step_cos + cosine * step_sin

    lax.fori_loop(0, ROTS, turn, (jnp.ones_like(step_cos), jnp.zeros_like(step_cos)))


def make_back(weights, stat, shares, offsets, queries):
    _, padded, wide_lanes = weights.shape
    return pl.pallas_call(
        back_kernel,
        out_shape=[
            jax.ShapeDtypeStruct((ROTS, 2 * padded, queries), bf16),
            jax.ShapeDtypeStruct((8, LANES), f32),
            jax.ShapeDtypeStruct((padded, LANES), f32),
        ],
        scratch_shapes=[pltpu.VMEM((ROTS, 2 * padded, wide_lanes), f32)],
        compiler_params=pltpu.CompilerParams(vmem_limit_bytes=VMEM_LIMIT),
        name="back",
    )(weights, stat, shares, offsets)


def sums_kernel(slot_ref, back_ref, weighted_ref, offset_ref, out_ref, wide_ref, *, classes):
    padded = offset_ref.shape[0]
    cycles = wide_ref.shape[1]
    turns = offset_ref[...] * (slot_ref[0].astype(f32) * (1.0 / ANG_STEP))
    cosine, sine_part = cos_sin_of_turns(turns)
    for i in range(GROUP):
        product = jnp.dot(back_ref[i], weighted_ref[0, i], preferred_element_type=f32)
        re = product[:padded, :cycles] - product[padded:, cycles:]
        im = product[:padded, cycles:] + product[padded:, :cycles]
        start = 2 * i * classes
        wide_ref[pl.ds(start, classes, stride=2), :] = (re * cosine - im * sine_part)[:classes]
        wide_ref[pl.ds(start + 1, classes, stride=2), :] = (re * sine_part + im * cosine)[:classes]
    out_ref[...] = wide_ref[...].astype(out_ref.dtype)


def class_sums_of(slot, back, weighted, offsets, classes, dtype):
    _, _, queries, double = weighted.shape
    cycles = double // 2
    rows = back.shape[1]
    block = 2 * GROUP * classes
    piece = pl.BlockSpec((block, cycles), lambda g, u: (g, 0))
    return pl.pallas_call(
        functools.partial(sums_kernel, classes=classes),
        grid_spec=pltpu.PrefetchScalarGridSpec(
            num_scalar_prefetch=1,
            grid=(ROTS // GROUP,),
            in_specs=[
                pl.BlockSpec((GROUP, rows, queries), lambda g, u: (g, 0, 0)),
                pl.BlockSpec((1, GROUP, queries, double), lambda g, u: (u[0], g, 0, 0)),
                pl.BlockSpec(offsets.shape, lambda g, u: (0, 0)),
            ],
            out_specs=piece,
            scratch_shapes=[pltpu.VMEM((block, cycles), f32)],
        ),
        out_shape=jax.ShapeDtypeStruct((ROTS * 2 * classes, cycles), dtype),
        compiler_params=pltpu.CompilerParams(vmem_limit_bytes=VMEM_LIMIT),
        name="class_sums",
    )(jnp.reshape(slot, (1,)).astype(jnp.int32), back, weighted, offsets)


def across(piece):
    return lax.ppermute(piece, "dp", [(d, d ^ 1) for d in range(8)])


def along(piece, pairs):
    return lax.ppermute(piece, "dp", [(2 * a + x, 2 * b + x) for a, b in pairs for x in range(2)])


def gather_on_line(piece, base, ctf_rows):
    index = lax.axis_index("dp")
    line, side = index // 2, index % 2
    _, steps = spectra_steps(base.shape[0])
    cuts = [0, 2 * steps // 13, 6 * steps // 13, 10 * steps // 13, steps]

    own_crossed = across(piece)
    near = along(piece, ((0, 1), (1, 0), (2, 3), (3, 2)))
    middle = along(piece, ((1, 2), (2, 1)))
    weighted = make_spectra(base, ctf_rows, cuts[0], cuts[1])
    weighted, near, middle, own_crossed = lax.optimization_barrier((weighted, near, middle, own_crossed))
    near_crossed = across(near)
    far_middle = along(near, ((1, 2), (2, 1)))
    end = along(middle, ((1, 0), (2, 3)))
    weighted = make_spectra(base, ctf_rows, cuts[1], cuts[2], weighted)
    weighted, far_middle, end, near_crossed = lax.optimization_barrier(
        (weighted, far_middle, end, near_crossed)
    )
    third = middle + end
    third_crossed = across(third)
    far_end = along(far_middle, ((1, 0), (2, 3)))
    weighted = make_spectra(base, ctf_rows, cuts[2], cuts[3], weighted)
    weighted, far_end, third_crossed = lax.optimization_barrier((weighted, far_end, third_crossed))
    fourth = far_middle + far_end
    fourth_crossed = across(fourth)
    weighted = make_spectra(base, ctf_rows, cuts[3], cuts[4], weighted)

    pieces = [piece, own_crossed, near, near_crossed, third, third_crossed, fourth, fourth_crossed]
    places = [line, line ^ 1, jnp.where(line < 2, 2, 1), jnp.where(line < 2, 3, 0)]
    slot_of = [2 * place + s for place in places for s in (side, 1 - side)]
    return weighted, pieces, slot_of


def reduce_on_line(back, weighted, offsets, classes):
    index = lax.axis_index("dp")
    line, side = index // 2, index % 2
    order = [jnp.where(line < 2, 3, 0), jnp.where(line < 2, 2, 1), line ^ 1, line]
    theirs = [class_sums_of(2 * z + 1 - side, back, weighted, offsets, classes, bf16) for z in order]
    ours = [class_sums_of(2 * z + side, back, weighted, offsets, classes, f32) for z in order]
    at_end = (line == 0) | (line == 3)

    crossed = [across(theirs[0])]
    crossed[0], theirs[1], theirs[2], ours[0], ours[1] = lax.optimization_barrier(
        (crossed[0], theirs[1], theirs[2], ours[0], ours[1])
    )
    crossed.append(across(theirs[1]))
    farthest = ours[0] + crossed[0].astype(f32)
    first = along(farthest.astype(bf16), ((0, 1), (3, 2)))
    crossed[1], theirs[2], theirs[3], ours[2], ours[3] = lax.optimization_barrier(
        (crossed[1], theirs[2], theirs[3], ours[2], ours[3])
    )
    crossed.append(across(theirs[2]))
    next_farthest = ours[1] + crossed[1].astype(f32)
    second = (jnp.where(at_end, next_farthest, farthest) + first.astype(f32)).astype(bf16)
    from_ends = along(second, ((0, 1), (3, 2)))
    from_middle = along(second, ((1, 2), (2, 1)))
    crossed[2], theirs[3] = lax.optimization_barrier((crossed[2], theirs[3]))
    crossed.append(across(theirs[3]))
    third = (next_farthest + from_ends.astype(f32)).astype(bf16)
    third = along(third, ((1, 2), (2, 1)))
    fourth = (ours[2] + crossed[2].astype(f32) + from_middle.astype(f32)).astype(bf16)
    fourth = along(fourth, ((0, 1), (1, 0), (2, 3), (3, 2)))
    return ours[3] + crossed[3].astype(f32) + third.astype(f32) + fourth.astype(f32)


def local(particles, references, ctf_table, rot_offset, prior_shift, defocus_group):
    count, _, angles, cycles = particles.shape
    own_rows, _, classes, _ = references.shape
    slots = angles // ROTS
    group_count = ctf_table.shape[0]
    devices = lax.axis_size("dp")

    first = (lax.axis_index("dp") * own_rows).astype(jnp.int32).reshape(1)
    rows = jnp.transpose(references, (0, 2, 1, 3)).reshape(own_rows * 2 * classes, cycles)
    piece, offsets = turn_references(first, rot_offset, rows)

    onehot = (defocus_group[:, None] == jnp.arange(group_count, dtype=jnp.int32)[None, :]).astype(f32)
    ctf_rows = jnp.dot(onehot, ctf_table, precision=lax.Precision.HIGHEST)
    base = make_base(particles, prior_shift)
    on_line = devices == 8 and own_rows == ROTS
    if on_line:
        weighted, pieces, slot_of = gather_on_line(piece, base, ctf_rows)
    else:
        gathered = lax.all_gather(piece, "dp", axis=0, tiled=True)
        gathered = gathered.reshape(slots, ROTS * 2 * classes, cycles)
        pieces = [gathered[j] for j in range(slots)]
        slot_of = list(range(slots))
        weighted = make_spectra(base, ctf_rows, 0, spectra_steps(count)[1])
    queries = weighted.shape[1]
    weighted = weighted.reshape(slots, ROTS, queries, 2 * cycles)

    early = 3 * slots // 4
    part = lax.axis_index("cls")
    corr, power = correlate(slot_of[:early], weighted, pieces[:early], classes, part)
    weights, stat, share = correlate(
        slot_of[early:], weighted, pieces[early:], classes, part, corr, power, ctf_rows, lax.axis_size("cls")
    )
    shares = lax.psum(share, "cls")
    back, evidence, posterior = make_back(weights, stat, shares, offsets, queries)
    log_evidence = evidence[0, :count]
    class_posterior = posterior[:classes, :count].T
    if on_line:
        class_rows = reduce_on_line(back, weighted, offsets, classes)
    else:
        sums = [class_sums_of(slot_of[u], back, weighted, offsets, classes, bf16) for u in range(slots)]
        summed = lax.psum_scatter(jnp.concatenate(sums, 0), "dp", scatter_dimension=0, tiled=True)
        class_rows = summed.astype(f32)
    class_sums = jnp.transpose(class_rows.reshape(own_rows, classes, 2, cycles), (0, 2, 1, 3))
    return (log_evidence, class_posterior, class_sums)


def solution(mesh):
    placed = (
        P("dp", None, None, None),
        P("dp", None, "cls", None),
        P(),
        P("cls"),
        P("dp", None),
        P("dp"),
    )
    return jax.shard_map(
        local,
        mesh=mesh,
        in_specs=placed,
        out_specs=(P("dp"), P("dp", "cls"), P("dp", None, "cls", None)),
        check_vma=False,
    )
```

```python
import functools
import math

import jax
import jax.numpy as jnp
import ml_dtypes
import numpy as np
from jax import lax
from jax.experimental import pallas as pl
from jax.experimental.pallas import tpu as pltpu
from jax.sharding import PartitionSpec as P

ROTS = 36
ANG_STEP = 8
SHIFT_SIDE = 5
SHIFTS = SHIFT_SIDE * SHIFT_SIDE
LANES = 128
GROUP = 12
ROWS = 16
APART = 17
FOLD = ROTS // 2 + 1

two_pi = 2.0 * math.pi
f32 = jnp.float32
bf16 = jnp.bfloat16
VMEM_LIMIT = 56 * 1024 * 1024


def fourier_rows(angles):
    index_grid = np.arange(angles)
    radians = (index_grid[:, None] * index_grid[None, :] % angles) * (two_pi / angles)
    cosine, sine_part = np.cos(radians), np.sin(radians)
    table_full = np.concatenate(
        [np.concatenate([cosine, sine_part], 1), np.concatenate([-sine_part, cosine], 1)], 0
    )
    return table_full.astype(np.float32).astype(ml_dtypes.bfloat16)


def shift_tables(angles, cycles):
    theta = np.arange(angles) * (two_pi / angles)
    radius = (np.arange(cycles) + 1) / (2.0 * cycles)
    turns = np.stack([np.cos(theta), np.sin(theta)])[:, :, None] * radius
    steps = np.arange(SHIFT_SIDE) - SHIFT_SIDE // 2
    phase = two_pi * turns[:, None] * steps[None, :, None, None]
    factors = np.stack([np.cos(phase), -np.sin(phase)], 2)
    return turns.astype(np.float32), factors.astype(np.float32)


def cos_sin_of_turns(turns):
    frac = turns - jnp.floor(turns + 0.5)
    w = frac * two_pi
    w2 = w * w
    cosine = jnp.full_like(w, 1.0 / math.factorial(16))
    for n in range(14, -1, -2):
        cosine = cosine * w2 + (-1.0) ** (n // 2) / math.factorial(n)
    sine_part = jnp.full_like(w, 1.0 / math.factorial(17))
    for n in range(15, 0, -2):
        sine_part = sine_part * w2 + (-1.0) ** (n // 2) / math.factorial(n)
    return cosine, sine_part * w


def base_kernel(shift_ref, part_ref, turns_ref, base_ref):
    here, _, angles, _ = part_ref.shape
    chunk = 32
    for q in range(here):
        p = pl.program_id(0) * here + q
        sx = shift_ref[0, p].astype(f32)
        sy = shift_ref[1, p].astype(f32)

        def turn(n, carry):
            rows = pl.ds(pl.multiple_of(n * chunk, chunk), chunk)
            cosine, sine_part = cos_sin_of_turns(sx * turns_ref[0, rows, :] + sy * turns_ref[1, rows, :])
            re = part_ref[q, 0, rows, :].astype(f32)
            im = part_ref[q, 1, rows, :].astype(f32)
            base_ref[q, 0, rows, :] = re * cosine + im * sine_part
            base_ref[q, 1, rows, :] = im * cosine - re * sine_part
            return carry

        lax.fori_loop(0, angles // chunk, turn, 0)


def make_base(particles, prior_shift):
    count, _, angles, cycles = particles.shape
    turns, _ = shift_tables(angles, cycles)
    here = count // 2
    image = pl.BlockSpec((here, 2, angles, cycles), lambda p: (p, 0, 0, 0))
    return pl.pallas_call(
        base_kernel,
        grid=(2,),
        in_specs=[
            pl.BlockSpec(memory_space=pltpu.SMEM),
            image,
            pl.BlockSpec(turns.shape, lambda p: (0, 0, 0)),
        ],
        out_specs=image,
        out_shape=jax.ShapeDtypeStruct(particles.shape, f32),
        compiler_params=pltpu.CompilerParams(vmem_limit_bytes=VMEM_LIMIT),
        name="centre",
    )(prior_shift.T, particles, turns)


def spectra_kernel(base_ref, ctf_ref, table_ref, *refs, per_step):
    factor_refs, refs = refs[: 2 * per_step], refs[2 * per_step :]
    chunks = ROWS // 2
    out_ref, turn_ref, re_ref, im_ref = refs[-4 - chunks : -chunks]
    data_refs = refs[-chunks:]
    count, _, angles, cycles = base_ref.shape
    chunk = 32

    for g in range(per_step):
        x_ref, y_ref = factor_refs[2 * g], factor_refs[2 * g + 1]
        for start in range(0, angles, chunk):
            rows = slice(start, start + chunk)
            xr, xi = x_ref[0, 0, 0, rows, :], x_ref[0, 0, 1, rows, :]
            yr, yi = y_ref[0, 0, 0, rows, :], y_ref[0, 0, 1, rows, :]
            turn_ref[g, 0, rows, :] = xr * yr - xi * yi
            turn_ref[g, 1, rows, :] = xr * yi + xi * yr

    def shift(n):
        for j in range(2):
            g, p = (2 * n + j) // count, (2 * n + j) % count
            lanes = slice(j * cycles, (j + 1) * cycles)
            for start in range(0, angles, chunk):
                rows = slice(start, start + chunk)
                tr, ti = turn_ref[g, 0, rows, :], turn_ref[g, 1, rows, :]
                gr, gi = base_ref[p, 0, rows, :], base_ref[p, 1, rows, :]
                data_refs[n][rows, lanes] = (gr * tr - gi * ti).astype(bf16)
                data_refs[n][angles + start : angles + start + chunk, lanes] = (gr * ti + gi * tr).astype(bf16)

    shift(0)
    for n in range(chunks):
        if n + 1 < chunks:
            shift(n + 1)
        spectrum = jnp.dot(table_ref[...], data_refs[n][...], preferred_element_type=f32)
        for j in range(2):
            row = 2 * n + j
            ctf_row = ctf_ref[row % count, :][None, :]
            part = spectrum[:, j * cycles : (j + 1) * cycles] * ctf_row
            re_ref[pl.ds(row, angles, stride=APART), :] = part[:angles]
            im_ref[pl.ds(row, angles, stride=APART), :] = part[angles:]
    for m in range(angles):
        out_ref[m, :, :cycles] = re_ref[m * APART : m * APART + ROWS, :].astype(bf16)
        out_ref[m, :, cycles:] = im_ref[m * APART : m * APART + ROWS, :].astype(bf16)


def spectra_steps(count):
    per_step = ROWS // count if count < ROWS else 1
    return per_step, -(-SHIFTS // per_step)


def make_spectra(base, ctf_rows, first, last, before=None, after=()):
    count, _, angles, cycles = base.shape
    per_step, steps = spectra_steps(count)
    _, factors = shift_tables(angles, cycles)
    full = lambda shape: pl.BlockSpec(shape, lambda i: (0,) * len(shape))

    def factor_spec(g, axis):
        def place(i):
            s = jnp.minimum((i + first) * per_step + g, SHIFTS - 1)
            a = lax.div(s, jnp.int32(SHIFT_SIDE))
            return (axis, s - a * SHIFT_SIDE if axis else a, 0, 0, 0)

        return pl.BlockSpec((1, 1, 2, angles, cycles), place)

    untouched = ([] if before is None else [before]) + list(after)
    in_specs = (
        [full(base.shape), full(ctf_rows.shape), full((2 * angles, 2 * angles))]
        + [factor_spec(g, axis) for g in range(per_step) for axis in range(2)]
        + [pl.BlockSpec(memory_space=pl.ANY)] * len(untouched)
    )
    return pl.pallas_call(
        functools.partial(spectra_kernel, per_step=per_step),
        grid=(last - first,),
        in_specs=in_specs,
        out_specs=pl.BlockSpec((angles, ROWS, 2 * cycles), lambda i: (0, i + first, 0)),
        out_shape=jax.ShapeDtypeStruct((angles, steps * ROWS, 2 * cycles), bf16),
        scratch_shapes=[
            pltpu.VMEM((per_step, 2, angles, cycles), f32),
            pltpu.VMEM((angles * APART, cycles), f32),
            pltpu.VMEM((angles * APART, cycles), f32),
        ]
        + [pltpu.VMEM((2 * angles, 2 * cycles), bf16)] * (ROWS // 2),
        input_output_aliases={} if before is None else {3 + 2 * per_step: 0},
        compiler_params=pltpu.CompilerParams(vmem_limit_bytes=VMEM_LIMIT),
        name="spectra",
    )(base, ctf_rows, fourier_rows(angles), *[factors] * (2 * per_step), *untouched)


def half_dft(even_values, odd_values):
    half = FOLD // 2
    cos_sums, sin_sums = [None] * FOLD, [None] * FOLD

    def weighted_sum(values, k, table, start):
        total = None
        for m in range(start, FOLD, 2):
            weight = float(table((k * m % ROTS) * two_pi / ROTS))
            if values[m] is None or abs(weight) < 1e-9:
                continue
            if abs(abs(weight) - 1.0) < 1e-9:
                term = values[m] if weight > 0 else -values[m]
            else:
                term = values[m] * weight
            total = term if total is None else total + term
        return jnp.zeros_like(values[1]) if total is None else total

    for k in range(half + 1):
        even = weighted_sum(even_values, k, math.cos, 0)
        odd = weighted_sum(even_values, k, math.cos, 1)
        cos_sums[k] = even + odd
        if k != half:
            cos_sums[FOLD - 1 - k] = even - odd
        if k:
            even = weighted_sum(odd_values, k, math.sin, 0)
            odd = weighted_sum(odd_values, k, math.sin, 1)
            sin_sums[k] = even + odd
            if k != half:
                sin_sums[FOLD - 1 - k] = odd - even
    return cos_sums, sin_sums


def turn_kernel(first_ref, offset_ref, references_ref, out_ref, column_ref, in_ref, wide_ref):
    rows, cycles = references_ref.shape
    classes = offset_ref.shape[0]
    own_rows = rows // (2 * classes)
    in_ref[...] = references_ref[...].astype(f32)
    row = lax.broadcasted_iota(jnp.int32, (8, LANES), 0)
    lane = lax.broadcasted_iota(jnp.int32, (8, LANES), 1)
    freq = (lane + first_ref[0]).astype(f32) * (1.0 / (ROTS * ANG_STEP))
    tables = []
    for start in range(0, classes, 8):
        column = jnp.zeros((8, LANES), jnp.int32)
        for c in range(start, min(start + 8, classes)):
            column = jnp.where(row == c - start, offset_ref[c], column)
        column = column.astype(f32)
        column_ref[start : start + 8, :] = column
        tables.append(cos_sin_of_turns(column * freq))
    cosine = jnp.concatenate([c for c, _ in tables], 0)
    sine_part = jnp.concatenate([s for _, s in tables], 0)
    for m in range(own_rows):
        re_rows = pl.ds(2 * m * classes, classes, stride=2)
        im_rows = pl.ds(2 * m * classes + 1, classes, stride=2)
        c, s = cosine[:classes, m : m + 1], sine_part[:classes, m : m + 1]
        re, im = in_ref[re_rows, :], in_ref[im_rows, :]
        wide_ref[re_rows, :] = re * c + im * s
        wide_ref[im_rows, :] = im * c - re * s
    out_ref[...] = wide_ref[...].astype(bf16)


def turn_references(first, offsets, references):
    padded = -(-offsets.shape[0] // 8) * 8
    return pl.pallas_call(
        turn_kernel,
        in_specs=[
            pl.BlockSpec(memory_space=pltpu.SMEM),
            pl.BlockSpec(memory_space=pltpu.SMEM),
            pl.BlockSpec(memory_space=pltpu.VMEM),
        ],
        out_shape=[
            jax.ShapeDtypeStruct(references.shape, bf16),
            jax.ShapeDtypeStruct((padded, LANES), f32),
        ],
        scratch_shapes=[pltpu.VMEM(references.shape, f32)] * 2,
        compiler_params=pltpu.CompilerParams(vmem_limit_bytes=VMEM_LIMIT),
        name="turn_references",
    )(first, offsets, references)


def correlate_kernel(*refs, slots, classes, padded, finish):
    part_ref, refs = refs[slots], refs[slots + 1 :]
    weighted_refs, refs = refs[:slots], refs[slots:]
    piece_refs, refs = refs[:slots], refs[slots:]
    if finish:
        before_ref, power_before_ref, ctf_ref, weight_ref, stat_ref, share_ref = refs[:6]
        corr_ref, wide_ref, power_ref = refs[6:]
    else:
        corr_ref, power_ref, wide_ref = refs
    group = pl.program_id(0)
    cycles = piece_refs[0].shape[1]
    queries = weighted_refs[0].shape[2]
    block = piece_refs[0].shape[0]

    @pl.when(group == 0)
    def _():
        wide_ref[:, block:, :] = jnp.zeros((slots, wide_ref.shape[1] - block, cycles), f32)
        power_ref[...] = power_before_ref[...] if finish else jnp.zeros_like(power_ref)

    for j in range(slots):
        wide_ref[j, :block, :] = piece_refs[j][...].astype(f32)
    power = power_ref[...]
    for i in range(GROUP):
        total = before_ref[i, :, :queries] if finish else None
        for j in range(slots):
            re = wide_ref[j, pl.ds(2 * i * classes, padded, stride=2), :]
            im = wide_ref[j, pl.ds(2 * i * classes + 1, padded, stride=2), :]
            power = power + (re * re + im * im)
            left = jnp.concatenate(
                [jnp.concatenate([re, im], 1), jnp.concatenate([-im, re], 1)], 0
            ).astype(bf16)
            part = lax.dot_general(
                left, weighted_refs[j][0, i], (((1,), (1,)), ((), ())), preferred_element_type=f32
            )
            total = part if total is None else total + part
        row = group * GROUP + i if finish else i
        corr_ref[row, :, :queries] = total
    power_ref[...] = power

    if not finish:
        return

    @pl.when(group == pl.num_programs(0) - 1)
    def _():
        count = ctf_ref.shape[0]
        angles = ROTS * ANG_STEP
        used = SHIFTS * count
        tiles = weight_ref.shape[2] // LANES
        ctf_row = ctf_ref[...]
        ctf_rows = jnp.concatenate([ctf_row * ctf_row] * (LANES // count), 0)
        bias = lax.dot_general(
            power_ref[...],
            ctf_rows,
            (((1,), (1,)), ((), ())),
            precision=lax.Precision.HIGHEST,
            preferred_element_type=f32,
        ) * (0.5 / angles)
        wide_ref[0, :padded, :] = bias
        rows_of = lambda base: lax.broadcasted_iota(jnp.int32, (8, LANES), 0) + base
        lanes_of = lambda base: lax.broadcasted_iota(jnp.int32, (8, LANES), 1) + base

        peak = jnp.full((8, LANES), -1e30, f32)
        for tile in range(tiles):
            lanes = slice(tile * LANES, (tile + 1) * LANES)

            def scores(n, peak):
                start = pl.multiple_of(n * 8, 8)
                rows = pl.ds(start, 8)
                low = pl.ds(padded + start, 8)
                valid = (rows_of(start) < classes) & (lanes_of(tile * LANES) < used)
                even_values = [corr_ref[0, rows, lanes]]
                odd_values = [None]
                for m in range(1, ROTS // 2):
                    even_values.append(corr_ref[m, rows, lanes] + corr_ref[ROTS - m, rows, lanes])
                    odd_values.append(corr_ref[m, low, lanes] - corr_ref[ROTS - m, low, lanes])
                even_values.append(corr_ref[ROTS // 2, rows, lanes])
                odd_values.append(None)
                cos_sums, sin_sums = half_dft(even_values, odd_values)
                bias = wide_ref[0, rows, :]
                for k in range(FOLD):
                    if k in (0, FOLD - 1):
                        results = [(k, cos_sums[k])]
                    else:
                        results = [(k, cos_sums[k] - sin_sums[k]), (ROTS - k, cos_sums[k] + sin_sums[k])]
                    for place, value in results:
                        value = jnp.where(valid, value * (1.0 / angles) - bias, -1e30)
                        weight_ref[place, rows, lanes] = value
                        peak = jnp.maximum(peak, value)
                return peak

            peak = lax.fori_loop(0, padded // 8, scores, peak)

        peak = jnp.broadcast_to(jnp.max(peak, axis=0, keepdims=True), (8, LANES))
        step = count
        while step < LANES:
            peak = jnp.maximum(peak, pltpu.roll(peak, step, 1))
            step *= 2
        stat_ref[0:8, :] = peak

        def masses(n, whole):
            rows = pl.ds(pl.multiple_of(n * 8, 8), 8)
            mass = jnp.zeros((8, LANES), f32)
            for tile in range(tiles):
                lanes = slice(tile * LANES, (tile + 1) * LANES)
                for k in range(ROTS):
                    value = jnp.exp(weight_ref[k, rows, lanes] - peak)
                    weight_ref[k, rows, lanes] = value
                    mass = mass + value
            step = count
            while step < LANES:
                mass = mass + pltpu.roll(mass, step, 1)
                step *= 2
            stat_ref[pl.ds(pl.multiple_of(8 + n * 8, 8), 8), :] = mass
            return whole + mass

        whole = lax.fori_loop(0, padded // 8, masses, jnp.zeros((8, LANES), f32))
        share = jnp.concatenate([peak[:1], jnp.sum(whole, axis=0, keepdims=True)], 0)
        for j in range(share_ref.shape[0]):
            share_ref[j] = jnp.where(part_ref[0] == j, share, 0.0)


def correlate(slot_of, weighted, pieces, classes, part, before=None, power=None, ctf_rows=None, parts=1):
    _, _, queries, double = weighted.shape
    cycles = double // 2
    slots = len(pieces)
    padded = -(-classes // 8) * 8
    wide_lanes = -(-queries // LANES) * LANES
    block = 2 * GROUP * classes
    finish = ctf_rows is not None
    full = lambda shape: pl.BlockSpec(shape, lambda g, *u: (0,) * len(shape))
    in_specs = [
        pl.BlockSpec((1, GROUP, queries, double), functools.partial(lambda j, g, *u: (u[j][0], g, 0, 0), j))
        for j in range(slots)
    ] + [pl.BlockSpec((block, cycles), lambda g, *u: (g, 0))] * slots
    corr_block = pl.BlockSpec((GROUP, 2 * padded, wide_lanes), lambda g, *u: (g, 0, 0))
    corr_shape = (ROTS, 2 * padded, wide_lanes)
    wide = pltpu.VMEM((slots, block + ROWS, cycles), f32)
    scalars = [jnp.reshape(n, (1,)).astype(jnp.int32) for n in (*slot_of, part)]
    operands = scalars + [weighted] * slots + list(pieces)
    if finish:
        in_specs += [corr_block, full((padded, cycles)), full(ctf_rows.shape)]
        operands += [before, power, ctf_rows]
        out_shapes = [(ROTS, padded, wide_lanes), (8 + padded, LANES), (parts, 2, LANES)]
        out_specs = [full(shape) for shape in out_shapes]
        scratch = [pltpu.VMEM(corr_shape, f32), wide, pltpu.VMEM((padded, cycles), f32)]
    else:
        out_shapes = [corr_shape, (padded, cycles)]
        out_specs = [corr_block, full((padded, cycles))]
        scratch = [wide]
    return pl.pallas_call(
        functools.partial(correlate_kernel, slots=slots, classes=classes, padded=padded, finish=finish),
        grid_spec=pltpu.PrefetchScalarGridSpec(
            num_scalar_prefetch=len(scalars),
            grid=(ROTS // GROUP,),
            in_specs=in_specs,
            out_specs=out_specs,
            scratch_shapes=scratch,
        ),
        out_shape=[jax.ShapeDtypeStruct(shape, f32) for shape in out_shapes],
        compiler_params=pltpu.CompilerParams(vmem_limit_bytes=VMEM_LIMIT),
        name="scores" if finish else "correlate",
    )(*operands)


def back_kernel(weight_ref, stat_ref, share_ref, offset_ref, out_ref, evidence_ref, posterior_ref, sum_ref):
    padded = weight_ref.shape[1]
    queries = out_ref.shape[2]
    shares = [share_ref[j] for j in range(share_ref.shape[0])]
    top = shares[0][:1]
    for share in shares[1:]:
        top = jnp.maximum(top, share[:1])
    mass = sum(share[1:] * jnp.exp(share[:1] - top) for share in shares)
    evidence = jnp.broadcast_to(top + jnp.log(mass), (8, LANES))
    scale = jnp.exp(stat_ref[:8, :] - evidence)
    evidence_ref[...] = evidence
    posterior_ref[...] = stat_ref[8:, :] * scale[:1]
    for tile in range(weight_ref.shape[2] // LANES):
        lanes = slice(tile * LANES, (tile + 1) * LANES)

        def transform(n, carry):
            start = pl.multiple_of(n * 8, 8)
            rows = pl.ds(start, 8)
            low = pl.ds(padded + start, 8)
            values = [weight_ref[k, rows, lanes] * scale for k in range(ROTS)]
            even_values = [values[0]] + [values[k] + values[ROTS - k] for k in range(1, ROTS // 2)]
            odd_values = [None] + [values[k] - values[ROTS - k] for k in range(1, ROTS // 2)] + [None]
            cos_sums, sin_sums = half_dft(even_values + [values[ROTS // 2]], odd_values)
            for m in range(FOLD):
                sine_part = jnp.zeros_like(scale) if m in (0, FOLD - 1) else sin_sums[m]
                sum_ref[m, rows, lanes] = cos_sums[m]
                sum_ref[m, low, lanes] = sine_part
                if m not in (0, FOLD - 1):
                    sum_ref[ROTS - m, rows, lanes] = cos_sums[m]
                    sum_ref[ROTS - m, low, lanes] = -sine_part
            return carry

        lax.fori_loop(0, padded // 8, transform, 0)

    step_cos, step_sin = cos_sin_of_turns(offset_ref[...] * (1.0 / (ROTS * ANG_STEP)))

    def turn(m, carry):
        cosine, sine_part = carry
        for tile in range(weight_ref.shape[2] // LANES):
            lanes = slice(tile * LANES, (tile + 1) * LANES)
            kept = slice(tile * LANES, min((tile + 1) * LANES, queries))
            re, im = sum_ref[m, :padded, lanes], sum_ref[m, padded:, lanes]
            turned = jnp.concatenate([re * cosine - im * sine_part, re * sine_part + im * cosine], 0)
            out_ref[m, :, kept] = turned[:, : kept.stop - kept.start].astype(bf16)
        return cosine * step_cos - sine_part * step_sin, sine_part * step_cos + cosine * step_sin

    lax.fori_loop(0, ROTS, turn, (jnp.ones_like(step_cos), jnp.zeros_like(step_cos)))


def make_back(weights, stat, shares, offsets, queries):
    _, padded, wide_lanes = weights.shape
    return pl.pallas_call(
        back_kernel,
        out_shape=[
            jax.ShapeDtypeStruct((ROTS, 2 * padded, queries), bf16),
            jax.ShapeDtypeStruct((8, LANES), f32),
            jax.ShapeDtypeStruct((padded, LANES), f32),
        ],
        scratch_shapes=[pltpu.VMEM((ROTS, 2 * padded, wide_lanes), f32)],
        compiler_params=pltpu.CompilerParams(vmem_limit_bytes=VMEM_LIMIT),
        name="back",
    )(weights, stat, shares, offsets)


def sums_kernel(slot_ref, back_ref, weighted_ref, offset_ref, out_ref, wide_ref, *, classes):
    padded = offset_ref.shape[0]
    cycles = wide_ref.shape[1]
    turns = offset_ref[...] * (slot_ref[0].astype(f32) * (1.0 / ANG_STEP))
    cosine, sine_part = cos_sin_of_turns(turns)
    for i in range(GROUP):
        product = jnp.dot(back_ref[i], weighted_ref[0, i], preferred_element_type=f32)
        re = product[:padded, :cycles] - product[padded:, cycles:]
        im = product[:padded, cycles:] + product[padded:, :cycles]
        start = 2 * i * classes
        wide_ref[pl.ds(start, classes, stride=2), :] = (re * cosine - im * sine_part)[:classes]
        wide_ref[pl.ds(start + 1, classes, stride=2), :] = (re * sine_part + im * cosine)[:classes]
    out_ref[...] = wide_ref[...].astype(out_ref.dtype)


def class_sums_of(slot, back, weighted, offsets, classes, dtype, groups=(0, ROTS // GROUP)):
    begin, end = groups
    _, _, queries, double = weighted.shape
    cycles = double // 2
    rows = back.shape[1]
    block = 2 * GROUP * classes
    piece = pl.BlockSpec((block, cycles), lambda g, u: (g, 0))
    return pl.pallas_call(
        functools.partial(sums_kernel, classes=classes),
        grid_spec=pltpu.PrefetchScalarGridSpec(
            num_scalar_prefetch=1,
            grid=(end - begin,),
            in_specs=[
                pl.BlockSpec((GROUP, rows, queries), lambda g, u: (g + begin, 0, 0)),
                pl.BlockSpec((1, GROUP, queries, double), lambda g, u: (u[0], g + begin, 0, 0)),
                pl.BlockSpec(offsets.shape, lambda g, u: (0, 0)),
            ],
            out_specs=piece,
            scratch_shapes=[pltpu.VMEM((block, cycles), f32)],
        ),
        out_shape=jax.ShapeDtypeStruct(((end - begin) * block, cycles), dtype),
        compiler_params=pltpu.CompilerParams(vmem_limit_bytes=VMEM_LIMIT),
        name="class_sums",
    )(jnp.reshape(slot, (1,)).astype(jnp.int32), back, weighted, offsets)


def across(piece):
    return lax.ppermute(piece, "dp", [(d, d ^ 1) for d in range(8)])


def along(piece, pairs):
    return lax.ppermute(piece, "dp", [(2 * a + x, 2 * b + x) for a, b in pairs for x in range(2)])


def gather_on_line(piece, base, ctf_rows):
    index = lax.axis_index("dp")
    line, side = index // 2, index % 2
    _, steps = spectra_steps(base.shape[0])
    cuts = [0, 3 * steps // 13, 8 * steps // 13, steps]

    own_crossed = across(piece)
    near = along(piece, ((0, 1), (1, 0), (2, 3), (3, 2)))
    middle = along(piece, ((1, 2), (2, 1)))
    weighted = make_spectra(base, ctf_rows, cuts[0], cuts[1])
    weighted, near, middle, own_crossed = lax.optimization_barrier((weighted, near, middle, own_crossed))
    near_crossed = across(near)
    far_middle = along(near, ((1, 2), (2, 1)))
    end = along(middle, ((1, 0), (2, 3)))
    weighted = make_spectra(base, ctf_rows, cuts[1], cuts[2], weighted)
    weighted, far_middle, end, near_crossed = lax.optimization_barrier(
        (weighted, far_middle, end, near_crossed)
    )
    third = middle + end
    third_crossed = across(third)
    far_end = along(far_middle, ((1, 0), (2, 3)))
    weighted = make_spectra(base, ctf_rows, cuts[2], cuts[3], weighted)
    weighted, far_end, third_crossed = lax.optimization_barrier((weighted, far_end, third_crossed))
    fourth = far_middle + far_end
    fourth_crossed = across(fourth)

    pieces = [piece, own_crossed, near, near_crossed, third, third_crossed, fourth, fourth_crossed]
    places = [line, line ^ 1, jnp.where(line < 2, 2, 1), jnp.where(line < 2, 3, 0)]
    slot_of = [2 * place + s for place in places for s in (side, 1 - side)]
    return weighted, pieces, slot_of


def add_kernel(own_ref, *refs):
    first = pl.program_id(0) == 0
    whole_ref, pairs, out_ref = refs[0], refs[1:-1], refs[-1]
    total = own_ref[...] + whole_ref[...].astype(f32)
    for n in range(0, len(pairs), 2):
        total = total + jnp.where(first, pairs[n][...], pairs[n + 1][...]).astype(f32)
    out_ref[...] = total


def add_pieces(own, whole, pairs, block):
    rows, cycles = own.shape
    spec = pl.BlockSpec((block, cycles), lambda g: (g, 0))
    head = pl.BlockSpec((block, cycles), lambda g: (0, 0))
    rest = pl.BlockSpec((block, cycles), lambda g: (jnp.maximum(g - 1, 0), 0))
    return pl.pallas_call(
        add_kernel,
        grid=(rows // block,),
        in_specs=[spec, spec] + [head, rest] * len(pairs),
        out_specs=spec,
        out_shape=jax.ShapeDtypeStruct(own.shape, f32),
        name="add_pieces",
    )(own, whole, *[part for pair in pairs for part in pair])


def reduce_on_line(back, weighted, offsets, classes):
    index = lax.axis_index("dp")
    line, side = index // 2, index % 2
    order = [jnp.where(line < 2, 3, 0), jnp.where(line < 2, 2, 1), line ^ 1, line]
    groups = ((0, 1), (1, ROTS // GROUP))
    block = 2 * GROUP * classes
    rows = [slice(a * block, b * block) for a, b in groups]

    def theirs(n, back, some=(0, ROTS // GROUP)):
        return class_sums_of(2 * order[n] + 1 - side, back, weighted, offsets, classes, bf16, some)

    def ours(n, back):
        return class_sums_of(2 * order[n] + side, back, weighted, offsets, classes, f32)

    def wide(piece):
        return piece.astype(f32)

    def then(back, *done):
        return lax.optimization_barrier((back, *done))[0]

    at_end = (line == 0) | (line == 3)
    away = [theirs(0, back, groups[0])]
    crossed = [across(away[0])]
    back = then(back, away[0])
    away.append(theirs(0, back, groups[1]))
    crossed.append(across(away[1]))
    back = then(back, away[1])
    own = [ours(0, back)]
    crossed[0], own[0] = lax.optimization_barrier((crossed[0], own[0]))
    farthest = [own[0][rows[0]] + wide(crossed[0])]
    message = farthest[0].astype(bf16)
    first = [along(message, ((0, 1), (3, 2)))]
    back = then(back, message)
    away.append(theirs(1, back))
    crossed.append(across(away[2]))
    back = then(back, away[2])
    own.append(ours(1, back))
    crossed[1], own[1] = lax.optimization_barrier((crossed[1], own[1]))
    farthest.append(own[0][rows[1]] + wide(crossed[1]))
    message = farthest[1].astype(bf16)
    first.append(along(message, ((0, 1), (3, 2))))
    back = then(back, message)
    away.append(theirs(2, back))
    crossed.append(across(away[3]))
    back = then(back, away[3])
    own.append(ours(2, back))
    back = then(back, own[2])
    away.append(theirs(3, back))
    crossed.append(across(away[4]))
    crossed[2], away[4] = lax.optimization_barrier((crossed[2], away[4]))
    next_farthest = [own[1][r] + wide(crossed[2][r]) for r in rows]
    second = [
        (jnp.where(at_end, b, a) + wide(c)).astype(bf16) for a, b, c in zip(farthest, next_farthest, first)
    ]
    from_ends = [along(piece, ((0, 1), (3, 2))) for piece in second]
    from_middle = [along(piece, ((1, 2), (2, 1))) for piece in second]
    back = then(back, *second)
    own.append(ours(3, back))
    message = (next_farthest[0] + wide(from_ends[0])).astype(bf16)
    third = [along(message, ((1, 2), (2, 1)))]
    crossed[3], from_middle[0], message = lax.optimization_barrier((crossed[3], from_middle[0], message))
    message = (own[2][rows[0]] + wide(crossed[3][rows[0]]) + wide(from_middle[0])).astype(bf16)
    fourth = [along(message, ((0, 1), (1, 0), (2, 3), (3, 2)))]
    message = (own[2][rows[1]] + wide(crossed[3][rows[1]]) + wide(from_middle[1])).astype(bf16)
    fourth.append(along(message, ((0, 1), (1, 0), (2, 3), (3, 2))))
    message = (next_farthest[1] + wide(from_ends[1])).astype(bf16)
    third.append(along(message, ((1, 2), (2, 1))))
    return add_pieces(own[3], crossed[4], (third, fourth), block)


def local(particles, references, ctf_table, rot_offset, prior_shift, defocus_group):
    count, _, angles, cycles = particles.shape
    own_rows, _, classes, _ = references.shape
    slots = angles // ROTS
    group_count = ctf_table.shape[0]
    devices = lax.axis_size("dp")

    first = (lax.axis_index("dp") * own_rows).astype(jnp.int32).reshape(1)
    rows = jnp.transpose(references, (0, 2, 1, 3)).reshape(own_rows * 2 * classes, cycles)
    piece, offsets = turn_references(first, rot_offset, rows)

    onehot = (defocus_group[:, None] == jnp.arange(group_count, dtype=jnp.int32)[None, :]).astype(f32)
    ctf_rows = jnp.dot(onehot, ctf_table, precision=lax.Precision.HIGHEST)
    base = make_base(particles, prior_shift)
    on_line = devices == 8 and own_rows == ROTS
    if on_line:
        weighted, pieces, slot_of = gather_on_line(piece, base, ctf_rows)
    else:
        gathered = lax.all_gather(piece, "dp", axis=0, tiled=True)
        gathered = gathered.reshape(slots, ROTS * 2 * classes, cycles)
        pieces = [gathered[j] for j in range(slots)]
        slot_of = list(range(slots))
        weighted = make_spectra(base, ctf_rows, 0, spectra_steps(count)[1])
    queries = weighted.shape[1]
    weighted = weighted.reshape(slots, ROTS, queries, 2 * cycles)

    early = slots - 1
    part = lax.axis_index("cls")
    corr, power = correlate(slot_of[:early], weighted, pieces[:early], classes, part)
    weights, stat, share = correlate(
        slot_of[early:], weighted, pieces[early:], classes, part, corr, power, ctf_rows, lax.axis_size("cls")
    )
    shares = lax.psum(share, "cls")
    back, evidence, posterior = make_back(weights, stat, shares, offsets, queries)
    log_evidence = evidence[0, :count]
    class_posterior = posterior[:classes, :count].T
    if on_line:
        class_rows = reduce_on_line(back, weighted, offsets, classes)
    else:
        sums = [class_sums_of(slot_of[u], back, weighted, offsets, classes, bf16) for u in range(slots)]
        summed = lax.psum_scatter(jnp.concatenate(sums, 0), "dp", scatter_dimension=0, tiled=True)
        class_rows = summed.astype(f32)
    class_sums = jnp.transpose(class_rows.reshape(own_rows, classes, 2, cycles), (0, 2, 1, 3))
    return (log_evidence, class_posterior, class_sums)


def solution(mesh):
    placed = (
        P("dp", None, None, None),
        P("dp", None, "cls", None),
        P(),
        P("cls"),
        P("dp", None),
        P("dp"),
    )
    return jax.shard_map(
        local,
        mesh=mesh,
        in_specs=placed,
        out_specs=(P("dp"), P("dp", "cls"), P("dp", None, "cls", None)),
        check_vma=False,
    )
```

```python
import functools
import math

import jax
import jax.numpy as jnp
import ml_dtypes
import numpy as np
from jax import lax
from jax.experimental import pallas as pl
from jax.experimental.pallas import tpu as pltpu
from jax.sharding import PartitionSpec as P

ROTS = 36
ANG_STEP = 8
SHIFT_SIDE = 5
SHIFTS = SHIFT_SIDE * SHIFT_SIDE
LANES = 128
GROUP = 12
ROWS = 16
APART = 17
FOLD = ROTS // 2 + 1

two_pi = 2.0 * math.pi
f32 = jnp.float32
bf16 = jnp.bfloat16
VMEM_LIMIT = 56 * 1024 * 1024


def fourier_rows(angles):
    index_grid = np.arange(angles)
    radians = (index_grid[:, None] * index_grid[None, :] % angles) * (two_pi / angles)
    cosine, sine_part = np.cos(radians), np.sin(radians)
    table_full = np.concatenate(
        [np.concatenate([cosine, sine_part], 1), np.concatenate([-sine_part, cosine], 1)], 0
    )
    return table_full.astype(np.float32).astype(ml_dtypes.bfloat16)


def shift_tables(angles, cycles):
    theta = np.arange(angles) * (two_pi / angles)
    radius = (np.arange(cycles) + 1) / (2.0 * cycles)
    turns = np.stack([np.cos(theta), np.sin(theta)])[:, :, None] * radius
    steps = np.arange(SHIFT_SIDE) - SHIFT_SIDE // 2
    phase = two_pi * turns[:, None] * steps[None, :, None, None]
    factors = np.stack([np.cos(phase), -np.sin(phase)], 2)
    return turns.astype(np.float32), factors.astype(np.float32)


def cos_sin_of_turns(turns):
    frac = turns - jnp.floor(turns + 0.5)
    w = frac * two_pi
    w2 = w * w
    cosine = jnp.full_like(w, 1.0 / math.factorial(16))
    for n in range(14, -1, -2):
        cosine = cosine * w2 + (-1.0) ** (n // 2) / math.factorial(n)
    sine_part = jnp.full_like(w, 1.0 / math.factorial(17))
    for n in range(15, 0, -2):
        sine_part = sine_part * w2 + (-1.0) ** (n // 2) / math.factorial(n)
    return cosine, sine_part * w


def base_kernel(shift_ref, part_ref, turns_ref, base_ref):
    here, _, angles, _ = part_ref.shape
    chunk = 32
    for q in range(here):
        p = pl.program_id(0) * here + q
        sx = shift_ref[0, p].astype(f32)
        sy = shift_ref[1, p].astype(f32)

        def turn(n, carry):
            rows = pl.ds(pl.multiple_of(n * chunk, chunk), chunk)
            cosine, sine_part = cos_sin_of_turns(sx * turns_ref[0, rows, :] + sy * turns_ref[1, rows, :])
            re = part_ref[q, 0, rows, :].astype(f32)
            im = part_ref[q, 1, rows, :].astype(f32)
            base_ref[q, 0, rows, :] = re * cosine + im * sine_part
            base_ref[q, 1, rows, :] = im * cosine - re * sine_part
            return carry

        lax.fori_loop(0, angles // chunk, turn, 0)


def make_base(particles, prior_shift):
    count, _, angles, cycles = particles.shape
    turns, _ = shift_tables(angles, cycles)
    here = count // 2
    image = pl.BlockSpec((here, 2, angles, cycles), lambda p: (p, 0, 0, 0))
    return pl.pallas_call(
        base_kernel,
        grid=(2,),
        in_specs=[
            pl.BlockSpec(memory_space=pltpu.SMEM),
            image,
            pl.BlockSpec(turns.shape, lambda p: (0, 0, 0)),
        ],
        out_specs=image,
        out_shape=jax.ShapeDtypeStruct(particles.shape, f32),
        compiler_params=pltpu.CompilerParams(vmem_limit_bytes=VMEM_LIMIT),
        name="centre",
    )(prior_shift.T, particles, turns)


def spectra_kernel(base_ref, ctf_ref, table_ref, *refs, per_step):
    factor_refs, refs = refs[: 2 * per_step], refs[2 * per_step :]
    chunks = ROWS // 2
    out_ref, turn_ref, re_ref, im_ref = refs[-4 - chunks : -chunks]
    data_refs = refs[-chunks:]
    count, _, angles, cycles = base_ref.shape
    chunk = 32

    for g in range(per_step):
        x_ref, y_ref = factor_refs[2 * g], factor_refs[2 * g + 1]
        for start in range(0, angles, chunk):
            rows = slice(start, start + chunk)
            xr, xi = x_ref[0, 0, 0, rows, :], x_ref[0, 0, 1, rows, :]
            yr, yi = y_ref[0, 0, 0, rows, :], y_ref[0, 0, 1, rows, :]
            turn_ref[g, 0, rows, :] = xr * yr - xi * yi
            turn_ref[g, 1, rows, :] = xr * yi + xi * yr

    def shift(n):
        for j in range(2):
            g, p = (2 * n + j) // count, (2 * n + j) % count
            lanes = slice(j * cycles, (j + 1) * cycles)
            for start in range(0, angles, chunk):
                rows = slice(start, start + chunk)
                tr, ti = turn_ref[g, 0, rows, :], turn_ref[g, 1, rows, :]
                gr, gi = base_ref[p, 0, rows, :], base_ref[p, 1, rows, :]
                data_refs[n][rows, lanes] = (gr * tr - gi * ti).astype(bf16)
                data_refs[n][angles + start : angles + start + chunk, lanes] = (gr * ti + gi * tr).astype(bf16)

    shift(0)
    for n in range(chunks):
        if n + 1 < chunks:
            shift(n + 1)
        spectrum = jnp.dot(table_ref[...], data_refs[n][...], preferred_element_type=f32)
        for j in range(2):
            row = 2 * n + j
            ctf_row = ctf_ref[row % count, :][None, :]
            part = spectrum[:, j * cycles : (j + 1) * cycles] * ctf_row
            re_ref[pl.ds(row, angles, stride=APART), :] = part[:angles]
            im_ref[pl.ds(row, angles, stride=APART), :] = part[angles:]
    for m in range(angles):
        out_ref[m, :, :cycles] = re_ref[m * APART : m * APART + ROWS, :].astype(bf16)
        out_ref[m, :, cycles:] = im_ref[m * APART : m * APART + ROWS, :].astype(bf16)


def spectra_steps(count):
    per_step = ROWS // count if count < ROWS else 1
    return per_step, -(-SHIFTS // per_step)


def make_spectra(base, ctf_rows, first, last, before=None, after=()):
    count, _, angles, cycles = base.shape
    per_step, steps = spectra_steps(count)
    _, factors = shift_tables(angles, cycles)
    full = lambda shape: pl.BlockSpec(shape, lambda i: (0,) * len(shape))

    def factor_spec(g, axis):
        def place(i):
            s = jnp.minimum((i + first) * per_step + g, SHIFTS - 1)
            a = lax.div(s, jnp.int32(SHIFT_SIDE))
            return (axis, s - a * SHIFT_SIDE if axis else a, 0, 0, 0)

        return pl.BlockSpec((1, 1, 2, angles, cycles), place)

    untouched = ([] if before is None else [before]) + list(after)
    in_specs = (
        [full(base.shape), full(ctf_rows.shape), full((2 * angles, 2 * angles))]
        + [factor_spec(g, axis) for g in range(per_step) for axis in range(2)]
        + [pl.BlockSpec(memory_space=pl.ANY)] * len(untouched)
    )
    return pl.pallas_call(
        functools.partial(spectra_kernel, per_step=per_step),
        grid=(last - first,),
        in_specs=in_specs,
        out_specs=pl.BlockSpec((angles, ROWS, 2 * cycles), lambda i: (0, i + first, 0)),
        out_shape=jax.ShapeDtypeStruct((angles, steps * ROWS, 2 * cycles), bf16),
        scratch_shapes=[
            pltpu.VMEM((per_step, 2, angles, cycles), f32),
            pltpu.VMEM((angles * APART, cycles), f32),
            pltpu.VMEM((angles * APART, cycles), f32),
        ]
        + [pltpu.VMEM((2 * angles, 2 * cycles), bf16)] * (ROWS // 2),
        input_output_aliases={} if before is None else {3 + 2 * per_step: 0},
        compiler_params=pltpu.CompilerParams(vmem_limit_bytes=VMEM_LIMIT),
        name="spectra",
    )(base, ctf_rows, fourier_rows(angles), *[factors] * (2 * per_step), *untouched)


def half_dft(even_values, odd_values):
    half = FOLD // 2
    cos_sums, sin_sums = [None] * FOLD, [None] * FOLD

    def weighted_sum(values, k, table, start):
        total = None
        for m in range(start, FOLD, 2):
            weight = float(table((k * m % ROTS) * two_pi / ROTS))
            if values[m] is None or abs(weight) < 1e-9:
                continue
            if abs(abs(weight) - 1.0) < 1e-9:
                term = values[m] if weight > 0 else -values[m]
            else:
                term = values[m] * weight
            total = term if total is None else total + term
        return jnp.zeros_like(values[1]) if total is None else total

    for k in range(half + 1):
        even = weighted_sum(even_values, k, math.cos, 0)
        odd = weighted_sum(even_values, k, math.cos, 1)
        cos_sums[k] = even + odd
        if k != half:
            cos_sums[FOLD - 1 - k] = even - odd
        if k:
            even = weighted_sum(odd_values, k, math.sin, 0)
            odd = weighted_sum(odd_values, k, math.sin, 1)
            sin_sums[k] = even + odd
            if k != half:
                sin_sums[FOLD - 1 - k] = odd - even
    return cos_sums, sin_sums


def turn_kernel(first_ref, offset_ref, references_ref, out_ref, column_ref, in_ref, wide_ref):
    rows, cycles = references_ref.shape
    classes = offset_ref.shape[0]
    own_rows = rows // (2 * classes)
    in_ref[...] = references_ref[...].astype(f32)
    row = lax.broadcasted_iota(jnp.int32, (8, LANES), 0)
    lane = lax.broadcasted_iota(jnp.int32, (8, LANES), 1)
    freq = (lane + first_ref[0]).astype(f32) * (1.0 / (ROTS * ANG_STEP))
    tables = []
    for start in range(0, classes, 8):
        column = jnp.zeros((8, LANES), jnp.int32)
        for c in range(start, min(start + 8, classes)):
            column = jnp.where(row == c - start, offset_ref[c], column)
        column = column.astype(f32)
        column_ref[start : start + 8, :] = column
        tables.append(cos_sin_of_turns(column * freq))
    cosine = jnp.concatenate([c for c, _ in tables], 0)
    sine_part = jnp.concatenate([s for _, s in tables], 0)
    for m in range(own_rows):
        re_rows = pl.ds(2 * m * classes, classes, stride=2)
        im_rows = pl.ds(2 * m * classes + 1, classes, stride=2)
        c, s = cosine[:classes, m : m + 1], sine_part[:classes, m : m + 1]
        re, im = in_ref[re_rows, :], in_ref[im_rows, :]
        wide_ref[re_rows, :] = re * c + im * s
        wide_ref[im_rows, :] = im * c - re * s
    out_ref[...] = wide_ref[...].astype(bf16)


def turn_references(first, offsets, references):
    padded = -(-offsets.shape[0] // 8) * 8
    return pl.pallas_call(
        turn_kernel,
        in_specs=[
            pl.BlockSpec(memory_space=pltpu.SMEM),
            pl.BlockSpec(memory_space=pltpu.SMEM),
            pl.BlockSpec(memory_space=pltpu.VMEM),
        ],
        out_shape=[
            jax.ShapeDtypeStruct(references.shape, bf16),
            jax.ShapeDtypeStruct((padded, LANES), f32),
        ],
        scratch_shapes=[pltpu.VMEM(references.shape, f32)] * 2,
        compiler_params=pltpu.CompilerParams(vmem_limit_bytes=VMEM_LIMIT),
        name="turn_references",
    )(first, offsets, references)


def correlate_kernel(*refs, slots, classes, padded, finish):
    part_ref, refs = refs[slots], refs[slots + 1 :]
    weighted_refs, refs = refs[:slots], refs[slots:]
    piece_refs, refs = refs[:slots], refs[slots:]
    if finish:
        before_ref, power_before_ref, ctf_ref, weight_ref, stat_ref, share_ref = refs[:6]
        corr_ref, wide_ref, power_ref = refs[6:]
    else:
        corr_ref, power_ref, wide_ref = refs
    group = pl.program_id(0)
    cycles = piece_refs[0].shape[1]
    queries = weighted_refs[0].shape[2]
    block = piece_refs[0].shape[0]

    @pl.when(group == 0)
    def _():
        wide_ref[:, block:, :] = jnp.zeros((slots, wide_ref.shape[1] - block, cycles), f32)
        power_ref[...] = power_before_ref[...] if finish else jnp.zeros_like(power_ref)

    for j in range(slots):
        wide_ref[j, :block, :] = piece_refs[j][...].astype(f32)
    power = power_ref[...]
    for i in range(GROUP):
        total = before_ref[i, :, :queries] if finish else None
        for j in range(slots):
            re = wide_ref[j, pl.ds(2 * i * classes, padded, stride=2), :]
            im = wide_ref[j, pl.ds(2 * i * classes + 1, padded, stride=2), :]
            power = power + (re * re + im * im)
            left = jnp.concatenate(
                [jnp.concatenate([re, im], 1), jnp.concatenate([-im, re], 1)], 0
            ).astype(bf16)
            part = lax.dot_general(
                left, weighted_refs[j][0, i], (((1,), (1,)), ((), ())), preferred_element_type=f32
            )
            total = part if total is None else total + part
        row = group * GROUP + i if finish else i
        corr_ref[row, :, :queries] = total
    power_ref[...] = power

    if not finish:
        return

    @pl.when(group == pl.num_programs(0) - 1)
    def _():
        count = ctf_ref.shape[0]
        angles = ROTS * ANG_STEP
        used = SHIFTS * count
        tiles = weight_ref.shape[2] // LANES
        ctf_row = ctf_ref[...]
        ctf_rows = jnp.concatenate([ctf_row * ctf_row] * (LANES // count), 0)
        bias = lax.dot_general(
            power_ref[...],
            ctf_rows,
            (((1,), (1,)), ((), ())),
            precision=lax.Precision.HIGHEST,
            preferred_element_type=f32,
        ) * (0.5 / angles)
        wide_ref[0, :padded, :] = bias
        rows_of = lambda base: lax.broadcasted_iota(jnp.int32, (8, LANES), 0) + base
        lanes_of = lambda base: lax.broadcasted_iota(jnp.int32, (8, LANES), 1) + base

        peak = jnp.full((8, LANES), -1e30, f32)
        for tile in range(tiles):
            lanes = slice(tile * LANES, (tile + 1) * LANES)

            def scores(n, peak):
                start = pl.multiple_of(n * 8, 8)
                rows = pl.ds(start, 8)
                low = pl.ds(padded + start, 8)
                valid = (rows_of(start) < classes) & (lanes_of(tile * LANES) < used)
                even_values = [corr_ref[0, rows, lanes]]
                odd_values = [None]
                for m in range(1, ROTS // 2):
                    even_values.append(corr_ref[m, rows, lanes] + corr_ref[ROTS - m, rows, lanes])
                    odd_values.append(corr_ref[m, low, lanes] - corr_ref[ROTS - m, low, lanes])
                even_values.append(corr_ref[ROTS // 2, rows, lanes])
                odd_values.append(None)
                cos_sums, sin_sums = half_dft(even_values, odd_values)
                bias = wide_ref[0, rows, :]
                for k in range(FOLD):
                    if k in (0, FOLD - 1):
                        results = [(k, cos_sums[k])]
                    else:
                        results = [(k, cos_sums[k] - sin_sums[k]), (ROTS - k, cos_sums[k] + sin_sums[k])]
                    for place, value in results:
                        value = jnp.where(valid, value * (1.0 / angles) - bias, -1e30)
                        weight_ref[place, rows, lanes] = value
                        peak = jnp.maximum(peak, value)
                return peak

            peak = lax.fori_loop(0, padded // 8, scores, peak)

        peak = jnp.broadcast_to(jnp.max(peak, axis=0, keepdims=True), (8, LANES))
        step = count
        while step < LANES:
            peak = jnp.maximum(peak, pltpu.roll(peak, step, 1))
            step *= 2
        stat_ref[0:8, :] = peak

        def masses(n, whole):
            rows = pl.ds(pl.multiple_of(n * 8, 8), 8)
            mass = jnp.zeros((8, LANES), f32)
            for tile in range(tiles):
                lanes = slice(tile * LANES, (tile + 1) * LANES)
                for k in range(ROTS):
                    value = jnp.exp(weight_ref[k, rows, lanes] - peak)
                    weight_ref[k, rows, lanes] = value
                    mass = mass + value
            step = count
            while step < LANES:
                mass = mass + pltpu.roll(mass, step, 1)
                step *= 2
            stat_ref[pl.ds(pl.multiple_of(8 + n * 8, 8), 8), :] = mass
            return whole + mass

        whole = lax.fori_loop(0, padded // 8, masses, jnp.zeros((8, LANES), f32))
        share = jnp.concatenate([peak[:1], jnp.sum(whole, axis=0, keepdims=True)], 0)
        for j in range(share_ref.shape[0]):
            share_ref[j] = jnp.where(part_ref[0] == j, share, 0.0)


def correlate(slot_of, weighted, pieces, classes, part, before=None, power=None, ctf_rows=None, parts=1):
    _, _, queries, double = weighted.shape
    cycles = double // 2
    slots = len(pieces)
    padded = -(-classes // 8) * 8
    wide_lanes = -(-queries // LANES) * LANES
    block = 2 * GROUP * classes
    finish = ctf_rows is not None
    full = lambda shape: pl.BlockSpec(shape, lambda g, *u: (0,) * len(shape))
    in_specs = [
        pl.BlockSpec((1, GROUP, queries, double), functools.partial(lambda j, g, *u: (u[j][0], g, 0, 0), j))
        for j in range(slots)
    ] + [pl.BlockSpec((block, cycles), lambda g, *u: (g, 0))] * slots
    corr_block = pl.BlockSpec((GROUP, 2 * padded, wide_lanes), lambda g, *u: (g, 0, 0))
    corr_shape = (ROTS, 2 * padded, wide_lanes)
    wide = pltpu.VMEM((slots, block + ROWS, cycles), f32)
    scalars = [jnp.reshape(n, (1,)).astype(jnp.int32) for n in (*slot_of, part)]
    operands = scalars + [weighted] * slots + list(pieces)
    if finish:
        in_specs += [corr_block, full((padded, cycles)), full(ctf_rows.shape)]
        operands += [before, power, ctf_rows]
        out_shapes = [(ROTS, padded, wide_lanes), (8 + padded, LANES), (parts, 2, LANES)]
        out_specs = [full(shape) for shape in out_shapes]
        scratch = [pltpu.VMEM(corr_shape, f32), wide, pltpu.VMEM((padded, cycles), f32)]
    else:
        out_shapes = [corr_shape, (padded, cycles)]
        out_specs = [corr_block, full((padded, cycles))]
        scratch = [wide]
    return pl.pallas_call(
        functools.partial(correlate_kernel, slots=slots, classes=classes, padded=padded, finish=finish),
        grid_spec=pltpu.PrefetchScalarGridSpec(
            num_scalar_prefetch=len(scalars),
            grid=(ROTS // GROUP,),
            in_specs=in_specs,
            out_specs=out_specs,
            scratch_shapes=scratch,
        ),
        out_shape=[jax.ShapeDtypeStruct(shape, f32) for shape in out_shapes],
        compiler_params=pltpu.CompilerParams(vmem_limit_bytes=VMEM_LIMIT),
        name="scores" if finish else "correlate",
    )(*operands)


def back_kernel(weight_ref, stat_ref, share_ref, offset_ref, out_ref, evidence_ref, posterior_ref, sum_ref):
    padded = weight_ref.shape[1]
    queries = out_ref.shape[2]
    shares = [share_ref[j] for j in range(share_ref.shape[0])]
    top = shares[0][:1]
    for share in shares[1:]:
        top = jnp.maximum(top, share[:1])
    mass = sum(share[1:] * jnp.exp(share[:1] - top) for share in shares)
    evidence = jnp.broadcast_to(top + jnp.log(mass), (8, LANES))
    scale = jnp.exp(stat_ref[:8, :] - evidence)
    evidence_ref[...] = evidence
    posterior_ref[...] = stat_ref[8:, :] * scale[:1]
    for tile in range(weight_ref.shape[2] // LANES):
        lanes = slice(tile * LANES, (tile + 1) * LANES)

        def transform(n, carry):
            start = pl.multiple_of(n * 8, 8)
            rows = pl.ds(start, 8)
            low = pl.ds(padded + start, 8)
            values = [weight_ref[k, rows, lanes] * scale for k in range(ROTS)]
            even_values = [values[0]] + [values[k] + values[ROTS - k] for k in range(1, ROTS // 2)]
            odd_values = [None] + [values[k] - values[ROTS - k] for k in range(1, ROTS // 2)] + [None]
            cos_sums, sin_sums = half_dft(even_values + [values[ROTS // 2]], odd_values)
            for m in range(FOLD):
                sine_part = jnp.zeros_like(scale) if m in (0, FOLD - 1) else sin_sums[m]
                sum_ref[m, rows, lanes] = cos_sums[m]
                sum_ref[m, low, lanes] = sine_part
                if m not in (0, FOLD - 1):
                    sum_ref[ROTS - m, rows, lanes] = cos_sums[m]
                    sum_ref[ROTS - m, low, lanes] = -sine_part
            return carry

        lax.fori_loop(0, padded // 8, transform, 0)

    step_cos, step_sin = cos_sin_of_turns(offset_ref[...] * (1.0 / (ROTS * ANG_STEP)))

    def turn(m, carry):
        cosine, sine_part = carry
        for tile in range(weight_ref.shape[2] // LANES):
            lanes = slice(tile * LANES, (tile + 1) * LANES)
            kept = slice(tile * LANES, min((tile + 1) * LANES, queries))
            re, im = sum_ref[m, :padded, lanes], sum_ref[m, padded:, lanes]
            turned = jnp.concatenate([re * cosine - im * sine_part, re * sine_part + im * cosine], 0)
            out_ref[m, :, kept] = turned[:, : kept.stop - kept.start].astype(bf16)
        return cosine * step_cos - sine_part * step_sin, sine_part * step_cos + cosine * step_sin

    lax.fori_loop(0, ROTS, turn, (jnp.ones_like(step_cos), jnp.zeros_like(step_cos)))


def make_back(weights, stat, shares, offsets, queries):
    _, padded, wide_lanes = weights.shape
    return pl.pallas_call(
        back_kernel,
        out_shape=[
            jax.ShapeDtypeStruct((ROTS, 2 * padded, queries), bf16),
            jax.ShapeDtypeStruct((8, LANES), f32),
            jax.ShapeDtypeStruct((padded, LANES), f32),
        ],
        scratch_shapes=[pltpu.VMEM((ROTS, 2 * padded, wide_lanes), f32)],
        compiler_params=pltpu.CompilerParams(vmem_limit_bytes=VMEM_LIMIT),
        name="back",
    )(weights, stat, shares, offsets)


def sums_kernel(*refs, count, classes):
    slot_refs, (back_ref, *refs) = refs[:count], refs[count:]
    weighted_refs, (offset_ref, *refs) = refs[:count], refs[count:]
    out_refs, wide_refs = refs[:count], refs[count:]
    padded = offset_ref.shape[0]
    cycles = wide_refs[0].shape[1]
    turns = [
        cos_sin_of_turns(offset_ref[...] * (slot_ref[0].astype(f32) * (1.0 / ANG_STEP)))
        for slot_ref in slot_refs
    ]
    for i in range(GROUP):
        for (cosine, sine_part), weighted_ref, wide_ref in zip(turns, weighted_refs, wide_refs):
            product = jnp.dot(back_ref[i], weighted_ref[0, i], preferred_element_type=f32)
            re = product[:padded, :cycles] - product[padded:, cycles:]
            im = product[:padded, cycles:] + product[padded:, :cycles]
            start = 2 * i * classes
            wide_ref[pl.ds(start, classes, stride=2), :] = (re * cosine - im * sine_part)[:classes]
            wide_ref[pl.ds(start + 1, classes, stride=2), :] = (re * sine_part + im * cosine)[:classes]
    for out_ref, wide_ref in zip(out_refs, wide_refs):
        out_ref[...] = wide_ref[...].astype(out_ref.dtype)


def class_sums_of(slots, back, weighted, offsets, classes, dtypes, groups=(0, ROTS // GROUP)):
    begin, end = groups
    _, _, queries, double = weighted.shape
    cycles = double // 2
    rows = back.shape[1]
    block = 2 * GROUP * classes
    count = len(slots)
    scalars = [jnp.reshape(slot, (1,)).astype(jnp.int32) for slot in slots]
    return pl.pallas_call(
        functools.partial(sums_kernel, count=count, classes=classes),
        grid_spec=pltpu.PrefetchScalarGridSpec(
            num_scalar_prefetch=count,
            grid=(end - begin,),
            in_specs=[pl.BlockSpec((GROUP, rows, queries), lambda g, *u: (g + begin, 0, 0))]
            + [
                pl.BlockSpec(
                    (1, GROUP, queries, double),
                    functools.partial(lambda j, g, *u: (u[j][0], g + begin, 0, 0), j),
                )
                for j in range(count)
            ]
            + [pl.BlockSpec(offsets.shape, lambda g, *u: (0, 0))],
            out_specs=[pl.BlockSpec((block, cycles), lambda g, *u: (g, 0))] * count,
            scratch_shapes=[pltpu.VMEM((block, cycles), f32)] * count,
        ),
        out_shape=[jax.ShapeDtypeStruct(((end - begin) * block, cycles), dtype) for dtype in dtypes],
        compiler_params=pltpu.CompilerParams(vmem_limit_bytes=VMEM_LIMIT),
        name="class_sums",
    )(*scalars, back, *[weighted] * count, offsets)


def across(piece):
    return lax.ppermute(piece, "dp", [(d, d ^ 1) for d in range(8)])


def along(piece, pairs):
    return lax.ppermute(piece, "dp", [(2 * a + x, 2 * b + x) for a, b in pairs for x in range(2)])


def gather_on_line(piece, base, ctf_rows):
    index = lax.axis_index("dp")
    line, side = index // 2, index % 2
    _, steps = spectra_steps(base.shape[0])
    cuts = [0, 3 * steps // 13, 8 * steps // 13, steps]

    own_crossed = across(piece)
    near = along(piece, ((0, 1), (1, 0), (2, 3), (3, 2)))
    middle = along(piece, ((1, 2), (2, 1)))
    weighted = make_spectra(base, ctf_rows, cuts[0], cuts[1])
    weighted, near, middle, own_crossed = lax.optimization_barrier((weighted, near, middle, own_crossed))
    near_crossed = across(near)
    far_middle = along(near, ((1, 2), (2, 1)))
    end = along(middle, ((1, 0), (2, 3)))
    weighted = make_spectra(base, ctf_rows, cuts[1], cuts[2], weighted)
    weighted, far_middle, end, near_crossed = lax.optimization_barrier(
        (weighted, far_middle, end, near_crossed)
    )
    third = middle + end
    third_crossed = across(third)
    far_end = along(far_middle, ((1, 0), (2, 3)))
    weighted = make_spectra(base, ctf_rows, cuts[2], cuts[3], weighted)
    weighted, far_end, third_crossed = lax.optimization_barrier((weighted, far_end, third_crossed))
    fourth = far_middle + far_end
    fourth_crossed = across(fourth)

    pieces = [piece, own_crossed, near, near_crossed, third, third_crossed, fourth, fourth_crossed]
    places = [line, line ^ 1, jnp.where(line < 2, 2, 1), jnp.where(line < 2, 3, 0)]
    slot_of = [2 * place + s for place in places for s in (side, 1 - side)]
    return weighted, pieces, slot_of


def add_kernel(own_ref, *refs):
    *whole_refs, head_ref, rest_ref, out_ref = refs
    total = own_ref[...]
    for ref in whole_refs:
        total = total + ref[...].astype(f32)
    part = jnp.where(pl.program_id(0) == 0, head_ref[...], rest_ref[...])
    out_ref[...] = total + part.astype(f32)


def add_pieces(own, whole, pair, block):
    rows, cycles = own.shape
    spec = pl.BlockSpec((block, cycles), lambda g: (g, 0))
    head = pl.BlockSpec((block, cycles), lambda g: (0, 0))
    rest = pl.BlockSpec((block, cycles), lambda g: (jnp.maximum(g - 1, 0), 0))
    return pl.pallas_call(
        add_kernel,
        grid=(rows // block,),
        in_specs=[spec] * (1 + len(whole)) + [head, rest],
        out_specs=spec,
        out_shape=jax.ShapeDtypeStruct(own.shape, f32),
        name="add_pieces",
    )(own, *whole, *pair)


def reduce_on_line(back, weighted, offsets, classes):
    index = lax.axis_index("dp")
    line, side = index // 2, index % 2
    order = [jnp.where(line < 2, 3, 0), jnp.where(line < 2, 2, 1), line ^ 1, line]
    theirs = [2 * z + 1 - side for z in order]
    ours = [2 * z + side for z in order]
    groups = ((0, 1), (1, ROTS // GROUP))
    block = 2 * GROUP * classes
    head, rest = [slice(a * block, b * block) for a, b in groups]
    to_middle, between = ((0, 1), (3, 2)), ((1, 2), (2, 1))
    neighbours = ((0, 1), (1, 0), (2, 3), (3, 2))

    def sums(slots, dtypes, back, some=(0, ROTS // GROUP)):
        return class_sums_of(slots, back, weighted, offsets, classes, dtypes, some)

    def wide(piece):
        return piece.astype(f32)

    def then(back, *done):
        return lax.optimization_barrier((back, *done))[0]

    (away,) = sums(theirs[:1], [bf16], back, groups[0])
    crossed_head = across(away)
    back = then(back, away)
    (away,) = sums(theirs[:1], [bf16], back, groups[1])
    crossed_rest = across(away)
    back = then(back, away)
    own_0, away = sums([ours[0], theirs[1]], [f32, bf16], back)
    crossed_1 = across(away)
    crossed_head, own_0 = lax.optimization_barrier((crossed_head, own_0))
    message = (own_0[head] + wide(crossed_head)).astype(bf16)
    first_head = along(message, to_middle)
    back = then(back, message)
    own_1, away = sums([ours[1], theirs[2]], [f32, bf16], back)
    crossed_2 = across(away)
    crossed_rest, own_1 = lax.optimization_barrier((crossed_rest, own_1))
    message = (own_0[rest] + wide(crossed_rest)).astype(bf16)
    first_rest = along(message, to_middle)
    back = then(back, message)
    message = (own_0[head] + wide(crossed_head) + wide(first_head)).astype(bf16)
    middle_head = along(message, between)
    back = then(back, message)
    own_2, away = sums([ours[2], theirs[3]], [f32, bf16], back)
    crossed_3 = across(away)
    crossed_1, first_rest, middle_head, own_2 = lax.optimization_barrier(
        (crossed_1, first_rest, middle_head, own_2)
    )
    message = (own_0[rest] + wide(crossed_rest) + wide(first_rest)).astype(bf16)
    middle_rest = along(message, between)
    from_end = along((own_1 + wide(crossed_1)).astype(bf16), to_middle)
    back = then(back, message)
    (own_3,) = sums(ours[3:], [f32], back)
    message = (own_2[head] + wide(crossed_2[head]) + wide(middle_head)).astype(bf16)
    last_head = along(message, neighbours)
    message = (own_2[rest] + wide(crossed_2[rest]) + wide(middle_rest)).astype(bf16)
    last_rest = along(message, neighbours)
    third = along((own_1 + wide(crossed_1) + wide(from_end)).astype(bf16), between)
    return add_pieces(own_3, (crossed_3, third), (last_head, last_rest), block)


def local(particles, references, ctf_table, rot_offset, prior_shift, defocus_group):
    count, _, angles, cycles = particles.shape
    own_rows, _, classes, _ = references.shape
    slots = angles // ROTS
    group_count = ctf_table.shape[0]
    devices = lax.axis_size("dp")

    first = (lax.axis_index("dp") * own_rows).astype(jnp.int32).reshape(1)
    rows = jnp.transpose(references, (0, 2, 1, 3)).reshape(own_rows * 2 * classes, cycles)
    piece, offsets = turn_references(first, rot_offset, rows)

    onehot = (defocus_group[:, None] == jnp.arange(group_count, dtype=jnp.int32)[None, :]).astype(f32)
    ctf_rows = jnp.dot(onehot, ctf_table, precision=lax.Precision.HIGHEST)
    base = make_base(particles, prior_shift)
    on_line = devices == 8 and own_rows == ROTS
    if on_line:
        weighted, pieces, slot_of = gather_on_line(piece, base, ctf_rows)
    else:
        gathered = lax.all_gather(piece, "dp", axis=0, tiled=True)
        gathered = gathered.reshape(slots, ROTS * 2 * classes, cycles)
        pieces = [gathered[j] for j in range(slots)]
        slot_of = list(range(slots))
        weighted = make_spectra(base, ctf_rows, 0, spectra_steps(count)[1])
    queries = weighted.shape[1]
    weighted = weighted.reshape(slots, ROTS, queries, 2 * cycles)

    early = slots - 1
    part = lax.axis_index("cls")
    corr, power = correlate(slot_of[:early], weighted, pieces[:early], classes, part)
    weights, stat, share = correlate(
        slot_of[early:], weighted, pieces[early:], classes, part, corr, power, ctf_rows, lax.axis_size("cls")
    )
    shares = lax.psum(share, "cls")
    back, evidence, posterior = make_back(weights, stat, shares, offsets, queries)
    log_evidence = evidence[0, :count]
    class_posterior = posterior[:classes, :count].T
    if on_line:
        class_rows = reduce_on_line(back, weighted, offsets, classes)
    else:
        sums = [class_sums_of([u], back, weighted, offsets, classes, [bf16])[0] for u in slot_of]
        summed = lax.psum_scatter(jnp.concatenate(sums, 0), "dp", scatter_dimension=0, tiled=True)
        class_rows = summed.astype(f32)
    class_sums = jnp.transpose(class_rows.reshape(own_rows, classes, 2, cycles), (0, 2, 1, 3))
    return (log_evidence, class_posterior, class_sums)


def solution(mesh):
    placed = (
        P("dp", None, None, None),
        P("dp", None, "cls", None),
        P(),
        P("cls"),
        P("dp", None),
        P("dp"),
    )
    return jax.shard_map(
        local,
        mesh=mesh,
        in_specs=placed,
        out_specs=(P("dp"), P("dp", "cls"), P("dp", None, "cls", None)),
        check_vma=False,
    )
```

```python
import functools
import math

import jax
import jax.numpy as jnp
import ml_dtypes
import numpy as np
from jax import lax
from jax.experimental import pallas as pl
from jax.experimental.pallas import tpu as pltpu
from jax.sharding import PartitionSpec as P

ROTS = 36
ANG_STEP = 8
SHIFT_SIDE = 5
SHIFTS = SHIFT_SIDE * SHIFT_SIDE
LANES = 128
GROUP = 12
ROWS = 16
APART = 17
FOLD = ROTS // 2 + 1

two_pi = 2.0 * math.pi
f32 = jnp.float32
bf16 = jnp.bfloat16
VMEM_LIMIT = 56 * 1024 * 1024


def fourier_rows(angles):
    index_grid = np.arange(angles)
    radians = (index_grid[:, None] * index_grid[None, :] % angles) * (two_pi / angles)
    cosine, sine_part = np.cos(radians), np.sin(radians)
    table_full = np.concatenate(
        [np.concatenate([cosine, sine_part], 1), np.concatenate([-sine_part, cosine], 1)], 0
    )
    return table_full.astype(np.float32).astype(ml_dtypes.bfloat16)


def shift_tables(angles, cycles):
    theta = np.arange(angles) * (two_pi / angles)
    radius = (np.arange(cycles) + 1) / (2.0 * cycles)
    turns = np.stack([np.cos(theta), np.sin(theta)])[:, :, None] * radius
    steps = np.arange(SHIFT_SIDE) - SHIFT_SIDE // 2
    phase = two_pi * turns[:, None] * steps[None, :, None, None]
    factors = np.stack([np.cos(phase), -np.sin(phase)], 2)
    return turns.astype(np.float32), factors.astype(np.float32)


def cos_sin_of_turns(turns):
    frac = turns - jnp.floor(turns + 0.5)
    w = frac * two_pi
    w2 = w * w
    cosine = jnp.full_like(w, 1.0 / math.factorial(16))
    for n in range(14, -1, -2):
        cosine = cosine * w2 + (-1.0) ** (n // 2) / math.factorial(n)
    sine_part = jnp.full_like(w, 1.0 / math.factorial(17))
    for n in range(15, 0, -2):
        sine_part = sine_part * w2 + (-1.0) ** (n // 2) / math.factorial(n)
    return cosine, sine_part * w


def base_kernel(shift_ref, part_ref, turns_ref, base_ref):
    here, _, angles, _ = part_ref.shape
    chunk = 32
    for q in range(here):
        p = pl.program_id(0) * here + q
        sx = shift_ref[0, p].astype(f32)
        sy = shift_ref[1, p].astype(f32)

        def turn(n, carry):
            rows = pl.ds(pl.multiple_of(n * chunk, chunk), chunk)
            cosine, sine_part = cos_sin_of_turns(sx * turns_ref[0, rows, :] + sy * turns_ref[1, rows, :])
            re = part_ref[q, 0, rows, :].astype(f32)
            im = part_ref[q, 1, rows, :].astype(f32)
            base_ref[q, 0, rows, :] = re * cosine + im * sine_part
            base_ref[q, 1, rows, :] = im * cosine - re * sine_part
            return carry

        lax.fori_loop(0, angles // chunk, turn, 0)


def make_base(particles, prior_shift):
    count, _, angles, cycles = particles.shape
    turns, _ = shift_tables(angles, cycles)
    here = count // 2
    image = pl.BlockSpec((here, 2, angles, cycles), lambda p: (p, 0, 0, 0))
    return pl.pallas_call(
        base_kernel,
        grid=(2,),
        in_specs=[
            pl.BlockSpec(memory_space=pltpu.SMEM),
            image,
            pl.BlockSpec(turns.shape, lambda p: (0, 0, 0)),
        ],
        out_specs=image,
        out_shape=jax.ShapeDtypeStruct(particles.shape, f32),
        compiler_params=pltpu.CompilerParams(vmem_limit_bytes=VMEM_LIMIT),
        name="centre",
    )(prior_shift.T, particles, turns)


def spectra_kernel(base_ref, ctf_ref, table_ref, *refs, per_step):
    factor_refs, refs = refs[: 2 * per_step], refs[2 * per_step :]
    chunks = ROWS // 2
    out_ref, turn_ref, re_ref, im_ref = refs[-4 - chunks : -chunks]
    data_refs = refs[-chunks:]
    count, _, angles, cycles = base_ref.shape
    chunk = 32

    for g in range(per_step):
        x_ref, y_ref = factor_refs[2 * g], factor_refs[2 * g + 1]
        for start in range(0, angles, chunk):
            rows = slice(start, start + chunk)
            xr, xi = x_ref[0, 0, 0, rows, :], x_ref[0, 0, 1, rows, :]
            yr, yi = y_ref[0, 0, 0, rows, :], y_ref[0, 0, 1, rows, :]
            turn_ref[g, 0, rows, :] = xr * yr - xi * yi
            turn_ref[g, 1, rows, :] = xr * yi + xi * yr

    def shift(n):
        for j in range(2):
            g, p = (2 * n + j) // count, (2 * n + j) % count
            lanes = slice(j * cycles, (j + 1) * cycles)
            for start in range(0, angles, chunk):
                rows = slice(start, start + chunk)
                tr, ti = turn_ref[g, 0, rows, :], turn_ref[g, 1, rows, :]
                gr, gi = base_ref[p, 0, rows, :], base_ref[p, 1, rows, :]
                data_refs[n][rows, lanes] = (gr * tr - gi * ti).astype(bf16)
                data_refs[n][angles + start : angles + start + chunk, lanes] = (gr * ti + gi * tr).astype(bf16)

    shift(0)
    for n in range(chunks):
        if n + 1 < chunks:
            shift(n + 1)
        spectrum = jnp.dot(table_ref[...], data_refs[n][...], preferred_element_type=f32)
        for j in range(2):
            row = 2 * n + j
            ctf_row = ctf_ref[row % count, :][None, :]
            part = spectrum[:, j * cycles : (j + 1) * cycles] * ctf_row
            re_ref[pl.ds(row, angles, stride=APART), :] = part[:angles]
            im_ref[pl.ds(row, angles, stride=APART), :] = part[angles:]
    for m in range(angles):
        out_ref[m, :, :cycles] = re_ref[m * APART : m * APART + ROWS, :].astype(bf16)
        out_ref[m, :, cycles:] = im_ref[m * APART : m * APART + ROWS, :].astype(bf16)


def spectra_steps(count):
    per_step = ROWS // count if count < ROWS else 1
    return per_step, -(-SHIFTS // per_step)


def make_spectra(base, ctf_rows, first, last, before=None, after=()):
    count, _, angles, cycles = base.shape
    per_step, steps = spectra_steps(count)
    _, factors = shift_tables(angles, cycles)
    full = lambda shape: pl.BlockSpec(shape, lambda i: (0,) * len(shape))

    def factor_spec(g, axis):
        def place(i):
            s = jnp.minimum((i + first) * per_step + g, SHIFTS - 1)
            a = lax.div(s, jnp.int32(SHIFT_SIDE))
            return (axis, s - a * SHIFT_SIDE if axis else a, 0, 0, 0)

        return pl.BlockSpec((1, 1, 2, angles, cycles), place)

    untouched = ([] if before is None else [before]) + list(after)
    in_specs = (
        [full(base.shape), full(ctf_rows.shape), full((2 * angles, 2 * angles))]
        + [factor_spec(g, axis) for g in range(per_step) for axis in range(2)]
        + [pl.BlockSpec(memory_space=pl.ANY)] * len(untouched)
    )
    return pl.pallas_call(
        functools.partial(spectra_kernel, per_step=per_step),
        grid=(last - first,),
        in_specs=in_specs,
        out_specs=pl.BlockSpec((angles, ROWS, 2 * cycles), lambda i: (0, i + first, 0)),
        out_shape=jax.ShapeDtypeStruct((angles, steps * ROWS, 2 * cycles), bf16),
        scratch_shapes=[
            pltpu.VMEM((per_step, 2, angles, cycles), f32),
            pltpu.VMEM((angles * APART, cycles), f32),
            pltpu.VMEM((angles * APART, cycles), f32),
        ]
        + [pltpu.VMEM((2 * angles, 2 * cycles), bf16)] * (ROWS // 2),
        input_output_aliases={} if before is None else {3 + 2 * per_step: 0},
        compiler_params=pltpu.CompilerParams(vmem_limit_bytes=VMEM_LIMIT),
        name="spectra",
    )(base, ctf_rows, fourier_rows(angles), *[factors] * (2 * per_step), *untouched)


def half_dft(even_values, odd_values):
    half = FOLD // 2
    cos_sums, sin_sums = [None] * FOLD, [None] * FOLD

    def weighted_sum(values, k, table, start):
        total = None
        for m in range(start, FOLD, 2):
            weight = float(table((k * m % ROTS) * two_pi / ROTS))
            if values[m] is None or abs(weight) < 1e-9:
                continue
            if abs(abs(weight) - 1.0) < 1e-9:
                term = values[m] if weight > 0 else -values[m]
            else:
                term = values[m] * weight
            total = term if total is None else total + term
        return jnp.zeros_like(values[1]) if total is None else total

    for k in range(half + 1):
        even = weighted_sum(even_values, k, math.cos, 0)
        odd = weighted_sum(even_values, k, math.cos, 1)
        cos_sums[k] = even + odd
        if k != half:
            cos_sums[FOLD - 1 - k] = even - odd
        if k:
            even = weighted_sum(odd_values, k, math.sin, 0)
            odd = weighted_sum(odd_values, k, math.sin, 1)
            sin_sums[k] = even + odd
            if k != half:
                sin_sums[FOLD - 1 - k] = odd - even
    return cos_sums, sin_sums


def turn_kernel(first_ref, offset_ref, references_ref, out_ref, column_ref, in_ref, wide_ref):
    rows, cycles = references_ref.shape
    classes = offset_ref.shape[0]
    own_rows = rows // (2 * classes)
    in_ref[...] = references_ref[...].astype(f32)
    row = lax.broadcasted_iota(jnp.int32, (8, LANES), 0)
    lane = lax.broadcasted_iota(jnp.int32, (8, LANES), 1)
    freq = (lane + first_ref[0]).astype(f32) * (1.0 / (ROTS * ANG_STEP))
    tables = []
    for start in range(0, classes, 8):
        column = jnp.zeros((8, LANES), jnp.int32)
        for c in range(start, min(start + 8, classes)):
            column = jnp.where(row == c - start, offset_ref[c], column)
        column = column.astype(f32)
        column_ref[start : start + 8, :] = column
        tables.append(cos_sin_of_turns(column * freq))
    cosine = jnp.concatenate([c for c, _ in tables], 0)
    sine_part = jnp.concatenate([s for _, s in tables], 0)
    for m in range(own_rows):
        re_rows = pl.ds(2 * m * classes, classes, stride=2)
        im_rows = pl.ds(2 * m * classes + 1, classes, stride=2)
        c, s = cosine[:classes, m : m + 1], sine_part[:classes, m : m + 1]
        re, im = in_ref[re_rows, :], in_ref[im_rows, :]
        wide_ref[re_rows, :] = re * c + im * s
        wide_ref[im_rows, :] = im * c - re * s
    out_ref[...] = wide_ref[...].astype(bf16)


def turn_references(first, offsets, references):
    padded = -(-offsets.shape[0] // 8) * 8
    return pl.pallas_call(
        turn_kernel,
        in_specs=[
            pl.BlockSpec(memory_space=pltpu.SMEM),
            pl.BlockSpec(memory_space=pltpu.SMEM),
            pl.BlockSpec(memory_space=pltpu.VMEM),
        ],
        out_shape=[
            jax.ShapeDtypeStruct(references.shape, bf16),
            jax.ShapeDtypeStruct((padded, LANES), f32),
        ],
        scratch_shapes=[pltpu.VMEM(references.shape, f32)] * 2,
        compiler_params=pltpu.CompilerParams(vmem_limit_bytes=VMEM_LIMIT),
        name="turn_references",
    )(first, offsets, references)


def correlate_kernel(*refs, slots, classes, padded, finish):
    part_ref, refs = refs[slots], refs[slots + 1 :]
    weighted_refs, refs = refs[:slots], refs[slots:]
    piece_refs, refs = refs[:slots], refs[slots:]
    if finish:
        before_ref, power_before_ref, ctf_ref, weight_ref, stat_ref, share_ref = refs[:6]
        corr_ref, wide_ref, power_ref = refs[6:]
    else:
        corr_ref, power_ref, wide_ref = refs
    group = pl.program_id(0)
    cycles = piece_refs[0].shape[1]
    queries = weighted_refs[0].shape[2]
    block = piece_refs[0].shape[0]

    @pl.when(group == 0)
    def _():
        wide_ref[:, block:, :] = jnp.zeros((slots, wide_ref.shape[1] - block, cycles), f32)
        power_ref[...] = power_before_ref[...] if finish else jnp.zeros_like(power_ref)

    for j in range(slots):
        wide_ref[j, :block, :] = piece_refs[j][...].astype(f32)
    power = power_ref[...]
    for i in range(GROUP):
        total = before_ref[i, :, :queries] if finish else None
        for j in range(slots):
            re = wide_ref[j, pl.ds(2 * i * classes, padded, stride=2), :]
            im = wide_ref[j, pl.ds(2 * i * classes + 1, padded, stride=2), :]
            power = power + (re * re + im * im)
            left = jnp.concatenate(
                [jnp.concatenate([re, im], 1), jnp.concatenate([-im, re], 1)], 0
            ).astype(bf16)
            part = lax.dot_general(
                left, weighted_refs[j][0, i], (((1,), (1,)), ((), ())), preferred_element_type=f32
            )
            total = part if total is None else total + part
        row = group * GROUP + i if finish else i
        corr_ref[row, :, :queries] = total
    power_ref[...] = power

    if not finish:
        return

    @pl.when(group == pl.num_programs(0) - 1)
    def _():
        count = ctf_ref.shape[0]
        angles = ROTS * ANG_STEP
        used = SHIFTS * count
        tiles = weight_ref.shape[2] // LANES
        ctf_row = ctf_ref[...]
        ctf_rows = jnp.concatenate([ctf_row * ctf_row] * (LANES // count), 0)
        bias = lax.dot_general(
            power_ref[...],
            ctf_rows,
            (((1,), (1,)), ((), ())),
            precision=lax.Precision.HIGHEST,
            preferred_element_type=f32,
        ) * (0.5 / angles)
        wide_ref[0, :padded, :] = bias
        rows_of = lambda base: lax.broadcasted_iota(jnp.int32, (8, LANES), 0) + base
        lanes_of = lambda base: lax.broadcasted_iota(jnp.int32, (8, LANES), 1) + base

        peak = jnp.full((8, LANES), -1e30, f32)
        for tile in range(tiles):
            lanes = slice(tile * LANES, (tile + 1) * LANES)

            def scores(n, peak):
                start = pl.multiple_of(n * 8, 8)
                rows = pl.ds(start, 8)
                low = pl.ds(padded + start, 8)
                valid = (rows_of(start) < classes) & (lanes_of(tile * LANES) < used)
                even_values = [corr_ref[0, rows, lanes]]
                odd_values = [None]
                for m in range(1, ROTS // 2):
                    even_values.append(corr_ref[m, rows, lanes] + corr_ref[ROTS - m, rows, lanes])
                    odd_values.append(corr_ref[m, low, lanes] - corr_ref[ROTS - m, low, lanes])
                even_values.append(corr_ref[ROTS // 2, rows, lanes])
                odd_values.append(None)
                cos_sums, sin_sums = half_dft(even_values, odd_values)
                bias = wide_ref[0, rows, :]
                for k in range(FOLD):
                    if k in (0, FOLD - 1):
                        results = [(k, cos_sums[k])]
                    else:
                        results = [(k, cos_sums[k] - sin_sums[k]), (ROTS - k, cos_sums[k] + sin_sums[k])]
                    for place, value in results:
                        value = jnp.where(valid, value * (1.0 / angles) - bias, -1e30)
                        weight_ref[place, rows, lanes] = value
                        peak = jnp.maximum(peak, value)
                return peak

            peak = lax.fori_loop(0, padded // 8, scores, peak)

        peak = jnp.broadcast_to(jnp.max(peak, axis=0, keepdims=True), (8, LANES))
        step = count
        while step < LANES:
            peak = jnp.maximum(peak, pltpu.roll(peak, step, 1))
            step *= 2
        stat_ref[0:8, :] = peak

        def masses(n, whole):
            rows = pl.ds(pl.multiple_of(n * 8, 8), 8)
            mass = jnp.zeros((8, LANES), f32)
            for tile in range(tiles):
                lanes = slice(tile * LANES, (tile + 1) * LANES)
                for k in range(ROTS):
                    value = jnp.exp(weight_ref[k, rows, lanes] - peak)
                    weight_ref[k, rows, lanes] = value
                    mass = mass + value
            step = count
            while step < LANES:
                mass = mass + pltpu.roll(mass, step, 1)
                step *= 2
            stat_ref[pl.ds(pl.multiple_of(8 + n * 8, 8), 8), :] = mass
            return whole + mass

        whole = lax.fori_loop(0, padded // 8, masses, jnp.zeros((8, LANES), f32))
        share = jnp.concatenate([peak[:1], jnp.sum(whole, axis=0, keepdims=True)], 0)
        for j in range(share_ref.shape[0]):
            share_ref[j] = jnp.where(part_ref[0] == j, share, 0.0)


def correlate(slot_of, weighted, pieces, classes, part, before=None, power=None, ctf_rows=None, parts=1):
    _, _, queries, double = weighted.shape
    cycles = double // 2
    slots = len(pieces)
    padded = -(-classes // 8) * 8
    wide_lanes = -(-queries // LANES) * LANES
    block = 2 * GROUP * classes
    finish = ctf_rows is not None
    full = lambda shape: pl.BlockSpec(shape, lambda g, *u: (0,) * len(shape))
    in_specs = [
        pl.BlockSpec((1, GROUP, queries, double), functools.partial(lambda j, g, *u: (u[j][0], g, 0, 0), j))
        for j in range(slots)
    ] + [pl.BlockSpec((block, cycles), lambda g, *u: (g, 0))] * slots
    corr_block = pl.BlockSpec((GROUP, 2 * padded, wide_lanes), lambda g, *u: (g, 0, 0))
    corr_shape = (ROTS, 2 * padded, wide_lanes)
    wide = pltpu.VMEM((slots, block + ROWS, cycles), f32)
    scalars = [jnp.reshape(n, (1,)).astype(jnp.int32) for n in (*slot_of, part)]
    operands = scalars + [weighted] * slots + list(pieces)
    if finish:
        in_specs += [corr_block, full((padded, cycles)), full(ctf_rows.shape)]
        operands += [before, power, ctf_rows]
        out_shapes = [(ROTS, padded, wide_lanes), (8 + padded, LANES), (parts, 2, LANES)]
        out_specs = [full(shape) for shape in out_shapes]
        scratch = [pltpu.VMEM(corr_shape, f32), wide, pltpu.VMEM((padded, cycles), f32)]
    else:
        out_shapes = [corr_shape, (padded, cycles)]
        out_specs = [corr_block, full((padded, cycles))]
        scratch = [wide]
    return pl.pallas_call(
        functools.partial(correlate_kernel, slots=slots, classes=classes, padded=padded, finish=finish),
        grid_spec=pltpu.PrefetchScalarGridSpec(
            num_scalar_prefetch=len(scalars),
            grid=(ROTS // GROUP,),
            in_specs=in_specs,
            out_specs=out_specs,
            scratch_shapes=scratch,
        ),
        out_shape=[jax.ShapeDtypeStruct(shape, f32) for shape in out_shapes],
        compiler_params=pltpu.CompilerParams(vmem_limit_bytes=VMEM_LIMIT),
        name="scores" if finish else "correlate",
    )(*operands)


def back_kernel(weight_ref, stat_ref, share_ref, offset_ref, out_ref, evidence_ref, posterior_ref, sum_ref):
    padded = weight_ref.shape[1]
    queries = out_ref.shape[2]
    shares = [share_ref[j] for j in range(share_ref.shape[0])]
    top = shares[0][:1]
    for share in shares[1:]:
        top = jnp.maximum(top, share[:1])
    mass = sum(share[1:] * jnp.exp(share[:1] - top) for share in shares)
    evidence = jnp.broadcast_to(top + jnp.log(mass), (8, LANES))
    scale = jnp.exp(stat_ref[:8, :] - evidence)
    evidence_ref[...] = evidence
    posterior_ref[...] = stat_ref[8:, :] * scale[:1]
    for tile in range(weight_ref.shape[2] // LANES):
        lanes = slice(tile * LANES, (tile + 1) * LANES)

        def transform(n, carry):
            start = pl.multiple_of(n * 8, 8)
            rows = pl.ds(start, 8)
            low = pl.ds(padded + start, 8)
            values = [weight_ref[k, rows, lanes] * scale for k in range(ROTS)]
            even_values = [values[0]] + [values[k] + values[ROTS - k] for k in range(1, ROTS // 2)]
            odd_values = [None] + [values[k] - values[ROTS - k] for k in range(1, ROTS // 2)] + [None]
            cos_sums, sin_sums = half_dft(even_values + [values[ROTS // 2]], odd_values)
            for m in range(FOLD):
                sine_part = jnp.zeros_like(scale) if m in (0, FOLD - 1) else sin_sums[m]
                sum_ref[m, rows, lanes] = cos_sums[m]
                sum_ref[m, low, lanes] = sine_part
                if m not in (0, FOLD - 1):
                    sum_ref[ROTS - m, rows, lanes] = cos_sums[m]
                    sum_ref[ROTS - m, low, lanes] = -sine_part
            return carry

        lax.fori_loop(0, padded // 8, transform, 0)

    step_cos, step_sin = cos_sin_of_turns(offset_ref[...] * (1.0 / (ROTS * ANG_STEP)))

    def turn(m, carry):
        cosine, sine_part = carry
        for tile in range(weight_ref.shape[2] // LANES):
            lanes = slice(tile * LANES, (tile + 1) * LANES)
            kept = slice(tile * LANES, min((tile + 1) * LANES, queries))
            re, im = sum_ref[m, :padded, lanes], sum_ref[m, padded:, lanes]
            turned = jnp.concatenate([re * cosine - im * sine_part, re * sine_part + im * cosine], 0)
            out_ref[m, :, kept] = turned[:, : kept.stop - kept.start].astype(bf16)
        return cosine * step_cos - sine_part * step_sin, sine_part * step_cos + cosine * step_sin

    lax.fori_loop(0, ROTS, turn, (jnp.ones_like(step_cos), jnp.zeros_like(step_cos)))


def make_back(weights, stat, shares, offsets, queries):
    _, padded, wide_lanes = weights.shape
    return pl.pallas_call(
        back_kernel,
        out_shape=[
            jax.ShapeDtypeStruct((ROTS, 2 * padded, queries), bf16),
            jax.ShapeDtypeStruct((8, LANES), f32),
            jax.ShapeDtypeStruct((padded, LANES), f32),
        ],
        scratch_shapes=[pltpu.VMEM((ROTS, 2 * padded, wide_lanes), f32)],
        compiler_params=pltpu.CompilerParams(vmem_limit_bytes=VMEM_LIMIT),
        name="back",
    )(weights, stat, shares, offsets)


def sums_kernel(*refs, count, classes):
    slot_refs, (back_ref, *refs) = refs[:count], refs[count:]
    weighted_refs, (offset_ref, *refs) = refs[:count], refs[count:]
    out_refs, wide_refs = refs[:count], refs[count:]
    padded = offset_ref.shape[0]
    cycles = wide_refs[0].shape[1]
    turns = [
        cos_sin_of_turns(offset_ref[...] * (slot_ref[0].astype(f32) * (1.0 / ANG_STEP)))
        for slot_ref in slot_refs
    ]
    for i in range(GROUP):
        for (cosine, sine_part), weighted_ref, wide_ref in zip(turns, weighted_refs, wide_refs):
            product = jnp.dot(back_ref[i], weighted_ref[0, i], preferred_element_type=f32)
            re = product[:padded, :cycles] - product[padded:, cycles:]
            im = product[:padded, cycles:] + product[padded:, :cycles]
            start = 2 * i * classes
            wide_ref[pl.ds(start, classes, stride=2), :] = (re * cosine - im * sine_part)[:classes]
            wide_ref[pl.ds(start + 1, classes, stride=2), :] = (re * sine_part + im * cosine)[:classes]
    for out_ref, wide_ref in zip(out_refs, wide_refs):
        out_ref[...] = wide_ref[...].astype(out_ref.dtype)


def class_sums_of(slots, back, weighted, offsets, classes, dtypes, groups=(0, ROTS // GROUP)):
    begin, end = groups
    _, _, queries, double = weighted.shape
    cycles = double // 2
    rows = back.shape[1]
    block = 2 * GROUP * classes
    count = len(slots)
    scalars = [jnp.reshape(slot, (1,)).astype(jnp.int32) for slot in slots]
    return pl.pallas_call(
        functools.partial(sums_kernel, count=count, classes=classes),
        grid_spec=pltpu.PrefetchScalarGridSpec(
            num_scalar_prefetch=count,
            grid=(end - begin,),
            in_specs=[pl.BlockSpec((GROUP, rows, queries), lambda g, *u: (g + begin, 0, 0))]
            + [
                pl.BlockSpec(
                    (1, GROUP, queries, double),
                    functools.partial(lambda j, g, *u: (u[j][0], g + begin, 0, 0), j),
                )
                for j in range(count)
            ]
            + [pl.BlockSpec(offsets.shape, lambda g, *u: (0, 0))],
            out_specs=[pl.BlockSpec((block, cycles), lambda g, *u: (g, 0))] * count,
            scratch_shapes=[pltpu.VMEM((block, cycles), f32)] * count,
        ),
        out_shape=[jax.ShapeDtypeStruct(((end - begin) * block, cycles), dtype) for dtype in dtypes],
        compiler_params=pltpu.CompilerParams(vmem_limit_bytes=VMEM_LIMIT),
        name="class_sums",
    )(*scalars, back, *[weighted] * count, offsets)


def across(piece):
    return lax.ppermute(piece, "dp", [(d, d ^ 1) for d in range(8)])


def along(piece, pairs):
    return lax.ppermute(piece, "dp", [(2 * a + x, 2 * b + x) for a, b in pairs for x in range(2)])


def gather_on_line(piece, base, ctf_rows):
    index = lax.axis_index("dp")
    line, side = index // 2, index % 2
    _, steps = spectra_steps(base.shape[0])
    cuts = [0, 3 * steps // 13, 8 * steps // 13, steps]

    own_crossed = across(piece)
    near = along(piece, ((0, 1), (1, 0), (2, 3), (3, 2)))
    middle = along(piece, ((1, 2), (2, 1)))
    weighted = make_spectra(base, ctf_rows, cuts[0], cuts[1])
    weighted, near, middle, own_crossed = lax.optimization_barrier((weighted, near, middle, own_crossed))
    near_crossed = across(near)
    far_middle = along(near, ((1, 2), (2, 1)))
    end = along(middle, ((1, 0), (2, 3)))
    weighted = make_spectra(base, ctf_rows, cuts[1], cuts[2], weighted)
    weighted, far_middle, end, near_crossed = lax.optimization_barrier(
        (weighted, far_middle, end, near_crossed)
    )
    third = middle + end
    third_crossed = across(third)
    far_end = along(far_middle, ((1, 0), (2, 3)))
    weighted = make_spectra(base, ctf_rows, cuts[2], cuts[3], weighted)
    weighted, far_end, third_crossed = lax.optimization_barrier((weighted, far_end, third_crossed))
    fourth = far_middle + far_end
    fourth_crossed = across(fourth)

    pieces = [piece, own_crossed, near, near_crossed, third, third_crossed, fourth, fourth_crossed]
    places = [line, line ^ 1, jnp.where(line < 2, 2, 1), jnp.where(line < 2, 3, 0)]
    slot_of = [2 * place + s for place in places for s in (side, 1 - side)]
    return weighted, pieces, slot_of


def add_kernel(own_ref, whole_ref, *refs, heads):
    pairs, out_ref = refs[:-1], refs[-1]
    total = own_ref[...] + whole_ref[...].astype(f32)
    for n in range(0, len(pairs), 2):
        part = jnp.where(pl.program_id(0) < heads, pairs[n][...], pairs[n + 1][...])
        total = total + part.astype(f32)
    out_ref[...] = total


def add_pieces(own, whole, pairs, block):
    rows, cycles = own.shape
    heads = pairs[0][0].shape[0] // block
    spec = pl.BlockSpec((block, cycles), lambda g: (g, 0))
    head = pl.BlockSpec((block, cycles), lambda g: (jnp.minimum(g, heads - 1), 0))
    rest = pl.BlockSpec((block, cycles), lambda g: (jnp.maximum(g - heads, 0), 0))
    return pl.pallas_call(
        functools.partial(add_kernel, heads=heads),
        grid=(rows // block,),
        in_specs=[spec, spec] + [head, rest] * len(pairs),
        out_specs=spec,
        out_shape=jax.ShapeDtypeStruct(own.shape, f32),
        compiler_params=pltpu.CompilerParams(vmem_limit_bytes=VMEM_LIMIT),
        name="add_pieces",
    )(own, whole, *[part for pair in pairs for part in pair])


def reduce_on_line(back, weighted, offsets, classes):
    index = lax.axis_index("dp")
    line, side = index // 2, index % 2
    order = [jnp.where(line < 2, 3, 0), jnp.where(line < 2, 2, 1), line ^ 1, line]
    theirs = [2 * z + 1 - side for z in order]
    ours = [2 * z + side for z in order]
    groups = ((0, 2), (2, ROTS // GROUP))
    block = 2 * GROUP * classes
    head, rest = [slice(a * block, b * block) for a, b in groups]
    to_middle, between = ((0, 1), (3, 2)), ((1, 2), (2, 1))
    neighbours = ((0, 1), (1, 0), (2, 3), (3, 2))

    def sums(slots, dtypes, back, some=(0, ROTS // GROUP)):
        return class_sums_of(slots, back, weighted, offsets, classes, dtypes, some)

    def wide(piece):
        return piece.astype(f32)

    def then(back, *done):
        return lax.optimization_barrier((back, *done))[0]

    (away,) = sums(theirs[:1], [bf16], back, groups[0])
    crossed_head = across(away)
    back = then(back, away)
    (away,) = sums(theirs[:1], [bf16], back, groups[1])
    crossed_rest = across(away)
    back = then(back, away)
    own_0, away = sums([ours[0], theirs[1]], [f32, bf16], back)
    crossed_1 = across(away)
    crossed_head, own_0 = lax.optimization_barrier((crossed_head, own_0))
    message = (own_0[head] + wide(crossed_head)).astype(bf16)
    first_head = along(message, to_middle)
    back = then(back, message)
    own_1, away = sums([ours[1], theirs[2]], [f32, bf16], back)
    crossed_2 = across(away)
    crossed_rest, own_1 = lax.optimization_barrier((crossed_rest, own_1))
    message = (own_0[rest] + wide(crossed_rest)).astype(bf16)
    first_rest = along(message, to_middle)
    back = then(back, message)
    message = (own_0[head] + wide(crossed_head) + wide(first_head)).astype(bf16)
    middle_head = along(message, between)
    back = then(back, message)
    own_2, away = sums([ours[2], theirs[3]], [f32, bf16], back)
    crossed_3 = across(away)
    crossed_1, first_rest, middle_head, own_2 = lax.optimization_barrier(
        (crossed_1, first_rest, middle_head, own_2)
    )
    messages = [(own_1[r] + wide(crossed_1[r])).astype(bf16) for r in (head, rest)]
    from_end = [along(message, to_middle) for message in messages]
    first_rest = then(first_rest, *messages)
    message = (own_0[rest] + wide(crossed_rest) + wide(first_rest)).astype(bf16)
    middle_rest = along(message, between)
    back = then(back, message)
    (own_3,) = sums(ours[3:], [f32], back)
    message = (own_2[head] + wide(crossed_2[head]) + wide(middle_head)).astype(bf16)
    last_head = along(message, neighbours)
    message = (own_1[head] + wide(crossed_1[head]) + wide(from_end[0])).astype(bf16)
    third_head = along(message, between)
    middle_rest = then(middle_rest, third_head)
    message = (own_2[rest] + wide(crossed_2[rest]) + wide(middle_rest)).astype(bf16)
    last_rest = along(message, neighbours)
    message = (own_1[rest] + wide(crossed_1[rest]) + wide(from_end[1])).astype(bf16)
    third_rest = along(message, between)
    return add_pieces(own_3, crossed_3, ((third_head, third_rest), (last_head, last_rest)), block)


def local(particles, references, ctf_table, rot_offset, prior_shift, defocus_group):
    count, _, angles, cycles = particles.shape
    own_rows, _, classes, _ = references.shape
    slots = angles // ROTS
    group_count = ctf_table.shape[0]
    devices = lax.axis_size("dp")

    first = (lax.axis_index("dp") * own_rows).astype(jnp.int32).reshape(1)
    rows = jnp.transpose(references, (0, 2, 1, 3)).reshape(own_rows * 2 * classes, cycles)
    piece, offsets = turn_references(first, rot_offset, rows)

    onehot = (defocus_group[:, None] == jnp.arange(group_count, dtype=jnp.int32)[None, :]).astype(f32)
    ctf_rows = jnp.dot(onehot, ctf_table, precision=lax.Precision.HIGHEST)
    base = make_base(particles, prior_shift)
    on_line = devices == 8 and own_rows == ROTS
    if on_line:
        weighted, pieces, slot_of = gather_on_line(piece, base, ctf_rows)
    else:
        gathered = lax.all_gather(piece, "dp", axis=0, tiled=True)
        gathered = gathered.reshape(slots, ROTS * 2 * classes, cycles)
        pieces = [gathered[j] for j in range(slots)]
        slot_of = list(range(slots))
        weighted = make_spectra(base, ctf_rows, 0, spectra_steps(count)[1])
    queries = weighted.shape[1]
    weighted = weighted.reshape(slots, ROTS, queries, 2 * cycles)

    early = slots - 1
    part = lax.axis_index("cls")
    corr, power = correlate(slot_of[:early], weighted, pieces[:early], classes, part)
    weights, stat, share = correlate(
        slot_of[early:], weighted, pieces[early:], classes, part, corr, power, ctf_rows, lax.axis_size("cls")
    )
    shares = lax.psum(share, "cls")
    back, evidence, posterior = make_back(weights, stat, shares, offsets, queries)
    log_evidence = evidence[0, :count]
    class_posterior = posterior[:classes, :count].T
    if on_line:
        class_rows = reduce_on_line(back, weighted, offsets, classes)
    else:
        sums = [class_sums_of([u], back, weighted, offsets, classes, [bf16])[0] for u in slot_of]
        summed = lax.psum_scatter(jnp.concatenate(sums, 0), "dp", scatter_dimension=0, tiled=True)
        class_rows = summed.astype(f32)
    class_sums = jnp.transpose(class_rows.reshape(own_rows, classes, 2, cycles), (0, 2, 1, 3))
    return (log_evidence, class_posterior, class_sums)


def solution(mesh):
    placed = (
        P("dp", None, None, None),
        P("dp", None, "cls", None),
        P(),
        P("cls"),
        P("dp", None),
        P("dp"),
    )
    return jax.shard_map(
        local,
        mesh=mesh,
        in_specs=placed,
        out_specs=(P("dp"), P("dp", "cls"), P("dp", None, "cls", None)),
        check_vma=False,
    )
```

```python
import functools
import math

import jax
import jax.numpy as jnp
import ml_dtypes
import numpy as np
from jax import lax
from jax.experimental import pallas as pl
from jax.experimental.pallas import tpu as pltpu
from jax.sharding import PartitionSpec as P

ROTS = 36
ANG_STEP = 8
SHIFT_SIDE = 5
SHIFTS = SHIFT_SIDE * SHIFT_SIDE
LANES = 128
GROUP = 12
ROWS = 16
APART = 17
FOLD = ROTS // 2 + 1

two_pi = 2.0 * math.pi
f32 = jnp.float32
bf16 = jnp.bfloat16
VMEM_LIMIT = 56 * 1024 * 1024


def fourier_rows(angles):
    index_grid = np.arange(angles)
    radians = (index_grid[:, None] * index_grid[None, :] % angles) * (two_pi / angles)
    cosine, sine_part = np.cos(radians), np.sin(radians)
    table_full = np.concatenate(
        [np.concatenate([cosine, sine_part], 1), np.concatenate([-sine_part, cosine], 1)], 0
    )
    return table_full.astype(np.float32).astype(ml_dtypes.bfloat16)


def shift_tables(angles, cycles):
    theta = np.arange(angles) * (two_pi / angles)
    radius = (np.arange(cycles) + 1) / (2.0 * cycles)
    turns = np.stack([np.cos(theta), np.sin(theta)])[:, :, None] * radius
    steps = np.arange(SHIFT_SIDE) - SHIFT_SIDE // 2
    phase = two_pi * turns[:, None] * steps[None, :, None, None]
    factors = np.stack([np.cos(phase), -np.sin(phase)], 2)
    return turns.astype(np.float32), factors.astype(np.float32)


def cos_sin_of_turns(turns):
    frac = turns - jnp.floor(turns + 0.5)
    w = frac * two_pi
    w2 = w * w
    cosine = jnp.full_like(w, 1.0 / math.factorial(16))
    for n in range(14, -1, -2):
        cosine = cosine * w2 + (-1.0) ** (n // 2) / math.factorial(n)
    sine_part = jnp.full_like(w, 1.0 / math.factorial(17))
    for n in range(15, 0, -2):
        sine_part = sine_part * w2 + (-1.0) ** (n // 2) / math.factorial(n)
    return cosine, sine_part * w


def base_kernel(shift_ref, part_ref, turns_ref, base_ref):
    here, _, angles, _ = part_ref.shape
    chunk = 32
    for q in range(here):
        p = pl.program_id(0) * here + q
        sx = shift_ref[0, p].astype(f32)
        sy = shift_ref[1, p].astype(f32)

        def turn(n, carry):
            rows = pl.ds(pl.multiple_of(n * chunk, chunk), chunk)
            cosine, sine_part = cos_sin_of_turns(sx * turns_ref[0, rows, :] + sy * turns_ref[1, rows, :])
            re = part_ref[q, 0, rows, :].astype(f32)
            im = part_ref[q, 1, rows, :].astype(f32)
            base_ref[q, 0, rows, :] = re * cosine + im * sine_part
            base_ref[q, 1, rows, :] = im * cosine - re * sine_part
            return carry

        lax.fori_loop(0, angles // chunk, turn, 0)


def make_base(particles, prior_shift):
    count, _, angles, cycles = particles.shape
    turns, _ = shift_tables(angles, cycles)
    here = count // 2
    image = pl.BlockSpec((here, 2, angles, cycles), lambda p: (p, 0, 0, 0))
    return pl.pallas_call(
        base_kernel,
        grid=(2,),
        in_specs=[
            pl.BlockSpec(memory_space=pltpu.SMEM),
            image,
            pl.BlockSpec(turns.shape, lambda p: (0, 0, 0)),
        ],
        out_specs=image,
        out_shape=jax.ShapeDtypeStruct(particles.shape, f32),
        compiler_params=pltpu.CompilerParams(vmem_limit_bytes=VMEM_LIMIT),
        name="centre",
    )(prior_shift.T, particles, turns)


def spectra_kernel(base_ref, ctf_ref, table_ref, *refs, per_step):
    factor_refs, refs = refs[: 2 * per_step], refs[2 * per_step :]
    chunks = ROWS // 2
    out_ref, turn_ref, re_ref, im_ref = refs[-4 - chunks : -chunks]
    data_refs = refs[-chunks:]
    count, _, angles, cycles = base_ref.shape
    chunk = 32

    for g in range(per_step):
        x_ref, y_ref = factor_refs[2 * g], factor_refs[2 * g + 1]
        for start in range(0, angles, chunk):
            rows = slice(start, start + chunk)
            xr, xi = x_ref[0, 0, 0, rows, :], x_ref[0, 0, 1, rows, :]
            yr, yi = y_ref[0, 0, 0, rows, :], y_ref[0, 0, 1, rows, :]
            turn_ref[g, 0, rows, :] = xr * yr - xi * yi
            turn_ref[g, 1, rows, :] = xr * yi + xi * yr

    def shift(n):
        for j in range(2):
            g, p = (2 * n + j) // count, (2 * n + j) % count
            lanes = slice(j * cycles, (j + 1) * cycles)
            for start in range(0, angles, chunk):
                rows = slice(start, start + chunk)
                tr, ti = turn_ref[g, 0, rows, :], turn_ref[g, 1, rows, :]
                gr, gi = base_ref[p, 0, rows, :], base_ref[p, 1, rows, :]
                data_refs[n][rows, lanes] = (gr * tr - gi * ti).astype(bf16)
                data_refs[n][angles + start : angles + start + chunk, lanes] = (gr * ti + gi * tr).astype(bf16)

    shift(0)
    for n in range(chunks):
        if n + 1 < chunks:
            shift(n + 1)
        spectrum = jnp.dot(table_ref[...], data_refs[n][...], preferred_element_type=f32)
        for j in range(2):
            row = 2 * n + j
            ctf_row = ctf_ref[row % count, :][None, :]
            part = spectrum[:, j * cycles : (j + 1) * cycles] * ctf_row
            re_ref[pl.ds(row, angles, stride=APART), :] = part[:angles]
            im_ref[pl.ds(row, angles, stride=APART), :] = part[angles:]
    for m in range(angles):
        out_ref[m, :, :cycles] = re_ref[m * APART : m * APART + ROWS, :].astype(bf16)
        out_ref[m, :, cycles:] = im_ref[m * APART : m * APART + ROWS, :].astype(bf16)


def spectra_steps(count):
    per_step = ROWS // count if count < ROWS else 1
    return per_step, -(-SHIFTS // per_step)


def make_spectra(base, ctf_rows, first, last, before=None, after=()):
    count, _, angles, cycles = base.shape
    per_step, steps = spectra_steps(count)
    _, factors = shift_tables(angles, cycles)
    full = lambda shape: pl.BlockSpec(shape, lambda i: (0,) * len(shape))

    def factor_spec(g, axis):
        def place(i):
            s = jnp.minimum((i + first) * per_step + g, SHIFTS - 1)
            a = lax.div(s, jnp.int32(SHIFT_SIDE))
            return (axis, s - a * SHIFT_SIDE if axis else a, 0, 0, 0)

        return pl.BlockSpec((1, 1, 2, angles, cycles), place)

    untouched = ([] if before is None else [before]) + list(after)
    in_specs = (
        [full(base.shape), full(ctf_rows.shape), full((2 * angles, 2 * angles))]
        + [factor_spec(g, axis) for g in range(per_step) for axis in range(2)]
        + [pl.BlockSpec(memory_space=pl.ANY)] * len(untouched)
    )
    return pl.pallas_call(
        functools.partial(spectra_kernel, per_step=per_step),
        grid=(last - first,),
        in_specs=in_specs,
        out_specs=pl.BlockSpec((angles, ROWS, 2 * cycles), lambda i: (0, i + first, 0)),
        out_shape=jax.ShapeDtypeStruct((angles, steps * ROWS, 2 * cycles), bf16),
        scratch_shapes=[
            pltpu.VMEM((per_step, 2, angles, cycles), f32),
            pltpu.VMEM((angles * APART, cycles), f32),
            pltpu.VMEM((angles * APART, cycles), f32),
        ]
        + [pltpu.VMEM((2 * angles, 2 * cycles), bf16)] * (ROWS // 2),
        input_output_aliases={} if before is None else {3 + 2 * per_step: 0},
        compiler_params=pltpu.CompilerParams(vmem_limit_bytes=VMEM_LIMIT),
        name="spectra",
    )(base, ctf_rows, fourier_rows(angles), *[factors] * (2 * per_step), *untouched)


def half_dft(even_values, odd_values):
    half = FOLD // 2
    cos_sums, sin_sums = [None] * FOLD, [None] * FOLD

    def weighted_sum(values, k, table, start):
        total = None
        for m in range(start, FOLD, 2):
            weight = float(table((k * m % ROTS) * two_pi / ROTS))
            if values[m] is None or abs(weight) < 1e-9:
                continue
            if abs(abs(weight) - 1.0) < 1e-9:
                term = values[m] if weight > 0 else -values[m]
            else:
                term = values[m] * weight
            total = term if total is None else total + term
        return jnp.zeros_like(values[1]) if total is None else total

    for k in range(half + 1):
        even = weighted_sum(even_values, k, math.cos, 0)
        odd = weighted_sum(even_values, k, math.cos, 1)
        cos_sums[k] = even + odd
        if k != half:
            cos_sums[FOLD - 1 - k] = even - odd
        if k:
            even = weighted_sum(odd_values, k, math.sin, 0)
            odd = weighted_sum(odd_values, k, math.sin, 1)
            sin_sums[k] = even + odd
            if k != half:
                sin_sums[FOLD - 1 - k] = odd - even
    return cos_sums, sin_sums


def turn_kernel(first_ref, offset_ref, references_ref, out_ref, column_ref, in_ref, wide_ref):
    rows, cycles = references_ref.shape
    classes = offset_ref.shape[0]
    own_rows = rows // (2 * classes)
    in_ref[...] = references_ref[...].astype(f32)
    row = lax.broadcasted_iota(jnp.int32, (8, LANES), 0)
    lane = lax.broadcasted_iota(jnp.int32, (8, LANES), 1)
    freq = (lane + first_ref[0]).astype(f32) * (1.0 / (ROTS * ANG_STEP))
    tables = []
    for start in range(0, classes, 8):
        column = jnp.zeros((8, LANES), jnp.int32)
        for c in range(start, min(start + 8, classes)):
            column = jnp.where(row == c - start, offset_ref[c], column)
        column = column.astype(f32)
        column_ref[start : start + 8, :] = column
        tables.append(cos_sin_of_turns(column * freq))
    cosine = jnp.concatenate([c for c, _ in tables], 0)
    sine_part = jnp.concatenate([s for _, s in tables], 0)
    for m in range(own_rows):
        re_rows = pl.ds(2 * m * classes, classes, stride=2)
        im_rows = pl.ds(2 * m * classes + 1, classes, stride=2)
        c, s = cosine[:classes, m : m + 1], sine_part[:classes, m : m + 1]
        re, im = in_ref[re_rows, :], in_ref[im_rows, :]
        wide_ref[re_rows, :] = re * c + im * s
        wide_ref[im_rows, :] = im * c - re * s
    out_ref[...] = wide_ref[...].astype(bf16)


def turn_references(first, offsets, references):
    padded = -(-offsets.shape[0] // 8) * 8
    return pl.pallas_call(
        turn_kernel,
        in_specs=[
            pl.BlockSpec(memory_space=pltpu.SMEM),
            pl.BlockSpec(memory_space=pltpu.SMEM),
            pl.BlockSpec(memory_space=pltpu.VMEM),
        ],
        out_shape=[
            jax.ShapeDtypeStruct(references.shape, bf16),
            jax.ShapeDtypeStruct((padded, LANES), f32),
        ],
        scratch_shapes=[pltpu.VMEM(references.shape, f32)] * 2,
        compiler_params=pltpu.CompilerParams(vmem_limit_bytes=VMEM_LIMIT),
        name="turn_references",
    )(first, offsets, references)


def correlate_kernel(*refs, slots, classes, padded, finish):
    part_ref, refs = refs[slots], refs[slots + 1 :]
    weighted_refs, refs = refs[:slots], refs[slots:]
    piece_refs, refs = refs[:slots], refs[slots:]
    if finish:
        before_ref, power_before_ref, ctf_ref, weight_ref, stat_ref, share_ref = refs[:6]
        corr_ref, wide_ref, power_ref = refs[6:]
    else:
        corr_ref, power_ref, wide_ref = refs
    group = pl.program_id(0)
    cycles = piece_refs[0].shape[1]
    queries = weighted_refs[0].shape[2]
    block = piece_refs[0].shape[0]

    @pl.when(group == 0)
    def _():
        wide_ref[:, block:, :] = jnp.zeros((slots, wide_ref.shape[1] - block, cycles), f32)
        power_ref[...] = power_before_ref[...] if finish else jnp.zeros_like(power_ref)

    for j in range(slots):
        wide_ref[j, :block, :] = piece_refs[j][...].astype(f32)
    power = power_ref[...]
    for i in range(GROUP):
        total = before_ref[i, :, :queries] if finish else None
        for j in range(slots):
            re = wide_ref[j, pl.ds(2 * i * classes, padded, stride=2), :]
            im = wide_ref[j, pl.ds(2 * i * classes + 1, padded, stride=2), :]
            power = power + (re * re + im * im)
            left = jnp.concatenate(
                [jnp.concatenate([re, im], 1), jnp.concatenate([-im, re], 1)], 0
            ).astype(bf16)
            part = lax.dot_general(
                left, weighted_refs[j][0, i], (((1,), (1,)), ((), ())), preferred_element_type=f32
            )
            total = part if total is None else total + part
        row = group * GROUP + i if finish else i
        corr_ref[row, :, :queries] = total
    power_ref[...] = power

    if not finish:
        return

    @pl.when(group == pl.num_programs(0) - 1)
    def _():
        count = ctf_ref.shape[0]
        angles = ROTS * ANG_STEP
        used = SHIFTS * count
        tiles = weight_ref.shape[2] // LANES
        ctf_row = ctf_ref[...]
        ctf_rows = jnp.concatenate([ctf_row * ctf_row] * (LANES // count), 0)
        bias = lax.dot_general(
            power_ref[...],
            ctf_rows,
            (((1,), (1,)), ((), ())),
            precision=lax.Precision.HIGHEST,
            preferred_element_type=f32,
        ) * (0.5 / angles)
        wide_ref[0, :padded, :] = bias
        rows_of = lambda base: lax.broadcasted_iota(jnp.int32, (8, LANES), 0) + base
        lanes_of = lambda base: lax.broadcasted_iota(jnp.int32, (8, LANES), 1) + base

        peak = jnp.full((8, LANES), -1e30, f32)
        for tile in range(tiles):
            lanes = slice(tile * LANES, (tile + 1) * LANES)

            def scores(n, peak):
                start = pl.multiple_of(n * 8, 8)
                rows = pl.ds(start, 8)
                low = pl.ds(padded + start, 8)
                valid = (rows_of(start) < classes) & (lanes_of(tile * LANES) < used)
                even_values = [corr_ref[0, rows, lanes]]
                odd_values = [None]
                for m in range(1, ROTS // 2):
                    even_values.append(corr_ref[m, rows, lanes] + corr_ref[ROTS - m, rows, lanes])
                    odd_values.append(corr_ref[m, low, lanes] - corr_ref[ROTS - m, low, lanes])
                even_values.append(corr_ref[ROTS // 2, rows, lanes])
                odd_values.append(None)
                cos_sums, sin_sums = half_dft(even_values, odd_values)
                bias = wide_ref[0, rows, :]
                for k in range(FOLD):
                    if k in (0, FOLD - 1):
                        results = [(k, cos_sums[k])]
                    else:
                        results = [(k, cos_sums[k] - sin_sums[k]), (ROTS - k, cos_sums[k] + sin_sums[k])]
                    for place, value in results:
                        value = jnp.where(valid, value * (1.0 / angles) - bias, -1e30)
                        weight_ref[place, rows, lanes] = value
                        peak = jnp.maximum(peak, value)
                return peak

            peak = lax.fori_loop(0, padded // 8, scores, peak)

        peak = jnp.broadcast_to(jnp.max(peak, axis=0, keepdims=True), (8, LANES))
        step = count
        while step < LANES:
            peak = jnp.maximum(peak, pltpu.roll(peak, step, 1))
            step *= 2
        stat_ref[0:8, :] = peak

        def masses(n, whole):
            rows = pl.ds(pl.multiple_of(n * 8, 8), 8)
            mass = jnp.zeros((8, LANES), f32)
            for tile in range(tiles):
                lanes = slice(tile * LANES, (tile + 1) * LANES)
                for k in range(ROTS):
                    value = jnp.exp(weight_ref[k, rows, lanes] - peak)
                    weight_ref[k, rows, lanes] = value
                    mass = mass + value
            step = count
            while step < LANES:
                mass = mass + pltpu.roll(mass, step, 1)
                step *= 2
            stat_ref[pl.ds(pl.multiple_of(8 + n * 8, 8), 8), :] = mass
            return whole + mass

        whole = lax.fori_loop(0, padded // 8, masses, jnp.zeros((8, LANES), f32))
        share = jnp.concatenate([peak[:1], jnp.sum(whole, axis=0, keepdims=True)], 0)
        for j in range(share_ref.shape[0]):
            share_ref[j] = jnp.where(part_ref[0] == j, share, 0.0)


def correlate(slot_of, weighted, pieces, classes, part, before=None, power=None, ctf_rows=None, parts=1):
    _, _, queries, double = weighted.shape
    cycles = double // 2
    slots = len(pieces)
    padded = -(-classes // 8) * 8
    wide_lanes = -(-queries // LANES) * LANES
    block = 2 * GROUP * classes
    finish = ctf_rows is not None
    full = lambda shape: pl.BlockSpec(shape, lambda g, *u: (0,) * len(shape))
    in_specs = [
        pl.BlockSpec((1, GROUP, queries, double), functools.partial(lambda j, g, *u: (u[j][0], g, 0, 0), j))
        for j in range(slots)
    ] + [pl.BlockSpec((block, cycles), lambda g, *u: (g, 0))] * slots
    corr_block = pl.BlockSpec((GROUP, 2 * padded, wide_lanes), lambda g, *u: (g, 0, 0))
    corr_shape = (ROTS, 2 * padded, wide_lanes)
    wide = pltpu.VMEM((slots, block + ROWS, cycles), f32)
    scalars = [jnp.reshape(n, (1,)).astype(jnp.int32) for n in (*slot_of, part)]
    operands = scalars + [weighted] * slots + list(pieces)
    if finish:
        in_specs += [corr_block, full((padded, cycles)), full(ctf_rows.shape)]
        operands += [before, power, ctf_rows]
        out_shapes = [(ROTS, padded, wide_lanes), (8 + padded, LANES), (parts, 2, LANES)]
        out_specs = [full(shape) for shape in out_shapes]
        scratch = [pltpu.VMEM(corr_shape, f32), wide, pltpu.VMEM((padded, cycles), f32)]
    else:
        out_shapes = [corr_shape, (padded, cycles)]
        out_specs = [corr_block, full((padded, cycles))]
        scratch = [wide]
    return pl.pallas_call(
        functools.partial(correlate_kernel, slots=slots, classes=classes, padded=padded, finish=finish),
        grid_spec=pltpu.PrefetchScalarGridSpec(
            num_scalar_prefetch=len(scalars),
            grid=(ROTS // GROUP,),
            in_specs=in_specs,
            out_specs=out_specs,
            scratch_shapes=scratch,
        ),
        out_shape=[jax.ShapeDtypeStruct(shape, f32) for shape in out_shapes],
        compiler_params=pltpu.CompilerParams(vmem_limit_bytes=VMEM_LIMIT),
        name="scores" if finish else "correlate",
    )(*operands)


def back_kernel(weight_ref, stat_ref, share_ref, offset_ref, out_ref, evidence_ref, posterior_ref, sum_ref):
    padded = weight_ref.shape[1]
    queries = out_ref.shape[2]
    shares = [share_ref[j] for j in range(share_ref.shape[0])]
    top = shares[0][:1]
    for share in shares[1:]:
        top = jnp.maximum(top, share[:1])
    mass = sum(share[1:] * jnp.exp(share[:1] - top) for share in shares)
    evidence = jnp.broadcast_to(top + jnp.log(mass), (8, LANES))
    scale = jnp.exp(stat_ref[:8, :] - evidence)
    evidence_ref[...] = evidence
    posterior_ref[...] = stat_ref[8:, :] * scale[:1]
    for tile in range(weight_ref.shape[2] // LANES):
        lanes = slice(tile * LANES, (tile + 1) * LANES)

        def transform(n, carry):
            start = pl.multiple_of(n * 8, 8)
            rows = pl.ds(start, 8)
            low = pl.ds(padded + start, 8)
            values = [weight_ref[k, rows, lanes] * scale for k in range(ROTS)]
            even_values = [values[0]] + [values[k] + values[ROTS - k] for k in range(1, ROTS // 2)]
            odd_values = [None] + [values[k] - values[ROTS - k] for k in range(1, ROTS // 2)] + [None]
            cos_sums, sin_sums = half_dft(even_values + [values[ROTS // 2]], odd_values)
            for m in range(FOLD):
                sine_part = jnp.zeros_like(scale) if m in (0, FOLD - 1) else sin_sums[m]
                sum_ref[m, rows, lanes] = cos_sums[m]
                sum_ref[m, low, lanes] = sine_part
                if m not in (0, FOLD - 1):
                    sum_ref[ROTS - m, rows, lanes] = cos_sums[m]
                    sum_ref[ROTS - m, low, lanes] = -sine_part
            return carry

        lax.fori_loop(0, padded // 8, transform, 0)

    step_cos, step_sin = cos_sin_of_turns(offset_ref[...] * (1.0 / (ROTS * ANG_STEP)))

    def turn(m, carry):
        cosine, sine_part = carry
        for tile in range(weight_ref.shape[2] // LANES):
            lanes = slice(tile * LANES, (tile + 1) * LANES)
            kept = slice(tile * LANES, min((tile + 1) * LANES, queries))
            re, im = sum_ref[m, :padded, lanes], sum_ref[m, padded:, lanes]
            turned = jnp.concatenate([re * cosine - im * sine_part, re * sine_part + im * cosine], 0)
            out_ref[m, :, kept] = turned[:, : kept.stop - kept.start].astype(bf16)
        return cosine * step_cos - sine_part * step_sin, sine_part * step_cos + cosine * step_sin

    lax.fori_loop(0, ROTS, turn, (jnp.ones_like(step_cos), jnp.zeros_like(step_cos)))


def make_back(weights, stat, shares, offsets, queries):
    _, padded, wide_lanes = weights.shape
    return pl.pallas_call(
        back_kernel,
        out_shape=[
            jax.ShapeDtypeStruct((ROTS, 2 * padded, queries), bf16),
            jax.ShapeDtypeStruct((8, LANES), f32),
            jax.ShapeDtypeStruct((padded, LANES), f32),
        ],
        scratch_shapes=[pltpu.VMEM((ROTS, 2 * padded, wide_lanes), f32)],
        compiler_params=pltpu.CompilerParams(vmem_limit_bytes=VMEM_LIMIT),
        name="back",
    )(weights, stat, shares, offsets)


def sums_kernel(*refs, count, classes):
    slot_refs, (back_ref, *refs) = refs[:count], refs[count:]
    weighted_refs, (offset_ref, *refs) = refs[:count], refs[count:]
    out_refs, wide_refs = refs[:count], refs[count:]
    padded = offset_ref.shape[0]
    cycles = wide_refs[0].shape[1]
    turns = [
        cos_sin_of_turns(offset_ref[...] * (slot_ref[0].astype(f32) * (1.0 / ANG_STEP)))
        for slot_ref in slot_refs
    ]
    for i in range(GROUP):
        for (cosine, sine_part), weighted_ref, wide_ref in zip(turns, weighted_refs, wide_refs):
            product = jnp.dot(back_ref[i], weighted_ref[0, i], preferred_element_type=f32)
            re = product[:padded, :cycles] - product[padded:, cycles:]
            im = product[:padded, cycles:] + product[padded:, :cycles]
            start = 2 * i * classes
            wide_ref[pl.ds(start, classes, stride=2), :] = (re * cosine - im * sine_part)[:classes]
            wide_ref[pl.ds(start + 1, classes, stride=2), :] = (re * sine_part + im * cosine)[:classes]
    for out_ref, wide_ref in zip(out_refs, wide_refs):
        out_ref[...] = wide_ref[...].astype(out_ref.dtype)


def class_sums_of(slots, back, weighted, offsets, classes, dtypes, groups=(0, ROTS // GROUP)):
    begin, end = groups
    _, _, queries, double = weighted.shape
    cycles = double // 2
    rows = back.shape[1]
    block = 2 * GROUP * classes
    count = len(slots)
    scalars = [jnp.reshape(slot, (1,)).astype(jnp.int32) for slot in slots]
    return pl.pallas_call(
        functools.partial(sums_kernel, count=count, classes=classes),
        grid_spec=pltpu.PrefetchScalarGridSpec(
            num_scalar_prefetch=count,
            grid=(end - begin,),
            in_specs=[pl.BlockSpec((GROUP, rows, queries), lambda g, *u: (g + begin, 0, 0))]
            + [
                pl.BlockSpec(
                    (1, GROUP, queries, double),
                    functools.partial(lambda j, g, *u: (u[j][0], g + begin, 0, 0), j),
                )
                for j in range(count)
            ]
            + [pl.BlockSpec(offsets.shape, lambda g, *u: (0, 0))],
            out_specs=[pl.BlockSpec((block, cycles), lambda g, *u: (g, 0))] * count,
            scratch_shapes=[pltpu.VMEM((block, cycles), f32)] * count,
        ),
        out_shape=[jax.ShapeDtypeStruct(((end - begin) * block, cycles), dtype) for dtype in dtypes],
        compiler_params=pltpu.CompilerParams(vmem_limit_bytes=VMEM_LIMIT),
        name="class_sums",
    )(*scalars, back, *[weighted] * count, offsets)


def across(piece):
    return lax.ppermute(piece, "dp", [(d, d ^ 1) for d in range(8)])


def along(piece, pairs):
    return lax.ppermute(piece, "dp", [(2 * a + x, 2 * b + x) for a, b in pairs for x in range(2)])


def gather_on_line(piece, base, ctf_rows):
    index = lax.axis_index("dp")
    line, side = index // 2, index % 2
    _, steps = spectra_steps(base.shape[0])
    cuts = [0, 3 * steps // 13, 8 * steps // 13, steps]

    own_crossed = across(piece)
    near = along(piece, ((0, 1), (1, 0), (2, 3), (3, 2)))
    middle = along(piece, ((1, 2), (2, 1)))
    weighted = make_spectra(base, ctf_rows, cuts[0], cuts[1])
    weighted, near, middle, own_crossed = lax.optimization_barrier((weighted, near, middle, own_crossed))
    near_crossed = across(near)
    far_middle = along(near, ((1, 2), (2, 1)))
    end = along(middle, ((1, 0), (2, 3)))
    weighted = make_spectra(base, ctf_rows, cuts[1], cuts[2], weighted)
    weighted, end = lax.optimization_barrier((weighted, end))
    weighted, near_crossed = lax.optimization_barrier((weighted, near_crossed))
    weighted, far_middle = lax.optimization_barrier((weighted, far_middle))
    third = middle + end
    third_crossed = across(third)
    far_end = along(far_middle, ((1, 0), (2, 3)))
    weighted = make_spectra(base, ctf_rows, cuts[2], cuts[3], weighted)
    weighted, far_end, third_crossed = lax.optimization_barrier((weighted, far_end, third_crossed))
    fourth = far_middle + far_end
    fourth_crossed = across(fourth)

    pieces = [piece, own_crossed, near, near_crossed, third, third_crossed, fourth, fourth_crossed]
    places = [line, line ^ 1, jnp.where(line < 2, 2, 1), jnp.where(line < 2, 3, 0)]
    slot_of = [2 * place + s for place in places for s in (side, 1 - side)]
    return weighted, pieces, slot_of


def add_kernel(own_ref, *refs):
    *whole_refs, head_ref, rest_ref, out_ref = refs
    total = own_ref[...]
    for ref in whole_refs:
        total = total + ref[...].astype(f32)
    part = jnp.where(pl.program_id(0) == 0, head_ref[...], rest_ref[...])
    out_ref[...] = total + part.astype(f32)


def add_pieces(own, whole, pair, block):
    rows, cycles = own.shape
    spec = pl.BlockSpec((block, cycles), lambda g: (g, 0))
    head = pl.BlockSpec((block, cycles), lambda g: (0, 0))
    rest = pl.BlockSpec((block, cycles), lambda g: (jnp.maximum(g - 1, 0), 0))
    return pl.pallas_call(
        add_kernel,
        grid=(rows // block,),
        in_specs=[spec] * (1 + len(whole)) + [head, rest],
        out_specs=spec,
        out_shape=jax.ShapeDtypeStruct(own.shape, f32),
        name="add_pieces",
    )(own, *whole, *pair)


def reduce_on_line(back, weighted, offsets, classes):
    index = lax.axis_index("dp")
    line, side = index // 2, index % 2
    order = [jnp.where(line < 2, 3, 0), jnp.where(line < 2, 2, 1), line ^ 1, line]
    theirs = [2 * z + 1 - side for z in order]
    ours = [2 * z + side for z in order]
    groups = ((0, 1), (1, ROTS // GROUP))
    block = 2 * GROUP * classes
    head, rest = [slice(a * block, b * block) for a, b in groups]
    to_middle, between = ((0, 1), (3, 2)), ((1, 2), (2, 1))
    neighbours = ((0, 1), (1, 0), (2, 3), (3, 2))

    def sums(slots, dtypes, back, some=(0, ROTS // GROUP)):
        return class_sums_of(slots, back, weighted, offsets, classes, dtypes, some)

    def wide(piece):
        return piece.astype(f32)

    def then(back, *done):
        return lax.optimization_barrier((back, *done))[0]

    (away,) = sums(theirs[:1], [bf16], back, groups[0])
    crossed_head = across(away)
    back = then(back, away)
    (away,) = sums(theirs[:1], [bf16], back, groups[1])
    crossed_rest = across(away)
    back = then(back, away)
    own_0, away = sums([ours[0], theirs[1]], [f32, bf16], back)
    crossed_1 = across(away)
    crossed_head, own_0 = lax.optimization_barrier((crossed_head, own_0))
    message = (own_0[head] + wide(crossed_head)).astype(bf16)
    first_head = along(message, to_middle)
    back = then(back, message)
    own_1, away = sums([ours[1], theirs[2]], [f32, bf16], back)
    crossed_2 = across(away)
    crossed_rest, own_1 = lax.optimization_barrier((crossed_rest, own_1))
    message = (own_0[rest] + wide(crossed_rest)).astype(bf16)
    first_rest = along(message, to_middle)
    back = then(back, message)
    message = (own_0[head] + wide(crossed_head) + wide(first_head)).astype(bf16)
    middle_head = along(message, between)
    back = then(back, message)
    own_2, away = sums([ours[2], theirs[3]], [f32, bf16], back)
    crossed_3 = across(away)
    crossed_1, first_rest, middle_head, own_2 = lax.optimization_barrier(
        (crossed_1, first_rest, middle_head, own_2)
    )
    message = (own_1 + wide(crossed_1)).astype(bf16)
    from_end = along(message, to_middle)
    first_rest = then(first_rest, message)
    message = (own_0[rest] + wide(crossed_rest) + wide(first_rest)).astype(bf16)
    middle_rest = along(message, between)
    back = then(back, message)
    (own_3,) = sums(ours[3:], [f32], back)
    message = (own_2[head] + wide(crossed_2[head]) + wide(middle_head)).astype(bf16)
    last_head = along(message, neighbours)
    from_end = then(from_end, crossed_2)
    message = (own_1 + wide(crossed_1) + wide(from_end)).astype(bf16)
    third = along(message, between)
    middle_rest = then(middle_rest, message)
    message = (own_2[rest] + wide(crossed_2[rest]) + wide(middle_rest)).astype(bf16)
    last_rest = along(message, neighbours)
    return add_pieces(own_3, (crossed_3, third), (last_head, last_rest), block)


def local(particles, references, ctf_table, rot_offset, prior_shift, defocus_group):
    count, _, angles, cycles = particles.shape
    own_rows, _, classes, _ = references.shape
    slots = angles // ROTS
    group_count = ctf_table.shape[0]
    devices = lax.axis_size("dp")

    first = (lax.axis_index("dp") * own_rows).astype(jnp.int32).reshape(1)
    rows = jnp.transpose(references, (0, 2, 1, 3)).reshape(own_rows * 2 * classes, cycles)
    piece, offsets = turn_references(first, rot_offset, rows)

    onehot = (defocus_group[:, None] == jnp.arange(group_count, dtype=jnp.int32)[None, :]).astype(f32)
    ctf_rows = jnp.dot(onehot, ctf_table, precision=lax.Precision.HIGHEST)
    base = make_base(particles, prior_shift)
    on_line = devices == 8 and own_rows == ROTS
    if on_line:
        weighted, pieces, slot_of = gather_on_line(piece, base, ctf_rows)
    else:
        gathered = lax.all_gather(piece, "dp", axis=0, tiled=True)
        gathered = gathered.reshape(slots, ROTS * 2 * classes, cycles)
        pieces = [gathered[j] for j in range(slots)]
        slot_of = list(range(slots))
        weighted = make_spectra(base, ctf_rows, 0, spectra_steps(count)[1])
    queries = weighted.shape[1]
    weighted = weighted.reshape(slots, ROTS, queries, 2 * cycles)

    early = slots - 1
    part = lax.axis_index("cls")
    corr, power = correlate(slot_of[:early], weighted, pieces[:early], classes, part)
    weights, stat, share = correlate(
        slot_of[early:], weighted, pieces[early:], classes, part, corr, power, ctf_rows, lax.axis_size("cls")
    )
    shares = lax.psum(share, "cls")
    back, evidence, posterior = make_back(weights, stat, shares, offsets, queries)
    log_evidence = evidence[0, :count]
    class_posterior = posterior[:classes, :count].T
    if on_line:
        class_rows = reduce_on_line(back, weighted, offsets, classes)
    else:
        sums = [class_sums_of([u], back, weighted, offsets, classes, [bf16])[0] for u in slot_of]
        summed = lax.psum_scatter(jnp.concatenate(sums, 0), "dp", scatter_dimension=0, tiled=True)
        class_rows = summed.astype(f32)
    class_sums = jnp.transpose(class_rows.reshape(own_rows, classes, 2, cycles), (0, 2, 1, 3))
    return (log_evidence, class_posterior, class_sums)


def solution(mesh):
    placed = (
        P("dp", None, None, None),
        P("dp", None, "cls", None),
        P(),
        P("cls"),
        P("dp", None),
        P("dp"),
    )
    return jax.shard_map(
        local,
        mesh=mesh,
        in_specs=placed,
        out_specs=(P("dp"), P("dp", "cls"), P("dp", None, "cls", None)),
        check_vma=False,
    )
```

```python
import functools
import math

import jax
import jax.numpy as jnp
import ml_dtypes
import numpy as np
from jax import lax
from jax.experimental import pallas as pl
from jax.experimental.pallas import tpu as pltpu
from jax.sharding import PartitionSpec as P

ROTS = 36
ANG_STEP = 8
SHIFT_SIDE = 5
SHIFTS = SHIFT_SIDE * SHIFT_SIDE
LANES = 128
GROUP = 12
ROWS = 16
APART = 17
FOLD = ROTS // 2 + 1

two_pi = 2.0 * math.pi
f32 = jnp.float32
bf16 = jnp.bfloat16
VMEM_LIMIT = 56 * 1024 * 1024


def fourier_rows(angles):
    index_grid = np.arange(angles)
    radians = (index_grid[:, None] * index_grid[None, :] % angles) * (two_pi / angles)
    cosine, sine_part = np.cos(radians), np.sin(radians)
    table_full = np.concatenate(
        [np.concatenate([cosine, sine_part], 1), np.concatenate([-sine_part, cosine], 1)], 0
    )
    return table_full.astype(np.float32).astype(ml_dtypes.bfloat16)


def shift_tables(angles, cycles):
    theta = np.arange(angles) * (two_pi / angles)
    radius = (np.arange(cycles) + 1) / (2.0 * cycles)
    turns = np.stack([np.cos(theta), np.sin(theta)])[:, :, None] * radius
    steps = np.arange(SHIFT_SIDE) - SHIFT_SIDE // 2
    phase = two_pi * turns[:, None] * steps[None, :, None, None]
    factors = np.stack([np.cos(phase), -np.sin(phase)], 2)
    return turns.astype(np.float32), factors.astype(np.float32)


def cos_sin_of_turns(turns):
    frac = turns - jnp.floor(turns + 0.5)
    w = frac * two_pi
    w2 = w * w
    cosine = jnp.full_like(w, 1.0 / math.factorial(16))
    for n in range(14, -1, -2):
        cosine = cosine * w2 + (-1.0) ** (n // 2) / math.factorial(n)
    sine_part = jnp.full_like(w, 1.0 / math.factorial(17))
    for n in range(15, 0, -2):
        sine_part = sine_part * w2 + (-1.0) ** (n // 2) / math.factorial(n)
    return cosine, sine_part * w


def base_kernel(shift_ref, part_ref, turns_ref, base_ref):
    here, _, angles, _ = part_ref.shape
    chunk = 32
    for q in range(here):
        p = pl.program_id(0) * here + q
        sx = shift_ref[0, p].astype(f32)
        sy = shift_ref[1, p].astype(f32)

        def turn(n, carry):
            rows = pl.ds(pl.multiple_of(n * chunk, chunk), chunk)
            cosine, sine_part = cos_sin_of_turns(sx * turns_ref[0, rows, :] + sy * turns_ref[1, rows, :])
            re = part_ref[q, 0, rows, :].astype(f32)
            im = part_ref[q, 1, rows, :].astype(f32)
            base_ref[q, 0, rows, :] = re * cosine + im * sine_part
            base_ref[q, 1, rows, :] = im * cosine - re * sine_part
            return carry

        lax.fori_loop(0, angles // chunk, turn, 0)


def make_base(particles, prior_shift):
    count, _, angles, cycles = particles.shape
    turns, _ = shift_tables(angles, cycles)
    here = count // 2
    image = pl.BlockSpec((here, 2, angles, cycles), lambda p: (p, 0, 0, 0))
    return pl.pallas_call(
        base_kernel,
        grid=(2,),
        in_specs=[
            pl.BlockSpec(memory_space=pltpu.SMEM),
            image,
            pl.BlockSpec(turns.shape, lambda p: (0, 0, 0)),
        ],
        out_specs=image,
        out_shape=jax.ShapeDtypeStruct(particles.shape, f32),
        compiler_params=pltpu.CompilerParams(vmem_limit_bytes=VMEM_LIMIT),
        name="centre",
    )(prior_shift.T, particles, turns)


def spectra_kernel(base_ref, ctf_ref, table_ref, *refs, per_step):
    factor_refs, refs = refs[: 2 * per_step], refs[2 * per_step :]
    chunks = ROWS // 2
    out_ref, turn_ref, re_ref, im_ref = refs[-4 - chunks : -chunks]
    data_refs = refs[-chunks:]
    count, _, angles, cycles = base_ref.shape
    chunk = 32

    for g in range(per_step):
        x_ref, y_ref = factor_refs[2 * g], factor_refs[2 * g + 1]
        for start in range(0, angles, chunk):
            rows = slice(start, start + chunk)
            xr, xi = x_ref[0, 0, 0, rows, :], x_ref[0, 0, 1, rows, :]
            yr, yi = y_ref[0, 0, 0, rows, :], y_ref[0, 0, 1, rows, :]
            turn_ref[g, 0, rows, :] = xr * yr - xi * yi
            turn_ref[g, 1, rows, :] = xr * yi + xi * yr

    def shift(n):
        for j in range(2):
            g, p = (2 * n + j) // count, (2 * n + j) % count
            lanes = slice(j * cycles, (j + 1) * cycles)
            for start in range(0, angles, chunk):
                rows = slice(start, start + chunk)
                tr, ti = turn_ref[g, 0, rows, :], turn_ref[g, 1, rows, :]
                gr, gi = base_ref[p, 0, rows, :], base_ref[p, 1, rows, :]
                data_refs[n][rows, lanes] = (gr * tr - gi * ti).astype(bf16)
                data_refs[n][angles + start : angles + start + chunk, lanes] = (gr * ti + gi * tr).astype(bf16)

    shift(0)
    for n in range(chunks):
        if n + 1 < chunks:
            shift(n + 1)
        spectrum = jnp.dot(table_ref[...], data_refs[n][...], preferred_element_type=f32)
        for j in range(2):
            row = 2 * n + j
            ctf_row = ctf_ref[row % count, :][None, :]
            part = spectrum[:, j * cycles : (j + 1) * cycles] * ctf_row
            re_ref[pl.ds(row, angles, stride=APART), :] = part[:angles]
            im_ref[pl.ds(row, angles, stride=APART), :] = part[angles:]
    for m in range(angles):
        out_ref[m, :, :cycles] = re_ref[m * APART : m * APART + ROWS, :].astype(bf16)
        out_ref[m, :, cycles:] = im_ref[m * APART : m * APART + ROWS, :].astype(bf16)


def spectra_steps(count):
    per_step = ROWS // count if count < ROWS else 1
    return per_step, -(-SHIFTS // per_step)


def make_spectra(base, ctf_rows, first, last, before=None, after=()):
    count, _, angles, cycles = base.shape
    per_step, steps = spectra_steps(count)
    _, factors = shift_tables(angles, cycles)
    full = lambda shape: pl.BlockSpec(shape, lambda i: (0,) * len(shape))

    def factor_spec(g, axis):
        def place(i):
            s = jnp.minimum((i + first) * per_step + g, SHIFTS - 1)
            a = lax.div(s, jnp.int32(SHIFT_SIDE))
            return (axis, s - a * SHIFT_SIDE if axis else a, 0, 0, 0)

        return pl.BlockSpec((1, 1, 2, angles, cycles), place)

    untouched = ([] if before is None else [before]) + list(after)
    in_specs = (
        [full(base.shape), full(ctf_rows.shape), full((2 * angles, 2 * angles))]
        + [factor_spec(g, axis) for g in range(per_step) for axis in range(2)]
        + [pl.BlockSpec(memory_space=pl.ANY)] * len(untouched)
    )
    return pl.pallas_call(
        functools.partial(spectra_kernel, per_step=per_step),
        grid=(last - first,),
        in_specs=in_specs,
        out_specs=pl.BlockSpec((angles, ROWS, 2 * cycles), lambda i: (0, i + first, 0)),
        out_shape=jax.ShapeDtypeStruct((angles, steps * ROWS, 2 * cycles), bf16),
        scratch_shapes=[
            pltpu.VMEM((per_step, 2, angles, cycles), f32),
            pltpu.VMEM((angles * APART, cycles), f32),
            pltpu.VMEM((angles * APART, cycles), f32),
        ]
        + [pltpu.VMEM((2 * angles, 2 * cycles), bf16)] * (ROWS // 2),
        input_output_aliases={} if before is None else {3 + 2 * per_step: 0},
        compiler_params=pltpu.CompilerParams(vmem_limit_bytes=VMEM_LIMIT),
        name="spectra",
    )(base, ctf_rows, fourier_rows(angles), *[factors] * (2 * per_step), *untouched)


def half_dft(even_values, odd_values):
    half = FOLD // 2
    cos_sums, sin_sums = [None] * FOLD, [None] * FOLD

    def weighted_sum(values, k, table, start):
        total = None
        for m in range(start, FOLD, 2):
            weight = float(table((k * m % ROTS) * two_pi / ROTS))
            if values[m] is None or abs(weight) < 1e-9:
                continue
            if abs(abs(weight) - 1.0) < 1e-9:
                term = values[m] if weight > 0 else -values[m]
            else:
                term = values[m] * weight
            total = term if total is None else total + term
        return jnp.zeros_like(values[1]) if total is None else total

    for k in range(half + 1):
        even = weighted_sum(even_values, k, math.cos, 0)
        odd = weighted_sum(even_values, k, math.cos, 1)
        cos_sums[k] = even + odd
        if k != half:
            cos_sums[FOLD - 1 - k] = even - odd
        if k:
            even = weighted_sum(odd_values, k, math.sin, 0)
            odd = weighted_sum(odd_values, k, math.sin, 1)
            sin_sums[k] = even + odd
            if k != half:
                sin_sums[FOLD - 1 - k] = odd - even
    return cos_sums, sin_sums


def turn_kernel(first_ref, offset_ref, references_ref, out_ref, column_ref, in_ref, wide_ref):
    rows, cycles = references_ref.shape
    classes = offset_ref.shape[0]
    own_rows = rows // (2 * classes)
    in_ref[...] = references_ref[...].astype(f32)
    row = lax.broadcasted_iota(jnp.int32, (8, LANES), 0)
    lane = lax.broadcasted_iota(jnp.int32, (8, LANES), 1)
    freq = (lane + first_ref[0]).astype(f32) * (1.0 / (ROTS * ANG_STEP))
    tables = []
    for start in range(0, classes, 8):
        column = jnp.zeros((8, LANES), jnp.int32)
        for c in range(start, min(start + 8, classes)):
            column = jnp.where(row == c - start, offset_ref[c], column)
        column = column.astype(f32)
        column_ref[start : start + 8, :] = column
        tables.append(cos_sin_of_turns(column * freq))
    cosine = jnp.concatenate([c for c, _ in tables], 0)
    sine_part = jnp.concatenate([s for _, s in tables], 0)
    for m in range(own_rows):
        re_rows = pl.ds(2 * m * classes, classes, stride=2)
        im_rows = pl.ds(2 * m * classes + 1, classes, stride=2)
        c, s = cosine[:classes, m : m + 1], sine_part[:classes, m : m + 1]
        re, im = in_ref[re_rows, :], in_ref[im_rows, :]
        wide_ref[re_rows, :] = re * c + im * s
        wide_ref[im_rows, :] = im * c - re * s
    out_ref[...] = wide_ref[...].astype(bf16)


def turn_references(first, offsets, references):
    padded = -(-offsets.shape[0] // 8) * 8
    return pl.pallas_call(
        turn_kernel,
        in_specs=[
            pl.BlockSpec(memory_space=pltpu.SMEM),
            pl.BlockSpec(memory_space=pltpu.SMEM),
            pl.BlockSpec(memory_space=pltpu.VMEM),
        ],
        out_shape=[
            jax.ShapeDtypeStruct(references.shape, bf16),
            jax.ShapeDtypeStruct((padded, LANES), f32),
        ],
        scratch_shapes=[pltpu.VMEM(references.shape, f32)] * 2,
        compiler_params=pltpu.CompilerParams(vmem_limit_bytes=VMEM_LIMIT),
        name="turn_references",
    )(first, offsets, references)


def correlate_kernel(*refs, slots, classes, padded, finish):
    part_ref, refs = refs[slots], refs[slots + 1 :]
    weighted_refs, refs = refs[:slots], refs[slots:]
    piece_refs, refs = refs[:slots], refs[slots:]
    if finish:
        before_ref, power_before_ref, ctf_ref, weight_ref, stat_ref, share_ref = refs[:6]
        corr_ref, wide_ref, power_ref = refs[6:]
    else:
        corr_ref, power_ref, wide_ref = refs
    group = pl.program_id(0)
    cycles = piece_refs[0].shape[1]
    queries = weighted_refs[0].shape[2]
    block = piece_refs[0].shape[0]

    @pl.when(group == 0)
    def _():
        wide_ref[:, block:, :] = jnp.zeros((slots, wide_ref.shape[1] - block, cycles), f32)
        power_ref[...] = power_before_ref[...] if finish else jnp.zeros_like(power_ref)

    for j in range(slots):
        wide_ref[j, :block, :] = piece_refs[j][...].astype(f32)
    power = power_ref[...]
    for i in range(GROUP):
        total = before_ref[i, :, :queries] if finish else None
        for j in range(slots):
            re = wide_ref[j, pl.ds(2 * i * classes, padded, stride=2), :]
            im = wide_ref[j, pl.ds(2 * i * classes + 1, padded, stride=2), :]
            power = power + (re * re + im * im)
            left = jnp.concatenate(
                [jnp.concatenate([re, im], 1), jnp.concatenate([-im, re], 1)], 0
            ).astype(bf16)
            part = lax.dot_general(
                left, weighted_refs[j][0, i], (((1,), (1,)), ((), ())), preferred_element_type=f32
            )
            total = part if total is None else total + part
        row = group * GROUP + i if finish else i
        corr_ref[row, :, :queries] = total
    power_ref[...] = power

    if not finish:
        return

    @pl.when(group == pl.num_programs(0) - 1)
    def _():
        count = ctf_ref.shape[0]
        angles = ROTS * ANG_STEP
        used = SHIFTS * count
        tiles = weight_ref.shape[2] // LANES
        ctf_row = ctf_ref[...]
        ctf_rows = jnp.concatenate([ctf_row * ctf_row] * (LANES // count), 0)
        bias = lax.dot_general(
            power_ref[...],
            ctf_rows,
            (((1,), (1,)), ((), ())),
            precision=lax.Precision.HIGHEST,
            preferred_element_type=f32,
        ) * (0.5 / angles)
        wide_ref[0, :padded, :] = bias
        rows_of = lambda base: lax.broadcasted_iota(jnp.int32, (8, LANES), 0) + base
        lanes_of = lambda base: lax.broadcasted_iota(jnp.int32, (8, LANES), 1) + base

        peak = jnp.full((8, LANES), -1e30, f32)
        for tile in range(tiles):
            lanes = slice(tile * LANES, (tile + 1) * LANES)

            def scores(n, peak):
                start = pl.multiple_of(n * 8, 8)
                rows = pl.ds(start, 8)
                low = pl.ds(padded + start, 8)
                valid = (rows_of(start) < classes) & (lanes_of(tile * LANES) < used)
                even_values = [corr_ref[0, rows, lanes]]
                odd_values = [None]
                for m in range(1, ROTS // 2):
                    even_values.append(corr_ref[m, rows, lanes] + corr_ref[ROTS - m, rows, lanes])
                    odd_values.append(corr_ref[m, low, lanes] - corr_ref[ROTS - m, low, lanes])
                even_values.append(corr_ref[ROTS // 2, rows, lanes])
                odd_values.append(None)
                cos_sums, sin_sums = half_dft(even_values, odd_values)
                bias = wide_ref[0, rows, :]
                for k in range(FOLD):
                    if k in (0, FOLD - 1):
                        results = [(k, cos_sums[k])]
                    else:
                        results = [(k, cos_sums[k] - sin_sums[k]), (ROTS - k, cos_sums[k] + sin_sums[k])]
                    for place, value in results:
                        value = jnp.where(valid, value * (1.0 / angles) - bias, -1e30)
                        weight_ref[place, rows, lanes] = value
                        peak = jnp.maximum(peak, value)
                return peak

            peak = lax.fori_loop(0, padded // 8, scores, peak)

        peak = jnp.broadcast_to(jnp.max(peak, axis=0, keepdims=True), (8, LANES))
        step = count
        while step < LANES:
            peak = jnp.maximum(peak, pltpu.roll(peak, step, 1))
            step *= 2
        stat_ref[0:8, :] = peak

        def masses(n, whole):
            rows = pl.ds(pl.multiple_of(n * 8, 8), 8)
            mass = jnp.zeros((8, LANES), f32)
            for tile in range(tiles):
                lanes = slice(tile * LANES, (tile + 1) * LANES)
                for k in range(ROTS):
                    value = jnp.exp(weight_ref[k, rows, lanes] - peak)
                    weight_ref[k, rows, lanes] = value
                    mass = mass + value
            step = count
            while step < LANES:
                mass = mass + pltpu.roll(mass, step, 1)
                step *= 2
            stat_ref[pl.ds(pl.multiple_of(8 + n * 8, 8), 8), :] = mass
            return whole + mass

        whole = lax.fori_loop(0, padded // 8, masses, jnp.zeros((8, LANES), f32))
        share = jnp.concatenate([peak[:1], jnp.sum(whole, axis=0, keepdims=True)], 0)
        for j in range(share_ref.shape[0]):
            share_ref[j] = jnp.where(part_ref[0] == j, share, 0.0)


def correlate(slot_of, weighted, pieces, classes, part, before=None, power=None, ctf_rows=None, parts=1):
    _, _, queries, double = weighted.shape
    cycles = double // 2
    slots = len(pieces)
    padded = -(-classes // 8) * 8
    wide_lanes = -(-queries // LANES) * LANES
    block = 2 * GROUP * classes
    finish = ctf_rows is not None
    full = lambda shape: pl.BlockSpec(shape, lambda g, *u: (0,) * len(shape))
    in_specs = [
        pl.BlockSpec((1, GROUP, queries, double), functools.partial(lambda j, g, *u: (u[j][0], g, 0, 0), j))
        for j in range(slots)
    ] + [pl.BlockSpec((block, cycles), lambda g, *u: (g, 0))] * slots
    corr_block = pl.BlockSpec((GROUP, 2 * padded, wide_lanes), lambda g, *u: (g, 0, 0))
    corr_shape = (ROTS, 2 * padded, wide_lanes)
    wide = pltpu.VMEM((slots, block + ROWS, cycles), f32)
    scalars = [jnp.reshape(n, (1,)).astype(jnp.int32) for n in (*slot_of, part)]
    operands = scalars + [weighted] * slots + list(pieces)
    if finish:
        in_specs += [corr_block, full((padded, cycles)), full(ctf_rows.shape)]
        operands += [before, power, ctf_rows]
        out_shapes = [(ROTS, padded, wide_lanes), (8 + padded, LANES), (parts, 2, LANES)]
        out_specs = [full(shape) for shape in out_shapes]
        scratch = [pltpu.VMEM(corr_shape, f32), wide, pltpu.VMEM((padded, cycles), f32)]
    else:
        out_shapes = [corr_shape, (padded, cycles)]
        out_specs = [corr_block, full((padded, cycles))]
        scratch = [wide]
    return pl.pallas_call(
        functools.partial(correlate_kernel, slots=slots, classes=classes, padded=padded, finish=finish),
        grid_spec=pltpu.PrefetchScalarGridSpec(
            num_scalar_prefetch=len(scalars),
            grid=(ROTS // GROUP,),
            in_specs=in_specs,
            out_specs=out_specs,
            scratch_shapes=scratch,
        ),
        out_shape=[jax.ShapeDtypeStruct(shape, f32) for shape in out_shapes],
        compiler_params=pltpu.CompilerParams(vmem_limit_bytes=VMEM_LIMIT),
        name="scores" if finish else "correlate",
    )(*operands)


def back_kernel(weight_ref, stat_ref, share_ref, offset_ref, out_ref, evidence_ref, posterior_ref, sum_ref):
    padded = weight_ref.shape[1]
    queries = out_ref.shape[2]
    shares = [share_ref[j] for j in range(share_ref.shape[0])]
    top = shares[0][:1]
    for share in shares[1:]:
        top = jnp.maximum(top, share[:1])
    mass = sum(share[1:] * jnp.exp(share[:1] - top) for share in shares)
    evidence = jnp.broadcast_to(top + jnp.log(mass), (8, LANES))
    scale = jnp.exp(stat_ref[:8, :] - evidence)
    evidence_ref[...] = evidence
    posterior_ref[...] = stat_ref[8:, :] * scale[:1]
    for tile in range(weight_ref.shape[2] // LANES):
        lanes = slice(tile * LANES, (tile + 1) * LANES)

        def transform(n, carry):
            start = pl.multiple_of(n * 8, 8)
            rows = pl.ds(start, 8)
            low = pl.ds(padded + start, 8)
            values = [weight_ref[k, rows, lanes] * scale for k in range(ROTS)]
            even_values = [values[0]] + [values[k] + values[ROTS - k] for k in range(1, ROTS // 2)]
            odd_values = [None] + [values[k] - values[ROTS - k] for k in range(1, ROTS // 2)] + [None]
            cos_sums, sin_sums = half_dft(even_values + [values[ROTS // 2]], odd_values)
            for m in range(FOLD):
                sine_part = jnp.zeros_like(scale) if m in (0, FOLD - 1) else sin_sums[m]
                sum_ref[m, rows, lanes] = cos_sums[m]
                sum_ref[m, low, lanes] = sine_part
                if m not in (0, FOLD - 1):
                    sum_ref[ROTS - m, rows, lanes] = cos_sums[m]
                    sum_ref[ROTS - m, low, lanes] = -sine_part
            return carry

        lax.fori_loop(0, padded // 8, transform, 0)

    step_cos, step_sin = cos_sin_of_turns(offset_ref[...] * (1.0 / (ROTS * ANG_STEP)))

    def turn(m, carry):
        cosine, sine_part = carry
        for tile in range(weight_ref.shape[2] // LANES):
            lanes = slice(tile * LANES, (tile + 1) * LANES)
            kept = slice(tile * LANES, min((tile + 1) * LANES, queries))
            re, im = sum_ref[m, :padded, lanes], sum_ref[m, padded:, lanes]
            turned = jnp.concatenate([re * cosine - im * sine_part, re * sine_part + im * cosine], 0)
            out_ref[m, :, kept] = turned[:, : kept.stop - kept.start].astype(bf16)
        return cosine * step_cos - sine_part * step_sin, sine_part * step_cos + cosine * step_sin

    lax.fori_loop(0, ROTS, turn, (jnp.ones_like(step_cos), jnp.zeros_like(step_cos)))


def make_back(weights, stat, shares, offsets, queries):
    _, padded, wide_lanes = weights.shape
    return pl.pallas_call(
        back_kernel,
        out_shape=[
            jax.ShapeDtypeStruct((ROTS, 2 * padded, queries), bf16),
            jax.ShapeDtypeStruct((8, LANES), f32),
            jax.ShapeDtypeStruct((padded, LANES), f32),
        ],
        scratch_shapes=[pltpu.VMEM((ROTS, 2 * padded, wide_lanes), f32)],
        compiler_params=pltpu.CompilerParams(vmem_limit_bytes=VMEM_LIMIT),
        name="back",
    )(weights, stat, shares, offsets)


def sums_kernel(*refs, count, classes):
    slot_refs, (back_ref, *refs) = refs[:count], refs[count:]
    weighted_refs, (offset_ref, *refs) = refs[:count], refs[count:]
    out_refs, wide_refs = refs[:count], refs[count:]
    padded = offset_ref.shape[0]
    cycles = wide_refs[0].shape[1]
    turns = [
        cos_sin_of_turns(offset_ref[...] * (slot_ref[0].astype(f32) * (1.0 / ANG_STEP)))
        for slot_ref in slot_refs
    ]
    for i in range(GROUP):
        for (cosine, sine_part), weighted_ref, wide_ref in zip(turns, weighted_refs, wide_refs):
            product = jnp.dot(back_ref[i], weighted_ref[0, i], preferred_element_type=f32)
            re = product[:padded, :cycles] - product[padded:, cycles:]
            im = product[:padded, cycles:] + product[padded:, :cycles]
            start = 2 * i * classes
            wide_ref[pl.ds(start, classes, stride=2), :] = (re * cosine - im * sine_part)[:classes]
            wide_ref[pl.ds(start + 1, classes, stride=2), :] = (re * sine_part + im * cosine)[:classes]
    for out_ref, wide_ref in zip(out_refs, wide_refs):
        out_ref[...] = wide_ref[...].astype(out_ref.dtype)


def class_sums_of(slots, back, weighted, offsets, classes, dtypes, groups=(0, ROTS // GROUP)):
    begin, end = groups
    _, _, queries, double = weighted.shape
    cycles = double // 2
    rows = back.shape[1]
    block = 2 * GROUP * classes
    count = len(slots)
    scalars = [jnp.reshape(slot, (1,)).astype(jnp.int32) for slot in slots]
    return pl.pallas_call(
        functools.partial(sums_kernel, count=count, classes=classes),
        grid_spec=pltpu.PrefetchScalarGridSpec(
            num_scalar_prefetch=count,
            grid=(end - begin,),
            in_specs=[pl.BlockSpec((GROUP, rows, queries), lambda g, *u: (g + begin, 0, 0))]
            + [
                pl.BlockSpec(
                    (1, GROUP, queries, double),
                    functools.partial(lambda j, g, *u: (u[j][0], g + begin, 0, 0), j),
                )
                for j in range(count)
            ]
            + [pl.BlockSpec(offsets.shape, lambda g, *u: (0, 0))],
            out_specs=[pl.BlockSpec((block, cycles), lambda g, *u: (g, 0))] * count,
            scratch_shapes=[pltpu.VMEM((block, cycles), f32)] * count,
        ),
        out_shape=[jax.ShapeDtypeStruct(((end - begin) * block, cycles), dtype) for dtype in dtypes],
        compiler_params=pltpu.CompilerParams(vmem_limit_bytes=VMEM_LIMIT),
        name="class_sums",
    )(*scalars, back, *[weighted] * count, offsets)


def across(piece):
    return lax.ppermute(piece, "dp", [(d, d ^ 1) for d in range(8)])


def along(piece, pairs):
    return lax.ppermute(piece, "dp", [(2 * a + x, 2 * b + x) for a, b in pairs for x in range(2)])


def gather_on_line(piece, base, ctf_rows):
    index = lax.axis_index("dp")
    line, side = index // 2, index % 2
    _, steps = spectra_steps(base.shape[0])
    cuts = [0, 3 * steps // 13, 8 * steps // 13, steps]

    own_crossed = across(piece)
    near = along(piece, ((0, 1), (1, 0), (2, 3), (3, 2)))
    middle = along(piece, ((1, 2), (2, 1)))
    weighted = make_spectra(base, ctf_rows, cuts[0], cuts[1])
    weighted, near, middle, own_crossed = lax.optimization_barrier((weighted, near, middle, own_crossed))
    near_crossed = across(near)
    far_middle = along(near, ((1, 2), (2, 1)))
    end = along(middle, ((1, 0), (2, 3)))
    weighted = make_spectra(base, ctf_rows, cuts[1], cuts[2], weighted)
    weighted, end = lax.optimization_barrier((weighted, end))
    weighted, near_crossed = lax.optimization_barrier((weighted, near_crossed))
    weighted, far_middle = lax.optimization_barrier((weighted, far_middle))
    third = middle + end
    third_crossed = across(third)
    far_end = along(far_middle, ((1, 0), (2, 3)))
    weighted = make_spectra(base, ctf_rows, cuts[2], cuts[3], weighted)
    weighted, far_end, third_crossed = lax.optimization_barrier((weighted, far_end, third_crossed))
    fourth = far_middle + far_end
    fourth_crossed = across(fourth)

    pieces = [piece, own_crossed, near, near_crossed, third, third_crossed, fourth, fourth_crossed]
    places = [line, line ^ 1, jnp.where(line < 2, 2, 1), jnp.where(line < 2, 3, 0)]
    slot_of = [2 * place + s for place in places for s in (side, 1 - side)]
    return weighted, pieces, slot_of


def reduce_on_line(back, weighted, offsets, classes):
    index = lax.axis_index("dp")
    line, side = index // 2, index % 2
    order = [jnp.where(line < 2, 3, 0), jnp.where(line < 2, 2, 1), line ^ 1, line]
    theirs = [2 * z + 1 - side for z in order]
    ours = [2 * z + side for z in order]
    groups = ((0, 1), (1, ROTS // GROUP))
    block = 2 * GROUP * classes
    head, rest = [slice(a * block, b * block) for a, b in groups]
    to_middle, between = ((0, 1), (3, 2)), ((1, 2), (2, 1))
    neighbours = ((0, 1), (1, 0), (2, 3), (3, 2))

    def sums(slots, dtypes, back, some=(0, ROTS // GROUP)):
        return class_sums_of(slots, back, weighted, offsets, classes, dtypes, some)

    def wide(piece):
        return piece.astype(f32)

    def then(back, *done):
        return lax.optimization_barrier((back, *done))[0]

    (away,) = sums(theirs[:1], [bf16], back, groups[0])
    crossed_head = across(away)
    back = then(back, away)
    (away,) = sums(theirs[:1], [bf16], back, groups[1])
    crossed_rest = across(away)
    back = then(back, away)
    own_0, away = sums([ours[0], theirs[1]], [f32, bf16], back)
    crossed_1 = across(away)
    crossed_head, own_0 = lax.optimization_barrier((crossed_head, own_0))
    message = (own_0[head] + wide(crossed_head)).astype(bf16)
    first_head = along(message, to_middle)
    back = then(back, message)
    own_1, away = sums([ours[1], theirs[2]], [f32, bf16], back)
    crossed_2 = across(away)
    crossed_rest, own_1 = lax.optimization_barrier((crossed_rest, own_1))
    message = (own_0[rest] + wide(crossed_rest)).astype(bf16)
    first_rest = along(message, to_middle)
    back = then(back, message)
    message = (own_0[head] + wide(crossed_head) + wide(first_head)).astype(bf16)
    middle_head = along(message, between)
    back = then(back, message)
    own_2, away = sums([ours[2], theirs[3]], [f32, bf16], back)
    crossed_3 = across(away)
    crossed_1, first_rest, middle_head, own_2 = lax.optimization_barrier(
        (crossed_1, first_rest, middle_head, own_2)
    )
    message = (own_1 + wide(crossed_1)).astype(bf16)
    from_end = along(message, to_middle)
    first_rest = then(first_rest, message)
    message = (own_0[rest] + wide(crossed_rest) + wide(first_rest)).astype(bf16)
    middle_rest = along(message, between)
    back = then(back, message)
    (own_3,) = sums(ours[3:], [f32], back)
    from_end = then(from_end, crossed_2)
    message = (own_1 + wide(crossed_1) + wide(from_end)).astype(bf16)
    third = along(message, between)
    middle_rest = then(middle_rest, message)
    middle = jnp.concatenate([middle_head, middle_rest], 0)
    last = along((own_2 + wide(crossed_2) + wide(middle)).astype(bf16), neighbours)
    return own_3 + wide(crossed_3) + wide(third) + wide(last)


def local(particles, references, ctf_table, rot_offset, prior_shift, defocus_group):
    count, _, angles, cycles = particles.shape
    own_rows, _, classes, _ = references.shape
    slots = angles // ROTS
    group_count = ctf_table.shape[0]
    devices = lax.axis_size("dp")

    first = (lax.axis_index("dp") * own_rows).astype(jnp.int32).reshape(1)
    rows = jnp.transpose(references, (0, 2, 1, 3)).reshape(own_rows * 2 * classes, cycles)
    piece, offsets = turn_references(first, rot_offset, rows)

    onehot = (defocus_group[:, None] == jnp.arange(group_count, dtype=jnp.int32)[None, :]).astype(f32)
    ctf_rows = jnp.dot(onehot, ctf_table, precision=lax.Precision.HIGHEST)
    base = make_base(particles, prior_shift)
    on_line = devices == 8 and own_rows == ROTS
    if on_line:
        weighted, pieces, slot_of = gather_on_line(piece, base, ctf_rows)
    else:
        gathered = lax.all_gather(piece, "dp", axis=0, tiled=True)
        gathered = gathered.reshape(slots, ROTS * 2 * classes, cycles)
        pieces = [gathered[j] for j in range(slots)]
        slot_of = list(range(slots))
        weighted = make_spectra(base, ctf_rows, 0, spectra_steps(count)[1])
    queries = weighted.shape[1]
    weighted = weighted.reshape(slots, ROTS, queries, 2 * cycles)

    early = slots - 1
    part = lax.axis_index("cls")
    corr, power = correlate(slot_of[:early], weighted, pieces[:early], classes, part)
    weights, stat, share = correlate(
        slot_of[early:], weighted, pieces[early:], classes, part, corr, power, ctf_rows, lax.axis_size("cls")
    )
    shares = lax.psum(share, "cls")
    back, evidence, posterior = make_back(weights, stat, shares, offsets, queries)
    log_evidence = evidence[0, :count]
    class_posterior = posterior[:classes, :count].T
    if on_line:
        class_rows = reduce_on_line(back, weighted, offsets, classes)
    else:
        sums = [class_sums_of([u], back, weighted, offsets, classes, [bf16])[0] for u in slot_of]
        summed = lax.psum_scatter(jnp.concatenate(sums, 0), "dp", scatter_dimension=0, tiled=True)
        class_rows = summed.astype(f32)
    class_sums = jnp.transpose(class_rows.reshape(own_rows, classes, 2, cycles), (0, 2, 1, 3))
    return (log_evidence, class_posterior, class_sums)


def solution(mesh):
    placed = (
        P("dp", None, None, None),
        P("dp", None, "cls", None),
        P(),
        P("cls"),
        P("dp", None),
        P("dp"),
    )
    return jax.shard_map(
        local,
        mesh=mesh,
        in_specs=placed,
        out_specs=(P("dp"), P("dp", "cls"), P("dp", None, "cls", None)),
        check_vma=False,
    )
```

```python
import functools
import math

import jax
import jax.numpy as jnp
import ml_dtypes
import numpy as np
from jax import lax
from jax.experimental import pallas as pl
from jax.experimental.pallas import tpu as pltpu
from jax.sharding import PartitionSpec as P

ROTS = 36
ANG_STEP = 8
SHIFT_SIDE = 5
SHIFTS = SHIFT_SIDE * SHIFT_SIDE
LANES = 128
GROUP = 12
ROWS = 16
APART = 17
FOLD = ROTS // 2 + 1

two_pi = 2.0 * math.pi
f32 = jnp.float32
bf16 = jnp.bfloat16
VMEM_LIMIT = 56 * 1024 * 1024


def fourier_rows(angles):
    index_grid = np.arange(angles)
    radians = (index_grid[:, None] * index_grid[None, :] % angles) * (two_pi / angles)
    cosine, sine_part = np.cos(radians), np.sin(radians)
    table_full = np.concatenate(
        [np.concatenate([cosine, sine_part], 1), np.concatenate([-sine_part, cosine], 1)], 0
    )
    return table_full.astype(np.float32).astype(ml_dtypes.bfloat16)


def shift_tables(angles, cycles):
    theta = np.arange(angles) * (two_pi / angles)
    radius = (np.arange(cycles) + 1) / (2.0 * cycles)
    turns = np.stack([np.cos(theta), np.sin(theta)])[:, :, None] * radius
    steps = np.arange(SHIFT_SIDE) - SHIFT_SIDE // 2
    phase = two_pi * turns[:, None] * steps[None, :, None, None]
    factors = np.stack([np.cos(phase), -np.sin(phase)], 2)
    return turns.astype(np.float32), factors.astype(np.float32)


def cos_sin_of_turns(turns):
    frac = turns - jnp.floor(turns + 0.5)
    w = frac * two_pi
    w2 = w * w
    cosine = jnp.full_like(w, 1.0 / math.factorial(16))
    for n in range(14, -1, -2):
        cosine = cosine * w2 + (-1.0) ** (n // 2) / math.factorial(n)
    sine_part = jnp.full_like(w, 1.0 / math.factorial(17))
    for n in range(15, 0, -2):
        sine_part = sine_part * w2 + (-1.0) ** (n // 2) / math.factorial(n)
    return cosine, sine_part * w


def base_kernel(shift_ref, part_ref, turns_ref, base_ref):
    here, _, angles, _ = part_ref.shape
    chunk = 32
    for q in range(here):
        p = pl.program_id(0) * here + q
        sx = shift_ref[0, p].astype(f32)
        sy = shift_ref[1, p].astype(f32)

        def turn(n, carry):
            rows = pl.ds(pl.multiple_of(n * chunk, chunk), chunk)
            cosine, sine_part = cos_sin_of_turns(sx * turns_ref[0, rows, :] + sy * turns_ref[1, rows, :])
            re = part_ref[q, 0, rows, :].astype(f32)
            im = part_ref[q, 1, rows, :].astype(f32)
            base_ref[q, 0, rows, :] = re * cosine + im * sine_part
            base_ref[q, 1, rows, :] = im * cosine - re * sine_part
            return carry

        lax.fori_loop(0, angles // chunk, turn, 0)


def make_base(particles, prior_shift):
    count, _, angles, cycles = particles.shape
    turns, _ = shift_tables(angles, cycles)
    here = count // 2
    image = pl.BlockSpec((here, 2, angles, cycles), lambda p: (p, 0, 0, 0))
    return pl.pallas_call(
        base_kernel,
        grid=(2,),
        in_specs=[
            pl.BlockSpec(memory_space=pltpu.SMEM),
            image,
            pl.BlockSpec(turns.shape, lambda p: (0, 0, 0)),
        ],
        out_specs=image,
        out_shape=jax.ShapeDtypeStruct(particles.shape, f32),
        compiler_params=pltpu.CompilerParams(vmem_limit_bytes=VMEM_LIMIT),
        name="centre",
    )(prior_shift.T, particles, turns)


def spectra_kernel(base_ref, ctf_ref, table_ref, *refs, per_step):
    factor_refs, refs = refs[: 2 * per_step], refs[2 * per_step :]
    chunks = ROWS // 2
    out_ref, turn_ref, re_ref, im_ref = refs[-4 - chunks : -chunks]
    data_refs = refs[-chunks:]
    count, _, angles, cycles = base_ref.shape
    chunk = 32

    for g in range(per_step):
        x_ref, y_ref = factor_refs[2 * g], factor_refs[2 * g + 1]
        for start in range(0, angles, chunk):
            rows = slice(start, start + chunk)
            xr, xi = x_ref[0, 0, 0, rows, :], x_ref[0, 0, 1, rows, :]
            yr, yi = y_ref[0, 0, 0, rows, :], y_ref[0, 0, 1, rows, :]
            turn_ref[g, 0, rows, :] = xr * yr - xi * yi
            turn_ref[g, 1, rows, :] = xr * yi + xi * yr

    def shift(n):
        for j in range(2):
            g, p = (2 * n + j) // count, (2 * n + j) % count
            lanes = slice(j * cycles, (j + 1) * cycles)
            for start in range(0, angles, chunk):
                rows = slice(start, start + chunk)
                tr, ti = turn_ref[g, 0, rows, :], turn_ref[g, 1, rows, :]
                gr, gi = base_ref[p, 0, rows, :], base_ref[p, 1, rows, :]
                data_refs[n][rows, lanes] = (gr * tr - gi * ti).astype(bf16)
                data_refs[n][angles + start : angles + start + chunk, lanes] = (gr * ti + gi * tr).astype(bf16)

    shift(0)
    for n in range(chunks):
        if n + 1 < chunks:
            shift(n + 1)
        spectrum = jnp.dot(table_ref[...], data_refs[n][...], preferred_element_type=f32)
        for j in range(2):
            row = 2 * n + j
            ctf_row = ctf_ref[row % count, :][None, :]
            part = spectrum[:, j * cycles : (j + 1) * cycles] * ctf_row
            re_ref[pl.ds(row, angles, stride=APART), :] = part[:angles]
            im_ref[pl.ds(row, angles, stride=APART), :] = part[angles:]
    for m in range(angles):
        out_ref[m, :, :cycles] = re_ref[m * APART : m * APART + ROWS, :].astype(bf16)
        out_ref[m, :, cycles:] = im_ref[m * APART : m * APART + ROWS, :].astype(bf16)


def spectra_steps(count):
    per_step = ROWS // count if count < ROWS else 1
    return per_step, -(-SHIFTS // per_step)


def make_spectra(base, ctf_rows, first, last, before=None, after=()):
    count, _, angles, cycles = base.shape
    per_step, steps = spectra_steps(count)
    _, factors = shift_tables(angles, cycles)
    full = lambda shape: pl.BlockSpec(shape, lambda i: (0,) * len(shape))

    def factor_spec(g, axis):
        def place(i):
            s = jnp.minimum((i + first) * per_step + g, SHIFTS - 1)
            a = lax.div(s, jnp.int32(SHIFT_SIDE))
            return (axis, s - a * SHIFT_SIDE if axis else a, 0, 0, 0)

        return pl.BlockSpec((1, 1, 2, angles, cycles), place)

    untouched = ([] if before is None else [before]) + list(after)
    in_specs = (
        [full(base.shape), full(ctf_rows.shape), full((2 * angles, 2 * angles))]
        + [factor_spec(g, axis) for g in range(per_step) for axis in range(2)]
        + [pl.BlockSpec(memory_space=pl.ANY)] * len(untouched)
    )
    return pl.pallas_call(
        functools.partial(spectra_kernel, per_step=per_step),
        grid=(last - first,),
        in_specs=in_specs,
        out_specs=pl.BlockSpec((angles, ROWS, 2 * cycles), lambda i: (0, i + first, 0)),
        out_shape=jax.ShapeDtypeStruct((angles, steps * ROWS, 2 * cycles), bf16),
        scratch_shapes=[
            pltpu.VMEM((per_step, 2, angles, cycles), f32),
            pltpu.VMEM((angles * APART, cycles), f32),
            pltpu.VMEM((angles * APART, cycles), f32),
        ]
        + [pltpu.VMEM((2 * angles, 2 * cycles), bf16)] * (ROWS // 2),
        input_output_aliases={} if before is None else {3 + 2 * per_step: 0},
        compiler_params=pltpu.CompilerParams(vmem_limit_bytes=VMEM_LIMIT),
        name="spectra",
    )(base, ctf_rows, fourier_rows(angles), *[factors] * (2 * per_step), *untouched)


def half_dft(even_values, odd_values):
    half = FOLD // 2
    cos_sums, sin_sums = [None] * FOLD, [None] * FOLD

    def weighted_sum(values, k, table, start):
        total = None
        for m in range(start, FOLD, 2):
            weight = float(table((k * m % ROTS) * two_pi / ROTS))
            if values[m] is None or abs(weight) < 1e-9:
                continue
            if abs(abs(weight) - 1.0) < 1e-9:
                term = values[m] if weight > 0 else -values[m]
            else:
                term = values[m] * weight
            total = term if total is None else total + term
        return jnp.zeros_like(values[1]) if total is None else total

    for k in range(half + 1):
        even = weighted_sum(even_values, k, math.cos, 0)
        odd = weighted_sum(even_values, k, math.cos, 1)
        cos_sums[k] = even + odd
        if k != half:
            cos_sums[FOLD - 1 - k] = even - odd
        if k:
            even = weighted_sum(odd_values, k, math.sin, 0)
            odd = weighted_sum(odd_values, k, math.sin, 1)
            sin_sums[k] = even + odd
            if k != half:
                sin_sums[FOLD - 1 - k] = odd - even
    return cos_sums, sin_sums


def turn_kernel(first_ref, offset_ref, references_ref, out_ref, column_ref, in_ref, wide_ref):
    rows, cycles = references_ref.shape
    classes = offset_ref.shape[0]
    own_rows = rows // (2 * classes)
    in_ref[...] = references_ref[...].astype(f32)
    row = lax.broadcasted_iota(jnp.int32, (8, LANES), 0)
    lane = lax.broadcasted_iota(jnp.int32, (8, LANES), 1)
    freq = (lane + first_ref[0]).astype(f32) * (1.0 / (ROTS * ANG_STEP))
    tables = []
    for start in range(0, classes, 8):
        column = jnp.zeros((8, LANES), jnp.int32)
        for c in range(start, min(start + 8, classes)):
            column = jnp.where(row == c - start, offset_ref[c], column)
        column = column.astype(f32)
        column_ref[start : start + 8, :] = column
        tables.append(cos_sin_of_turns(column * freq))
    cosine = jnp.concatenate([c for c, _ in tables], 0)
    sine_part = jnp.concatenate([s for _, s in tables], 0)
    for m in range(own_rows):
        re_rows = pl.ds(2 * m * classes, classes, stride=2)
        im_rows = pl.ds(2 * m * classes + 1, classes, stride=2)
        c, s = cosine[:classes, m : m + 1], sine_part[:classes, m : m + 1]
        re, im = in_ref[re_rows, :], in_ref[im_rows, :]
        wide_ref[re_rows, :] = re * c + im * s
        wide_ref[im_rows, :] = im * c - re * s
    out_ref[...] = wide_ref[...].astype(bf16)


def turn_references(first, offsets, references):
    padded = -(-offsets.shape[0] // 8) * 8
    return pl.pallas_call(
        turn_kernel,
        in_specs=[
            pl.BlockSpec(memory_space=pltpu.SMEM),
            pl.BlockSpec(memory_space=pltpu.SMEM),
            pl.BlockSpec(memory_space=pltpu.VMEM),
        ],
        out_shape=[
            jax.ShapeDtypeStruct(references.shape, bf16),
            jax.ShapeDtypeStruct((padded, LANES), f32),
        ],
        scratch_shapes=[pltpu.VMEM(references.shape, f32)] * 2,
        compiler_params=pltpu.CompilerParams(vmem_limit_bytes=VMEM_LIMIT),
        name="turn_references",
    )(first, offsets, references)


def correlate_kernel(*refs, slots, classes, padded, finish):
    part_ref, refs = refs[slots], refs[slots + 1 :]
    weighted_refs, refs = refs[:slots], refs[slots:]
    piece_refs, refs = refs[:slots], refs[slots:]
    if finish:
        before_ref, power_before_ref, ctf_ref, weight_ref, stat_ref, share_ref = refs[:6]
        corr_ref, wide_ref, power_ref = refs[6:]
    else:
        corr_ref, power_ref, wide_ref = refs
    group = pl.program_id(0)
    cycles = piece_refs[0].shape[1]
    queries = weighted_refs[0].shape[2]
    block = piece_refs[0].shape[0]

    @pl.when(group == 0)
    def _():
        wide_ref[:, block:, :] = jnp.zeros((slots, wide_ref.shape[1] - block, cycles), f32)
        power_ref[...] = power_before_ref[...] if finish else jnp.zeros_like(power_ref)

    for j in range(slots):
        wide_ref[j, :block, :] = piece_refs[j][...].astype(f32)
    power = power_ref[...]
    for i in range(GROUP):
        total = before_ref[i, :, :queries] if finish else None
        for j in range(slots):
            re = wide_ref[j, pl.ds(2 * i * classes, padded, stride=2), :]
            im = wide_ref[j, pl.ds(2 * i * classes + 1, padded, stride=2), :]
            power = power + (re * re + im * im)
            left = jnp.concatenate(
                [jnp.concatenate([re, im], 1), jnp.concatenate([-im, re], 1)], 0
            ).astype(bf16)
            part = lax.dot_general(
                left, weighted_refs[j][0, i], (((1,), (1,)), ((), ())), preferred_element_type=f32
            )
            total = part if total is None else total + part
        row = group * GROUP + i if finish else i
        corr_ref[row, :, :queries] = total
    power_ref[...] = power

    if not finish:
        return

    @pl.when(group == pl.num_programs(0) - 1)
    def _():
        count = ctf_ref.shape[0]
        angles = ROTS * ANG_STEP
        used = SHIFTS * count
        tiles = weight_ref.shape[2] // LANES
        ctf_row = ctf_ref[...]
        ctf_rows = jnp.concatenate([ctf_row * ctf_row] * (LANES // count), 0)
        bias = lax.dot_general(
            power_ref[...],
            ctf_rows,
            (((1,), (1,)), ((), ())),
            precision=lax.Precision.HIGHEST,
            preferred_element_type=f32,
        ) * (0.5 / angles)
        wide_ref[0, :padded, :] = bias
        rows_of = lambda base: lax.broadcasted_iota(jnp.int32, (8, LANES), 0) + base
        lanes_of = lambda base: lax.broadcasted_iota(jnp.int32, (8, LANES), 1) + base

        peak = jnp.full((8, LANES), -1e30, f32)
        for tile in range(tiles):
            lanes = slice(tile * LANES, (tile + 1) * LANES)

            def scores(n, peak):
                start = pl.multiple_of(n * 8, 8)
                rows = pl.ds(start, 8)
                low = pl.ds(padded + start, 8)
                valid = (rows_of(start) < classes) & (lanes_of(tile * LANES) < used)
                even_values = [corr_ref[0, rows, lanes]]
                odd_values = [None]
                for m in range(1, ROTS // 2):
                    even_values.append(corr_ref[m, rows, lanes] + corr_ref[ROTS - m, rows, lanes])
                    odd_values.append(corr_ref[m, low, lanes] - corr_ref[ROTS - m, low, lanes])
                even_values.append(corr_ref[ROTS // 2, rows, lanes])
                odd_values.append(None)
                cos_sums, sin_sums = half_dft(even_values, odd_values)
                bias = wide_ref[0, rows, :]
                for k in range(FOLD):
                    if k in (0, FOLD - 1):
                        results = [(k, cos_sums[k])]
                    else:
                        results = [(k, cos_sums[k] - sin_sums[k]), (ROTS - k, cos_sums[k] + sin_sums[k])]
                    for place, value in results:
                        value = jnp.where(valid, value * (1.0 / angles) - bias, -1e30)
                        weight_ref[place, rows, lanes] = value
                        peak = jnp.maximum(peak, value)
                return peak

            peak = lax.fori_loop(0, padded // 8, scores, peak)

        peak = jnp.broadcast_to(jnp.max(peak, axis=0, keepdims=True), (8, LANES))
        step = count
        while step < LANES:
            peak = jnp.maximum(peak, pltpu.roll(peak, step, 1))
            step *= 2
        stat_ref[0:8, :] = peak

        def masses(n, whole):
            rows = pl.ds(pl.multiple_of(n * 8, 8), 8)
            mass = jnp.zeros((8, LANES), f32)
            for tile in range(tiles):
                lanes = slice(tile * LANES, (tile + 1) * LANES)
                for k in range(ROTS):
                    value = jnp.exp(weight_ref[k, rows, lanes] - peak)
                    weight_ref[k, rows, lanes] = value
                    mass = mass + value
            step = count
            while step < LANES:
                mass = mass + pltpu.roll(mass, step, 1)
                step *= 2
            stat_ref[pl.ds(pl.multiple_of(8 + n * 8, 8), 8), :] = mass
            return whole + mass

        whole = lax.fori_loop(0, padded // 8, masses, jnp.zeros((8, LANES), f32))
        share = jnp.concatenate([peak[:1], jnp.sum(whole, axis=0, keepdims=True)], 0)
        for j in range(share_ref.shape[0]):
            share_ref[j] = jnp.where(part_ref[0] == j, share, 0.0)


def correlate(slot_of, weighted, pieces, classes, part, before=None, power=None, ctf_rows=None, parts=1):
    _, _, queries, double = weighted.shape
    cycles = double // 2
    slots = len(pieces)
    padded = -(-classes // 8) * 8
    wide_lanes = -(-queries // LANES) * LANES
    block = 2 * GROUP * classes
    finish = ctf_rows is not None
    full = lambda shape: pl.BlockSpec(shape, lambda g, *u: (0,) * len(shape))
    in_specs = [
        pl.BlockSpec((1, GROUP, queries, double), functools.partial(lambda j, g, *u: (u[j][0], g, 0, 0), j))
        for j in range(slots)
    ] + [pl.BlockSpec((block, cycles), lambda g, *u: (g, 0))] * slots
    corr_block = pl.BlockSpec((GROUP, 2 * padded, wide_lanes), lambda g, *u: (g, 0, 0))
    corr_shape = (ROTS, 2 * padded, wide_lanes)
    wide = pltpu.VMEM((slots, block + ROWS, cycles), f32)
    scalars = [jnp.reshape(n, (1,)).astype(jnp.int32) for n in (*slot_of, part)]
    operands = scalars + [weighted] * slots + list(pieces)
    if finish:
        in_specs += [corr_block, full((padded, cycles)), full(ctf_rows.shape)]
        operands += [before, power, ctf_rows]
        out_shapes = [(ROTS, padded, wide_lanes), (8 + padded, LANES), (parts, 2, LANES)]
        out_specs = [full(shape) for shape in out_shapes]
        scratch = [pltpu.VMEM(corr_shape, f32), wide, pltpu.VMEM((padded, cycles), f32)]
    else:
        out_shapes = [corr_shape, (padded, cycles)]
        out_specs = [corr_block, full((padded, cycles))]
        scratch = [wide]
    return pl.pallas_call(
        functools.partial(correlate_kernel, slots=slots, classes=classes, padded=padded, finish=finish),
        grid_spec=pltpu.PrefetchScalarGridSpec(
            num_scalar_prefetch=len(scalars),
            grid=(ROTS // GROUP,),
            in_specs=in_specs,
            out_specs=out_specs,
            scratch_shapes=scratch,
        ),
        out_shape=[jax.ShapeDtypeStruct(shape, f32) for shape in out_shapes],
        compiler_params=pltpu.CompilerParams(vmem_limit_bytes=VMEM_LIMIT),
        name="scores" if finish else "correlate",
    )(*operands)


def back_kernel(weight_ref, stat_ref, share_ref, offset_ref, out_ref, evidence_ref, posterior_ref, sum_ref):
    padded = weight_ref.shape[1]
    queries = out_ref.shape[2]
    shares = [share_ref[j] for j in range(share_ref.shape[0])]
    top = shares[0][:1]
    for share in shares[1:]:
        top = jnp.maximum(top, share[:1])
    mass = sum(share[1:] * jnp.exp(share[:1] - top) for share in shares)
    evidence = jnp.broadcast_to(top + jnp.log(mass), (8, LANES))
    scale = jnp.exp(stat_ref[:8, :] - evidence)
    evidence_ref[...] = evidence
    posterior_ref[...] = stat_ref[8:, :] * scale[:1]
    for tile in range(weight_ref.shape[2] // LANES):
        lanes = slice(tile * LANES, (tile + 1) * LANES)

        def transform(n, carry):
            start = pl.multiple_of(n * 8, 8)
            rows = pl.ds(start, 8)
            low = pl.ds(padded + start, 8)
            values = [weight_ref[k, rows, lanes] * scale for k in range(ROTS)]
            even_values = [values[0]] + [values[k] + values[ROTS - k] for k in range(1, ROTS // 2)]
            odd_values = [None] + [values[k] - values[ROTS - k] for k in range(1, ROTS // 2)] + [None]
            cos_sums, sin_sums = half_dft(even_values + [values[ROTS // 2]], odd_values)
            for m in range(FOLD):
                sine_part = jnp.zeros_like(scale) if m in (0, FOLD - 1) else sin_sums[m]
                sum_ref[m, rows, lanes] = cos_sums[m]
                sum_ref[m, low, lanes] = sine_part
                if m not in (0, FOLD - 1):
                    sum_ref[ROTS - m, rows, lanes] = cos_sums[m]
                    sum_ref[ROTS - m, low, lanes] = -sine_part
            return carry

        lax.fori_loop(0, padded // 8, transform, 0)

    step_cos, step_sin = cos_sin_of_turns(offset_ref[...] * (1.0 / (ROTS * ANG_STEP)))

    def turn(m, carry):
        cosine, sine_part = carry
        for tile in range(weight_ref.shape[2] // LANES):
            lanes = slice(tile * LANES, (tile + 1) * LANES)
            kept = slice(tile * LANES, min((tile + 1) * LANES, queries))
            re, im = sum_ref[m, :padded, lanes], sum_ref[m, padded:, lanes]
            turned = jnp.concatenate([re * cosine - im * sine_part, re * sine_part + im * cosine], 0)
            out_ref[m, :, kept] = turned[:, : kept.stop - kept.start].astype(bf16)
        return cosine * step_cos - sine_part * step_sin, sine_part * step_cos + cosine * step_sin

    lax.fori_loop(0, ROTS, turn, (jnp.ones_like(step_cos), jnp.zeros_like(step_cos)))


def make_back(weights, stat, shares, offsets, queries):
    _, padded, wide_lanes = weights.shape
    return pl.pallas_call(
        back_kernel,
        out_shape=[
            jax.ShapeDtypeStruct((ROTS, 2 * padded, queries), bf16),
            jax.ShapeDtypeStruct((8, LANES), f32),
            jax.ShapeDtypeStruct((padded, LANES), f32),
        ],
        scratch_shapes=[pltpu.VMEM((ROTS, 2 * padded, wide_lanes), f32)],
        compiler_params=pltpu.CompilerParams(vmem_limit_bytes=VMEM_LIMIT),
        name="back",
    )(weights, stat, shares, offsets)


def sums_kernel(*refs, count, classes):
    slot_refs, (back_ref, *refs) = refs[:count], refs[count:]
    weighted_refs, (offset_ref, *refs) = refs[:count], refs[count:]
    out_refs, wide_refs = refs[:count], refs[count:]
    padded = offset_ref.shape[0]
    cycles = wide_refs[0].shape[1]
    turns = [
        cos_sin_of_turns(offset_ref[...] * (slot_ref[0].astype(f32) * (1.0 / ANG_STEP)))
        for slot_ref in slot_refs
    ]
    for i in range(GROUP):
        for (cosine, sine_part), weighted_ref, wide_ref in zip(turns, weighted_refs, wide_refs):
            product = jnp.dot(back_ref[i], weighted_ref[0, i], preferred_element_type=f32)
            re = product[:padded, :cycles] - product[padded:, cycles:]
            im = product[:padded, cycles:] + product[padded:, :cycles]
            start = 2 * i * classes
            wide_ref[pl.ds(start, classes, stride=2), :] = (re * cosine - im * sine_part)[:classes]
            wide_ref[pl.ds(start + 1, classes, stride=2), :] = (re * sine_part + im * cosine)[:classes]
    for out_ref, wide_ref in zip(out_refs, wide_refs):
        out_ref[...] = wide_ref[...].astype(out_ref.dtype)


def class_sums_of(slots, back, weighted, offsets, classes, dtypes, groups=(0, ROTS // GROUP)):
    begin, end = groups
    _, _, queries, double = weighted.shape
    cycles = double // 2
    rows = back.shape[1]
    block = 2 * GROUP * classes
    count = len(slots)
    scalars = [jnp.reshape(slot, (1,)).astype(jnp.int32) for slot in slots]
    return pl.pallas_call(
        functools.partial(sums_kernel, count=count, classes=classes),
        grid_spec=pltpu.PrefetchScalarGridSpec(
            num_scalar_prefetch=count,
            grid=(end - begin,),
            in_specs=[pl.BlockSpec((GROUP, rows, queries), lambda g, *u: (g + begin, 0, 0))]
            + [
                pl.BlockSpec(
                    (1, GROUP, queries, double),
                    functools.partial(lambda j, g, *u: (u[j][0], g + begin, 0, 0), j),
                )
                for j in range(count)
            ]
            + [pl.BlockSpec(offsets.shape, lambda g, *u: (0, 0))],
            out_specs=[pl.BlockSpec((block, cycles), lambda g, *u: (g, 0))] * count,
            scratch_shapes=[pltpu.VMEM((block, cycles), f32)] * count,
        ),
        out_shape=[jax.ShapeDtypeStruct(((end - begin) * block, cycles), dtype) for dtype in dtypes],
        compiler_params=pltpu.CompilerParams(vmem_limit_bytes=VMEM_LIMIT),
        name="class_sums",
    )(*scalars, back, *[weighted] * count, offsets)


def across(piece):
    return lax.ppermute(piece, "dp", [(d, d ^ 1) for d in range(8)])


def along(piece, pairs):
    return lax.ppermute(piece, "dp", [(2 * a + x, 2 * b + x) for a, b in pairs for x in range(2)])


def gather_on_line(piece, base, ctf_rows):
    index = lax.axis_index("dp")
    line, side = index // 2, index % 2
    _, steps = spectra_steps(base.shape[0])
    cuts = [0, 3 * steps // 13, 8 * steps // 13, steps]

    own_crossed = across(piece)
    near = along(piece, ((0, 1), (1, 0), (2, 3), (3, 2)))
    middle = along(piece, ((1, 2), (2, 1)))
    weighted = make_spectra(base, ctf_rows, cuts[0], cuts[1])
    weighted, own_crossed = lax.optimization_barrier((weighted, own_crossed))
    weighted, near, middle = lax.optimization_barrier((weighted, near, middle))
    near_crossed = across(near)
    far_middle = along(near, ((1, 2), (2, 1)))
    end = along(middle, ((1, 0), (2, 3)))
    weighted = make_spectra(base, ctf_rows, cuts[1], cuts[2], weighted)
    weighted, end = lax.optimization_barrier((weighted, end))
    weighted, near_crossed = lax.optimization_barrier((weighted, near_crossed))
    weighted, far_middle = lax.optimization_barrier((weighted, far_middle))
    third = middle + end
    third_crossed = across(third)
    far_end = along(far_middle, ((1, 0), (2, 3)))
    weighted = make_spectra(base, ctf_rows, cuts[2], cuts[3], weighted)
    weighted, far_end, third_crossed = lax.optimization_barrier((weighted, far_end, third_crossed))
    fourth = far_middle + far_end
    fourth_crossed = across(fourth)

    pieces = [piece, own_crossed, near, near_crossed, third, third_crossed, fourth, fourth_crossed]
    places = [line, line ^ 1, jnp.where(line < 2, 2, 1), jnp.where(line < 2, 3, 0)]
    slot_of = [2 * place + s for place in places for s in (side, 1 - side)]
    return weighted, pieces, slot_of


def reduce_on_line(back, weighted, offsets, classes):
    index = lax.axis_index("dp")
    line, side = index // 2, index % 2
    order = [jnp.where(line < 2, 3, 0), jnp.where(line < 2, 2, 1), line ^ 1, line]
    theirs = [2 * z + 1 - side for z in order]
    ours = [2 * z + side for z in order]
    groups = ((0, 1), (1, ROTS // GROUP))
    block = 2 * GROUP * classes
    head, rest = [slice(a * block, b * block) for a, b in groups]
    to_middle, between = ((0, 1), (3, 2)), ((1, 2), (2, 1))
    neighbours = ((0, 1), (1, 0), (2, 3), (3, 2))

    def sums(slots, dtypes, back, some=(0, ROTS // GROUP)):
        return class_sums_of(slots, back, weighted, offsets, classes, dtypes, some)

    def wide(piece):
        return piece.astype(f32)

    def then(back, *done):
        return lax.optimization_barrier((back, *done))[0]

    (away,) = sums(theirs[:1], [bf16], back, groups[0])
    crossed_head = across(away)
    back = then(back, away)
    (away,) = sums(theirs[:1], [bf16], back, groups[1])
    crossed_rest = across(away)
    back = then(back, away)
    own_0, away = sums([ours[0], theirs[1]], [f32, bf16], back)
    crossed_1 = across(away)
    crossed_head, own_0 = lax.optimization_barrier((crossed_head, own_0))
    message = (own_0[head] + wide(crossed_head)).astype(bf16)
    first_head = along(message, to_middle)
    back = then(back, message)
    own_1, away = sums([ours[1], theirs[2]], [f32, bf16], back)
    crossed_2 = across(away)
    crossed_rest, own_1 = lax.optimization_barrier((crossed_rest, own_1))
    message = (own_0[rest] + wide(crossed_rest)).astype(bf16)
    first_rest = along(message, to_middle)
    back = then(back, message)
    first_head = then(first_head, message)
    message = (own_0[head] + wide(crossed_head) + wide(first_head)).astype(bf16)
    middle_head = along(message, between)
    back = then(back, message)
    own_2, away = sums([ours[2], theirs[3]], [f32, bf16], back)
    crossed_3 = across(away)
    crossed_1, middle_head, own_2 = lax.optimization_barrier((crossed_1, middle_head, own_2))
    message = (own_1 + wide(crossed_1)).astype(bf16)
    from_end = along(message, to_middle)
    first_rest = then(first_rest, message)
    message = (own_0[rest] + wide(crossed_rest) + wide(first_rest)).astype(bf16)
    middle_rest = along(message, between)
    back = then(back, message)
    (own_3,) = sums(ours[3:], [f32], back)
    from_end = then(from_end, crossed_2)
    message = (own_1 + wide(crossed_1) + wide(from_end)).astype(bf16)
    third = along(message, between)
    middle_rest = then(middle_rest, message)
    middle = jnp.concatenate([middle_head, middle_rest], 0)
    last = along((own_2 + wide(crossed_2) + wide(middle)).astype(bf16), neighbours)
    return own_3 + wide(crossed_3) + wide(third) + wide(last)


def local(particles, references, ctf_table, rot_offset, prior_shift, defocus_group):
    count, _, angles, cycles = particles.shape
    own_rows, _, classes, _ = references.shape
    slots = angles // ROTS
    group_count = ctf_table.shape[0]
    devices = lax.axis_size("dp")

    first = (lax.axis_index("dp") * own_rows).astype(jnp.int32).reshape(1)
    rows = jnp.transpose(references, (0, 2, 1, 3)).reshape(own_rows * 2 * classes, cycles)
    piece, offsets = turn_references(first, rot_offset, rows)

    onehot = (defocus_group[:, None] == jnp.arange(group_count, dtype=jnp.int32)[None, :]).astype(f32)
    ctf_rows = jnp.dot(onehot, ctf_table, precision=lax.Precision.HIGHEST)
    base = make_base(particles, prior_shift)
    on_line = devices == 8 and own_rows == ROTS
    if on_line:
        weighted, pieces, slot_of = gather_on_line(piece, base, ctf_rows)
    else:
        gathered = lax.all_gather(piece, "dp", axis=0, tiled=True)
        gathered = gathered.reshape(slots, ROTS * 2 * classes, cycles)
        pieces = [gathered[j] for j in range(slots)]
        slot_of = list(range(slots))
        weighted = make_spectra(base, ctf_rows, 0, spectra_steps(count)[1])
    queries = weighted.shape[1]
    weighted = weighted.reshape(slots, ROTS, queries, 2 * cycles)

    early = slots - 1
    part = lax.axis_index("cls")
    corr, power = correlate(slot_of[:early], weighted, pieces[:early], classes, part)
    weights, stat, share = correlate(
        slot_of[early:], weighted, pieces[early:], classes, part, corr, power, ctf_rows, lax.axis_size("cls")
    )
    shares = lax.psum(share, "cls")
    back, evidence, posterior = make_back(weights, stat, shares, offsets, queries)
    log_evidence = evidence[0, :count]
    class_posterior = posterior[:classes, :count].T
    if on_line:
        class_rows = reduce_on_line(back, weighted, offsets, classes)
    else:
        sums = [class_sums_of([u], back, weighted, offsets, classes, [bf16])[0] for u in slot_of]
        summed = lax.psum_scatter(jnp.concatenate(sums, 0), "dp", scatter_dimension=0, tiled=True)
        class_rows = summed.astype(f32)
    class_sums = jnp.transpose(class_rows.reshape(own_rows, classes, 2, cycles), (0, 2, 1, 3))
    return (log_evidence, class_posterior, class_sums)


def solution(mesh):
    placed = (
        P("dp", None, None, None),
        P("dp", None, "cls", None),
        P(),
        P("cls"),
        P("dp", None),
        P("dp"),
    )
    return jax.shard_map(
        local,
        mesh=mesh,
        in_specs=placed,
        out_specs=(P("dp"), P("dp", "cls"), P("dp", None, "cls", None)),
        check_vma=False,
    )
```

```python
import functools
import math

import jax
import jax.numpy as jnp
import ml_dtypes
import numpy as np
from jax import lax
from jax.experimental import pallas as pl
from jax.experimental.pallas import tpu as pltpu
from jax.sharding import PartitionSpec as P

ROTS = 36
ANG_STEP = 8
SHIFT_SIDE = 5
SHIFTS = SHIFT_SIDE * SHIFT_SIDE
LANES = 128
GROUP = 12
ROWS = 16
APART = 17
FOLD = ROTS // 2 + 1

two_pi = 2.0 * math.pi
f32 = jnp.float32
bf16 = jnp.bfloat16
VMEM_LIMIT = 56 * 1024 * 1024


def fourier_rows(angles):
    index_grid = np.arange(angles)
    radians = (index_grid[:, None] * index_grid[None, :] % angles) * (two_pi / angles)
    cosine, sine_part = np.cos(radians), np.sin(radians)
    table_full = np.concatenate(
        [np.concatenate([cosine, sine_part], 1), np.concatenate([-sine_part, cosine], 1)], 0
    )
    return table_full.astype(np.float32).astype(ml_dtypes.bfloat16)


def shift_tables(angles, cycles):
    theta = np.arange(angles) * (two_pi / angles)
    radius = (np.arange(cycles) + 1) / (2.0 * cycles)
    turns = np.stack([np.cos(theta), np.sin(theta)])[:, :, None] * radius
    steps = np.arange(SHIFT_SIDE) - SHIFT_SIDE // 2
    phase = two_pi * turns[:, None] * steps[None, :, None, None]
    factors = np.stack([np.cos(phase), -np.sin(phase)], 2)
    return turns.astype(np.float32), factors.astype(np.float32)


def cos_sin_of_turns(turns):
    frac = turns - jnp.floor(turns + 0.5)
    w = frac * two_pi
    w2 = w * w
    cosine = jnp.full_like(w, 1.0 / math.factorial(16))
    for n in range(14, -1, -2):
        cosine = cosine * w2 + (-1.0) ** (n // 2) / math.factorial(n)
    sine_part = jnp.full_like(w, 1.0 / math.factorial(17))
    for n in range(15, 0, -2):
        sine_part = sine_part * w2 + (-1.0) ** (n // 2) / math.factorial(n)
    return cosine, sine_part * w


def base_kernel(shift_ref, part_ref, turns_ref, base_ref):
    here, _, angles, _ = part_ref.shape
    chunk = 32
    for q in range(here):
        p = pl.program_id(0) * here + q
        sx = shift_ref[0, p].astype(f32)
        sy = shift_ref[1, p].astype(f32)

        def turn(n, carry):
            rows = pl.ds(pl.multiple_of(n * chunk, chunk), chunk)
            cosine, sine_part = cos_sin_of_turns(sx * turns_ref[0, rows, :] + sy * turns_ref[1, rows, :])
            re = part_ref[q, 0, rows, :].astype(f32)
            im = part_ref[q, 1, rows, :].astype(f32)
            base_ref[q, 0, rows, :] = re * cosine + im * sine_part
            base_ref[q, 1, rows, :] = im * cosine - re * sine_part
            return carry

        lax.fori_loop(0, angles // chunk, turn, 0)


def make_base(particles, prior_shift):
    count, _, angles, cycles = particles.shape
    turns, _ = shift_tables(angles, cycles)
    here = count // 2
    image = pl.BlockSpec((here, 2, angles, cycles), lambda p: (p, 0, 0, 0))
    return pl.pallas_call(
        base_kernel,
        grid=(2,),
        in_specs=[
            pl.BlockSpec(memory_space=pltpu.SMEM),
            image,
            pl.BlockSpec(turns.shape, lambda p: (0, 0, 0)),
        ],
        out_specs=image,
        out_shape=jax.ShapeDtypeStruct(particles.shape, f32),
        compiler_params=pltpu.CompilerParams(vmem_limit_bytes=VMEM_LIMIT),
        name="centre",
    )(prior_shift.T, particles, turns)


def spectra_kernel(base_ref, ctf_ref, table_ref, *refs, per_step):
    factor_refs, refs = refs[: 2 * per_step], refs[2 * per_step :]
    chunks = ROWS // 2
    out_ref, turn_ref, re_ref, im_ref = refs[-4 - chunks : -chunks]
    data_refs = refs[-chunks:]
    count, _, angles, cycles = base_ref.shape
    chunk = 32

    for g in range(per_step):
        x_ref, y_ref = factor_refs[2 * g], factor_refs[2 * g + 1]
        for start in range(0, angles, chunk):
            rows = slice(start, start + chunk)
            xr, xi = x_ref[0, 0, 0, rows, :], x_ref[0, 0, 1, rows, :]
            yr, yi = y_ref[0, 0, 0, rows, :], y_ref[0, 0, 1, rows, :]
            turn_ref[g, 0, rows, :] = xr * yr - xi * yi
            turn_ref[g, 1, rows, :] = xr * yi + xi * yr

    def shift(n):
        for j in range(2):
            g, p = (2 * n + j) // count, (2 * n + j) % count
            lanes = slice(j * cycles, (j + 1) * cycles)
            for start in range(0, angles, chunk):
                rows = slice(start, start + chunk)
                tr, ti = turn_ref[g, 0, rows, :], turn_ref[g, 1, rows, :]
                gr, gi = base_ref[p, 0, rows, :], base_ref[p, 1, rows, :]
                data_refs[n][rows, lanes] = (gr * tr - gi * ti).astype(bf16)
                data_refs[n][angles + start : angles + start + chunk, lanes] = (gr * ti + gi * tr).astype(bf16)

    shift(0)
    for n in range(chunks):
        if n + 1 < chunks:
            shift(n + 1)
        spectrum = jnp.dot(table_ref[...], data_refs[n][...], preferred_element_type=f32)
        for j in range(2):
            row = 2 * n + j
            ctf_row = ctf_ref[row % count, :][None, :]
            part = spectrum[:, j * cycles : (j + 1) * cycles] * ctf_row
            re_ref[pl.ds(row, angles, stride=APART), :] = part[:angles]
            im_ref[pl.ds(row, angles, stride=APART), :] = part[angles:]
    for m in range(angles):
        out_ref[m, :, :cycles] = re_ref[m * APART : m * APART + ROWS, :].astype(bf16)
        out_ref[m, :, cycles:] = im_ref[m * APART : m * APART + ROWS, :].astype(bf16)


def spectra_steps(count):
    per_step = ROWS // count if count < ROWS else 1
    return per_step, -(-SHIFTS // per_step)


def make_spectra(base, ctf_rows, first, last, before=None, after=()):
    count, _, angles, cycles = base.shape
    per_step, steps = spectra_steps(count)
    _, factors = shift_tables(angles, cycles)
    full = lambda shape: pl.BlockSpec(shape, lambda i: (0,) * len(shape))

    def factor_spec(g, axis):
        def place(i):
            s = jnp.minimum((i + first) * per_step + g, SHIFTS - 1)
            a = lax.div(s, jnp.int32(SHIFT_SIDE))
            return (axis, s - a * SHIFT_SIDE if axis else a, 0, 0, 0)

        return pl.BlockSpec((1, 1, 2, angles, cycles), place)

    untouched = ([] if before is None else [before]) + list(after)
    in_specs = (
        [full(base.shape), full(ctf_rows.shape), full((2 * angles, 2 * angles))]
        + [factor_spec(g, axis) for g in range(per_step) for axis in range(2)]
        + [pl.BlockSpec(memory_space=pl.ANY)] * len(untouched)
    )
    return pl.pallas_call(
        functools.partial(spectra_kernel, per_step=per_step),
        grid=(last - first,),
        in_specs=in_specs,
        out_specs=pl.BlockSpec((angles, ROWS, 2 * cycles), lambda i: (0, i + first, 0)),
        out_shape=jax.ShapeDtypeStruct((angles, steps * ROWS, 2 * cycles), bf16),
        scratch_shapes=[
            pltpu.VMEM((per_step, 2, angles, cycles), f32),
            pltpu.VMEM((angles * APART, cycles), f32),
            pltpu.VMEM((angles * APART, cycles), f32),
        ]
        + [pltpu.VMEM((2 * angles, 2 * cycles), bf16)] * (ROWS // 2),
        input_output_aliases={} if before is None else {3 + 2 * per_step: 0},
        compiler_params=pltpu.CompilerParams(vmem_limit_bytes=VMEM_LIMIT),
        name="spectra",
    )(base, ctf_rows, fourier_rows(angles), *[factors] * (2 * per_step), *untouched)


def half_dft(even_values, odd_values):
    half = FOLD // 2
    cos_sums, sin_sums = [None] * FOLD, [None] * FOLD

    def weighted_sum(values, k, table, start):
        total = None
        for m in range(start, FOLD, 2):
            weight = float(table((k * m % ROTS) * two_pi / ROTS))
            if values[m] is None or abs(weight) < 1e-9:
                continue
            if abs(abs(weight) - 1.0) < 1e-9:
                term = values[m] if weight > 0 else -values[m]
            else:
                term = values[m] * weight
            total = term if total is None else total + term
        return jnp.zeros_like(values[1]) if total is None else total

    for k in range(half + 1):
        even = weighted_sum(even_values, k, math.cos, 0)
        odd = weighted_sum(even_values, k, math.cos, 1)
        cos_sums[k] = even + odd
        if k != half:
            cos_sums[FOLD - 1 - k] = even - odd
        if k:
            even = weighted_sum(odd_values, k, math.sin, 0)
            odd = weighted_sum(odd_values, k, math.sin, 1)
            sin_sums[k] = even + odd
            if k != half:
                sin_sums[FOLD - 1 - k] = odd - even
    return cos_sums, sin_sums


def turn_kernel(first_ref, offset_ref, references_ref, out_ref, column_ref, in_ref, wide_ref):
    rows, cycles = references_ref.shape
    classes = offset_ref.shape[0]
    own_rows = rows // (2 * classes)
    in_ref[...] = references_ref[...].astype(f32)
    row = lax.broadcasted_iota(jnp.int32, (8, LANES), 0)
    lane = lax.broadcasted_iota(jnp.int32, (8, LANES), 1)
    freq = (lane + first_ref[0]).astype(f32) * (1.0 / (ROTS * ANG_STEP))
    tables = []
    for start in range(0, classes, 8):
        column = jnp.zeros((8, LANES), jnp.int32)
        for c in range(start, min(start + 8, classes)):
            column = jnp.where(row == c - start, offset_ref[c], column)
        column = column.astype(f32)
        column_ref[start : start + 8, :] = column
        tables.append(cos_sin_of_turns(column * freq))
    cosine = jnp.concatenate([c for c, _ in tables], 0)
    sine_part = jnp.concatenate([s for _, s in tables], 0)
    for m in range(own_rows):
        re_rows = pl.ds(2 * m * classes, classes, stride=2)
        im_rows = pl.ds(2 * m * classes + 1, classes, stride=2)
        c, s = cosine[:classes, m : m + 1], sine_part[:classes, m : m + 1]
        re, im = in_ref[re_rows, :], in_ref[im_rows, :]
        wide_ref[re_rows, :] = re * c + im * s
        wide_ref[im_rows, :] = im * c - re * s
    out_ref[...] = wide_ref[...].astype(bf16)


def turn_references(first, offsets, references):
    padded = -(-offsets.shape[0] // 8) * 8
    return pl.pallas_call(
        turn_kernel,
        in_specs=[
            pl.BlockSpec(memory_space=pltpu.SMEM),
            pl.BlockSpec(memory_space=pltpu.SMEM),
            pl.BlockSpec(memory_space=pltpu.VMEM),
        ],
        out_shape=[
            jax.ShapeDtypeStruct(references.shape, bf16),
            jax.ShapeDtypeStruct((padded, LANES), f32),
        ],
        scratch_shapes=[pltpu.VMEM(references.shape, f32)] * 2,
        compiler_params=pltpu.CompilerParams(vmem_limit_bytes=VMEM_LIMIT),
        name="turn_references",
    )(first, offsets, references)


def correlate_kernel(*refs, slots, classes, padded, finish):
    part_ref, refs = refs[slots], refs[slots + 1 :]
    weighted_refs, refs = refs[:slots], refs[slots:]
    piece_refs, refs = refs[:slots], refs[slots:]
    if finish:
        before_ref, power_before_ref, ctf_ref, weight_ref, stat_ref, share_ref = refs[:6]
        corr_ref, wide_ref, power_ref = refs[6:]
    else:
        corr_ref, power_ref, wide_ref = refs
    group = pl.program_id(0)
    cycles = piece_refs[0].shape[1]
    queries = weighted_refs[0].shape[2]
    block = piece_refs[0].shape[0]

    @pl.when(group == 0)
    def _():
        wide_ref[:, block:, :] = jnp.zeros((slots, wide_ref.shape[1] - block, cycles), f32)
        power_ref[...] = power_before_ref[...] if finish else jnp.zeros_like(power_ref)

    for j in range(slots):
        wide_ref[j, :block, :] = piece_refs[j][...].astype(f32)
    power = power_ref[...]
    for i in range(GROUP):
        total = before_ref[i, :, :queries] if finish else None
        for j in range(slots):
            re = wide_ref[j, pl.ds(2 * i * classes, padded, stride=2), :]
            im = wide_ref[j, pl.ds(2 * i * classes + 1, padded, stride=2), :]
            power = power + (re * re + im * im)
            left = jnp.concatenate(
                [jnp.concatenate([re, im], 1), jnp.concatenate([-im, re], 1)], 0
            ).astype(bf16)
            part = lax.dot_general(
                left, weighted_refs[j][0, i], (((1,), (1,)), ((), ())), preferred_element_type=f32
            )
            total = part if total is None else total + part
        row = group * GROUP + i if finish else i
        corr_ref[row, :, :queries] = total
    power_ref[...] = power

    if not finish:
        return

    @pl.when(group == pl.num_programs(0) - 1)
    def _():
        count = ctf_ref.shape[0]
        angles = ROTS * ANG_STEP
        used = SHIFTS * count
        tiles = weight_ref.shape[2] // LANES
        ctf_row = ctf_ref[...]
        ctf_rows = jnp.concatenate([ctf_row * ctf_row] * (LANES // count), 0)
        bias = lax.dot_general(
            power_ref[...],
            ctf_rows,
            (((1,), (1,)), ((), ())),
            precision=lax.Precision.HIGHEST,
            preferred_element_type=f32,
        ) * (0.5 / angles)
        wide_ref[0, :padded, :] = bias
        rows_of = lambda base: lax.broadcasted_iota(jnp.int32, (8, LANES), 0) + base
        lanes_of = lambda base: lax.broadcasted_iota(jnp.int32, (8, LANES), 1) + base

        peak = jnp.full((8, LANES), -1e30, f32)
        for tile in range(tiles):
            lanes = slice(tile * LANES, (tile + 1) * LANES)

            def scores(n, peak):
                start = pl.multiple_of(n * 8, 8)
                rows = pl.ds(start, 8)
                low = pl.ds(padded + start, 8)
                valid = (rows_of(start) < classes) & (lanes_of(tile * LANES) < used)
                even_values = [corr_ref[0, rows, lanes]]
                odd_values = [None]
                for m in range(1, ROTS // 2):
                    even_values.append(corr_ref[m, rows, lanes] + corr_ref[ROTS - m, rows, lanes])
                    odd_values.append(corr_ref[m, low, lanes] - corr_ref[ROTS - m, low, lanes])
                even_values.append(corr_ref[ROTS // 2, rows, lanes])
                odd_values.append(None)
                cos_sums, sin_sums = half_dft(even_values, odd_values)
                bias = wide_ref[0, rows, :]
                for k in range(FOLD):
                    if k in (0, FOLD - 1):
                        results = [(k, cos_sums[k])]
                    else:
                        results = [(k, cos_sums[k] - sin_sums[k]), (ROTS - k, cos_sums[k] + sin_sums[k])]
                    for place, value in results:
                        value = jnp.where(valid, value * (1.0 / angles) - bias, -1e30)
                        weight_ref[place, rows, lanes] = value
                        peak = jnp.maximum(peak, value)
                return peak

            peak = lax.fori_loop(0, padded // 8, scores, peak)

        peak = jnp.broadcast_to(jnp.max(peak, axis=0, keepdims=True), (8, LANES))
        step = count
        while step < LANES:
            peak = jnp.maximum(peak, pltpu.roll(peak, step, 1))
            step *= 2
        stat_ref[0:8, :] = peak

        def masses(n, whole):
            rows = pl.ds(pl.multiple_of(n * 8, 8), 8)
            mass = jnp.zeros((8, LANES), f32)
            for tile in range(tiles):
                lanes = slice(tile * LANES, (tile + 1) * LANES)
                for k in range(ROTS):
                    value = jnp.exp(weight_ref[k, rows, lanes] - peak)
                    weight_ref[k, rows, lanes] = value
                    mass = mass + value
            step = count
            while step < LANES:
                mass = mass + pltpu.roll(mass, step, 1)
                step *= 2
            stat_ref[pl.ds(pl.multiple_of(8 + n * 8, 8), 8), :] = mass
            return whole + mass

        whole = lax.fori_loop(0, padded // 8, masses, jnp.zeros((8, LANES), f32))
        share = jnp.concatenate([peak[:1], jnp.sum(whole, axis=0, keepdims=True)], 0)
        for j in range(share_ref.shape[0]):
            share_ref[j] = jnp.where(part_ref[0] == j, share, 0.0)


def correlate(slot_of, weighted, pieces, classes, part, before=None, power=None, ctf_rows=None, parts=1):
    _, _, queries, double = weighted.shape
    cycles = double // 2
    slots = len(pieces)
    padded = -(-classes // 8) * 8
    wide_lanes = -(-queries // LANES) * LANES
    block = 2 * GROUP * classes
    finish = ctf_rows is not None
    full = lambda shape: pl.BlockSpec(shape, lambda g, *u: (0,) * len(shape))
    in_specs = [
        pl.BlockSpec((1, GROUP, queries, double), functools.partial(lambda j, g, *u: (u[j][0], g, 0, 0), j))
        for j in range(slots)
    ] + [pl.BlockSpec((block, cycles), lambda g, *u: (g, 0))] * slots
    corr_block = pl.BlockSpec((GROUP, 2 * padded, wide_lanes), lambda g, *u: (g, 0, 0))
    corr_shape = (ROTS, 2 * padded, wide_lanes)
    wide = pltpu.VMEM((slots, block + ROWS, cycles), f32)
    scalars = [jnp.reshape(n, (1,)).astype(jnp.int32) for n in (*slot_of, part)]
    operands = scalars + [weighted] * slots + list(pieces)
    if finish:
        in_specs += [corr_block, full((padded, cycles)), full(ctf_rows.shape)]
        operands += [before, power, ctf_rows]
        out_shapes = [(ROTS, padded, wide_lanes), (8 + padded, LANES), (parts, 2, LANES)]
        out_specs = [full(shape) for shape in out_shapes]
        scratch = [pltpu.VMEM(corr_shape, f32), wide, pltpu.VMEM((padded, cycles), f32)]
    else:
        out_shapes = [corr_shape, (padded, cycles)]
        out_specs = [corr_block, full((padded, cycles))]
        scratch = [wide]
    return pl.pallas_call(
        functools.partial(correlate_kernel, slots=slots, classes=classes, padded=padded, finish=finish),
        grid_spec=pltpu.PrefetchScalarGridSpec(
            num_scalar_prefetch=len(scalars),
            grid=(ROTS // GROUP,),
            in_specs=in_specs,
            out_specs=out_specs,
            scratch_shapes=scratch,
        ),
        out_shape=[jax.ShapeDtypeStruct(shape, f32) for shape in out_shapes],
        compiler_params=pltpu.CompilerParams(vmem_limit_bytes=VMEM_LIMIT),
        name="scores" if finish else "correlate",
    )(*operands)


def back_kernel(weight_ref, stat_ref, share_ref, offset_ref, out_ref, evidence_ref, posterior_ref, sum_ref):
    padded = weight_ref.shape[1]
    queries = out_ref.shape[2]
    shares = [share_ref[j] for j in range(share_ref.shape[0])]
    top = shares[0][:1]
    for share in shares[1:]:
        top = jnp.maximum(top, share[:1])
    mass = sum(share[1:] * jnp.exp(share[:1] - top) for share in shares)
    evidence = jnp.broadcast_to(top + jnp.log(mass), (8, LANES))
    scale = jnp.exp(stat_ref[:8, :] - evidence)
    evidence_ref[...] = evidence
    posterior_ref[...] = stat_ref[8:, :] * scale[:1]
    for tile in range(weight_ref.shape[2] // LANES):
        lanes = slice(tile * LANES, (tile + 1) * LANES)

        def transform(n, carry):
            start = pl.multiple_of(n * 8, 8)
            rows = pl.ds(start, 8)
            low = pl.ds(padded + start, 8)
            values = [weight_ref[k, rows, lanes] * scale for k in range(ROTS)]
            even_values = [values[0]] + [values[k] + values[ROTS - k] for k in range(1, ROTS // 2)]
            odd_values = [None] + [values[k] - values[ROTS - k] for k in range(1, ROTS // 2)] + [None]
            cos_sums, sin_sums = half_dft(even_values + [values[ROTS // 2]], odd_values)
            for m in range(FOLD):
                sine_part = jnp.zeros_like(scale) if m in (0, FOLD - 1) else sin_sums[m]
                sum_ref[m, rows, lanes] = cos_sums[m]
                sum_ref[m, low, lanes] = sine_part
                if m not in (0, FOLD - 1):
                    sum_ref[ROTS - m, rows, lanes] = cos_sums[m]
                    sum_ref[ROTS - m, low, lanes] = -sine_part
            return carry

        lax.fori_loop(0, padded // 8, transform, 0)

    step_cos, step_sin = cos_sin_of_turns(offset_ref[...] * (1.0 / (ROTS * ANG_STEP)))

    def turn(m, carry):
        cosine, sine_part = carry
        for tile in range(weight_ref.shape[2] // LANES):
            lanes = slice(tile * LANES, (tile + 1) * LANES)
            kept = slice(tile * LANES, min((tile + 1) * LANES, queries))
            re, im = sum_ref[m, :padded, lanes], sum_ref[m, padded:, lanes]
            turned = jnp.concatenate([re * cosine - im * sine_part, re * sine_part + im * cosine], 0)
            out_ref[m, :, kept] = turned[:, : kept.stop - kept.start].astype(bf16)
        return cosine * step_cos - sine_part * step_sin, sine_part * step_cos + cosine * step_sin

    lax.fori_loop(0, ROTS, turn, (jnp.ones_like(step_cos), jnp.zeros_like(step_cos)))


def make_back(weights, stat, shares, offsets, queries):
    _, padded, wide_lanes = weights.shape
    return pl.pallas_call(
        back_kernel,
        out_shape=[
            jax.ShapeDtypeStruct((ROTS, 2 * padded, queries), bf16),
            jax.ShapeDtypeStruct((8, LANES), f32),
            jax.ShapeDtypeStruct((padded, LANES), f32),
        ],
        scratch_shapes=[pltpu.VMEM((ROTS, 2 * padded, wide_lanes), f32)],
        compiler_params=pltpu.CompilerParams(vmem_limit_bytes=VMEM_LIMIT),
        name="back",
    )(weights, stat, shares, offsets)


def sums_kernel(*refs, count, classes):
    slot_refs, (back_ref, *refs) = refs[:count], refs[count:]
    weighted_refs, (offset_ref, *refs) = refs[:count], refs[count:]
    out_refs, wide_refs = refs[:count], refs[count:]
    padded = offset_ref.shape[0]
    cycles = wide_refs[0].shape[1]
    turns = [
        cos_sin_of_turns(offset_ref[...] * (slot_ref[0].astype(f32) * (1.0 / ANG_STEP)))
        for slot_ref in slot_refs
    ]
    for i in range(GROUP):
        for (cosine, sine_part), weighted_ref, wide_ref in zip(turns, weighted_refs, wide_refs):
            product = jnp.dot(back_ref[i], weighted_ref[0, i], preferred_element_type=f32)
            re = product[:padded, :cycles] - product[padded:, cycles:]
            im = product[:padded, cycles:] + product[padded:, :cycles]
            start = 2 * i * classes
            wide_ref[pl.ds(start, classes, stride=2), :] = (re * cosine - im * sine_part)[:classes]
            wide_ref[pl.ds(start + 1, classes, stride=2), :] = (re * sine_part + im * cosine)[:classes]
    for out_ref, wide_ref in zip(out_refs, wide_refs):
        out_ref[...] = wide_ref[...].astype(out_ref.dtype)


def class_sums_of(slots, back, weighted, offsets, classes, dtypes, groups=(0, ROTS // GROUP)):
    begin, end = groups
    _, _, queries, double = weighted.shape
    cycles = double // 2
    rows = back.shape[1]
    block = 2 * GROUP * classes
    count = len(slots)
    scalars = [jnp.reshape(slot, (1,)).astype(jnp.int32) for slot in slots]
    return pl.pallas_call(
        functools.partial(sums_kernel, count=count, classes=classes),
        grid_spec=pltpu.PrefetchScalarGridSpec(
            num_scalar_prefetch=count,
            grid=(end - begin,),
            in_specs=[pl.BlockSpec((GROUP, rows, queries), lambda g, *u: (g + begin, 0, 0))]
            + [
                pl.BlockSpec(
                    (1, GROUP, queries, double),
                    functools.partial(lambda j, g, *u: (u[j][0], g + begin, 0, 0), j),
                )
                for j in range(count)
            ]
            + [pl.BlockSpec(offsets.shape, lambda g, *u: (0, 0))],
            out_specs=[pl.BlockSpec((block, cycles), lambda g, *u: (g, 0))] * count,
            scratch_shapes=[pltpu.VMEM((block, cycles), f32)] * count,
        ),
        out_shape=[jax.ShapeDtypeStruct(((end - begin) * block, cycles), dtype) for dtype in dtypes],
        compiler_params=pltpu.CompilerParams(vmem_limit_bytes=VMEM_LIMIT),
        name="class_sums",
    )(*scalars, back, *[weighted] * count, offsets)


def across(piece):
    return lax.ppermute(piece, "dp", [(d, d ^ 1) for d in range(8)])


def along(piece, pairs):
    return lax.ppermute(piece, "dp", [(2 * a + x, 2 * b + x) for a, b in pairs for x in range(2)])


def gather_on_line(piece, base, ctf_rows):
    index = lax.axis_index("dp")
    line, side = index // 2, index % 2
    _, steps = spectra_steps(base.shape[0])
    cuts = [0, 3 * steps // 13, 8 * steps // 13, steps]

    own_crossed = across(piece)
    near = along(piece, ((0, 1), (1, 0), (2, 3), (3, 2)))
    middle = along(piece, ((1, 2), (2, 1)))
    weighted = make_spectra(base, ctf_rows, cuts[0], cuts[1])
    weighted, middle = lax.optimization_barrier((weighted, middle))
    weighted, own_crossed = lax.optimization_barrier((weighted, own_crossed))
    weighted, near = lax.optimization_barrier((weighted, near))
    near_crossed = across(near)
    far_middle = along(near, ((1, 2), (2, 1)))
    end = along(middle, ((1, 0), (2, 3)))
    weighted = make_spectra(base, ctf_rows, cuts[1], cuts[2], weighted)
    weighted, end = lax.optimization_barrier((weighted, end))
    weighted, near_crossed = lax.optimization_barrier((weighted, near_crossed))
    weighted, far_middle = lax.optimization_barrier((weighted, far_middle))
    third = middle + end
    third_crossed = across(third)
    far_end = along(far_middle, ((1, 0), (2, 3)))
    weighted = make_spectra(base, ctf_rows, cuts[2], cuts[3], weighted)
    weighted, far_end, third_crossed = lax.optimization_barrier((weighted, far_end, third_crossed))
    fourth = far_middle + far_end
    fourth_crossed = across(fourth)

    pieces = [piece, own_crossed, near, near_crossed, third, third_crossed, fourth, fourth_crossed]
    places = [line, line ^ 1, jnp.where(line < 2, 2, 1), jnp.where(line < 2, 3, 0)]
    slot_of = [2 * place + s for place in places for s in (side, 1 - side)]
    return weighted, pieces, slot_of


def reduce_on_line(back, weighted, offsets, classes):
    index = lax.axis_index("dp")
    line, side = index // 2, index % 2
    order = [jnp.where(line < 2, 3, 0), jnp.where(line < 2, 2, 1), line ^ 1, line]
    theirs = [2 * z + 1 - side for z in order]
    ours = [2 * z + side for z in order]
    groups = ((0, 1), (1, ROTS // GROUP))
    block = 2 * GROUP * classes
    head, rest = [slice(a * block, b * block) for a, b in groups]
    to_middle, between = ((0, 1), (3, 2)), ((1, 2), (2, 1))
    neighbours = ((0, 1), (1, 0), (2, 3), (3, 2))

    def sums(slots, dtypes, back, some=(0, ROTS // GROUP)):
        return class_sums_of(slots, back, weighted, offsets, classes, dtypes, some)

    def wide(piece):
        return piece.astype(f32)

    def then(back, *done):
        return lax.optimization_barrier((back, *done))[0]

    (away,) = sums(theirs[:1], [bf16], back, groups[0])
    crossed_head = across(away)
    back = then(back, away)
    (away,) = sums(theirs[:1], [bf16], back, groups[1])
    crossed_rest = across(away)
    back = then(back, away)
    own_0, away = sums([ours[0], theirs[1]], [f32, bf16], back)
    crossed_1 = across(away)
    crossed_head, own_0 = lax.optimization_barrier((crossed_head, own_0))
    message = (own_0[head] + wide(crossed_head)).astype(bf16)
    first_head = along(message, to_middle)
    back = then(back, message)
    own_1, away = sums([ours[1], theirs[2]], [f32, bf16], back)
    crossed_2 = across(away)
    crossed_rest, own_1 = lax.optimization_barrier((crossed_rest, own_1))
    message = (own_0[rest] + wide(crossed_rest)).astype(bf16)
    first_rest = along(message, to_middle)
    back = then(back, message)
    message = (own_0[head] + wide(crossed_head) + wide(first_head)).astype(bf16)
    middle_head = along(message, between)
    back = then(back, message)
    own_2, away = sums([ours[2], theirs[3]], [f32, bf16], back)
    crossed_3 = across(away)
    crossed_1, middle_head, own_2 = lax.optimization_barrier((crossed_1, middle_head, own_2))
    message = (own_1 + wide(crossed_1)).astype(bf16)
    from_end = along(message, to_middle)
    first_rest = then(first_rest, message)
    message = (own_0[rest] + wide(crossed_rest) + wide(first_rest)).astype(bf16)
    middle_rest = along(message, between)
    back = then(back, message)
    (own_3,) = sums(ours[3:], [f32], back)
    from_end = then(from_end, crossed_2)
    message = (own_1 + wide(crossed_1) + wide(from_end)).astype(bf16)
    third = along(message, between)
    middle_rest = then(middle_rest, message)
    middle = jnp.concatenate([middle_head, middle_rest], 0)
    last = along((own_2 + wide(crossed_2) + wide(middle)).astype(bf16), neighbours)
    return own_3 + wide(crossed_3) + wide(third) + wide(last)


def local(particles, references, ctf_table, rot_offset, prior_shift, defocus_group):
    count, _, angles, cycles = particles.shape
    own_rows, _, classes, _ = references.shape
    slots = angles // ROTS
    group_count = ctf_table.shape[0]
    devices = lax.axis_size("dp")

    first = (lax.axis_index("dp") * own_rows).astype(jnp.int32).reshape(1)
    rows = jnp.transpose(references, (0, 2, 1, 3)).reshape(own_rows * 2 * classes, cycles)
    piece, offsets = turn_references(first, rot_offset, rows)

    onehot = (defocus_group[:, None] == jnp.arange(group_count, dtype=jnp.int32)[None, :]).astype(f32)
    ctf_rows = jnp.dot(onehot, ctf_table, precision=lax.Precision.HIGHEST)
    base = make_base(particles, prior_shift)
    on_line = devices == 8 and own_rows == ROTS
    if on_line:
        weighted, pieces, slot_of = gather_on_line(piece, base, ctf_rows)
    else:
        gathered = lax.all_gather(piece, "dp", axis=0, tiled=True)
        gathered = gathered.reshape(slots, ROTS * 2 * classes, cycles)
        pieces = [gathered[j] for j in range(slots)]
        slot_of = list(range(slots))
        weighted = make_spectra(base, ctf_rows, 0, spectra_steps(count)[1])
    queries = weighted.shape[1]
    weighted = weighted.reshape(slots, ROTS, queries, 2 * cycles)

    early = slots - 1
    part = lax.axis_index("cls")
    corr, power = correlate(slot_of[:early], weighted, pieces[:early], classes, part)
    weights, stat, share = correlate(
        slot_of[early:], weighted, pieces[early:], classes, part, corr, power, ctf_rows, lax.axis_size("cls")
    )
    shares = lax.psum(share, "cls")
    back, evidence, posterior = make_back(weights, stat, shares, offsets, queries)
    log_evidence = evidence[0, :count]
    class_posterior = posterior[:classes, :count].T
    if on_line:
        class_rows = reduce_on_line(back, weighted, offsets, classes)
    else:
        sums = [class_sums_of([u], back, weighted, offsets, classes, [bf16])[0] for u in slot_of]
        summed = lax.psum_scatter(jnp.concatenate(sums, 0), "dp", scatter_dimension=0, tiled=True)
        class_rows = summed.astype(f32)
    class_sums = jnp.transpose(class_rows.reshape(own_rows, classes, 2, cycles), (0, 2, 1, 3))
    return (log_evidence, class_posterior, class_sums)


def solution(mesh):
    placed = (
        P("dp", None, None, None),
        P("dp", None, "cls", None),
        P(),
        P("cls"),
        P("dp", None),
        P("dp"),
    )
    return jax.shard_map(
        local,
        mesh=mesh,
        in_specs=placed,
        out_specs=(P("dp"), P("dp", "cls"), P("dp", None, "cls", None)),
        check_vma=False,
    )
```

```python
import functools
import math

import jax
import jax.numpy as jnp
import ml_dtypes
import numpy as np
from jax import lax
from jax.experimental import pallas as pl
from jax.experimental.pallas import tpu as pltpu
from jax.sharding import PartitionSpec as P

ROTS = 36
ANG_STEP = 8
SHIFT_SIDE = 5
SHIFTS = SHIFT_SIDE * SHIFT_SIDE
LANES = 128
GROUP = 12
ROWS = 16
APART = 17
FOLD = ROTS // 2 + 1

two_pi = 2.0 * math.pi
f32 = jnp.float32
bf16 = jnp.bfloat16
VMEM_LIMIT = 56 * 1024 * 1024


def fourier_rows(angles):
    index_grid = np.arange(angles)
    radians = (index_grid[:, None] * index_grid[None, :] % angles) * (two_pi / angles)
    cosine, sine_part = np.cos(radians), np.sin(radians)
    table_full = np.concatenate(
        [np.concatenate([cosine, sine_part], 1), np.concatenate([-sine_part, cosine], 1)], 0
    )
    return table_full.astype(np.float32).astype(ml_dtypes.bfloat16)


def shift_tables(angles, cycles):
    theta = np.arange(angles) * (two_pi / angles)
    radius = (np.arange(cycles) + 1) / (2.0 * cycles)
    turns = np.stack([np.cos(theta), np.sin(theta)])[:, :, None] * radius
    steps = np.arange(SHIFT_SIDE) - SHIFT_SIDE // 2
    phase = two_pi * turns[:, None] * steps[None, :, None, None]
    factors = np.stack([np.cos(phase), -np.sin(phase)], 2)
    return turns.astype(np.float32), factors.astype(np.float32)


def cos_sin_of_turns(turns):
    frac = turns - jnp.floor(turns + 0.5)
    w = frac * two_pi
    w2 = w * w
    cosine = jnp.full_like(w, 1.0 / math.factorial(16))
    for n in range(14, -1, -2):
        cosine = cosine * w2 + (-1.0) ** (n // 2) / math.factorial(n)
    sine_part = jnp.full_like(w, 1.0 / math.factorial(17))
    for n in range(15, 0, -2):
        sine_part = sine_part * w2 + (-1.0) ** (n // 2) / math.factorial(n)
    return cosine, sine_part * w


def base_kernel(shift_ref, part_ref, turns_ref, base_ref):
    here, _, angles, _ = part_ref.shape
    chunk = 32
    for q in range(here):
        p = pl.program_id(0) * here + q
        sx = shift_ref[0, p].astype(f32)
        sy = shift_ref[1, p].astype(f32)

        def turn(n, carry):
            rows = pl.ds(pl.multiple_of(n * chunk, chunk), chunk)
            cosine, sine_part = cos_sin_of_turns(sx * turns_ref[0, rows, :] + sy * turns_ref[1, rows, :])
            re = part_ref[q, 0, rows, :].astype(f32)
            im = part_ref[q, 1, rows, :].astype(f32)
            base_ref[q, 0, rows, :] = re * cosine + im * sine_part
            base_ref[q, 1, rows, :] = im * cosine - re * sine_part
            return carry

        lax.fori_loop(0, angles // chunk, turn, 0)


def make_base(particles, prior_shift):
    count, _, angles, cycles = particles.shape
    turns, _ = shift_tables(angles, cycles)
    here = count // 2
    image = pl.BlockSpec((here, 2, angles, cycles), lambda p: (p, 0, 0, 0))
    return pl.pallas_call(
        base_kernel,
        grid=(2,),
        in_specs=[
            pl.BlockSpec(memory_space=pltpu.SMEM),
            image,
            pl.BlockSpec(turns.shape, lambda p: (0, 0, 0)),
        ],
        out_specs=image,
        out_shape=jax.ShapeDtypeStruct(particles.shape, f32),
        compiler_params=pltpu.CompilerParams(vmem_limit_bytes=VMEM_LIMIT),
        name="centre",
    )(prior_shift.T, particles, turns)


def spectra_kernel(base_ref, ctf_ref, table_ref, *refs, per_step):
    factor_refs, refs = refs[: 2 * per_step], refs[2 * per_step :]
    chunks = ROWS // 2
    out_ref, turn_ref, re_ref, im_ref = refs[-4 - chunks : -chunks]
    data_refs = refs[-chunks:]
    count, _, angles, cycles = base_ref.shape
    chunk = 32

    for g in range(per_step):
        x_ref, y_ref = factor_refs[2 * g], factor_refs[2 * g + 1]
        for start in range(0, angles, chunk):
            rows = slice(start, start + chunk)
            xr, xi = x_ref[0, 0, 0, rows, :], x_ref[0, 0, 1, rows, :]
            yr, yi = y_ref[0, 0, 0, rows, :], y_ref[0, 0, 1, rows, :]
            turn_ref[g, 0, rows, :] = xr * yr - xi * yi
            turn_ref[g, 1, rows, :] = xr * yi + xi * yr

    def shift(n):
        for j in range(2):
            g, p = (2 * n + j) // count, (2 * n + j) % count
            lanes = slice(j * cycles, (j + 1) * cycles)
            for start in range(0, angles, chunk):
                rows = slice(start, start + chunk)
                tr, ti = turn_ref[g, 0, rows, :], turn_ref[g, 1, rows, :]
                gr, gi = base_ref[p, 0, rows, :], base_ref[p, 1, rows, :]
                data_refs[n][rows, lanes] = (gr * tr - gi * ti).astype(bf16)
                data_refs[n][angles + start : angles + start + chunk, lanes] = (gr * ti + gi * tr).astype(bf16)

    shift(0)
    for n in range(chunks):
        if n + 1 < chunks:
            shift(n + 1)
        spectrum = jnp.dot(table_ref[...], data_refs[n][...], preferred_element_type=f32)
        for j in range(2):
            row = 2 * n + j
            ctf_row = ctf_ref[row % count, :][None, :]
            part = spectrum[:, j * cycles : (j + 1) * cycles] * ctf_row
            re_ref[pl.ds(row, angles, stride=APART), :] = part[:angles]
            im_ref[pl.ds(row, angles, stride=APART), :] = part[angles:]
    for m in range(angles):
        out_ref[m, :, :cycles] = re_ref[m * APART : m * APART + ROWS, :].astype(bf16)
        out_ref[m, :, cycles:] = im_ref[m * APART : m * APART + ROWS, :].astype(bf16)


def spectra_steps(count):
    per_step = ROWS // count if count < ROWS else 1
    return per_step, -(-SHIFTS // per_step)


def make_spectra(base, ctf_rows, first, last, before=None, after=()):
    count, _, angles, cycles = base.shape
    per_step, steps = spectra_steps(count)
    _, factors = shift_tables(angles, cycles)
    full = lambda shape: pl.BlockSpec(shape, lambda i: (0,) * len(shape))

    def factor_spec(g, axis):
        def place(i):
            s = jnp.minimum((i + first) * per_step + g, SHIFTS - 1)
            a = lax.div(s, jnp.int32(SHIFT_SIDE))
            return (axis, s - a * SHIFT_SIDE if axis else a, 0, 0, 0)

        return pl.BlockSpec((1, 1, 2, angles, cycles), place)

    untouched = ([] if before is None else [before]) + list(after)
    in_specs = (
        [full(base.shape), full(ctf_rows.shape), full((2 * angles, 2 * angles))]
        + [factor_spec(g, axis) for g in range(per_step) for axis in range(2)]
        + [pl.BlockSpec(memory_space=pl.ANY)] * len(untouched)
    )
    return pl.pallas_call(
        functools.partial(spectra_kernel, per_step=per_step),
        grid=(last - first,),
        in_specs=in_specs,
        out_specs=pl.BlockSpec((angles, ROWS, 2 * cycles), lambda i: (0, i + first, 0)),
        out_shape=jax.ShapeDtypeStruct((angles, steps * ROWS, 2 * cycles), bf16),
        scratch_shapes=[
            pltpu.VMEM((per_step, 2, angles, cycles), f32),
            pltpu.VMEM((angles * APART, cycles), f32),
            pltpu.VMEM((angles * APART, cycles), f32),
        ]
        + [pltpu.VMEM((2 * angles, 2 * cycles), bf16)] * (ROWS // 2),
        input_output_aliases={} if before is None else {3 + 2 * per_step: 0},
        compiler_params=pltpu.CompilerParams(vmem_limit_bytes=VMEM_LIMIT),
        name="spectra",
    )(base, ctf_rows, fourier_rows(angles), *[factors] * (2 * per_step), *untouched)


def half_dft(even_values, odd_values):
    half = FOLD // 2
    cos_sums, sin_sums = [None] * FOLD, [None] * FOLD

    def weighted_sum(values, k, table, start):
        total = None
        for m in range(start, FOLD, 2):
            weight = float(table((k * m % ROTS) * two_pi / ROTS))
            if values[m] is None or abs(weight) < 1e-9:
                continue
            if abs(abs(weight) - 1.0) < 1e-9:
                term = values[m] if weight > 0 else -values[m]
            else:
                term = values[m] * weight
            total = term if total is None else total + term
        return jnp.zeros_like(values[1]) if total is None else total

    for k in range(half + 1):
        even = weighted_sum(even_values, k, math.cos, 0)
        odd = weighted_sum(even_values, k, math.cos, 1)
        cos_sums[k] = even + odd
        if k != half:
            cos_sums[FOLD - 1 - k] = even - odd
        if k:
            even = weighted_sum(odd_values, k, math.sin, 0)
            odd = weighted_sum(odd_values, k, math.sin, 1)
            sin_sums[k] = even + odd
            if k != half:
                sin_sums[FOLD - 1 - k] = odd - even
    return cos_sums, sin_sums


def turn_kernel(first_ref, offset_ref, references_ref, out_ref, column_ref, in_ref, wide_ref):
    rows, cycles = references_ref.shape
    classes = offset_ref.shape[0]
    own_rows = rows // (2 * classes)
    in_ref[...] = references_ref[...].astype(f32)
    row = lax.broadcasted_iota(jnp.int32, (8, LANES), 0)
    lane = lax.broadcasted_iota(jnp.int32, (8, LANES), 1)
    freq = (lane + first_ref[0]).astype(f32) * (1.0 / (ROTS * ANG_STEP))
    tables = []
    for start in range(0, classes, 8):
        column = jnp.zeros((8, LANES), jnp.int32)
        for c in range(start, min(start + 8, classes)):
            column = jnp.where(row == c - start, offset_ref[c], column)
        column = column.astype(f32)
        column_ref[start : start + 8, :] = column
        tables.append(cos_sin_of_turns(column * freq))
    cosine = jnp.concatenate([c for c, _ in tables], 0)
    sine_part = jnp.concatenate([s for _, s in tables], 0)
    for m in range(own_rows):
        re_rows = pl.ds(2 * m * classes, classes, stride=2)
        im_rows = pl.ds(2 * m * classes + 1, classes, stride=2)
        c, s = cosine[:classes, m : m + 1], sine_part[:classes, m : m + 1]
        re, im = in_ref[re_rows, :], in_ref[im_rows, :]
        wide_ref[re_rows, :] = re * c + im * s
        wide_ref[im_rows, :] = im * c - re * s
    out_ref[...] = wide_ref[...].astype(bf16)


def turn_references(first, offsets, references):
    padded = -(-offsets.shape[0] // 8) * 8
    return pl.pallas_call(
        turn_kernel,
        in_specs=[
            pl.BlockSpec(memory_space=pltpu.SMEM),
            pl.BlockSpec(memory_space=pltpu.SMEM),
            pl.BlockSpec(memory_space=pltpu.VMEM),
        ],
        out_shape=[
            jax.ShapeDtypeStruct(references.shape, bf16),
            jax.ShapeDtypeStruct((padded, LANES), f32),
        ],
        scratch_shapes=[pltpu.VMEM(references.shape, f32)] * 2,
        compiler_params=pltpu.CompilerParams(vmem_limit_bytes=VMEM_LIMIT),
        name="turn_references",
    )(first, offsets, references)


def correlate_kernel(*refs, slots, classes, padded, finish):
    part_ref, refs = refs[slots], refs[slots + 1 :]
    weighted_refs, refs = refs[:slots], refs[slots:]
    piece_refs, refs = refs[:slots], refs[slots:]
    if finish:
        before_ref, power_before_ref, ctf_ref, weight_ref, stat_ref, share_ref = refs[:6]
        corr_ref, wide_ref, power_ref = refs[6:]
    else:
        corr_ref, power_ref, wide_ref = refs
    group = pl.program_id(0)
    cycles = piece_refs[0].shape[1]
    queries = weighted_refs[0].shape[2]
    block = piece_refs[0].shape[0]

    @pl.when(group == 0)
    def _():
        wide_ref[:, block:, :] = jnp.zeros((slots, wide_ref.shape[1] - block, cycles), f32)
        power_ref[...] = power_before_ref[...] if finish else jnp.zeros_like(power_ref)

    for j in range(slots):
        wide_ref[j, :block, :] = piece_refs[j][...].astype(f32)
    power = power_ref[...]
    for i in range(GROUP):
        total = before_ref[i, :, :queries] if finish else None
        for j in range(slots):
            re = wide_ref[j, pl.ds(2 * i * classes, padded, stride=2), :]
            im = wide_ref[j, pl.ds(2 * i * classes + 1, padded, stride=2), :]
            power = power + (re * re + im * im)
            left = jnp.concatenate(
                [jnp.concatenate([re, im], 1), jnp.concatenate([-im, re], 1)], 0
            ).astype(bf16)
            part = lax.dot_general(
                left, weighted_refs[j][0, i], (((1,), (1,)), ((), ())), preferred_element_type=f32
            )
            total = part if total is None else total + part
        row = group * GROUP + i if finish else i
        corr_ref[row, :, :queries] = total
    power_ref[...] = power

    if not finish:
        return

    @pl.when(group == pl.num_programs(0) - 1)
    def _():
        count = ctf_ref.shape[0]
        angles = ROTS * ANG_STEP
        used = SHIFTS * count
        tiles = weight_ref.shape[2] // LANES
        ctf_row = ctf_ref[...]
        ctf_rows = jnp.concatenate([ctf_row * ctf_row] * (LANES // count), 0)
        bias = lax.dot_general(
            power_ref[...],
            ctf_rows,
            (((1,), (1,)), ((), ())),
            precision=lax.Precision.HIGHEST,
            preferred_element_type=f32,
        ) * (0.5 / angles)
        wide_ref[0, :padded, :] = bias
        rows_of = lambda base: lax.broadcasted_iota(jnp.int32, (8, LANES), 0) + base
        lanes_of = lambda base: lax.broadcasted_iota(jnp.int32, (8, LANES), 1) + base

        peak = jnp.full((8, LANES), -1e30, f32)
        for tile in range(tiles):
            lanes = slice(tile * LANES, (tile + 1) * LANES)

            def scores(n, peak):
                start = pl.multiple_of(n * 8, 8)
                rows = pl.ds(start, 8)
                low = pl.ds(padded + start, 8)
                valid = (rows_of(start) < classes) & (lanes_of(tile * LANES) < used)
                even_values = [corr_ref[0, rows, lanes]]
                odd_values = [None]
                for m in range(1, ROTS // 2):
                    even_values.append(corr_ref[m, rows, lanes] + corr_ref[ROTS - m, rows, lanes])
                    odd_values.append(corr_ref[m, low, lanes] - corr_ref[ROTS - m, low, lanes])
                even_values.append(corr_ref[ROTS // 2, rows, lanes])
                odd_values.append(None)
                cos_sums, sin_sums = half_dft(even_values, odd_values)
                bias = wide_ref[0, rows, :]
                for k in range(FOLD):
                    if k in (0, FOLD - 1):
                        results = [(k, cos_sums[k])]
                    else:
                        results = [(k, cos_sums[k] - sin_sums[k]), (ROTS - k, cos_sums[k] + sin_sums[k])]
                    for place, value in results:
                        value = jnp.where(valid, value * (1.0 / angles) - bias, -1e30)
                        weight_ref[place, rows, lanes] = value
                        peak = jnp.maximum(peak, value)
                return peak

            peak = lax.fori_loop(0, padded // 8, scores, peak)

        peak = jnp.broadcast_to(jnp.max(peak, axis=0, keepdims=True), (8, LANES))
        step = count
        while step < LANES:
            peak = jnp.maximum(peak, pltpu.roll(peak, step, 1))
            step *= 2
        stat_ref[0:8, :] = peak

        def masses(n, whole):
            rows = pl.ds(pl.multiple_of(n * 8, 8), 8)
            mass = jnp.zeros((8, LANES), f32)
            for tile in range(tiles):
                lanes = slice(tile * LANES, (tile + 1) * LANES)
                for k in range(ROTS):
                    value = jnp.exp(weight_ref[k, rows, lanes] - peak)
                    weight_ref[k, rows, lanes] = value
                    mass = mass + value
            step = count
            while step < LANES:
                mass = mass + pltpu.roll(mass, step, 1)
                step *= 2
            stat_ref[pl.ds(pl.multiple_of(8 + n * 8, 8), 8), :] = mass
            return whole + mass

        whole = lax.fori_loop(0, padded // 8, masses, jnp.zeros((8, LANES), f32))
        share = jnp.concatenate([peak[:1], jnp.sum(whole, axis=0, keepdims=True)], 0)
        for j in range(share_ref.shape[0]):
            share_ref[j] = jnp.where(part_ref[0] == j, share, 0.0)


def correlate(slot_of, weighted, pieces, classes, part, before=None, power=None, ctf_rows=None, parts=1):
    _, _, queries, double = weighted.shape
    cycles = double // 2
    slots = len(pieces)
    padded = -(-classes // 8) * 8
    wide_lanes = -(-queries // LANES) * LANES
    block = 2 * GROUP * classes
    finish = ctf_rows is not None
    full = lambda shape: pl.BlockSpec(shape, lambda g, *u: (0,) * len(shape))
    in_specs = [
        pl.BlockSpec((1, GROUP, queries, double), functools.partial(lambda j, g, *u: (u[j][0], g, 0, 0), j))
        for j in range(slots)
    ] + [pl.BlockSpec((block, cycles), lambda g, *u: (g, 0))] * slots
    corr_block = pl.BlockSpec((GROUP, 2 * padded, wide_lanes), lambda g, *u: (g, 0, 0))
    corr_shape = (ROTS, 2 * padded, wide_lanes)
    wide = pltpu.VMEM((slots, block + ROWS, cycles), f32)
    scalars = [jnp.reshape(n, (1,)).astype(jnp.int32) for n in (*slot_of, part)]
    operands = scalars + [weighted] * slots + list(pieces)
    if finish:
        in_specs += [corr_block, full((padded, cycles)), full(ctf_rows.shape)]
        operands += [before, power, ctf_rows]
        out_shapes = [(ROTS, padded, wide_lanes), (8 + padded, LANES), (parts, 2, LANES)]
        out_specs = [full(shape) for shape in out_shapes]
        scratch = [pltpu.VMEM(corr_shape, f32), wide, pltpu.VMEM((padded, cycles), f32)]
    else:
        out_shapes = [corr_shape, (padded, cycles)]
        out_specs = [corr_block, full((padded, cycles))]
        scratch = [wide]
    return pl.pallas_call(
        functools.partial(correlate_kernel, slots=slots, classes=classes, padded=padded, finish=finish),
        grid_spec=pltpu.PrefetchScalarGridSpec(
            num_scalar_prefetch=len(scalars),
            grid=(ROTS // GROUP,),
            in_specs=in_specs,
            out_specs=out_specs,
            scratch_shapes=scratch,
        ),
        out_shape=[jax.ShapeDtypeStruct(shape, f32) for shape in out_shapes],
        compiler_params=pltpu.CompilerParams(vmem_limit_bytes=VMEM_LIMIT),
        name="scores" if finish else "correlate",
    )(*operands)


def back_kernel(weight_ref, stat_ref, share_ref, offset_ref, out_ref, evidence_ref, posterior_ref, sum_ref):
    padded = weight_ref.shape[1]
    queries = out_ref.shape[2]
    shares = [share_ref[j] for j in range(share_ref.shape[0])]
    top = shares[0][:1]
    for share in shares[1:]:
        top = jnp.maximum(top, share[:1])
    mass = sum(share[1:] * jnp.exp(share[:1] - top) for share in shares)
    evidence = jnp.broadcast_to(top + jnp.log(mass), (8, LANES))
    scale = jnp.exp(stat_ref[:8, :] - evidence)
    evidence_ref[...] = evidence
    posterior_ref[...] = stat_ref[8:, :] * scale[:1]
    for tile in range(weight_ref.shape[2] // LANES):
        lanes = slice(tile * LANES, (tile + 1) * LANES)

        def transform(n, carry):
            start = pl.multiple_of(n * 8, 8)
            rows = pl.ds(start, 8)
            low = pl.ds(padded + start, 8)
            values = [weight_ref[k, rows, lanes] * scale for k in range(ROTS)]
            even_values = [values[0]] + [values[k] + values[ROTS - k] for k in range(1, ROTS // 2)]
            odd_values = [None] + [values[k] - values[ROTS - k] for k in range(1, ROTS // 2)] + [None]
            cos_sums, sin_sums = half_dft(even_values + [values[ROTS // 2]], odd_values)
            for m in range(FOLD):
                sine_part = jnp.zeros_like(scale) if m in (0, FOLD - 1) else sin_sums[m]
                sum_ref[m, rows, lanes] = cos_sums[m]
                sum_ref[m, low, lanes] = sine_part
            return carry

        lax.fori_loop(0, padded // 8, transform, 0)

    step_cos, step_sin = cos_sin_of_turns(offset_ref[...] * (1.0 / (ROTS * ANG_STEP)))

    def turn(m, carry):
        cosine, sine_part = carry
        place = jnp.minimum(m, ROTS - m)
        sign = jnp.where(m < FOLD, 1.0, -1.0).astype(f32)
        for tile in range(weight_ref.shape[2] // LANES):
            lanes = slice(tile * LANES, (tile + 1) * LANES)
            kept = slice(tile * LANES, min((tile + 1) * LANES, queries))
            re, im = sum_ref[place, :padded, lanes], sum_ref[place, padded:, lanes] * sign
            turned = jnp.concatenate([re * cosine - im * sine_part, re * sine_part + im * cosine], 0)
            out_ref[m, :, kept] = turned[:, : kept.stop - kept.start].astype(bf16)
        return cosine * step_cos - sine_part * step_sin, sine_part * step_cos + cosine * step_sin

    lax.fori_loop(0, ROTS, turn, (jnp.ones_like(step_cos), jnp.zeros_like(step_cos)))


def make_back(weights, stat, shares, offsets, queries):
    _, padded, wide_lanes = weights.shape
    return pl.pallas_call(
        back_kernel,
        out_shape=[
            jax.ShapeDtypeStruct((ROTS, 2 * padded, queries), bf16),
            jax.ShapeDtypeStruct((8, LANES), f32),
            jax.ShapeDtypeStruct((padded, LANES), f32),
        ],
        scratch_shapes=[pltpu.VMEM((FOLD, 2 * padded, wide_lanes), f32)],
        compiler_params=pltpu.CompilerParams(vmem_limit_bytes=VMEM_LIMIT),
        name="back",
    )(weights, stat, shares, offsets)


def sums_kernel(*refs, count, classes):
    slot_refs, (back_ref, *refs) = refs[:count], refs[count:]
    weighted_refs, (offset_ref, *refs) = refs[:count], refs[count:]
    out_refs, wide_refs = refs[:count], refs[count:]
    padded = offset_ref.shape[0]
    cycles = wide_refs[0].shape[1]
    turns = [
        cos_sin_of_turns(offset_ref[...] * (slot_ref[0].astype(f32) * (1.0 / ANG_STEP)))
        for slot_ref in slot_refs
    ]
    for i in range(GROUP):
        for (cosine, sine_part), weighted_ref, wide_ref in zip(turns, weighted_refs, wide_refs):
            product = jnp.dot(back_ref[i], weighted_ref[0, i], preferred_element_type=f32)
            re = product[:padded, :cycles] - product[padded:, cycles:]
            im = product[:padded, cycles:] + product[padded:, :cycles]
            start = 2 * i * classes
            wide_ref[pl.ds(start, classes, stride=2), :] = (re * cosine - im * sine_part)[:classes]
            wide_ref[pl.ds(start + 1, classes, stride=2), :] = (re * sine_part + im * cosine)[:classes]
    for out_ref, wide_ref in zip(out_refs, wide_refs):
        out_ref[...] = wide_ref[...].astype(out_ref.dtype)


def class_sums_of(slots, back, weighted, offsets, classes, dtypes, groups=(0, ROTS // GROUP)):
    begin, end = groups
    _, _, queries, double = weighted.shape
    cycles = double // 2
    rows = back.shape[1]
    block = 2 * GROUP * classes
    count = len(slots)
    scalars = [jnp.reshape(slot, (1,)).astype(jnp.int32) for slot in slots]
    return pl.pallas_call(
        functools.partial(sums_kernel, count=count, classes=classes),
        grid_spec=pltpu.PrefetchScalarGridSpec(
            num_scalar_prefetch=count,
            grid=(end - begin,),
            in_specs=[pl.BlockSpec((GROUP, rows, queries), lambda g, *u: (g + begin, 0, 0))]
            + [
                pl.BlockSpec(
                    (1, GROUP, queries, double),
                    functools.partial(lambda j, g, *u: (u[j][0], g + begin, 0, 0), j),
                )
                for j in range(count)
            ]
            + [pl.BlockSpec(offsets.shape, lambda g, *u: (0, 0))],
            out_specs=[pl.BlockSpec((block, cycles), lambda g, *u: (g, 0))] * count,
            scratch_shapes=[pltpu.VMEM((block, cycles), f32)] * count,
        ),
        out_shape=[jax.ShapeDtypeStruct(((end - begin) * block, cycles), dtype) for dtype in dtypes],
        compiler_params=pltpu.CompilerParams(vmem_limit_bytes=VMEM_LIMIT),
        name="class_sums",
    )(*scalars, back, *[weighted] * count, offsets)


def across(piece):
    return lax.ppermute(piece, "dp", [(d, d ^ 1) for d in range(8)])


def along(piece, pairs):
    return lax.ppermute(piece, "dp", [(2 * a + x, 2 * b + x) for a, b in pairs for x in range(2)])


def gather_on_line(piece, base, ctf_rows):
    index = lax.axis_index("dp")
    line, side = index // 2, index % 2
    _, steps = spectra_steps(base.shape[0])
    cuts = [0, 3 * steps // 13, 8 * steps // 13, steps]

    own_crossed = across(piece)
    near = along(piece, ((0, 1), (1, 0), (2, 3), (3, 2)))
    middle = along(piece, ((1, 2), (2, 1)))
    weighted = make_spectra(base, ctf_rows, cuts[0], cuts[1])
    weighted, own_crossed = lax.optimization_barrier((weighted, own_crossed))
    weighted, near, middle = lax.optimization_barrier((weighted, near, middle))
    near_crossed = across(near)
    far_middle = along(near, ((1, 2), (2, 1)))
    end = along(middle, ((1, 0), (2, 3)))
    weighted = make_spectra(base, ctf_rows, cuts[1], cuts[2], weighted)
    weighted, end = lax.optimization_barrier((weighted, end))
    weighted, near_crossed = lax.optimization_barrier((weighted, near_crossed))
    weighted, far_middle = lax.optimization_barrier((weighted, far_middle))
    third = middle + end
    third_crossed = across(third)
    far_end = along(far_middle, ((1, 0), (2, 3)))
    weighted = make_spectra(base, ctf_rows, cuts[2], cuts[3], weighted)
    weighted, far_end, third_crossed = lax.optimization_barrier((weighted, far_end, third_crossed))
    fourth = far_middle + far_end
    fourth_crossed = across(fourth)

    pieces = [piece, own_crossed, near, near_crossed, third, third_crossed, fourth, fourth_crossed]
    places = [line, line ^ 1, jnp.where(line < 2, 2, 1), jnp.where(line < 2, 3, 0)]
    slot_of = [2 * place + s for place in places for s in (side, 1 - side)]
    return weighted, pieces, slot_of


def reduce_on_line(back, weighted, offsets, classes):
    index = lax.axis_index("dp")
    line, side = index // 2, index % 2
    order = [jnp.where(line < 2, 3, 0), jnp.where(line < 2, 2, 1), line ^ 1, line]
    theirs = [2 * z + 1 - side for z in order]
    ours = [2 * z + side for z in order]
    groups = ((0, 1), (1, ROTS // GROUP))
    block = 2 * GROUP * classes
    head, rest = [slice(a * block, b * block) for a, b in groups]
    to_middle, between = ((0, 1), (3, 2)), ((1, 2), (2, 1))
    neighbours = ((0, 1), (1, 0), (2, 3), (3, 2))

    def sums(slots, dtypes, back, some=(0, ROTS // GROUP)):
        return class_sums_of(slots, back, weighted, offsets, classes, dtypes, some)

    def wide(piece):
        return piece.astype(f32)

    def then(back, *done):
        return lax.optimization_barrier((back, *done))[0]

    (away,) = sums(theirs[:1], [bf16], back, groups[0])
    crossed_head = across(away)
    back = then(back, away)
    (away,) = sums(theirs[:1], [bf16], back, groups[1])
    crossed_rest = across(away)
    back = then(back, away)
    own_0, away = sums([ours[0], theirs[1]], [f32, bf16], back)
    crossed_1 = across(away)
    crossed_head, own_0 = lax.optimization_barrier((crossed_head, own_0))
    message = (own_0[head] + wide(crossed_head)).astype(bf16)
    first_head = along(message, to_middle)
    back = then(back, message)
    own_1, away = sums([ours[1], theirs[2]], [f32, bf16], back)
    crossed_2 = across(away)
    crossed_rest, own_1 = lax.optimization_barrier((crossed_rest, own_1))
    message = (own_0[rest] + wide(crossed_rest)).astype(bf16)
    first_rest = along(message, to_middle)
    back = then(back, message)
    first_head = then(first_head, message)
    message = (own_0[head] + wide(crossed_head) + wide(first_head)).astype(bf16)
    middle_head = along(message, between)
    back = then(back, message)
    own_2, away = sums([ours[2], theirs[3]], [f32, bf16], back)
    crossed_3 = across(away)
    crossed_1, middle_head, own_2 = lax.optimization_barrier((crossed_1, middle_head, own_2))
    message = (own_1 + wide(crossed_1)).astype(bf16)
    from_end = along(message, to_middle)
    first_rest = then(first_rest, message)
    message = (own_0[rest] + wide(crossed_rest) + wide(first_rest)).astype(bf16)
    middle_rest = along(message, between)
    back = then(back, message)
    (own_3,) = sums(ours[3:], [f32], back)
    from_end = then(from_end, crossed_2)
    message = (own_1 + wide(crossed_1) + wide(from_end)).astype(bf16)
    third = along(message, between)
    middle_rest = then(middle_rest, message)
    middle = jnp.concatenate([middle_head, middle_rest], 0)
    last = along((own_2 + wide(crossed_2) + wide(middle)).astype(bf16), neighbours)
    return own_3 + wide(crossed_3) + wide(third) + wide(last)


def local(particles, references, ctf_table, rot_offset, prior_shift, defocus_group):
    count, _, angles, cycles = particles.shape
    own_rows, _, classes, _ = references.shape
    slots = angles // ROTS
    group_count = ctf_table.shape[0]
    devices = lax.axis_size("dp")

    first = (lax.axis_index("dp") * own_rows).astype(jnp.int32).reshape(1)
    rows = jnp.transpose(references, (0, 2, 1, 3)).reshape(own_rows * 2 * classes, cycles)
    piece, offsets = turn_references(first, rot_offset, rows)

    onehot = (defocus_group[:, None] == jnp.arange(group_count, dtype=jnp.int32)[None, :]).astype(f32)
    ctf_rows = jnp.dot(onehot, ctf_table, precision=lax.Precision.HIGHEST)
    base = make_base(particles, prior_shift)
    on_line = devices == 8 and own_rows == ROTS
    if on_line:
        weighted, pieces, slot_of = gather_on_line(piece, base, ctf_rows)
    else:
        gathered = lax.all_gather(piece, "dp", axis=0, tiled=True)
        gathered = gathered.reshape(slots, ROTS * 2 * classes, cycles)
        pieces = [gathered[j] for j in range(slots)]
        slot_of = list(range(slots))
        weighted = make_spectra(base, ctf_rows, 0, spectra_steps(count)[1])
    queries = weighted.shape[1]
    weighted = weighted.reshape(slots, ROTS, queries, 2 * cycles)

    early = slots - 1
    part = lax.axis_index("cls")
    corr, power = correlate(slot_of[:early], weighted, pieces[:early], classes, part)
    weights, stat, share = correlate(
        slot_of[early:], weighted, pieces[early:], classes, part, corr, power, ctf_rows, lax.axis_size("cls")
    )
    shares = lax.psum(share, "cls")
    back, evidence, posterior = make_back(weights, stat, shares, offsets, queries)
    log_evidence = evidence[0, :count]
    class_posterior = posterior[:classes, :count].T
    if on_line:
        class_rows = reduce_on_line(back, weighted, offsets, classes)
    else:
        sums = [class_sums_of([u], back, weighted, offsets, classes, [bf16])[0] for u in slot_of]
        summed = lax.psum_scatter(jnp.concatenate(sums, 0), "dp", scatter_dimension=0, tiled=True)
        class_rows = summed.astype(f32)
    class_sums = jnp.transpose(class_rows.reshape(own_rows, classes, 2, cycles), (0, 2, 1, 3))
    return (log_evidence, class_posterior, class_sums)


def solution(mesh):
    placed = (
        P("dp", None, None, None),
        P("dp", None, "cls", None),
        P(),
        P("cls"),
        P("dp", None),
        P("dp"),
    )
    return jax.shard_map(
        local,
        mesh=mesh,
        in_specs=placed,
        out_specs=(P("dp"), P("dp", "cls"), P("dp", None, "cls", None)),
        check_vma=False,
    )
```
